32 devices in a mesh: dp: 8 (over z, x), tensor: 4 (over y, core).
Axes of the slice: x: 2, y: 2, z: 4, core: 2. Of those that a mesh axis runs over, the one named last changes fastest.
Arguments:
- resid: float32 [8192, 768], P('dp'), may hold values from -6 to 6
- cotangent: float32 [8192, 768], P('dp'), may hold values from -6 to 6
- master_in: float32 [1, 768, 7, 768], P(None, 'dp', None, 'tensor'), may hold values from -0.21875 to 0.21875
- moment1_in: float32 [1, 768, 7, 768], P(None, 'dp', None, 'tensor'), may hold values from -8192 to 8192
- moment2_in: float32 [1, 768, 7, 768], P(None, 'dp', None, 'tensor'), may hold values from 0 to 8192
- master_out: float32 [1, 5, 768, 768], P(None, None, 'tensor', 'dp'), may hold values from -0.875 to 0.875
- moment1_out: float32 [1, 5, 768, 768], P(None, None, 'tensor', 'dp'), may hold values from -8192 to 8192
- moment2_out: float32 [1, 5, 768, 768], P(None, None, 'tensor', 'dp'), may hold values from 0 to 8192
- master_bias: float32 [1, 6, 768], P(None, None, 'tensor'), may hold values from -3 to 3
- moment1_bias: float32 [1, 6, 768], P(None, None, 'tensor'), may hold values from -8192 to 8192
- moment2_bias: float32 [1, 6, 768], P(None, None, 'tensor'), may hold values from 0 to 8192
- master_vec: float32 [1, 6, 768], replicated, may hold values from -1.2 to 1.3, as said below
- moment1_vec: float32 [1, 6, 768], replicated, may hold values from -8192 to 8192
- moment2_vec: float32 [1, 6, 768], replicated, may hold values from 0 to 8192
Outputs:
- out_stream: float32 [8192, 768], P(('dp', 'tensor'))
- grad_stream: float32 [8192, 768], P(('dp', 'tensor'))
- new_moment1_in: float32 [1, 768, 7, 768], P(None, 'dp', None, 'tensor')
- new_moment2_in: float32 [1, 768, 7, 768], P(None, 'dp', None, 'tensor')
- new_master_in: float32 [1, 768, 7, 768], P(None, 'dp', None, 'tensor')
- new_moment1_out: float32 [1, 5, 768, 768], P(None, None, 'tensor', 'dp')
- new_moment2_out: float32 [1, 5, 768, 768], P(None, None, 'tensor', 'dp')
- new_master_out: float32 [1, 5, 768, 768], P(None, None, 'tensor', 'dp')
- new_moment1_bias: float32 [1, 6, 768], P(None, None, 'tensor')
- new_moment2_bias: float32 [1, 6, 768], P(None, None, 'tensor')
- new_master_bias: float32 [1, 6, 768], P(None, None, 'tensor')
- new_moment1_vec: float32 [1, 6, 768], replicated
- new_moment2_vec: float32 [1, 6, 768], replicated
- new_master_vec: float32 [1, 6, 768], replicated
The draws below stay inside these ranges and needn't reach their ends.
Inputs may be any that keep to these rules, and one draw needn't show every extreme that they name: `master_vec`: rows 0 and 2 of each block lie within 0.7 to 1.3.
All inputs are finite; a program needn't handle non-finite values.
Results may differ from the reference program's by a relative error of at most 0.014.
Values may be sent and summed in bfloat16 or wider, within the bound.
A program may use at most 128 MiB of HBM per device.

```python
import math
import jax
import jax.numpy as jnp
from jax import lax

D = 768
HD = 64
SEQ_DEV = 1
LEN = 1024
LAYERS = 1
STEP = 10
TOKENS = 8192
N_DP = 8
N_TENSOR = 4


COEF_IN = [0.05, 0.05, 0.2, 0.3, 0.3, 0.3, 0.3]


COEF_OUT = [0.05, 0.06, 0.06, 0.06, 0.06]


COEF_BIAS = [0.05, 0.2, 0.3, 0.3, 0.3, 0.3]


COEF_VEC = [0.4, 0.4, 0.6, 0.6, 0.15, 0.15]


def moment_draw(key, shape, coefs, axis_pos, power):
    view = [1] * len(shape)
    view[axis_pos] = len(coefs)
    scale = (jnp.asarray(coefs, jnp.float32) * math.sqrt(TOKENS)).reshape(view)
    if power == 1:
        return 0.111 * scale * jnp.clip(jax.random.normal(key, shape, jnp.float32), -4.0, 4.0)
    factor = jnp.exp(jax.random.uniform(key, shape, jnp.float32, 0.0, math.log(4.0)))
    return 0.0526 * scale * scale * factor


def draw_moment1_in(key, part):
    key = jax.random.fold_in(key, 11)
    return moment_draw(key, (LAYERS, D, 7, D), COEF_IN, 2, 1)


def draw_moment2_in(key, part):
    key = jax.random.fold_in(key, 12)
    return moment_draw(key, (LAYERS, D, 7, D), COEF_IN, 2, 2)


def draw_moment1_out(key, part):
    key = jax.random.fold_in(key, 13)
    return moment_draw(key, (LAYERS, 5, D, D), COEF_OUT, 1, 1)


def draw_moment2_out(key, part):
    key = jax.random.fold_in(key, 14)
    return moment_draw(key, (LAYERS, 5, D, D), COEF_OUT, 1, 2)


def draw_moment1_bias(key, part):
    key = jax.random.fold_in(key, 15)
    return moment_draw(key, (LAYERS, 6, D), COEF_BIAS, 1, 1)


def draw_moment2_bias(key, part):
    key = jax.random.fold_in(key, 16)
    return moment_draw(key, (LAYERS, 6, D), COEF_BIAS, 1, 2)


def draw_moment1_vec(key, part):
    key = jax.random.fold_in(key, 17)
    return moment_draw(key, (LAYERS, 6, D), COEF_VEC, 1, 1)


def draw_moment2_vec(key, part):
    key = jax.random.fold_in(key, 18)
    return moment_draw(key, (LAYERS, 6, D), COEF_VEC, 1, 2)


def draw_master_vec(key, part):
    key = jax.random.fold_in(key, 19)
    gain_key, shift_key = jax.random.split(key)
    gains = 1.0 + 0.3 * jax.random.uniform(gain_key, (LAYERS, 6, D), jnp.float32, -1.0, 1.0)
    shifts = jnp.clip(0.3 * jax.random.normal(shift_key, (LAYERS, 6, D), jnp.float32), -1.2, 1.2)
    row_ids = jnp.arange(6).reshape(1, 6, 1)
    is_gain = (row_ids == 0) | (row_ids == 2)
    return jnp.where(is_gain, gains, shifts)


def shard_levels(own_key, shape, shards, smallest, largest):
    level, own = 1.0, jax.random.fold_in(own_key, 6)
    for position, parts in shards:
        steps = jnp.exp(jax.random.uniform(jax.random.fold_in(own, position), (parts,), jnp.float32, smallest / len(shards), largest / len(shards)))
        level = level * jnp.repeat(steps, shape[position] // parts).reshape([-1 if axis == position else 1 for axis in range(len(shape))])
    return level


def gaussian(rng, extent, spread, reach, cuts=(), kind=jnp.bfloat16):
    values = jax.random.normal(rng, extent, jnp.float32) * spread
    if len(cuts) > 0:
        values = shard_levels(rng, extent, cuts, -0.22, 0.18) * values
    return jnp.clip(values, min=-reach, max=reach).astype(kind)


def setup_inputs(seed: int = 0) -> dict:
    seeds = jax.random.split(jax.random.key(seed), 15)
    return {
        "resid": gaussian(seeds[0], (TOKENS, D), 1.0, 6.0, ((0, 8),), jnp.float32),
        "cotangent": gaussian(seeds[1], (TOKENS, D), 1.0, 6.0, ((0, 8),), jnp.float32),
        "master_in": gaussian(seeds[2], (LAYERS, D, 7, D), D ** -0.5, 0.21875, ((1, 8), (3, 4)), jnp.float32),
        "moment1_in": draw_moment1_in(jax.random.fold_in(seeds[14], 71), 0),
        "moment2_in": draw_moment2_in(jax.random.fold_in(seeds[14], 71), 0),
        "master_out": gaussian(seeds[5], (LAYERS, 5, D, D), (D // 16) ** -0.5, 0.875, ((2, 4), (3, 8)), jnp.float32),
        "moment1_out": draw_moment1_out(jax.random.fold_in(seeds[14], 71), 0),
        "moment2_out": draw_moment2_out(jax.random.fold_in(seeds[14], 71), 0),
        "master_bias": gaussian(seeds[8], (LAYERS, 6, D), 0.5, 3.0, ((2, 4),), jnp.float32),
        "moment1_bias": draw_moment1_bias(jax.random.fold_in(seeds[14], 71), 0),
        "moment2_bias": draw_moment2_bias(jax.random.fold_in(seeds[14], 71), 0),
        "master_vec": draw_master_vec(jax.random.fold_in(seeds[14], 71), 0),
        "moment1_vec": draw_moment1_vec(jax.random.fold_in(seeds[14], 71), 0),
        "moment2_vec": draw_moment2_vec(jax.random.fold_in(seeds[14], 71), 0),
    }


EPS = 1e-05
BRANCH_SCALE = 48 ** (-0.5)
BETA_ONE = 0.9
BETA_TWO = 0.95
ADAM_EPS = 1e-08
DECAY = 0.1
SMALL_RATE = 0.3
MASKED = -1e+30
HIGH = lax.Precision.HIGHEST

@jax.custom_vjp
def low(v):
    return lax.optimization_barrier(v.astype(jnp.bfloat16)).astype(jnp.float32)

@jax.custom_vjp
def low_back(v):
    return v

def low_keep(v):
    return (low(v), None)

def low_pass(kept, grad):
    return (grad,)

def back_keep(v):
    return (v, None)

def back_low(kept, grad):
    return (low(grad),)
low.defvjp(low_keep, low_pass)
low_back.defvjp(back_keep, back_low)

def matmul(left, right):
    return jnp.dot(left, right, precision=HIGH)

def rounded(value):
    return low(low_back(value))

def layer_norm(stream, gain, shift):
    center = stream - lax.optimization_barrier(jnp.mean(stream, -1, keepdims=True))
    inverse = lax.rsqrt(lax.optimization_barrier(jnp.mean(center * center, -1, keepdims=True)) + EPS)
    return center * inverse * gain + shift

def attention(queries, key_rows, value_rows, seq_count):
    heads = queries.shape[1] // HD
    shape4 = (seq_count, LEN, heads, HD)
    scores = jnp.einsum('sqhd,skhd->shqk', queries.reshape(shape4), key_rows.reshape(shape4), precision=HIGH) * HD ** (-0.5)
    scores = low_back(scores)
    positions = jnp.arange(LEN)
    causal = positions[:, None] >= positions[None, :]
    scores = jnp.where(causal, scores, MASKED)
    weights = low(jax.nn.softmax(scores, -1))
    mixed = jnp.einsum('shqk,skhd->sqhd', weights, value_rows.reshape(shape4), precision=HIGH)
    return mixed.reshape(seq_count * LEN, heads * HD)

def layer_forward(stream, w_in, w_out, bias, vector):
    seq_count = stream.shape[0] // LEN
    head_cols = D // N_TENSOR
    normed = low(layer_norm(stream, vector[0], vector[1]))
    attn_total = jnp.zeros_like(stream)
    for group_idx in range(N_TENSOR):
        col_range = slice(group_idx * head_cols, (group_idx + 1) * head_cols)
        normed_use = low_back(normed)
        queries = rounded(matmul(normed_use, w_in[:, 0, col_range]) + bias[0, col_range])
        key_rows = rounded(matmul(normed_use, w_in[:, 1, col_range]))
        value_rows = rounded(matmul(normed_use, w_in[:, 2, col_range]) + bias[1, col_range])
        mixed = rounded(attention(queries, key_rows, value_rows, seq_count))
        attn_total = attn_total + low(matmul(mixed, w_out[0, col_range, :]))
    attended = low_back(attn_total + vector[4])
    middle = stream + BRANCH_SCALE * attended
    hidden_in = low(layer_norm(middle, vector[2], vector[3]))
    mlp_total = jnp.zeros_like(stream)
    for group_idx in range(N_TENSOR):
        col_range = slice(group_idx * head_cols, (group_idx + 1) * head_cols)
        hidden_use = low_back(hidden_in)
        w_up = w_in[:, 3:7, col_range].reshape(D, 4 * head_cols)
        pre_act = low_back(matmul(hidden_use, w_up) + bias[2:6, col_range].reshape(4 * head_cols))
        activated = rounded(jax.nn.gelu(pre_act, approximate=True))
        w_down = w_out[1:5, col_range, :].reshape(4 * head_cols, D)
        mlp_total = mlp_total + low(matmul(activated, w_down))
    return middle + BRANCH_SCALE * low_back(mlp_total + vector[5])

def adam_step(master, first, second, gradient, rate, decay):
    first_new = BETA_ONE * first + (1 - BETA_ONE) * gradient
    second_new = BETA_TWO * second + (1 - BETA_TWO) * gradient * gradient
    direction = first_new / (1 - BETA_ONE ** STEP) / (jnp.sqrt(second_new / (1 - BETA_TWO ** STEP)) + ADAM_EPS)
    return (first_new, second_new, master - rate * (direction + decay * master))

def reference(resid, cotangent, master_in, moment1_in, moment2_in, master_out, moment1_out, moment2_out, master_bias, moment1_bias, moment2_bias, master_vec, moment1_vec, moment2_vec):
    params = (low(master_in), low(master_out), master_bias, master_vec)

    def network(weights, stream):
        for layer_idx in range(LAYERS):
            stream = layer_forward(stream, weights[0][layer_idx], weights[1][layer_idx], weights[2][layer_idx], weights[3][layer_idx])
        return stream
    total_seqs = SEQ_DEV * N_DP
    per_scan = math.gcd(total_seqs, max(1, 4096 // LEN))
    scan_count = total_seqs // per_scan
    inputs = resid.reshape(scan_count, per_scan * LEN, D)
    incoming = cotangent.reshape(scan_count, per_scan * LEN, D)

    def scan_body(totals, item):
        block_in, block_grad = item
        result, pull = jax.vjp(network, params, block_in)
        param_grads, input_grad = pull(block_grad)
        return (jax.tree.map(jnp.add, totals, param_grads), (result, input_grad))
    zeros = jax.tree.map(jnp.zeros_like, params)
    totals, (outputs, input_grads) = lax.scan(scan_body, zeros, (inputs, incoming))
    first_in, second_in, new_in = adam_step(master_in, moment1_in, moment2_in, totals[0], 0.5 * D ** (-0.5), DECAY)
    first_out, second_out, new_out = adam_step(master_out, moment1_out, moment2_out, totals[1], 2.0 * D ** (-0.5), DECAY)
    first_bias, second_bias, new_bias = adam_step(master_bias, moment1_bias, moment2_bias, totals[2], SMALL_RATE, 0.0)
    first_vec, second_vec, new_vec = adam_step(master_vec, moment1_vec, moment2_vec, totals[3], SMALL_RATE, 0.0)
    return (outputs.reshape(TOKENS, D), input_grads.reshape(TOKENS, D), first_in, second_in, new_in, first_out, second_out, new_out, first_bias, second_bias, new_bias, first_vec, second_vec, new_vec)
```

```python
import functools

import jax
import jax.numpy as jnp
from jax import lax
from jax.experimental import pallas as pl
from jax.experimental.pallas import tpu as pltpu
from jax.sharding import PartitionSpec as P

D = 768
HD = 64
LEN = 1024
LAYERS = 1
STEP = 10


EPS = 1e-05
BRANCH_SCALE = 48 ** (-0.5)
BETA_ONE = 0.9
BETA_TWO = 0.95
ADAM_EPS = 1e-08
DECAY = 0.1
SMALL_RATE = 0.3
MASKED = -1e30


def norm_rows(stream, gain, shift):
    center = stream - jnp.mean(stream, -1, keepdims=True)
    inverse = lax.rsqrt(jnp.mean(center * center, -1, keepdims=True) + EPS)
    scaled = center * inverse
    return (scaled * gain + shift, scaled, inverse)


def norm_back(grad_out, scaled, inverse, gain):
    weighted = grad_out * gain
    centered = weighted - jnp.mean(weighted, -1, keepdims=True)
    return inverse * (centered - scaled * jnp.mean(weighted * scaled, -1, keepdims=True))


def plain_dot(left, right):
    return jnp.dot(left, right, preferred_element_type=jnp.float32)


def left_dot(left, right):
    return lax.dot_general(
        left, right, (((0,), (0,)), ((), ())), preferred_element_type=jnp.float32
    )


def right_dot(left, right):
    return lax.dot_general(
        left, right, (((1,), (1,)), ((), ())), preferred_element_type=jnp.float32
    )


def smooth_gate(values_in):
    return jax.nn.gelu(values_in, approximate=True)


def tensor_rows(array_in):
    quarter = array_in.shape[0] // lax.axis_size("tensor")
    return lax.dynamic_slice_in_dim(array_in, lax.axis_index("tensor") * quarter, quarter, 0)


def own_rows(array_in):
    return tensor_rows(array_in)


def branch_total(partial_sum):
    return lax.psum(partial_sum.astype(jnp.bfloat16), "tensor").astype(jnp.float32)


def grad_total(partial_sum):
    return lax.psum(partial_sum.astype(jnp.bfloat16), "tensor").astype(jnp.float32)


def causal_scores(queries, key_rows, first, last):
    block_rows = last - first
    scores = jnp.einsum(
        "qhd,khd->hqk", queries[first:last], key_rows[:last], preferred_element_type=jnp.float32
    ) * HD ** (-0.5)
    query_pos = lax.broadcasted_iota(jnp.int32, (block_rows, last), 0) + first
    key_pos = lax.broadcasted_iota(jnp.int32, (block_rows, last), 1)
    return jnp.where(query_pos >= key_pos, scores, MASKED)


def attend_sequence(operands):
    queries, key_rows, value_rows = operands
    block_rows = min(512, LEN)
    outputs = []
    totals = []
    for block_idx in range(LEN // block_rows):
        first = block_idx * block_rows
        last = first + block_rows
        scores = causal_scores(queries, key_rows, first, last)
        highest = jnp.max(scores, -1, keepdims=True)
        expo = jnp.exp(scores - highest)
        summed = jnp.sum(expo, -1, keepdims=True)
        weights = (expo / summed).astype(jnp.bfloat16)
        mixed = jnp.einsum(
            "hqk,khd->qhd", weights, value_rows[:last], preferred_element_type=jnp.float32
        )
        outputs.append(mixed.astype(jnp.bfloat16))
        totals.append((highest + jnp.log(summed))[..., 0])
    return (jnp.concatenate(outputs, 0), jnp.concatenate(totals, 1))


def attend_back(operands):
    queries, key_rows, value_rows, log_total, grad_mixed = operands
    block_rows = min(512, LEN)
    d_keys = jnp.zeros(key_rows.shape, jnp.float32)
    d_values = jnp.zeros(value_rows.shape, jnp.float32)
    d_queries = []
    for block_idx in range(LEN // block_rows):
        first = block_idx * block_rows
        last = first + block_rows
        scores = causal_scores(queries, key_rows, first, last)
        probs = jnp.exp(scores - log_total[:, first:last, None])
        d_probs = jnp.einsum(
            "qhd,khd->hqk",
            grad_mixed[first:last],
            value_rows[:last],
            preferred_element_type=jnp.float32,
        )
        inner = jnp.sum(probs * d_probs, -1, keepdims=True)
        d_scores = (probs * (d_probs - inner)).astype(jnp.bfloat16)
        d_queries.append(
            jnp.einsum(
                "hqk,khd->qhd", d_scores, key_rows[:last], preferred_element_type=jnp.float32
            )
            * HD ** (-0.5)
        )
        key_part = jnp.einsum(
            "hqk,qhd->khd", d_scores, queries[first:last], preferred_element_type=jnp.float32
        ) * HD ** (-0.5)
        value_part = jnp.einsum(
            "hqk,qhd->khd",
            probs.astype(jnp.bfloat16),
            grad_mixed[first:last],
            preferred_element_type=jnp.float32,
        )
        d_keys = d_keys.at[:last].add(key_part)
        d_values = d_values.at[:last].add(value_part)
    return (jnp.concatenate(d_queries, 0), d_keys, d_values)


def layer_forward(stream, w_in, w_out, bias, vector):
    model_width = w_in.shape[0]
    head_cols = w_in.shape[2]
    heads_here = head_cols // HD
    normed, scaled_one, inverse_one = norm_rows(stream, vector[0], vector[1])
    normed_low = normed.astype(jnp.bfloat16)
    seq_count = normed_low.shape[0] // LEN
    shape4 = (seq_count, LEN, heads_here, HD)
    w_qkv = w_in[:, 0:3].reshape(model_width, 3 * head_cols)
    projected = plain_dot(normed_low, w_qkv)
    queries = (projected[:, :head_cols] + bias[0]).astype(jnp.bfloat16).reshape(shape4)
    key_rows = projected[:, head_cols : 2 * head_cols].astype(jnp.bfloat16).reshape(shape4)
    value_rows = (projected[:, 2 * head_cols :] + bias[1]).astype(jnp.bfloat16).reshape(shape4)
    mixed, log_total = lax.map(attend_sequence, (queries, key_rows, value_rows))
    mixed_low = mixed.reshape(-1, head_cols)
    attended = branch_total(plain_dot(mixed_low, w_out[0])) + vector[4]
    middle = stream + BRANCH_SCALE * attended
    hidden, scaled_two, inverse_two = norm_rows(middle, vector[2], vector[3])
    hidden_low = hidden.astype(jnp.bfloat16)
    w_up = w_in[:, 3:].reshape(model_width, 4 * head_cols)
    pre_act = plain_dot(hidden_low, w_up) + bias[2:].reshape(4 * head_cols)
    act_low = smooth_gate(pre_act).astype(jnp.bfloat16)
    w_down = w_out[1:].reshape(4 * head_cols, model_width)
    mlp_out = branch_total(plain_dot(act_low, w_down)) + vector[5]
    result = middle + BRANCH_SCALE * mlp_out
    kept = (
        scaled_one,
        inverse_one,
        normed_low,
        queries,
        key_rows,
        value_rows,
        log_total,
        mixed_low,
        scaled_two,
        inverse_two,
        hidden_low,
        pre_act,
        act_low,
    )
    return (result, kept)


def layer_backward(gradient, w_in, w_out, vector, kept):
    (
        scaled_one,
        inverse_one,
        normed_low,
        queries,
        key_rows,
        value_rows,
        log_total,
        mixed_low,
        scaled_two,
        inverse_two,
        hidden_low,
        pre_act,
        act_low,
    ) = kept
    model_width = w_in.shape[0]
    head_cols = w_in.shape[2]
    w_qkv = w_in[:, 0:3].reshape(model_width, 3 * head_cols)
    w_up = w_in[:, 3:].reshape(model_width, 4 * head_cols)
    w_down = w_out[1:].reshape(4 * head_cols, model_width)
    d_mlp = (BRANCH_SCALE * gradient).astype(jnp.bfloat16)
    g_bdown = jnp.sum(own_rows(d_mlp).astype(jnp.float32), 0)
    g_down = left_dot(act_low, d_mlp).reshape(4, head_cols, model_width)
    d_act = right_dot(d_mlp, w_down).astype(jnp.bfloat16)
    gate_value, gate_pull = jax.vjp(smooth_gate, pre_act)
    d_pre = gate_pull(d_act.astype(jnp.float32))[0].astype(jnp.bfloat16)
    g_bup = jnp.sum(d_pre.astype(jnp.float32), 0)
    g_up = left_dot(hidden_low, d_pre).reshape(model_width, 4, head_cols)
    d_hidden = grad_total(right_dot(d_pre, w_up))
    g_gain_two = jnp.sum(own_rows(d_hidden * scaled_two), 0)
    g_shift_two = jnp.sum(own_rows(d_hidden), 0)
    d_middle = gradient + norm_back(d_hidden, scaled_two, inverse_two, vector[2])
    d_attn = (BRANCH_SCALE * d_middle).astype(jnp.bfloat16)
    g_bproj = jnp.sum(own_rows(d_attn).astype(jnp.float32), 0)
    g_proj = left_dot(mixed_low, d_attn)
    d_mixed = right_dot(d_attn, w_out[0]).astype(jnp.bfloat16)
    d_queries, d_keys, d_values = lax.map(
        attend_back, (queries, key_rows, value_rows, log_total, d_mixed.reshape(queries.shape))
    )
    d_qkv = jnp.concatenate(
        [
            d_queries.reshape(-1, head_cols),
            d_keys.reshape(-1, head_cols),
            d_values.reshape(-1, head_cols),
        ],
        1,
    ).astype(jnp.bfloat16)
    g_qkv = left_dot(normed_low, d_qkv).reshape(model_width, 3, head_cols)
    g_bq = jnp.sum(d_qkv[:, :head_cols].astype(jnp.float32), 0)
    g_bv = jnp.sum(d_qkv[:, 2 * head_cols :].astype(jnp.float32), 0)
    d_normed = grad_total(right_dot(d_qkv, w_qkv))
    g_gain_one = jnp.sum(own_rows(d_normed * scaled_one), 0)
    g_shift_one = jnp.sum(own_rows(d_normed), 0)
    d_stream = d_middle + norm_back(d_normed, scaled_one, inverse_one, vector[0])
    g_in = jnp.concatenate([g_qkv, g_up], 1)
    g_out = jnp.concatenate([g_proj[None], g_down], 0)
    g_bias = jnp.concatenate([g_bq[None], g_bv[None], g_bup.reshape(4, head_cols)], 0)
    g_vector = jnp.stack([g_gain_one, g_shift_one, g_gain_two, g_shift_two, g_bproj, g_bdown])
    return (d_stream, g_in, g_out, g_bias, g_vector)


def adam_step(master, first, second, gradient, rate, decay):
    first_new = BETA_ONE * first + (1 - BETA_ONE) * gradient
    second_new = BETA_TWO * second + (1 - BETA_TWO) * gradient * gradient
    direction = (
        first_new / (1 - BETA_ONE**STEP) / (jnp.sqrt(second_new / (1 - BETA_TWO**STEP)) + ADAM_EPS)
    )
    return (first_new, second_new, master - rate * (direction + decay * master))


def shards(
    resid,
    cotangent,
    master_in,
    moment1_in,
    moment2_in,
    master_out,
    moment1_out,
    moment2_out,
    master_bias,
    moment1_bias,
    moment2_bias,
    master_vec,
    moment1_vec,
    moment2_vec,
):
    weights_in, weights_out = (
        lax.all_gather(master_in.astype(jnp.bfloat16), "dp", axis=1, tiled=True),
        lax.all_gather(master_out.astype(jnp.bfloat16), "dp", axis=3, tiled=True),
    )
    stream = resid
    gradient = cotangent
    layer_idx = 0
    stream, kept = layer_forward(
        stream,
        weights_in[layer_idx],
        weights_out[layer_idx],
        master_bias[layer_idx],
        master_vec[layer_idx],
    )
    kept_list = [kept]
    list_in = [None] * LAYERS
    list_out = [None] * LAYERS
    list_bias = [None] * LAYERS
    list_vector = [None] * LAYERS
    layer_idx = 0
    gradient, g_in, g_out, g_bias, g_vector = layer_backward(
        gradient,
        weights_in[layer_idx],
        weights_out[layer_idx],
        master_vec[layer_idx],
        kept_list[layer_idx],
    )
    list_in[layer_idx] = g_in
    list_out[layer_idx] = g_out
    list_bias[layer_idx] = g_bias
    list_vector[layer_idx] = g_vector
    summed_in = jnp.stack(list_in)
    summed_out = jnp.stack(list_out)
    summed_in, summed_out = (
        lax.psum_scatter(summed_in, "dp", scatter_dimension=1, tiled=True),
        lax.psum_scatter(summed_out, "dp", scatter_dimension=3, tiled=True),
    )
    summed_bias = lax.psum(jnp.stack(list_bias), "dp")
    summed_vector = lax.psum(jnp.stack(list_vector), ("dp", "tensor"))
    first_in, second_in, new_in = adam_step(
        master_in, moment1_in, moment2_in, summed_in, 0.5 * D ** (-0.5), DECAY
    )
    first_out, second_out, new_out = adam_step(
        master_out, moment1_out, moment2_out, summed_out, 2.0 * D ** (-0.5), DECAY
    )
    first_bias, second_bias, new_bias = adam_step(
        master_bias, moment1_bias, moment2_bias, summed_bias, SMALL_RATE, 0.0
    )
    first_vec, second_vec, new_vec = adam_step(
        master_vec, moment1_vec, moment2_vec, summed_vector, SMALL_RATE, 0.0
    )
    return (
        own_rows(stream),
        own_rows(gradient),
        first_in,
        second_in,
        new_in,
        first_out,
        second_out,
        new_out,
        first_bias,
        second_bias,
        new_bias,
        first_vec,
        second_vec,
        new_vec,
    )


MESH_IDS = pl.DeviceIdType.MESH
F32 = jnp.float32
BF16 = jnp.bfloat16
NN = (((1,), (0,)), ((), ()))
NT = (((1,), (1,)), ((), ()))
TN = (((0,), (0,)), ((), ()))
GELU_A = (2.0 / 3.141592653589793) ** 0.5
GELU_B = 0.044715


def mm(left, right, dims=NN):
    return lax.dot_general(left, right, dims, preferred_element_type=F32)


def rows_at(start, size, align):
    return pl.ds(pl.multiple_of(start, align), size)


def block_kernel(
    sizes,
    resid_h,
    cot_h,
    win,
    wout,
    bias,
    vec,
    out_o,
    grad_o,
    gsum_o,
    small_o,
    resid,
    cot,
    inv1,
    normed,
    dmlp,
    w,
    q_s,
    k_s,
    v_s,
    e_s,
    linv,
    mixed,
    ps,
    crecv,
    fin,
    ysend,
    yrecv,
    mid,
    xhat2,
    inv2,
    hidden,
    act_s,
    dpre,
    dattn,
    dk_s,
    dv_s,
    dqkv,
    gmat,
    xr,
    zs,
    zr,
    sm,
    smx,
    smz,
    smy,
    smc,
    lsem,
    ssem,
    rsem,
):
    tokens, width, quarter, heads, shard = sizes
    dp = lax.axis_index("dp")
    ten = lax.axis_index("tensor")
    z = lax.div(dp, 2)
    x = lax.rem(dp, 2)
    y = lax.div(ten, 2)
    c = lax.rem(ten, 2)
    x_dev = (dp + 1 - 2 * x, ten)
    c_dev = (dp, ten + 1 - 2 * c)
    y_dev = (dp, ten + 2 - 4 * y)

    def z_other(j):
        if j == 1:
            return z + 1 - 2 * lax.rem(z, 2)
        if j == 2:
            return lax.rem(z + 2, 4)
        return 3 - z

    def z_dev(j):
        return (2 * z_other(j) + x, ten)

    def rcopy(src, dst, idx, dev):
        return pltpu.make_async_remote_copy(
            src_ref=src,
            dst_ref=dst,
            send_sem=ssem.at[idx],
            recv_sem=rsem.at[idx],
            device_id=dev,
            device_id_type=MESH_IDS,
        )

    barrier = pltpu.get_barrier_semaphore()
    peers = [x_dev, c_dev, y_dev, z_dev(1), z_dev(2), z_dev(3)]
    for dev in peers:
        pl.semaphore_signal(barrier, inc=1, device_id=dev, device_id_type=MESH_IDS)
    load_resid = pltpu.make_async_copy(resid_h, resid, lsem.at[0])
    load_cot = pltpu.make_async_copy(cot_h, cot, lsem.at[1])
    load_resid.start()
    load_cot.start()

    mine = rows_at(dp * shard, shard, shard)
    wout_t = [jnp.transpose(wout[i]) for i in range(5)]
    w[0, mine, :] = jnp.concatenate([win[0], win[1], win[2], wout_t[0]], 1).astype(BF16)
    w[1, mine, :] = jnp.concatenate([win[3 + i] for i in range(4)], 1).astype(BF16)
    w[2, mine, :] = jnp.concatenate(wout_t[1:], 1).astype(BF16)

    pl.semaphore_wait(barrier, len(peers))

    def piece(b, owner):
        return w.at[b, rows_at(owner * shard, shard, shard), :]

    def ag_x(b):
        return rcopy(piece(b, dp), piece(b, dp), b, x_dev)

    def ag_z(b, j):
        return rcopy(piece(b, dp), piece(b, dp), 3 + 3 * b + j - 1, z_dev(j))

    def ag_f(b, j):
        owner = 2 * z_other(j) + x
        return rcopy(piece(b, owner), piece(b, owner), 12 + 3 * b + j - 1, x_dev)

    def ag_start(b):
        for j in (1, 2, 3):
            ag_z(b, j).start()
        ag_x(b).start()

    def ag_forward(b):
        for j in (1, 2, 3):
            ag_z(b, j).wait_recv()
            ag_f(b, j).start()

    def ag_finish(b):
        ag_x(b).wait_recv()
        for j in (1, 2, 3):
            ag_f(b, j).wait_recv()

    def ag_drain(b):
        ag_x(b).wait_send()
        for j in (1, 2, 3):
            ag_z(b, j).wait_send()
            ag_f(b, j).wait_send()

    ag_start(0)

    load_resid.wait()
    load_cot.wait()
    gain_one, shift_one = vec[0:1, :], vec[1:2, :]

    own = rows_at(ten * quarter, quarter, quarter)
    mid[...] = resid[own, :]
    xhat = resid

    def first_norm(r, carry):
        rows = rows_at(r * 128, 128, 128)
        part = resid[rows, :]
        center = part - jnp.mean(part, -1, keepdims=True)
        inverse = lax.rsqrt(jnp.mean(center * center, -1, keepdims=True) + EPS)
        scaled = center * inverse
        xhat[rows, :] = scaled
        inv1[rows, :] = inverse
        normed[rows, :] = (scaled * gain_one + shift_one).astype(BF16)
        dmlp[rows, :] = (cot[rows, :] * BRANCH_SCALE).astype(BF16)
        return carry

    lax.fori_loop(0, tokens // 128, first_norm, 0)
    sm[...] = jnp.zeros_like(sm)
    sm[5:6, :] = jnp.sum(dmlp[own, :].astype(F32), 0, keepdims=True)
    mixed[...] = jnp.zeros_like(mixed)
    dqkv[...] = jnp.zeros_like(dqkv)

    ag_forward(0)
    ag_finish(0)
    ag_start(1)

    bias_q, bias_v = bias[0:1, :], bias[1:2, :]
    hc = heads * HD

    def project(r, carry):
        rows = rows_at(r * 256, 256, 256)
        got = mm(normed[rows, :], w[0, :, 0:640])
        queries = (got[:, 0:hc] + bias_q).astype(BF16) * jnp.asarray(HD**-0.5, BF16)
        key_rows = got[:, hc : 2 * hc].astype(BF16)
        value_rows = (got[:, 2 * hc : 3 * hc] + bias_v).astype(BF16)
        for h in range(heads):
            q_s[h, rows, :] = queries[:, h * HD : (h + 1) * HD]
            k_s[h, rows, :] = key_rows[:, h * HD : (h + 1) * HD]
            v_s[h, rows, :] = value_rows[:, h * HD : (h + 1) * HD]
        return carry

    lax.fori_loop(0, tokens // 256, project, 0)

    def attend(i):
        first, last = i * quarter, (i + 1) * quarter
        rows = slice(first, last)
        causal = lax.broadcasted_iota(jnp.int32, (quarter, quarter), 0) >= lax.broadcasted_iota(
            jnp.int32, (quarter, quarter), 1
        )
        for h in range(heads):
            queries = q_s[h, rows, :]
            diag = jnp.where(causal, mm(queries, k_s[h, rows, :], NT), MASKED)
            highest = jnp.max(diag, -1, keepdims=True)
            if i > 0:
                wide = mm(queries, k_s[h, 0:first, :], NT)
                highest = jnp.maximum(highest, jnp.max(wide, -1, keepdims=True))
            e_diag = jnp.exp(diag - highest)
            summed = jnp.sum(e_diag, -1, keepdims=True)
            e_diag = e_diag.astype(BF16)
            e_s[h, rows, first:last] = e_diag
            total = mm(e_diag, v_s[h, rows, :])
            if i > 0:
                e_wide = jnp.exp(wide - highest)
                summed = summed + jnp.sum(e_wide, -1, keepdims=True)
                e_wide = e_wide.astype(BF16)
                e_s[h, rows, 0:first] = e_wide
                total = total + mm(e_wide, v_s[h, 0:first, :])
            inverse = 1.0 / summed
            linv[h, rows, :] = inverse
            mixed[rows, (h + 1) * HD : (h + 2) * HD] = (total * inverse).astype(BF16)

    def rs_order(s, local_first):
        half = lax.div(s, 2)
        odd = lax.rem(s, 2)
        near = half if not local_first else 1 - half
        yq = near * y + (1 - near) * (1 - y)
        cq = odd * c + (1 - odd) * (1 - c)
        return 2 * yq + cq, half, odd, near

    def rs_core(k, half):
        return rcopy(ps.at[k % 2, half], crecv.at[k, half], 21 + 2 * k + half, c_dev)

    def rs_y(k):
        return rcopy(ysend.at[k], yrecv.at[k], 29 + k, y_dev)

    def rs_loop(k, compute, local_first=False, start_y=True, prepare=None):
        if k >= 2:
            rs_core_drain(k - 2)

        def step(s, carry):
            which, half, odd, near = rs_order(s, local_first)
            if prepare is not None:
                prepare(s)
            part = compute(which)

            @pl.when(odd == 0)
            def _():
                ps[k % 2, half] = part.astype(BF16)
                rs_core(k, half).start()

            @pl.when(odd == 1)
            def _():
                rs_core(k, half).wait_recv()
                total = part + crecv[k, half].astype(F32)

                @pl.when(near == 0)
                def _():
                    ysend[k] = total.astype(BF16)
                    if start_y:
                        rs_y(k).start()

                @pl.when(near == 1)
                def _():
                    fin[k] = total

            return carry

        lax.fori_loop(0, 4, step, 0)

    def rs_result(k):
        rs_y(k).wait_recv()
        return fin[k] + yrecv[k].astype(F32)

    def rs_core_drain(k):
        for half in range(2):
            rs_core(k, half).wait_send()


    def attend_proj(which):
        for i in range(tokens // quarter):

            @pl.when(which == i)
            def _():
                attend(i)

        return mm(mixed[rows_at(which * quarter, quarter, quarter), :], w[0, :, 512:768], NT)

    rs_loop(0, attend_proj)

    def q_rows(ref, which):
        return ref.at[rows_at(which * quarter, quarter, quarter), :]

    def qg_y(g, ref):
        return rcopy(q_rows(ref, ten), q_rows(ref, ten), 33 + g, y_dev)

    def qg_c(g, ref):
        return rcopy(q_rows(ref, ten), q_rows(ref, ten), 35 + g, c_dev)

    def qg_f(g, ref):
        far = ten + 2 - 4 * y
        return rcopy(q_rows(ref, far), q_rows(ref, far), 37 + g, c_dev)

    def qg_drain(g, ref):
        qg_y(g, ref).wait_send()
        qg_c(g, ref).wait_send()
        qg_f(g, ref).wait_send()

    ag_forward(1)
    ag_start(2)

    mid[...] = mid[...] + BRANCH_SCALE * (rs_result(0) + vec[4:5, :])
    center = mid[...] - jnp.mean(mid[...], -1, keepdims=True)
    inverse = lax.rsqrt(jnp.mean(center * center, -1, keepdims=True) + EPS)
    scaled = center * inverse
    xhat2[...] = scaled
    inv2[...] = inverse
    hidden[own, :] = (scaled * vec[2:3, :] + vec[3:4, :]).astype(BF16)
    qg_y(0, hidden).start()
    qg_c(0, hidden).start()

    ag_finish(1)
    ag_forward(2)
    ag_finish(2)

    bias_up = jnp.concatenate([bias[2 + i : 3 + i, :] for i in range(4)], 1)

    def wait_hidden(s):
        @pl.when(s == 0)
        def _():
            qg_c(0, hidden).wait_recv()

        @pl.when(s == 2)
        def _():
            qg_y(0, hidden).wait_recv()
            qg_f(0, hidden).start()
            qg_f(0, hidden).wait_recv()

    def feed_forward(which):
        rows = rows_at(which * quarter, quarter, quarter)
        hq = hidden[rows, :]
        gq = dmlp[rows, :]
        for t in range(width // 256):
            cols = slice(t * 256, (t + 1) * 256)
            pre = mm(hq, w[1, :, cols]) + bias_up[:, cols]
            square = pre * pre
            tanh = jnp.tanh(GELU_A * (pre + GELU_B * (square * pre)))
            half_up = 0.5 + 0.5 * tanh
            act_s[rows, cols] = (pre * half_up).astype(BF16)
            slope = half_up + 0.5 * pre * (1.0 - tanh * tanh) * (
                GELU_A + (3.0 * GELU_A * GELU_B) * square
            )
            d_act = mm(gq, w[2, :, cols]).astype(BF16).astype(F32)
            d_low = (slope * d_act).astype(BF16)
            dpre[rows, cols] = d_low
            sm[6:7, cols] = sm[6:7, cols] + jnp.sum(d_low.astype(F32), 0, keepdims=True)
        return mm(dpre[rows, :], w[1], NT)

    rs_loop(1, feed_forward, local_first=True, prepare=wait_hidden)

    def branch(which):
        rows = rows_at(which * quarter, quarter, quarter)
        return mm(act_s[rows, :], w[2], NT)

    rs_loop(2, branch, start_y=False)

    def grad_block(b, left, right):
        def tile(t, carry):
            cols = rows_at(t * 256, 256, 256)
            gmat[b, cols, :] = mm(left[:, cols], right[...], TN).astype(BF16)
            return carry

        lax.fori_loop(0, width // 256, tile, 0)

    def g_rows(b, owner):
        return gmat.at[b, rows_at(owner * shard, shard, shard), :]

    def gx(b, zi):
        return rcopy(g_rows(b, 2 * zi + 1 - x), xr.at[b, zi], 39 + 4 * b + zi, x_dev)

    def gz(b, j):
        return rcopy(zs.at[b, j - 1], zr.at[b, j - 1], 51 + 3 * b + j - 1, z_dev(j))

    def g_start(b):
        for zi in range(4):
            gx(b, zi).start()

    def g_middle(b):
        for zi in range(4):
            gx(b, zi).wait_recv()
        for j in (1, 2, 3):
            zo = z_other(j)
            mine_x = gmat[b, rows_at((2 * zo + x) * shard, shard, shard), :].astype(F32)
            zs[b, j - 1] = (mine_x + xr[b, zo].astype(F32)).astype(BF16)
            gz(b, j).start()

    def g_finish(b):
        total = gmat[b, mine, :].astype(F32) + xr[b, z].astype(F32)
        for j in (1, 2, 3):
            gz(b, j).wait_recv()
            total = total + zr[b, j - 1].astype(F32)
        gsum_o[b] = total

    def g_drain(b):
        for zi in range(4):
            gx(b, zi).wait_send()
        for j in (1, 2, 3):
            gz(b, j).wait_send()

    grad_block(1, hidden, dpre)
    g_start(1)
    grad_block(2, dmlp, act_s)
    g_start(2)

    d_hidden = rs_result(1)
    scaled = xhat2[...]
    sm[2:3, :] = jnp.sum(d_hidden * scaled, 0, keepdims=True)
    sm[3:4, :] = jnp.sum(d_hidden, 0, keepdims=True)
    weighted = d_hidden * vec[2:3, :]
    d_mid = cot[own, :] + inv2[...] * (
        weighted
        - jnp.mean(weighted, -1, keepdims=True)
        - scaled * jnp.mean(weighted * scaled, -1, keepdims=True)
    )
    fin[1] = d_mid
    d_attn = (BRANCH_SCALE * d_mid).astype(BF16)
    dattn[own, :] = d_attn
    sm[4:5, :] = jnp.sum(d_attn.astype(F32), 0, keepdims=True)
    qg_y(1, dattn).start()
    qg_c(1, dattn).start()

    dk_s[...] = jnp.zeros_like(dk_s)
    dv_s[...] = jnp.zeros_like(dv_s)

    def attend_back(i):
        first, last = i * quarter, (i + 1) * quarter
        rows = slice(first, last)
        d_mixed = mm(dattn[rows, :], w[0, :, 512:768]).astype(BF16)
        for h in range(heads):
            cols = slice((h + 1) * HD, (h + 2) * HD)
            d_out = d_mixed[:, cols].astype(F32)
            inverse = linv[h, rows, :]
            d_scaled = d_out * inverse
            inner = jnp.sum(d_scaled * mixed[rows, cols].astype(F32), -1, keepdims=True)
            d_scaled = d_scaled.astype(BF16)
            expo = e_s[h, rows, 0:last]
            d_probs = mm(d_scaled, v_s[h, 0:last, :], NT)
            d_scores = (expo.astype(F32) * (d_probs - inner)).astype(BF16)
            d_q = mm(d_scores, k_s[h, 0:last, :]) * HD**-0.5
            dqkv[rows, h * HD : (h + 1) * HD] = d_q.astype(BF16)
            dk_s[h, 0:last, :] = dk_s[h, 0:last, :] + mm(d_scores, q_s[h, rows, :], TN)
            dv_s[h, 0:last, :] = dv_s[h, 0:last, :] + mm(expo, d_scaled, TN)

    def back_step(s, carry):
        half = lax.div(s, 2)
        odd = lax.rem(s, 2)
        yq = (1 - half) * y + half * (1 - y)
        cq = (1 - odd) * c + odd * (1 - c)
        which = 2 * yq + cq

        @pl.when(s == 1)
        def _():
            qg_c(1, dattn).wait_recv()

        @pl.when(s == 2)
        def _():
            g_middle(1)
            qg_y(1, dattn).wait_recv()
            qg_f(1, dattn).start()
            rs_y(2).start()

        @pl.when(s == 3)
        def _():
            qg_f(1, dattn).wait_recv()

        for i in range(tokens // quarter):

            @pl.when(which == i)
            def _():
                attend_back(i)

        return carry

    lax.fori_loop(0, 4, back_step, 0)

    for h in range(heads):
        dqkv[:, hc + h * HD : hc + (h + 1) * HD] = dk_s[h].astype(BF16)
        dqkv[:, 2 * hc + h * HD : 2 * hc + (h + 1) * HD] = dv_s[h].astype(BF16)

    def tile_zero(t, carry):
        cols = rows_at(t * 256, 256, 256)
        g_qkv = mm(normed[:, cols], dqkv[...], TN)
        g_proj = mm(dattn[:, cols], mixed[...], TN)
        gmat[0, cols, 0:512] = g_qkv[:, 0:512].astype(BF16)
        gmat[0, cols, 512:640] = (g_qkv[:, 512:640] + g_proj[:, 0:128]).astype(BF16)
        gmat[0, cols, 640:768] = g_proj[:, 128:256].astype(BF16)
        return carry

    lax.fori_loop(0, width // 256, tile_zero, 0)
    g_start(0)

    def first_back(which):
        rows = rows_at(which * quarter, quarter, quarter)
        d_low = dqkv[rows, :]
        part = mm(d_low, w[0, :, 0:640], NT)
        rounded = part.astype(BF16).astype(F32)
        sm[0:1, :] = sm[0:1, :] + jnp.sum(rounded * xhat[rows, :], 0, keepdims=True)
        sm[1:2, :] = sm[1:2, :] + jnp.sum(rounded, 0, keepdims=True)
        sums = jnp.sum(d_low.astype(F32), 0, keepdims=True)
        sm[7:8, 0:hc] = sm[7:8, 0:hc] + sums[:, 0:hc]
        sm[7:8, 256 : 256 + hc] = sm[7:8, 256 : 256 + hc] + sums[:, 2 * hc : 3 * hc]
        return part

    rs_loop(3, first_back)

    small_x = rcopy(sm, smx, 60, x_dev)
    small_x.start()
    g_middle(2)
    g_finish(1)
    small_x.wait_recv()
    smz[z] = sm[...] + smx[...]

    def small_z(j):
        return rcopy(smz.at[z], smz.at[z], 61 + j - 1, z_dev(j))

    for j in (1, 2, 3):
        small_z(j).start()
    g_middle(0)
    out_o[...] = mid[...] + BRANCH_SCALE * (rs_result(2) + vec[5:6, :])
    for j in (1, 2, 3):
        rcopy(smz.at[z_other(j)], smz.at[z_other(j)], 61 + j - 1, z_dev(j)).wait_recv()
    smy[0] = (smz[0] + smz[1]) + (smz[2] + smz[3])
    small_y = rcopy(smy.at[0], smy.at[1], 64, y_dev)
    small_y.start()
    g_finish(2)

    d_normed = rs_result(3)
    scaled = xhat[own, :]
    weighted = d_normed * gain_one
    grad_o[...] = fin[1] + inv1[own, :] * (
        weighted
        - jnp.mean(weighted, -1, keepdims=True)
        - scaled * jnp.mean(weighted * scaled, -1, keepdims=True)
    )
    small_y.wait_recv()
    smc[0] = smy[0] + smy[1]
    small_c = rcopy(smc.at[0], smc.at[1], 65, c_dev)
    small_c.start()
    g_finish(0)
    small_c.wait_recv()
    small_o[0:6, :] = smc[0, 0:6, :] + smc[1, 0:6, :]
    small_o[6:8, :] = smy[0, 6:8, :]

    for b in range(3):
        ag_drain(b)
        g_drain(b)
    for k in range(4):
        rs_y(k).wait_send()
    rs_core_drain(2)
    rs_core_drain(3)
    qg_drain(0, hidden)
    qg_drain(1, dattn)
    small_x.wait_send()
    for j in (1, 2, 3):
        small_z(j).wait_send()
    small_y.wait_send()
    small_c.wait_send()


def run_block(resid, cotangent, win, wout, bias, vec, rows, n_dp):
    tokens, width = resid.shape
    quarter = tokens // 4
    head_cols = win.shape[2]
    heads = head_cols // HD
    sizes = (tokens, width, quarter, heads, rows)
    vm = pltpu.VMEM
    scratch = [
        vm((tokens, width), F32),
        vm((tokens, width), F32),
        vm((tokens, 1), F32),
        vm((tokens, width), BF16),
        vm((tokens, width), BF16),
        vm((3, width, width), BF16),
        vm((heads, tokens, HD), BF16),
        vm((heads, tokens, HD), BF16),
        vm((heads, tokens, HD), BF16),
        vm((heads, tokens, tokens), BF16),
        vm((heads, tokens, 1), F32),
        vm((tokens, 256), BF16),
        vm((2, 2, quarter, width), BF16),
        vm((4, 2, quarter, width), BF16),
        vm((4, quarter, width), F32),
        vm((4, quarter, width), BF16),
        vm((4, quarter, width), BF16),
        vm((quarter, width), F32),
        vm((quarter, width), F32),
        vm((quarter, 1), F32),
        vm((tokens, width), BF16),
        vm((tokens, width), BF16),
        vm((tokens, width), BF16),
        vm((tokens, width), BF16),
        vm((heads, tokens, HD), F32),
        vm((heads, tokens, HD), F32),
        vm((tokens, 640), BF16),
        vm((3, width, width), BF16),
        vm((3, 4, rows, width), BF16),
        vm((3, 3, rows, width), BF16),
        vm((3, 3, rows, width), BF16),
        vm((8, width), F32),
        vm((8, width), F32),
        vm((4, 8, width), F32),
        vm((2, 8, width), F32),
        vm((2, 8, width), F32),
        pltpu.SemaphoreType.DMA((2,)),
        pltpu.SemaphoreType.DMA((66,)),
        pltpu.SemaphoreType.DMA((66,)),
    ]
    whole = pl.BlockSpec(memory_space=pltpu.VMEM)
    return pl.pallas_call(
        functools.partial(block_kernel, sizes),
        out_shape=(
            jax.ShapeDtypeStruct((quarter, width), F32),
            jax.ShapeDtypeStruct((quarter, width), F32),
            jax.ShapeDtypeStruct((3, rows, width), F32),
            jax.ShapeDtypeStruct((8, width), F32),
        ),
        in_specs=[pl.BlockSpec(memory_space=pl.ANY)] * 2 + [whole] * 4,
        out_specs=[whole] * 4,
        scratch_shapes=scratch,
        compiler_params=pltpu.CompilerParams(
            collective_id=1, has_side_effects=True, vmem_limit_bytes=62 << 20
        ),
        name="block",
    )(resid, cotangent, win, wout, bias, vec)


def fused_shards(
    resid,
    cotangent,
    master_in,
    moment1_in,
    moment2_in,
    master_out,
    moment1_out,
    moment2_out,
    master_bias,
    moment1_bias,
    moment2_bias,
    master_vec,
    moment1_vec,
    moment2_vec,
):
    rows = master_in.shape[1]
    hc = master_in.shape[3]
    out_rows, grad_rows, g_sum, small = run_block(
        resid,
        cotangent,
        jnp.transpose(master_in[0], (1, 0, 2)),
        master_out[0],
        master_bias[0],
        master_vec[0],
        rows,
        lax.axis_size("dp"),
    )
    kinds = g_sum.reshape(3, rows, 4, hc)
    g_in = jnp.concatenate([kinds[0, :, 0:3], kinds[1]], 1)[None]
    g_out = jnp.transpose(
        jnp.concatenate([kinds[0, :, 3:4], kinds[2]], 1), (1, 2, 0)
    )[None]
    g_bias = jnp.concatenate(
        [small[7:8, 0:hc], small[7:8, 256 : 256 + hc], small[6].reshape(4, hc)], 0
    )[None]
    g_vec = small[None, 0:6]
    first_in, second_in, new_in = adam_step(
        master_in, moment1_in, moment2_in, g_in, 0.5 * D ** (-0.5), DECAY
    )
    first_out, second_out, new_out = adam_step(
        master_out, moment1_out, moment2_out, g_out, 2.0 * D ** (-0.5), DECAY
    )
    first_bias, second_bias, new_bias = adam_step(
        master_bias, moment1_bias, moment2_bias, g_bias, SMALL_RATE, 0.0
    )
    first_vec, second_vec, new_vec = adam_step(
        master_vec, moment1_vec, moment2_vec, g_vec, SMALL_RATE, 0.0
    )
    return (
        out_rows,
        grad_rows,
        first_in,
        second_in,
        new_in,
        first_out,
        second_out,
        new_out,
        first_bias,
        second_bias,
        new_bias,
        first_vec,
        second_vec,
        new_vec,
    )


def solution(mesh):
    fused = mesh.shape["dp"] == 8 and mesh.shape["tensor"] == 4
    return jax.shard_map(
        fused_shards if fused else shards,
        mesh=mesh,
        in_specs=(
            P("dp", None),
            P("dp", None),
            P(None, "dp", None, "tensor"),
            P(None, "dp", None, "tensor"),
            P(None, "dp", None, "tensor"),
            P(None, None, "tensor", "dp"),
            P(None, None, "tensor", "dp"),
            P(None, None, "tensor", "dp"),
            P(None, None, "tensor"),
            P(None, None, "tensor"),
            P(None, None, "tensor"),
            P(),
            P(),
            P(),
        ),
        out_specs=(
            P(("dp", "tensor"), None),
            P(("dp", "tensor"), None),
            P(None, "dp", None, "tensor"),
            P(None, "dp", None, "tensor"),
            P(None, "dp", None, "tensor"),
            P(None, None, "tensor", "dp"),
            P(None, None, "tensor", "dp"),
            P(None, None, "tensor", "dp"),
            P(None, None, "tensor"),
            P(None, None, "tensor"),
            P(None, None, "tensor"),
            P(),
            P(),
            P(),
        ),
        check_vma=False,
    )
```

```python
import functools

import jax
import jax.numpy as jnp
from jax import lax
from jax.experimental import pallas as pl
from jax.experimental.pallas import tpu as pltpu
from jax.sharding import PartitionSpec as P

D = 768
HD = 64
LEN = 1024
LAYERS = 1
STEP = 10


EPS = 1e-05
BRANCH_SCALE = 48 ** (-0.5)
BETA_ONE = 0.9
BETA_TWO = 0.95
ADAM_EPS = 1e-08
DECAY = 0.1
SMALL_RATE = 0.3
MASKED = -1e30


def norm_rows(stream, gain, shift):
    center = stream - jnp.mean(stream, -1, keepdims=True)
    inverse = lax.rsqrt(jnp.mean(center * center, -1, keepdims=True) + EPS)
    scaled = center * inverse
    return (scaled * gain + shift, scaled, inverse)


def norm_back(grad_out, scaled, inverse, gain):
    weighted = grad_out * gain
    centered = weighted - jnp.mean(weighted, -1, keepdims=True)
    return inverse * (centered - scaled * jnp.mean(weighted * scaled, -1, keepdims=True))


def plain_dot(left, right):
    return jnp.dot(left, right, preferred_element_type=jnp.float32)


def left_dot(left, right):
    return lax.dot_general(
        left, right, (((0,), (0,)), ((), ())), preferred_element_type=jnp.float32
    )


def right_dot(left, right):
    return lax.dot_general(
        left, right, (((1,), (1,)), ((), ())), preferred_element_type=jnp.float32
    )


def smooth_gate(values_in):
    return jax.nn.gelu(values_in, approximate=True)


def tensor_rows(array_in):
    quarter = array_in.shape[0] // lax.axis_size("tensor")
    return lax.dynamic_slice_in_dim(array_in, lax.axis_index("tensor") * quarter, quarter, 0)


def own_rows(array_in):
    return tensor_rows(array_in)


def branch_total(partial_sum):
    return lax.psum(partial_sum.astype(jnp.bfloat16), "tensor").astype(jnp.float32)


def grad_total(partial_sum):
    return lax.psum(partial_sum.astype(jnp.bfloat16), "tensor").astype(jnp.float32)


def causal_scores(queries, key_rows, first, last):
    block_rows = last - first
    scores = jnp.einsum(
        "qhd,khd->hqk", queries[first:last], key_rows[:last], preferred_element_type=jnp.float32
    ) * HD ** (-0.5)
    query_pos = lax.broadcasted_iota(jnp.int32, (block_rows, last), 0) + first
    key_pos = lax.broadcasted_iota(jnp.int32, (block_rows, last), 1)
    return jnp.where(query_pos >= key_pos, scores, MASKED)


def attend_sequence(operands):
    queries, key_rows, value_rows = operands
    block_rows = min(512, LEN)
    outputs = []
    totals = []
    for block_idx in range(LEN // block_rows):
        first = block_idx * block_rows
        last = first + block_rows
        scores = causal_scores(queries, key_rows, first, last)
        highest = jnp.max(scores, -1, keepdims=True)
        expo = jnp.exp(scores - highest)
        summed = jnp.sum(expo, -1, keepdims=True)
        weights = (expo / summed).astype(jnp.bfloat16)
        mixed = jnp.einsum(
            "hqk,khd->qhd", weights, value_rows[:last], preferred_element_type=jnp.float32
        )
        outputs.append(mixed.astype(jnp.bfloat16))
        totals.append((highest + jnp.log(summed))[..., 0])
    return (jnp.concatenate(outputs, 0), jnp.concatenate(totals, 1))


def attend_back(operands):
    queries, key_rows, value_rows, log_total, grad_mixed = operands
    block_rows = min(512, LEN)
    d_keys = jnp.zeros(key_rows.shape, jnp.float32)
    d_values = jnp.zeros(value_rows.shape, jnp.float32)
    d_queries = []
    for block_idx in range(LEN // block_rows):
        first = block_idx * block_rows
        last = first + block_rows
        scores = causal_scores(queries, key_rows, first, last)
        probs = jnp.exp(scores - log_total[:, first:last, None])
        d_probs = jnp.einsum(
            "qhd,khd->hqk",
            grad_mixed[first:last],
            value_rows[:last],
            preferred_element_type=jnp.float32,
        )
        inner = jnp.sum(probs * d_probs, -1, keepdims=True)
        d_scores = (probs * (d_probs - inner)).astype(jnp.bfloat16)
        d_queries.append(
            jnp.einsum(
                "hqk,khd->qhd", d_scores, key_rows[:last], preferred_element_type=jnp.float32
            )
            * HD ** (-0.5)
        )
        key_part = jnp.einsum(
            "hqk,qhd->khd", d_scores, queries[first:last], preferred_element_type=jnp.float32
        ) * HD ** (-0.5)
        value_part = jnp.einsum(
            "hqk,qhd->khd",
            probs.astype(jnp.bfloat16),
            grad_mixed[first:last],
            preferred_element_type=jnp.float32,
        )
        d_keys = d_keys.at[:last].add(key_part)
        d_values = d_values.at[:last].add(value_part)
    return (jnp.concatenate(d_queries, 0), d_keys, d_values)


def layer_forward(stream, w_in, w_out, bias, vector):
    model_width = w_in.shape[0]
    head_cols = w_in.shape[2]
    heads_here = head_cols // HD
    normed, scaled_one, inverse_one = norm_rows(stream, vector[0], vector[1])
    normed_low = normed.astype(jnp.bfloat16)
    seq_count = normed_low.shape[0] // LEN
    shape4 = (seq_count, LEN, heads_here, HD)
    w_qkv = w_in[:, 0:3].reshape(model_width, 3 * head_cols)
    projected = plain_dot(normed_low, w_qkv)
    queries = (projected[:, :head_cols] + bias[0]).astype(jnp.bfloat16).reshape(shape4)
    key_rows = projected[:, head_cols : 2 * head_cols].astype(jnp.bfloat16).reshape(shape4)
    value_rows = (projected[:, 2 * head_cols :] + bias[1]).astype(jnp.bfloat16).reshape(shape4)
    mixed, log_total = lax.map(attend_sequence, (queries, key_rows, value_rows))
    mixed_low = mixed.reshape(-1, head_cols)
    attended = branch_total(plain_dot(mixed_low, w_out[0])) + vector[4]
    middle = stream + BRANCH_SCALE * attended
    hidden, scaled_two, inverse_two = norm_rows(middle, vector[2], vector[3])
    hidden_low = hidden.astype(jnp.bfloat16)
    w_up = w_in[:, 3:].reshape(model_width, 4 * head_cols)
    pre_act = plain_dot(hidden_low, w_up) + bias[2:].reshape(4 * head_cols)
    act_low = smooth_gate(pre_act).astype(jnp.bfloat16)
    w_down = w_out[1:].reshape(4 * head_cols, model_width)
    mlp_out = branch_total(plain_dot(act_low, w_down)) + vector[5]
    result = middle + BRANCH_SCALE * mlp_out
    kept = (
        scaled_one,
        inverse_one,
        normed_low,
        queries,
        key_rows,
        value_rows,
        log_total,
        mixed_low,
        scaled_two,
        inverse_two,
        hidden_low,
        pre_act,
        act_low,
    )
    return (result, kept)


def layer_backward(gradient, w_in, w_out, vector, kept):
    (
        scaled_one,
        inverse_one,
        normed_low,
        queries,
        key_rows,
        value_rows,
        log_total,
        mixed_low,
        scaled_two,
        inverse_two,
        hidden_low,
        pre_act,
        act_low,
    ) = kept
    model_width = w_in.shape[0]
    head_cols = w_in.shape[2]
    w_qkv = w_in[:, 0:3].reshape(model_width, 3 * head_cols)
    w_up = w_in[:, 3:].reshape(model_width, 4 * head_cols)
    w_down = w_out[1:].reshape(4 * head_cols, model_width)
    d_mlp = (BRANCH_SCALE * gradient).astype(jnp.bfloat16)
    g_bdown = jnp.sum(own_rows(d_mlp).astype(jnp.float32), 0)
    g_down = left_dot(act_low, d_mlp).reshape(4, head_cols, model_width)
    d_act = right_dot(d_mlp, w_down).astype(jnp.bfloat16)
    gate_value, gate_pull = jax.vjp(smooth_gate, pre_act)
    d_pre = gate_pull(d_act.astype(jnp.float32))[0].astype(jnp.bfloat16)
    g_bup = jnp.sum(d_pre.astype(jnp.float32), 0)
    g_up = left_dot(hidden_low, d_pre).reshape(model_width, 4, head_cols)
    d_hidden = grad_total(right_dot(d_pre, w_up))
    g_gain_two = jnp.sum(own_rows(d_hidden * scaled_two), 0)
    g_shift_two = jnp.sum(own_rows(d_hidden), 0)
    d_middle = gradient + norm_back(d_hidden, scaled_two, inverse_two, vector[2])
    d_attn = (BRANCH_SCALE * d_middle).astype(jnp.bfloat16)
    g_bproj = jnp.sum(own_rows(d_attn).astype(jnp.float32), 0)
    g_proj = left_dot(mixed_low, d_attn)
    d_mixed = right_dot(d_attn, w_out[0]).astype(jnp.bfloat16)
    d_queries, d_keys, d_values = lax.map(
        attend_back, (queries, key_rows, value_rows, log_total, d_mixed.reshape(queries.shape))
    )
    d_qkv = jnp.concatenate(
        [
            d_queries.reshape(-1, head_cols),
            d_keys.reshape(-1, head_cols),
            d_values.reshape(-1, head_cols),
        ],
        1,
    ).astype(jnp.bfloat16)
    g_qkv = left_dot(normed_low, d_qkv).reshape(model_width, 3, head_cols)
    g_bq = jnp.sum(d_qkv[:, :head_cols].astype(jnp.float32), 0)
    g_bv = jnp.sum(d_qkv[:, 2 * head_cols :].astype(jnp.float32), 0)
    d_normed = grad_total(right_dot(d_qkv, w_qkv))
    g_gain_one = jnp.sum(own_rows(d_normed * scaled_one), 0)
    g_shift_one = jnp.sum(own_rows(d_normed), 0)
    d_stream = d_middle + norm_back(d_normed, scaled_one, inverse_one, vector[0])
    g_in = jnp.concatenate([g_qkv, g_up], 1)
    g_out = jnp.concatenate([g_proj[None], g_down], 0)
    g_bias = jnp.concatenate([g_bq[None], g_bv[None], g_bup.reshape(4, head_cols)], 0)
    g_vector = jnp.stack([g_gain_one, g_shift_one, g_gain_two, g_shift_two, g_bproj, g_bdown])
    return (d_stream, g_in, g_out, g_bias, g_vector)


def adam_step(master, first, second, gradient, rate, decay):
    first_new = BETA_ONE * first + (1 - BETA_ONE) * gradient
    second_new = BETA_TWO * second + (1 - BETA_TWO) * gradient * gradient
    direction = (
        first_new / (1 - BETA_ONE**STEP) / (jnp.sqrt(second_new / (1 - BETA_TWO**STEP)) + ADAM_EPS)
    )
    return (first_new, second_new, master - rate * (direction + decay * master))


def shards(
    resid,
    cotangent,
    master_in,
    moment1_in,
    moment2_in,
    master_out,
    moment1_out,
    moment2_out,
    master_bias,
    moment1_bias,
    moment2_bias,
    master_vec,
    moment1_vec,
    moment2_vec,
):
    weights_in, weights_out = (
        lax.all_gather(master_in.astype(jnp.bfloat16), "dp", axis=1, tiled=True),
        lax.all_gather(master_out.astype(jnp.bfloat16), "dp", axis=3, tiled=True),
    )
    stream = resid
    gradient = cotangent
    layer_idx = 0
    stream, kept = layer_forward(
        stream,
        weights_in[layer_idx],
        weights_out[layer_idx],
        master_bias[layer_idx],
        master_vec[layer_idx],
    )
    kept_list = [kept]
    list_in = [None] * LAYERS
    list_out = [None] * LAYERS
    list_bias = [None] * LAYERS
    list_vector = [None] * LAYERS
    layer_idx = 0
    gradient, g_in, g_out, g_bias, g_vector = layer_backward(
        gradient,
        weights_in[layer_idx],
        weights_out[layer_idx],
        master_vec[layer_idx],
        kept_list[layer_idx],
    )
    list_in[layer_idx] = g_in
    list_out[layer_idx] = g_out
    list_bias[layer_idx] = g_bias
    list_vector[layer_idx] = g_vector
    summed_in = jnp.stack(list_in)
    summed_out = jnp.stack(list_out)
    summed_in, summed_out = (
        lax.psum_scatter(summed_in, "dp", scatter_dimension=1, tiled=True),
        lax.psum_scatter(summed_out, "dp", scatter_dimension=3, tiled=True),
    )
    summed_bias = lax.psum(jnp.stack(list_bias), "dp")
    summed_vector = lax.psum(jnp.stack(list_vector), ("dp", "tensor"))
    first_in, second_in, new_in = adam_step(
        master_in, moment1_in, moment2_in, summed_in, 0.5 * D ** (-0.5), DECAY
    )
    first_out, second_out, new_out = adam_step(
        master_out, moment1_out, moment2_out, summed_out, 2.0 * D ** (-0.5), DECAY
    )
    first_bias, second_bias, new_bias = adam_step(
        master_bias, moment1_bias, moment2_bias, summed_bias, SMALL_RATE, 0.0
    )
    first_vec, second_vec, new_vec = adam_step(
        master_vec, moment1_vec, moment2_vec, summed_vector, SMALL_RATE, 0.0
    )
    return (
        own_rows(stream),
        own_rows(gradient),
        first_in,
        second_in,
        new_in,
        first_out,
        second_out,
        new_out,
        first_bias,
        second_bias,
        new_bias,
        first_vec,
        second_vec,
        new_vec,
    )


MESH_IDS = pl.DeviceIdType.MESH
F32 = jnp.float32
BF16 = jnp.bfloat16
NN = (((1,), (0,)), ((), ()))
NT = (((1,), (1,)), ((), ()))
TN = (((0,), (0,)), ((), ()))
GELU_A = (2.0 / 3.141592653589793) ** 0.5
GELU_B = 0.044715


def mm(left, right, dims=NN):
    return lax.dot_general(left, right, dims, preferred_element_type=F32)


def rows_at(start, size, align):
    return pl.ds(pl.multiple_of(start, align), size)


def block_kernel(
    sizes,
    resid_h,
    cot_h,
    win,
    wout,
    bias,
    vec,
    out_o,
    grad_o,
    gsum_o,
    small_o,
    resid,
    cot,
    inv1,
    normed,
    dmlp,
    w,
    q_s,
    k_s,
    v_s,
    e_s,
    linv,
    mixed,
    ps,
    crecv,
    fin,
    ysend,
    yrecv,
    mid,
    xhat2,
    inv2,
    hidden,
    act_s,
    dpre,
    dattn,
    dk_s,
    dv_s,
    dqkv,
    gmat,
    xr,
    zs,
    zr,
    sm,
    smx,
    smz,
    smy,
    smc,
    lsem,
    ssem,
    rsem,
):
    tokens, width, quarter, heads, shard = sizes
    dp = lax.axis_index("dp")
    ten = lax.axis_index("tensor")
    z = lax.div(dp, 2)
    x = lax.rem(dp, 2)
    y = lax.div(ten, 2)
    c = lax.rem(ten, 2)
    x_dev = (dp + 1 - 2 * x, ten)
    c_dev = (dp, ten + 1 - 2 * c)
    y_dev = (dp, ten + 2 - 4 * y)

    def z_other(j):
        if j == 1:
            return z + 1 - 2 * lax.rem(z, 2)
        if j == 2:
            return lax.rem(z + 2, 4)
        return 3 - z

    def z_dev(j):
        return (2 * z_other(j) + x, ten)

    def rcopy(src, dst, idx, dev, recv_idx=None):
        return pltpu.make_async_remote_copy(
            src_ref=src,
            dst_ref=dst,
            send_sem=ssem.at[idx],
            recv_sem=rsem.at[idx if recv_idx is None else recv_idx],
            device_id=dev,
            device_id_type=MESH_IDS,
        )

    barrier = pltpu.get_barrier_semaphore()
    peers = [x_dev, c_dev, y_dev, z_dev(1), z_dev(2), z_dev(3)]
    for dev in peers:
        pl.semaphore_signal(barrier, inc=1, device_id=dev, device_id_type=MESH_IDS)
    load_resid = pltpu.make_async_copy(resid_h, resid, lsem.at[0])
    load_cot = pltpu.make_async_copy(cot_h, cot, lsem.at[1])
    load_resid.start()
    load_cot.start()

    mine = rows_at(dp * shard, shard, shard)
    out_t = [jnp.transpose(wout[i]) for i in range(5)]
    w[0, mine, :] = jnp.concatenate([win[0], win[1], win[2], out_t[0]], 1).astype(BF16)

    pl.semaphore_wait(barrier, len(peers))

    is_end = 1 - lax.rem(lax.div(z + 1, 2), 2)
    is_mid = 1 - is_end
    upper = lax.div(z, 2)
    pair_dev = (2 * z_other(1) + x, ten)
    mid_dev = (2 * (2 - upper) + x, ten)
    owner_z = (z_other(1), 2 - upper, 3 - 3 * upper)
    ag_parts = (2, 1, 1)
    ag_base = (0, 18, 27)

    def piece(b, zi, p):
        size = shard // ag_parts[b]
        return w.at[b, rows_at((2 * zi + x) * shard + p * size, size, size), :]

    def ag_copy(b, zi, p, send, recv, dev):
        src = piece(b, zi, p)
        n = ag_parts[b]
        return rcopy(src, src, ag_base[b] + n * send + p, dev, ag_base[b] + n * recv + p)

    def ag_pair(b, p):
        return ag_copy(b, z, p, 0, 0, pair_dev)

    def ag_mid(b, p):
        return ag_copy(b, z, p, 1, 1, mid_dev)

    def ag_onward(b, i, p):
        if i == 0:
            return ag_copy(b, owner_z[0], p, 2, 2, mid_dev)
        return ag_copy(b, owner_z[i], p, 2 + i, i, pair_dev)

    def ag_x(b, i, p):
        return ag_copy(b, z if i == 0 else owner_z[i - 1], p, 5 + i, 4 + i, x_dev)

    def ag_start(b):
        for p in range(ag_parts[b]):
            ag_x(b, 0, p).start()
            ag_pair(b, p).start()

            @pl.when(is_mid == 1)
            def _():
                ag_mid(b, p).start()

    def ag_pump(b, i):
        for p in range(ag_parts[b]):
            ag_copy(b, owner_z[i], p, i, i, x_dev).wait_recv()

            @pl.when(is_mid == 1)
            def _():
                ag_onward(b, i, p).start()

            ag_x(b, 1 + i, p).start()

    def ag_finish(b):
        for p in range(ag_parts[b]):
            for i in range(4):
                ag_x(b, i, p).wait_recv()

    def ag_drain(b):
        for p in range(ag_parts[b]):
            ag_pair(b, p).wait_send()
            for i in range(4):
                ag_x(b, i, p).wait_send()

            @pl.when(is_mid == 1)
            def _():
                ag_mid(b, p).wait_send()
                for i in range(3):
                    ag_onward(b, i, p).wait_send()

    ag_start(0)
    w[1, mine, :] = jnp.concatenate([win[3 + i] for i in range(4)], 1).astype(BF16)
    w[2, mine, :] = jnp.concatenate(out_t[1:], 1).astype(BF16)

    load_resid.wait()
    load_cot.wait()
    gain_one, shift_one = vec[0], vec[1]

    own = rows_at(ten * quarter, quarter, quarter)
    mid[...] = resid[own, :]
    xhat = resid

    def first_norm(r, carry):
        rows = rows_at(r * 128, 128, 128)
        part = resid[rows, :]
        center = part - jnp.mean(part, -1, keepdims=True)
        inverse = lax.rsqrt(jnp.mean(center * center, -1, keepdims=True) + EPS)
        scaled = center * inverse
        xhat[rows, :] = scaled
        inv1[rows, :] = inverse
        normed[rows, :] = (scaled * gain_one + shift_one).astype(BF16)
        dmlp[rows, :] = (cot[rows, :] * BRANCH_SCALE).astype(BF16)
        return carry

    lax.fori_loop(0, tokens // 128, first_norm, 0)
    ag_pump(0, 0)
    sm[...] = jnp.zeros_like(sm)
    sm[5:6, :] = jnp.sum(dmlp[own, :].astype(F32), 0, keepdims=True)
    mixed[...] = jnp.zeros_like(mixed)
    dqkv[...] = jnp.zeros_like(dqkv)

    ag_pump(0, 1)
    ag_pump(0, 2)
    ag_start(1)
    ag_finish(0)

    bias_q, bias_v = bias[0], bias[1]
    hc = heads * HD

    def project(r, carry):
        rows = rows_at(r * 256, 256, 256)
        got = mm(normed[rows, :], w[0, :, 0:640])
        queries = (got[:, 0:hc] + bias_q).astype(BF16) * jnp.asarray(HD**-0.5, BF16)
        key_rows = got[:, hc : 2 * hc].astype(BF16)
        value_rows = (got[:, 2 * hc : 3 * hc] + bias_v).astype(BF16)
        for h in range(heads):
            q_s[h, rows, :] = queries[:, h * HD : (h + 1) * HD]
            k_s[h, rows, :] = key_rows[:, h * HD : (h + 1) * HD]
            v_s[h, rows, :] = value_rows[:, h * HD : (h + 1) * HD]
        return carry

    lax.fori_loop(0, tokens // 256, project, 0)

    def attend(i):
        first, last = i * quarter, (i + 1) * quarter
        rows = slice(first, last)
        causal = lax.broadcasted_iota(jnp.int32, (quarter, quarter), 0) >= lax.broadcasted_iota(
            jnp.int32, (quarter, quarter), 1
        )
        for h in range(heads):
            queries = q_s[h, rows, :]
            diag = jnp.where(causal, mm(queries, k_s[h, rows, :], NT), MASKED)
            highest = jnp.max(diag, -1, keepdims=True)
            if i > 0:
                wide = mm(queries, k_s[h, 0:first, :], NT)
                highest = jnp.maximum(highest, jnp.max(wide, -1, keepdims=True))
            e_diag = jnp.exp(diag - highest)
            summed = jnp.sum(e_diag, -1, keepdims=True)
            e_diag = e_diag.astype(BF16)
            e_s[h, rows, first:last] = e_diag
            total = mm(e_diag, v_s[h, rows, :])
            if i > 0:
                e_wide = jnp.exp(wide - highest)
                summed = summed + jnp.sum(e_wide, -1, keepdims=True)
                e_wide = e_wide.astype(BF16)
                e_s[h, rows, 0:first] = e_wide
                total = total + mm(e_wide, v_s[h, 0:first, :])
            inverse = 1.0 / summed
            linv[h, rows, :] = inverse
            mixed[rows, (h + 1) * HD : (h + 2) * HD] = (total * inverse).astype(BF16)

    def rs_order(s):
        half = lax.div(s, 2)
        odd = lax.rem(s, 2)
        near = half
        yq = near * y + (1 - near) * (1 - y)
        cq = odd * c + (1 - odd) * (1 - c)
        return 2 * yq + cq, half, odd, near

    def rs_core(k, half):
        return rcopy(ps.at[k % 2, half], crecv.at[k, half], 36 + 2 * k + half, c_dev)

    def rs_y(k):
        return rcopy(ysend.at[k], yrecv.at[k], 44 + k, y_dev)

    def rs_loop(k, compute, start_y=True, prepare=None):
        if k >= 2:
            rs_core_drain(k - 2)

        def step(s, carry):
            which, half, odd, near = rs_order(s)
            if prepare is not None:
                prepare(s)
            part = compute(which)

            @pl.when(odd == 0)
            def _():
                ps[k % 2, half] = part.astype(BF16)
                rs_core(k, half).start()

            @pl.when(odd == 1)
            def _():
                rs_core(k, half).wait_recv()
                total = part + crecv[k, half].astype(F32)

                @pl.when(near == 0)
                def _():
                    ysend[k] = total.astype(BF16)
                    if start_y:
                        rs_y(k).start()

                @pl.when(near == 1)
                def _():
                    fin[k] = total

            return carry

        lax.fori_loop(0, 4, step, 0)

    def rs_result(k):
        rs_y(k).wait_recv()
        return fin[k] + yrecv[k].astype(F32)

    def rs_core_drain(k):
        for half in range(2):
            rs_core(k, half).wait_send()


    def pump_up(s):
        for i in range(3):

            @pl.when(s == 1 + i)
            def _():
                ag_pump(1, i)

    def attend_proj(which):
        for i in range(tokens // quarter):

            @pl.when(which == i)
            def _():
                attend(i)

        return mm(mixed[rows_at(which * quarter, quarter, quarter), :], w[0, :, 512:768], NT)

    rs_loop(0, attend_proj, prepare=pump_up)

    def q_rows(ref, which):
        return ref.at[rows_at(which * quarter, quarter, quarter), :]

    def qg_y(g, ref):
        return rcopy(q_rows(ref, ten), q_rows(ref, ten), 48 + g, y_dev)

    def qg_c(g, ref):
        return rcopy(q_rows(ref, ten), q_rows(ref, ten), 50 + g, c_dev)

    def qg_f(g, ref):
        far = ten + 2 - 4 * y
        return rcopy(q_rows(ref, far), q_rows(ref, far), 52 + g, c_dev)

    def qg_drain(g, ref):
        qg_y(g, ref).wait_send()
        qg_c(g, ref).wait_send()
        qg_f(g, ref).wait_send()

    ag_start(2)

    mid[...] = mid[...] + BRANCH_SCALE * (rs_result(0) + vec[4])
    center = mid[...] - jnp.mean(mid[...], -1, keepdims=True)
    inverse = lax.rsqrt(jnp.mean(center * center, -1, keepdims=True) + EPS)
    scaled = center * inverse
    xhat2[...] = scaled
    inv2[...] = inverse
    hidden[own, :] = (scaled * vec[2] + vec[3]).astype(BF16)
    qg_y(0, hidden).start()
    qg_c(0, hidden).start()

    ag_pump(2, 0)
    ag_finish(1)

    bias_up = jnp.concatenate([bias[2 + i] for i in range(4)], 1)

    def forward_units(which):
        rows = rows_at(which * quarter, quarter, quarter)
        hq = hidden[rows, :]
        for t in range(width // 256):
            cols = slice(t * 256, (t + 1) * 256)
            pre = mm(hq, w[1, :, cols]) + bias_up[:, cols]
            square = pre * pre
            tanh = jnp.tanh(GELU_A * (pre + GELU_B * (square * pre)))
            half_up = 0.5 + 0.5 * tanh
            act_s[rows, cols] = (pre * half_up).astype(BF16)
            slope = half_up + 0.5 * pre * (1.0 - tanh * tanh) * (
                GELU_A + (3.0 * GELU_A * GELU_B) * square
            )
            dpre[rows, cols] = slope.astype(BF16)

    def near_units(s, carry):
        @pl.when(s == 1)
        def _():
            qg_c(0, hidden).wait_recv()
            ag_pump(2, 1)

        forward_units(2 * y + lax.rem(s + c, 2))
        return carry

    lax.fori_loop(0, 2, near_units, 0)
    qg_y(0, hidden).wait_recv()
    qg_f(0, hidden).start()
    ag_pump(2, 2)

    def far_units(s, carry):
        @pl.when(s == 1)
        def _():
            qg_f(0, hidden).wait_recv()

        forward_units(2 * (1 - y) + lax.rem(s + c, 2))
        return carry

    lax.fori_loop(0, 2, far_units, 0)

    def grad_block(b, left, right):
        def tile(t, carry):
            cols = rows_at(t * 256, 256, 256)
            gmat[b, cols, :] = mm(left[:, cols], right[...], TN).astype(BF16)
            return carry

        lax.fori_loop(0, width // 256, tile, 0)

    def g_rows(b, owner):
        return gmat.at[b, rows_at(owner * shard, shard, shard), :]

    def gx(b, zi):
        return rcopy(g_rows(b, 2 * zi + 1 - x), xr.at[b, zi], 54 + 4 * b + zi, x_dev)

    def gz(b, j):
        return rcopy(zs.at[b, j - 1], zr.at[b, j - 1], 66 + 3 * b + j - 1, z_dev(j))

    def g_start(b):
        for j in (3, 2, 1, 0):
            gx(b, z_other(j) if j else z).start()

    def g_pump(b, j):
        zo = z_other(j)
        gx(b, zo).wait_recv()
        mine_x = gmat[b, rows_at((2 * zo + x) * shard, shard, shard), :].astype(F32)
        zs[b, j - 1] = (mine_x + xr[b, zo].astype(F32)).astype(BF16)
        gz(b, j).start()

    def g_finish(b):
        gx(b, z).wait_recv()
        total = gmat[b, mine, :].astype(F32) + xr[b, z].astype(F32)
        for j in (1, 2, 3):
            gz(b, j).wait_recv()
            total = total + zr[b, j - 1].astype(F32)
        gsum_o[b] = total

    def g_drain(b):
        for zi in range(4):
            gx(b, zi).wait_send()
        for j in (1, 2, 3):
            gz(b, j).wait_send()

    grad_block(2, dmlp, act_s)
    g_start(2)
    ag_finish(2)

    def backward_units(which):
        rows = rows_at(which * quarter, quarter, quarter)
        gq = dmlp[rows, :]
        for t in range(width // 256):
            cols = slice(t * 256, (t + 1) * 256)
            d_act = mm(gq, w[2, :, cols]).astype(BF16).astype(F32)
            d_low = (dpre[rows, cols].astype(F32) * d_act).astype(BF16)
            dpre[rows, cols] = d_low
            sm[6:7, cols] = sm[6:7, cols] + jnp.sum(d_low.astype(F32), 0, keepdims=True)
        return mm(dpre[rows, :], w[1], NT)

    rs_loop(1, backward_units)
    g_pump(2, 3)
    grad_block(1, hidden, dpre)
    g_start(1)
    g_pump(2, 2)

    def branch(which):
        rows = rows_at(which * quarter, quarter, quarter)
        return mm(act_s[rows, :], w[2], NT)

    rs_loop(2, branch, start_y=False)

    g_pump(2, 1)

    d_hidden = rs_result(1)
    scaled = xhat2[...]
    sm[2:3, :] = jnp.sum(d_hidden * scaled, 0, keepdims=True)
    sm[3:4, :] = jnp.sum(d_hidden, 0, keepdims=True)
    weighted = d_hidden * vec[2]
    d_mid = cot[own, :] + inv2[...] * (
        weighted
        - jnp.mean(weighted, -1, keepdims=True)
        - scaled * jnp.mean(weighted * scaled, -1, keepdims=True)
    )
    fin[1] = d_mid
    d_attn = (BRANCH_SCALE * d_mid).astype(BF16)
    dattn[own, :] = d_attn
    sm[4:5, :] = jnp.sum(d_attn.astype(F32), 0, keepdims=True)
    qg_y(1, dattn).start()
    qg_c(1, dattn).start()

    dk_s[...] = jnp.zeros_like(dk_s)
    dv_s[...] = jnp.zeros_like(dv_s)

    def attend_back(i):
        first, last = i * quarter, (i + 1) * quarter
        rows = slice(first, last)
        d_mixed = mm(dattn[rows, :], w[0, :, 512:768]).astype(BF16)
        for h in range(heads):
            cols = slice((h + 1) * HD, (h + 2) * HD)
            d_out = d_mixed[:, cols].astype(F32)
            inverse = linv[h, rows, :]
            d_scaled = d_out * inverse
            inner = jnp.sum(d_scaled * mixed[rows, cols].astype(F32), -1, keepdims=True)
            d_scaled = d_scaled.astype(BF16)
            expo = e_s[h, rows, 0:last]
            d_probs = mm(d_scaled, v_s[h, 0:last, :], NT)
            d_scores = (expo.astype(F32) * (d_probs - inner)).astype(BF16)
            d_q = mm(d_scores, k_s[h, 0:last, :]) * HD**-0.5
            dqkv[rows, h * HD : (h + 1) * HD] = d_q.astype(BF16)
            dk_s[h, 0:last, :] = dk_s[h, 0:last, :] + mm(d_scores, q_s[h, rows, :], TN)
            dv_s[h, 0:last, :] = dv_s[h, 0:last, :] + mm(expo, d_scaled, TN)

    def back_step(s, carry):
        half = lax.div(s, 2)
        odd = lax.rem(s, 2)
        yq = (1 - half) * y + half * (1 - y)
        cq = (1 - odd) * c + odd * (1 - c)
        which = 2 * yq + cq

        @pl.when(s == 1)
        def _():
            qg_c(1, dattn).wait_recv()

        @pl.when(s == 2)
        def _():
            g_pump(1, 3)
            g_pump(1, 2)
            qg_y(1, dattn).wait_recv()
            qg_f(1, dattn).start()
            rs_y(2).start()

        @pl.when(s == 3)
        def _():
            qg_f(1, dattn).wait_recv()
            g_pump(1, 1)

        for i in range(tokens // quarter):

            @pl.when(which == i)
            def _():
                attend_back(i)

        return carry

    lax.fori_loop(0, 4, back_step, 0)

    for h in range(heads):
        dqkv[:, hc + h * HD : hc + (h + 1) * HD] = dk_s[h].astype(BF16)
        dqkv[:, 2 * hc + h * HD : 2 * hc + (h + 1) * HD] = dv_s[h].astype(BF16)

    def zero_rows(zo):
        def tile(zi):
            cols = slice(zi * 2 * shard, (zi + 1) * 2 * shard)
            g_qkv = mm(normed[:, cols], dqkv[...], TN)
            g_proj = mm(dattn[:, cols], mixed[...], TN)
            gmat[0, cols, 0:512] = g_qkv[:, 0:512].astype(BF16)
            gmat[0, cols, 512:640] = (g_qkv[:, 512:640] + g_proj[:, 0:128]).astype(BF16)
            gmat[0, cols, 640:768] = g_proj[:, 128:256].astype(BF16)

        for zi in range(4):

            @pl.when(zo == zi)
            def _():
                tile(zi)

        gx(0, zo).start()

    def zero_pair(first, second):
        def step(s, carry):
            zero_rows((1 - s) * first + s * second)
            return carry

        lax.fori_loop(0, 2, step, 0)

    zero_pair(z_other(3), z_other(2))

    def first_back(which):
        rows = rows_at(which * quarter, quarter, quarter)
        d_low = dqkv[rows, :]
        part = mm(d_low, w[0, :, 0:640], NT)
        rounded = part.astype(BF16).astype(F32)
        sm[0:1, :] = sm[0:1, :] + jnp.sum(rounded * xhat[rows, :], 0, keepdims=True)
        sm[1:2, :] = sm[1:2, :] + jnp.sum(rounded, 0, keepdims=True)
        sums = jnp.sum(d_low.astype(F32), 0, keepdims=True)
        sm[7:8, 0:hc] = sm[7:8, 0:hc] + sums[:, 0:hc]
        sm[7:8, 256 : 256 + hc] = sm[7:8, 256 : 256 + hc] + sums[:, 2 * hc : 3 * hc]
        return part

    rs_loop(3, first_back)

    small_x = rcopy(sm, smx, 75, x_dev)
    small_x.start()
    zero_pair(z_other(1), z)
    g_pump(0, 3)
    small_x.wait_recv()
    smz[z] = sm[...] + smx[...]

    def small_z(j):
        return rcopy(smz.at[z], smz.at[z], 76 + j - 1, z_dev(j))

    for j in (3, 2, 1):
        small_z(j).start()
    g_pump(0, 2)
    g_finish(2)
    g_finish(1)
    out_o[...] = mid[...] + BRANCH_SCALE * (rs_result(2) + vec[5])
    g_pump(0, 1)
    for j in (1, 2, 3):
        rcopy(smz.at[z_other(j)], smz.at[z_other(j)], 76 + j - 1, z_dev(j)).wait_recv()
    smy[0] = (smz[0] + smz[1]) + (smz[2] + smz[3])
    small_y = rcopy(smy.at[0], smy.at[1], 79, y_dev)
    small_y.start()

    d_normed = rs_result(3)
    scaled = xhat[own, :]
    weighted = d_normed * gain_one
    grad_o[...] = fin[1] + inv1[own, :] * (
        weighted
        - jnp.mean(weighted, -1, keepdims=True)
        - scaled * jnp.mean(weighted * scaled, -1, keepdims=True)
    )
    small_y.wait_recv()
    smc[0] = smy[0] + smy[1]
    small_c = rcopy(smc.at[0], smc.at[1], 80, c_dev)
    small_c.start()
    g_finish(0)
    small_c.wait_recv()
    small_o[0:6, :] = smc[0, 0:6, :] + smc[1, 0:6, :]
    small_o[6:8, :] = smy[0, 6:8, :]

    for b in range(3):
        ag_drain(b)
        g_drain(b)
    for k in range(4):
        rs_y(k).wait_send()
    rs_core_drain(2)
    rs_core_drain(3)
    qg_drain(0, hidden)
    qg_drain(1, dattn)
    small_x.wait_send()
    for j in (1, 2, 3):
        small_z(j).wait_send()
    small_y.wait_send()
    small_c.wait_send()


def run_block(resid, cotangent, win, wout, bias, vec, rows, n_dp):
    tokens, width = resid.shape
    quarter = tokens // 4
    head_cols = win.shape[2]
    heads = head_cols // HD
    sizes = (tokens, width, quarter, heads, rows)
    vm = pltpu.VMEM
    scratch = [
        vm((tokens, width), F32),
        vm((tokens, width), F32),
        vm((tokens, 1), F32),
        vm((tokens, width), BF16),
        vm((tokens, width), BF16),
        vm((3, width, width), BF16),
        vm((heads, tokens, HD), BF16),
        vm((heads, tokens, HD), BF16),
        vm((heads, tokens, HD), BF16),
        vm((heads, tokens, tokens), BF16),
        vm((heads, tokens, 1), F32),
        vm((tokens, 256), BF16),
        vm((2, 2, quarter, width), BF16),
        vm((4, 2, quarter, width), BF16),
        vm((4, quarter, width), F32),
        vm((4, quarter, width), BF16),
        vm((4, quarter, width), BF16),
        vm((quarter, width), F32),
        vm((quarter, width), F32),
        vm((quarter, 1), F32),
        vm((tokens, width), BF16),
        vm((tokens, width), BF16),
        vm((tokens, width), BF16),
        vm((tokens, width), BF16),
        vm((heads, tokens, HD), F32),
        vm((heads, tokens, HD), F32),
        vm((tokens, 640), BF16),
        vm((3, width, width), BF16),
        vm((3, 4, rows, width), BF16),
        vm((3, 3, rows, width), BF16),
        vm((3, 3, rows, width), BF16),
        vm((8, width), F32),
        vm((8, width), F32),
        vm((4, 8, width), F32),
        vm((2, 8, width), F32),
        vm((2, 8, width), F32),
        pltpu.SemaphoreType.DMA((2,)),
        pltpu.SemaphoreType.DMA((81,)),
        pltpu.SemaphoreType.DMA((81,)),
    ]
    whole = pl.BlockSpec(memory_space=pltpu.VMEM)
    return pl.pallas_call(
        functools.partial(block_kernel, sizes),
        out_shape=(
            jax.ShapeDtypeStruct((quarter, width), F32),
            jax.ShapeDtypeStruct((quarter, width), F32),
            jax.ShapeDtypeStruct((3, rows, width), F32),
            jax.ShapeDtypeStruct((8, width), F32),
        ),
        in_specs=[pl.BlockSpec(memory_space=pl.ANY)] * 2 + [whole] * 4,
        out_specs=[whole] * 4,
        scratch_shapes=scratch,
        compiler_params=pltpu.CompilerParams(
            collective_id=1, has_side_effects=True, vmem_limit_bytes=62 << 20
        ),
        name="block",
    )(resid, cotangent, win, wout, bias, vec)


def adam_kernel(
    sizes,
    out_h,
    grad_h,
    gsum,
    small,
    win,
    m1_in,
    m2_in,
    wout,
    m1_out,
    m2_out,
    wb,
    m1_b,
    m2_b,
    wv,
    m1_v,
    m2_v,
    *refs,
):
    out_o, grad_o = refs[0:2]
    outs = refs[2:14]
    vin = refs[14:17]
    vout = refs[17:20]
    rin = refs[20:23]
    rout = refs[23:26]
    sems = refs[26]
    hc = sizes
    count = [0]

    def copy(src, dst):
        made = pltpu.make_async_copy(src, dst, sems.at[count[0]])
        count[0] += 1
        made.start()
        return made

    loads_in = [copy(src, dst) for src, dst in zip((m1_in, m2_in, win), vin)]
    loads_out = [copy(src, dst) for src, dst in zip((m1_out, m2_out, wout), vout)]
    done = [copy(out_h, out_o), copy(grad_h, grad_o)]
    rate_in, rate_out = 0.5 * D ** (-0.5), 2.0 * D ** (-0.5)

    for i in range(6):
        new = adam_step(wv[i], m1_v[i], m2_v[i], small[i : i + 1, :], SMALL_RATE, 0.0)
        for ref, value in zip(outs[9:12], new):
            ref[i] = value
        at = (7, 0) if i == 0 else (7, 256) if i == 1 else (6, (i - 2) * hc)
        part = small[at[0] : at[0] + 1, at[1] : at[1] + hc]
        new = adam_step(wb[i], m1_b[i], m2_b[i], part, SMALL_RATE, 0.0)
        for ref, value in zip(outs[6:9], new):
            ref[i] = value

    for load in loads_in:
        load.wait()
    for i in range(7):
        b, at = (0, i * hc) if i < 3 else (1, (i - 3) * hc)
        new = adam_step(vin[2][i], vin[0][i], vin[1][i], gsum[b, :, at : at + hc], rate_in, DECAY)
        for ref, value in zip(rin, new):
            ref[i] = value
    done += [copy(src, dst) for src, dst in zip(rin, outs[0:3])]
    for load in loads_out:
        load.wait()
    for i in range(5):
        b, at = (0, 3 * hc) if i < 1 else (2, (i - 1) * hc)
        part = jnp.transpose(gsum[b, :, at : at + hc])
        new = adam_step(vout[2][i], vout[0][i], vout[1][i], part, rate_out, DECAY)
        for ref, value in zip(rout, new):
            ref[i] = value
    done += [copy(src, dst) for src, dst in zip(rout, outs[3:6])]
    for made in done:
        made.wait()


def run_adam(*operands):
    hc = operands[4].shape[2]
    shapes = [operands[0], operands[1], *operands[4:16]]
    hbm = pl.BlockSpec(memory_space=pl.ANY)
    whole = pl.BlockSpec(memory_space=pltpu.VMEM)
    big_in, big_out = operands[4].shape, operands[7].shape
    return pl.pallas_call(
        functools.partial(adam_kernel, hc),
        out_shape=[jax.ShapeDtypeStruct(a.shape, F32) for a in shapes],
        in_specs=[hbm] * 2 + [whole] * 2 + [hbm] * 6 + [whole] * 6,
        out_specs=[hbm] * 8 + [whole] * 6,
        scratch_shapes=[pltpu.VMEM(big_in, F32)] * 3
        + [pltpu.VMEM(big_out, F32)] * 3
        + [pltpu.VMEM(big_in, F32)] * 3
        + [pltpu.VMEM(big_out, F32)] * 3
        + [pltpu.SemaphoreType.DMA((14,))],
        compiler_params=pltpu.CompilerParams(vmem_limit_bytes=62 << 20),
        name="adam",
    )(*operands)


def fused_shards(
    resid,
    cotangent,
    master_in,
    moment1_in,
    moment2_in,
    master_out,
    moment1_out,
    moment2_out,
    master_bias,
    moment1_bias,
    moment2_bias,
    master_vec,
    moment1_vec,
    moment2_vec,
):
    rows = master_in.shape[1]
    hc = master_in.shape[3]
    turned = [jnp.transpose(a[0], (1, 0, 2)) for a in (master_in, moment1_in, moment2_in)]
    plain = [a[0] for a in (master_out, moment1_out, moment2_out)]
    biases = [a.reshape(6, 1, hc) for a in (master_bias, moment1_bias, moment2_bias)]
    vectors = [a.reshape(6, 1, D) for a in (master_vec, moment1_vec, moment2_vec)]
    sums = run_block(
        resid, cotangent, turned[0], plain[0], biases[0], vectors[0], rows, lax.axis_size("dp")
    )
    new = run_adam(*sums, *turned, *plain, *biases, *vectors)
    return (
        new[0],
        new[1],
        *[jnp.transpose(a, (1, 0, 2))[None] for a in new[2:5]],
        *[a[None] for a in new[5:8]],
        *[a.reshape(1, 6, hc) for a in new[8:11]],
        *[a.reshape(1, 6, D) for a in new[11:14]],
    )


def solution(mesh):
    fused = mesh.shape["dp"] == 8 and mesh.shape["tensor"] == 4
    return jax.shard_map(
        fused_shards if fused else shards,
        mesh=mesh,
        in_specs=(
            P("dp", None),
            P("dp", None),
            P(None, "dp", None, "tensor"),
            P(None, "dp", None, "tensor"),
            P(None, "dp", None, "tensor"),
            P(None, None, "tensor", "dp"),
            P(None, None, "tensor", "dp"),
            P(None, None, "tensor", "dp"),
            P(None, None, "tensor"),
            P(None, None, "tensor"),
            P(None, None, "tensor"),
            P(),
            P(),
            P(),
        ),
        out_specs=(
            P(("dp", "tensor"), None),
            P(("dp", "tensor"), None),
            P(None, "dp", None, "tensor"),
            P(None, "dp", None, "tensor"),
            P(None, "dp", None, "tensor"),
            P(None, None, "tensor", "dp"),
            P(None, None, "tensor", "dp"),
            P(None, None, "tensor", "dp"),
            P(None, None, "tensor"),
            P(None, None, "tensor"),
            P(None, None, "tensor"),
            P(),
            P(),
            P(),
        ),
        check_vma=False,
    )
```

```python
import functools

import jax
import jax.numpy as jnp
from jax import lax
from jax.experimental import pallas as pl
from jax.experimental.pallas import tpu as pltpu
from jax.sharding import PartitionSpec as P

D = 768
HD = 64
LEN = 1024
LAYERS = 1
STEP = 10


EPS = 1e-05
BRANCH_SCALE = 48 ** (-0.5)
BETA_ONE = 0.9
BETA_TWO = 0.95
ADAM_EPS = 1e-08
DECAY = 0.1
SMALL_RATE = 0.3
MASKED = -1e30


def norm_rows(stream, gain, shift):
    center = stream - jnp.mean(stream, -1, keepdims=True)
    inverse = lax.rsqrt(jnp.mean(center * center, -1, keepdims=True) + EPS)
    scaled = center * inverse
    return (scaled * gain + shift, scaled, inverse)


def norm_back(grad_out, scaled, inverse, gain):
    weighted = grad_out * gain
    centered = weighted - jnp.mean(weighted, -1, keepdims=True)
    return inverse * (centered - scaled * jnp.mean(weighted * scaled, -1, keepdims=True))


def plain_dot(left, right):
    return jnp.dot(left, right, preferred_element_type=jnp.float32)


def left_dot(left, right):
    return lax.dot_general(
        left, right, (((0,), (0,)), ((), ())), preferred_element_type=jnp.float32
    )


def right_dot(left, right):
    return lax.dot_general(
        left, right, (((1,), (1,)), ((), ())), preferred_element_type=jnp.float32
    )


def smooth_gate(values_in):
    return jax.nn.gelu(values_in, approximate=True)


def tensor_rows(array_in):
    quarter = array_in.shape[0] // lax.axis_size("tensor")
    return lax.dynamic_slice_in_dim(array_in, lax.axis_index("tensor") * quarter, quarter, 0)


def own_rows(array_in):
    return tensor_rows(array_in)


def branch_total(partial_sum):
    return lax.psum(partial_sum.astype(jnp.bfloat16), "tensor").astype(jnp.float32)


def grad_total(partial_sum):
    return lax.psum(partial_sum.astype(jnp.bfloat16), "tensor").astype(jnp.float32)


def causal_scores(queries, key_rows, first, last):
    block_rows = last - first
    scores = jnp.einsum(
        "qhd,khd->hqk", queries[first:last], key_rows[:last], preferred_element_type=jnp.float32
    ) * HD ** (-0.5)
    query_pos = lax.broadcasted_iota(jnp.int32, (block_rows, last), 0) + first
    key_pos = lax.broadcasted_iota(jnp.int32, (block_rows, last), 1)
    return jnp.where(query_pos >= key_pos, scores, MASKED)


def attend_sequence(operands):
    queries, key_rows, value_rows = operands
    block_rows = min(512, LEN)
    outputs = []
    totals = []
    for block_idx in range(LEN // block_rows):
        first = block_idx * block_rows
        last = first + block_rows
        scores = causal_scores(queries, key_rows, first, last)
        highest = jnp.max(scores, -1, keepdims=True)
        expo = jnp.exp(scores - highest)
        summed = jnp.sum(expo, -1, keepdims=True)
        weights = (expo / summed).astype(jnp.bfloat16)
        mixed = jnp.einsum(
            "hqk,khd->qhd", weights, value_rows[:last], preferred_element_type=jnp.float32
        )
        outputs.append(mixed.astype(jnp.bfloat16))
        totals.append((highest + jnp.log(summed))[..., 0])
    return (jnp.concatenate(outputs, 0), jnp.concatenate(totals, 1))


def attend_back(operands):
    queries, key_rows, value_rows, log_total, grad_mixed = operands
    block_rows = min(512, LEN)
    d_keys = jnp.zeros(key_rows.shape, jnp.float32)
    d_values = jnp.zeros(value_rows.shape, jnp.float32)
    d_queries = []
    for block_idx in range(LEN // block_rows):
        first = block_idx * block_rows
        last = first + block_rows
        scores = causal_scores(queries, key_rows, first, last)
        probs = jnp.exp(scores - log_total[:, first:last, None])
        d_probs = jnp.einsum(
            "qhd,khd->hqk",
            grad_mixed[first:last],
            value_rows[:last],
            preferred_element_type=jnp.float32,
        )
        inner = jnp.sum(probs * d_probs, -1, keepdims=True)
        d_scores = (probs * (d_probs - inner)).astype(jnp.bfloat16)
        d_queries.append(
            jnp.einsum(
                "hqk,khd->qhd", d_scores, key_rows[:last], preferred_element_type=jnp.float32
            )
            * HD ** (-0.5)
        )
        key_part = jnp.einsum(
            "hqk,qhd->khd", d_scores, queries[first:last], preferred_element_type=jnp.float32
        ) * HD ** (-0.5)
        value_part = jnp.einsum(
            "hqk,qhd->khd",
            probs.astype(jnp.bfloat16),
            grad_mixed[first:last],
            preferred_element_type=jnp.float32,
        )
        d_keys = d_keys.at[:last].add(key_part)
        d_values = d_values.at[:last].add(value_part)
    return (jnp.concatenate(d_queries, 0), d_keys, d_values)


def layer_forward(stream, w_in, w_out, bias, vector):
    model_width = w_in.shape[0]
    head_cols = w_in.shape[2]
    heads_here = head_cols // HD
    normed, scaled_one, inverse_one = norm_rows(stream, vector[0], vector[1])
    normed_low = normed.astype(jnp.bfloat16)
    seq_count = normed_low.shape[0] // LEN
    shape4 = (seq_count, LEN, heads_here, HD)
    w_qkv = w_in[:, 0:3].reshape(model_width, 3 * head_cols)
    projected = plain_dot(normed_low, w_qkv)
    queries = (projected[:, :head_cols] + bias[0]).astype(jnp.bfloat16).reshape(shape4)
    key_rows = projected[:, head_cols : 2 * head_cols].astype(jnp.bfloat16).reshape(shape4)
    value_rows = (projected[:, 2 * head_cols :] + bias[1]).astype(jnp.bfloat16).reshape(shape4)
    mixed, log_total = lax.map(attend_sequence, (queries, key_rows, value_rows))
    mixed_low = mixed.reshape(-1, head_cols)
    attended = branch_total(plain_dot(mixed_low, w_out[0])) + vector[4]
    middle = stream + BRANCH_SCALE * attended
    hidden, scaled_two, inverse_two = norm_rows(middle, vector[2], vector[3])
    hidden_low = hidden.astype(jnp.bfloat16)
    w_up = w_in[:, 3:].reshape(model_width, 4 * head_cols)
    pre_act = plain_dot(hidden_low, w_up) + bias[2:].reshape(4 * head_cols)
    act_low = smooth_gate(pre_act).astype(jnp.bfloat16)
    w_down = w_out[1:].reshape(4 * head_cols, model_width)
    mlp_out = branch_total(plain_dot(act_low, w_down)) + vector[5]
    result = middle + BRANCH_SCALE * mlp_out
    kept = (
        scaled_one,
        inverse_one,
        normed_low,
        queries,
        key_rows,
        value_rows,
        log_total,
        mixed_low,
        scaled_two,
        inverse_two,
        hidden_low,
        pre_act,
        act_low,
    )
    return (result, kept)


def layer_backward(gradient, w_in, w_out, vector, kept):
    (
        scaled_one,
        inverse_one,
        normed_low,
        queries,
        key_rows,
        value_rows,
        log_total,
        mixed_low,
        scaled_two,
        inverse_two,
        hidden_low,
        pre_act,
        act_low,
    ) = kept
    model_width = w_in.shape[0]
    head_cols = w_in.shape[2]
    w_qkv = w_in[:, 0:3].reshape(model_width, 3 * head_cols)
    w_up = w_in[:, 3:].reshape(model_width, 4 * head_cols)
    w_down = w_out[1:].reshape(4 * head_cols, model_width)
    d_mlp = (BRANCH_SCALE * gradient).astype(jnp.bfloat16)
    g_bdown = jnp.sum(own_rows(d_mlp).astype(jnp.float32), 0)
    g_down = left_dot(act_low, d_mlp).reshape(4, head_cols, model_width)
    d_act = right_dot(d_mlp, w_down).astype(jnp.bfloat16)
    gate_value, gate_pull = jax.vjp(smooth_gate, pre_act)
    d_pre = gate_pull(d_act.astype(jnp.float32))[0].astype(jnp.bfloat16)
    g_bup = jnp.sum(d_pre.astype(jnp.float32), 0)
    g_up = left_dot(hidden_low, d_pre).reshape(model_width, 4, head_cols)
    d_hidden = grad_total(right_dot(d_pre, w_up))
    g_gain_two = jnp.sum(own_rows(d_hidden * scaled_two), 0)
    g_shift_two = jnp.sum(own_rows(d_hidden), 0)
    d_middle = gradient + norm_back(d_hidden, scaled_two, inverse_two, vector[2])
    d_attn = (BRANCH_SCALE * d_middle).astype(jnp.bfloat16)
    g_bproj = jnp.sum(own_rows(d_attn).astype(jnp.float32), 0)
    g_proj = left_dot(mixed_low, d_attn)
    d_mixed = right_dot(d_attn, w_out[0]).astype(jnp.bfloat16)
    d_queries, d_keys, d_values = lax.map(
        attend_back, (queries, key_rows, value_rows, log_total, d_mixed.reshape(queries.shape))
    )
    d_qkv = jnp.concatenate(
        [
            d_queries.reshape(-1, head_cols),
            d_keys.reshape(-1, head_cols),
            d_values.reshape(-1, head_cols),
        ],
        1,
    ).astype(jnp.bfloat16)
    g_qkv = left_dot(normed_low, d_qkv).reshape(model_width, 3, head_cols)
    g_bq = jnp.sum(d_qkv[:, :head_cols].astype(jnp.float32), 0)
    g_bv = jnp.sum(d_qkv[:, 2 * head_cols :].astype(jnp.float32), 0)
    d_normed = grad_total(right_dot(d_qkv, w_qkv))
    g_gain_one = jnp.sum(own_rows(d_normed * scaled_one), 0)
    g_shift_one = jnp.sum(own_rows(d_normed), 0)
    d_stream = d_middle + norm_back(d_normed, scaled_one, inverse_one, vector[0])
    g_in = jnp.concatenate([g_qkv, g_up], 1)
    g_out = jnp.concatenate([g_proj[None], g_down], 0)
    g_bias = jnp.concatenate([g_bq[None], g_bv[None], g_bup.reshape(4, head_cols)], 0)
    g_vector = jnp.stack([g_gain_one, g_shift_one, g_gain_two, g_shift_two, g_bproj, g_bdown])
    return (d_stream, g_in, g_out, g_bias, g_vector)


def adam_step(master, first, second, gradient, rate, decay):
    first_new = BETA_ONE * first + (1 - BETA_ONE) * gradient
    second_new = BETA_TWO * second + (1 - BETA_TWO) * gradient * gradient
    direction = (
        first_new / (1 - BETA_ONE**STEP) / (jnp.sqrt(second_new / (1 - BETA_TWO**STEP)) + ADAM_EPS)
    )
    return (first_new, second_new, master - rate * (direction + decay * master))


def shards(
    resid,
    cotangent,
    master_in,
    moment1_in,
    moment2_in,
    master_out,
    moment1_out,
    moment2_out,
    master_bias,
    moment1_bias,
    moment2_bias,
    master_vec,
    moment1_vec,
    moment2_vec,
):
    weights_in, weights_out = (
        lax.all_gather(master_in.astype(jnp.bfloat16), "dp", axis=1, tiled=True),
        lax.all_gather(master_out.astype(jnp.bfloat16), "dp", axis=3, tiled=True),
    )
    stream = resid
    gradient = cotangent
    layer_idx = 0
    stream, kept = layer_forward(
        stream,
        weights_in[layer_idx],
        weights_out[layer_idx],
        master_bias[layer_idx],
        master_vec[layer_idx],
    )
    kept_list = [kept]
    list_in = [None] * LAYERS
    list_out = [None] * LAYERS
    list_bias = [None] * LAYERS
    list_vector = [None] * LAYERS
    layer_idx = 0
    gradient, g_in, g_out, g_bias, g_vector = layer_backward(
        gradient,
        weights_in[layer_idx],
        weights_out[layer_idx],
        master_vec[layer_idx],
        kept_list[layer_idx],
    )
    list_in[layer_idx] = g_in
    list_out[layer_idx] = g_out
    list_bias[layer_idx] = g_bias
    list_vector[layer_idx] = g_vector
    summed_in = jnp.stack(list_in)
    summed_out = jnp.stack(list_out)
    summed_in, summed_out = (
        lax.psum_scatter(summed_in, "dp", scatter_dimension=1, tiled=True),
        lax.psum_scatter(summed_out, "dp", scatter_dimension=3, tiled=True),
    )
    summed_bias = lax.psum(jnp.stack(list_bias), "dp")
    summed_vector = lax.psum(jnp.stack(list_vector), ("dp", "tensor"))
    first_in, second_in, new_in = adam_step(
        master_in, moment1_in, moment2_in, summed_in, 0.5 * D ** (-0.5), DECAY
    )
    first_out, second_out, new_out = adam_step(
        master_out, moment1_out, moment2_out, summed_out, 2.0 * D ** (-0.5), DECAY
    )
    first_bias, second_bias, new_bias = adam_step(
        master_bias, moment1_bias, moment2_bias, summed_bias, SMALL_RATE, 0.0
    )
    first_vec, second_vec, new_vec = adam_step(
        master_vec, moment1_vec, moment2_vec, summed_vector, SMALL_RATE, 0.0
    )
    return (
        own_rows(stream),
        own_rows(gradient),
        first_in,
        second_in,
        new_in,
        first_out,
        second_out,
        new_out,
        first_bias,
        second_bias,
        new_bias,
        first_vec,
        second_vec,
        new_vec,
    )


MESH_IDS = pl.DeviceIdType.MESH
F32 = jnp.float32
BF16 = jnp.bfloat16
NN = (((1,), (0,)), ((), ()))
NT = (((1,), (1,)), ((), ()))
TN = (((0,), (0,)), ((), ()))
GELU_A = (2.0 / 3.141592653589793) ** 0.5
GELU_B = 0.044715


def mm(left, right, dims=NN):
    return lax.dot_general(left, right, dims, preferred_element_type=F32)


def rows_at(start, size, align):
    return pl.ds(pl.multiple_of(start, align), size)


def block_kernel(
    sizes,
    resid_h,
    cot_h,
    win_h,
    wout_h,
    bias,
    vec,
    out_o,
    grad_o,
    gsum_o,
    small_o,
    win,
    wout,
    resid,
    cot,
    inv1,
    normed,
    dmlp,
    w,
    q_s,
    k_s,
    v_s,
    e_s,
    linv,
    mixed,
    ps,
    crecv,
    fin,
    ysend,
    yrecv,
    mid,
    xhat2,
    inv2,
    normed_t,
    hidden,
    act_s,
    dpre,
    dattn,
    dmix,
    dk_s,
    dv_s,
    dqkv,
    gproj,
    gmat,
    xr,
    zs,
    zr,
    sm,
    smx,
    smz,
    smy,
    smc,
    lsem,
    ssem,
    rsem,
):
    tokens, width, quarter, heads, shard = sizes
    dp = lax.axis_index("dp")
    ten = lax.axis_index("tensor")
    z = lax.div(dp, 2)
    x = lax.rem(dp, 2)
    y = lax.div(ten, 2)
    c = lax.rem(ten, 2)
    x_dev = (dp + 1 - 2 * x, ten)
    c_dev = (dp, ten + 1 - 2 * c)
    y_dev = (dp, ten + 2 - 4 * y)

    def z_other(j):
        if j == 1:
            return z + 1 - 2 * lax.rem(z, 2)
        if j == 2:
            return lax.rem(z + 2, 4)
        return 3 - z

    def z_dev(j):
        return (2 * z_other(j) + x, ten)

    def rcopy(src, dst, idx, dev, recv_idx=None):
        return pltpu.make_async_remote_copy(
            src_ref=src,
            dst_ref=dst,
            send_sem=ssem.at[idx],
            recv_sem=rsem.at[idx if recv_idx is None else recv_idx],
            device_id=dev,
            device_id_type=MESH_IDS,
        )

    barrier = pltpu.get_barrier_semaphore()
    peers = [x_dev, c_dev, y_dev, z_dev(1), z_dev(2), z_dev(3)]
    for dev in peers:
        pl.semaphore_signal(barrier, inc=1, device_id=dev, device_id_type=MESH_IDS)
    load_win = pltpu.make_async_copy(win_h, win, lsem.at[2])
    load_wout = pltpu.make_async_copy(wout_h, wout, lsem.at[3])
    load_win.start()
    load_wout.start()
    load_resid = pltpu.make_async_copy(resid_h, resid, lsem.at[0])
    load_cot = pltpu.make_async_copy(cot_h, cot, lsem.at[1])
    load_resid.start()
    load_cot.start()

    mine = rows_at(dp * shard, shard, shard)
    load_win.wait()
    load_wout.wait()
    out_t = [jnp.transpose(wout[i]) for i in range(5)]
    by_head = [win[i, :, h * HD : (h + 1) * HD] for h in range(heads) for i in range(3)]
    w[0, mine, :] = jnp.concatenate([*by_head, out_t[0]], 1).astype(BF16)

    w[1, mine, :] = jnp.concatenate([win[3 + i] for i in range(4)], 1).astype(BF16)
    w[2, mine, :] = jnp.concatenate(out_t[1:], 1).astype(BF16)
    pl.semaphore_wait(barrier, len(peers))

    is_end = 1 - lax.rem(lax.div(z + 1, 2), 2)
    is_mid = 1 - is_end
    upper = lax.div(z, 2)
    pair_dev = (2 * z_other(1) + x, ten)
    mid_dev = (2 * (2 - upper) + x, ten)
    owner_z = (z_other(1), 2 - upper, 3 - 3 * upper)
    ag_parts = (2, 1, 1)
    ag_base = (0, 18, 27)

    def piece(b, zi, p):
        size = shard // ag_parts[b]
        return w.at[b, rows_at((2 * zi + x) * shard + p * size, size, size), :]

    def ag_copy(b, zi, p, send, recv, dev):
        src = piece(b, zi, p)
        n = ag_parts[b]
        return rcopy(src, src, ag_base[b] + n * send + p, dev, ag_base[b] + n * recv + p)

    def ag_pair(b, p):
        return ag_copy(b, z, p, 0, 0, pair_dev)

    def ag_mid(b, p):
        return ag_copy(b, z, p, 1, 1, mid_dev)

    def ag_onward(b, i, p):
        if i == 0:
            return ag_copy(b, owner_z[0], p, 2, 2, mid_dev)
        return ag_copy(b, owner_z[i], p, 2 + i, i, pair_dev)

    def ag_x(b, i, p):
        return ag_copy(b, z if i == 0 else owner_z[i - 1], p, 5 + i, 4 + i, x_dev)

    def ag_start_x(b):
        for p in range(ag_parts[b]):
            ag_x(b, 0, p).start()

    def ag_start_z(b):
        for p in range(ag_parts[b]):
            ag_pair(b, p).start()

            @pl.when(is_mid == 1)
            def _():
                ag_mid(b, p).start()

    def ag_arrive(b, i, p):
        ag_copy(b, owner_z[i], p, i, i, x_dev).wait_recv()

    def pump_end(b, i, p=0):
        @pl.when(is_end == 1)
        def _():
            ag_arrive(b, i, p)
            ag_x(b, 1 + i, p).start()

    def pump_mid(b, i, p=0):
        @pl.when(is_mid == 1)
        def _():
            ag_arrive(b, i, p)
            ag_onward(b, i, p).start()
            ag_x(b, 1 + i, p).start()

    def ag_finish(b):
        for p in range(ag_parts[b]):
            for i in range(4):
                ag_x(b, i, p).wait_recv()

    def ag_drain(b):
        for p in range(ag_parts[b]):
            ag_pair(b, p).wait_send()
            for i in range(4):
                ag_x(b, i, p).wait_send()

            @pl.when(is_mid == 1)
            def _():
                ag_mid(b, p).wait_send()
                for i in range(3):
                    ag_onward(b, i, p).wait_send()

    ag_start_x(0)
    ag_start_z(0)

    @pl.when(is_end == 1)
    def _():
        for b in (1, 2):
            ag_pair(b, 0).start()

    load_resid.wait()
    load_cot.wait()
    gain_one, shift_one = vec[0], vec[1]

    own = rows_at(ten * quarter, quarter, quarter)
    mid[...] = resid[own, :]
    xhat = resid

    def first_norm(r, carry):
        rows = rows_at(r * 128, 128, 128)
        part = resid[rows, :]
        center = part - jnp.mean(part, -1, keepdims=True)
        inverse = lax.rsqrt(jnp.mean(center * center, -1, keepdims=True) + EPS)
        scaled = center * inverse
        xhat[rows, :] = scaled
        inv1[rows, :] = inverse
        normed[rows, :] = (scaled * gain_one + shift_one).astype(BF16)
        dmlp[rows, :] = (cot[rows, :] * BRANCH_SCALE).astype(BF16)
        return carry

    lax.fori_loop(0, tokens // 128, first_norm, 0)
    for i, p in ((0, 0), (1, 0), (0, 1), (1, 1), (2, 0), (2, 1)):
        pump_mid(0, i, p)
    for i, p in ((0, 0), (0, 1), (1, 0), (1, 1), (2, 0), (2, 1)):
        pump_end(0, i, p)
    sm[...] = jnp.zeros_like(sm)
    sm[5:6, :] = jnp.sum(dmlp[own, :].astype(F32), 0, keepdims=True)
    mixed[...] = jnp.zeros_like(mixed)
    dqkv[...] = jnp.zeros_like(dqkv)

    ag_start_x(1)
    ag_start_x(2)

    @pl.when(is_mid == 1)
    def _():
        ag_start_z(1)

    for i in range(3):
        pump_mid(1, i)

    @pl.when(is_mid == 1)
    def _():
        ag_start_z(2)

    pump_mid(2, 0)
    ag_finish(0)
    pump_end(1, 0)

    hc = heads * HD
    no_bias = jnp.zeros((1, HD), F32)
    bias_qkv = []
    for h in range(heads):
        at = slice(h * HD, (h + 1) * HD)
        bias_qkv += [bias[0, :, at], no_bias, bias[1, :, at]]
    bias_qkv = jnp.concatenate([*bias_qkv, no_bias], 1)

    def project(r, carry):
        rows = rows_at(r * 256, 256, 256)
        got = (mm(normed[rows, :], w[0, :, 0:640]) + bias_qkv).astype(BF16)
        for h in range(heads):
            at = 3 * h * HD
            q_s[h, rows, :] = got[:, at : at + HD] * jnp.asarray(HD**-0.5, BF16)
            k_s[h, rows, :] = got[:, at + HD : at + 2 * HD]
            v_s[h, rows, :] = got[:, at + 2 * HD : at + 3 * HD]
        return carry

    lax.fori_loop(0, tokens // 256, project, 0)
    pump_end(1, 1)

    def attend(i):
        first, last = i * quarter, (i + 1) * quarter
        rows = slice(first, last)
        causal = lax.broadcasted_iota(jnp.int32, (quarter, quarter), 0) >= lax.broadcasted_iota(
            jnp.int32, (quarter, quarter), 1
        )
        for h in range(heads):
            queries = q_s[h, rows, :]
            diag = jnp.where(causal, mm(queries, k_s[h, rows, :], NT), MASKED)
            highest = jnp.max(diag, -1, keepdims=True)
            if i > 0:
                wide = mm(queries, k_s[h, 0:first, :], NT)
                highest = jnp.maximum(highest, jnp.max(wide, -1, keepdims=True))
            e_diag = jnp.exp(diag - highest)
            summed = jnp.sum(e_diag, -1, keepdims=True)
            e_diag = e_diag.astype(BF16)
            e_s[h, rows, first:last] = e_diag
            total = mm(e_diag, v_s[h, rows, :])
            if i > 0:
                e_wide = jnp.exp(wide - highest)
                summed = summed + jnp.sum(e_wide, -1, keepdims=True)
                e_wide = e_wide.astype(BF16)
                e_s[h, rows, 0:first] = e_wide
                total = total + mm(e_wide, v_s[h, 0:first, :])
            inverse = 1.0 / summed
            linv[h, rows, :] = inverse
            mixed[rows, (h + 1) * HD : (h + 2) * HD] = (total * inverse).astype(BF16)

    def rs_core(k, half):
        return rcopy(ps.at[k % 2, half], crecv.at[k, half], 36 + 2 * k + half, c_dev)

    def rs_y(k):
        return rcopy(ysend.at[k], yrecv.at[k], 44 + k, y_dev)

    def rs_pair(k, near, compute, start_y=True, prepare=None, filler=None):
        half = 1 if near else 0
        if k >= 2:
            rs_core(k - 2, half).wait_send()

        def step(s, carry):
            yq = y if near else 1 - y
            if prepare is not None:
                prepare(s)
            part = compute(2 * yq + lax.rem(1 - s + c, 2))

            @pl.when(s == 0)
            def _():
                ps[k % 2, half] = part.astype(BF16)
                rs_core(k, half).start()

            @pl.when(s == 1)
            def _():
                if filler is not None:
                    fin[(k + 1) % 3] = part
                    filler()
                    kept = fin[(k + 1) % 3]
                else:
                    kept = part
                rs_core(k, half).wait_recv()
                total = kept + crecv[k, half].astype(F32)
                if near:
                    fin[k % 3] = total
                else:
                    ysend[k] = total.astype(BF16)
                    if start_y:
                        rs_y(k).start()

            return carry

        lax.fori_loop(0, 2, step, 0)

    def rs_result(k):
        rs_y(k).wait_recv()
        return fin[k % 3] + yrecv[k].astype(F32)

    def pump_far(s):
        @pl.when(s == 1)
        def _():
            pump_end(1, 2)
            pump_mid(2, 1)

    def pump_near(s):
        @pl.when(s == 0)
        def _():
            pump_mid(2, 2)

        @pl.when(s == 1)
        def _():
            pump_end(2, 0)

    def attend_proj(which):
        for i in range(tokens // quarter):

            @pl.when(which == i)
            def _():
                attend(i)

        return mm(mixed[rows_at(which * quarter, quarter, quarter), :], w[0, :, 512:768], NT)

    rs_pair(0, False, attend_proj, prepare=pump_far)
    rs_pair(0, True, attend_proj, prepare=pump_near)

    def q_rows(ref, which):
        return ref.at[rows_at(which * quarter, quarter, quarter), :]

    def qg_y(g, ref):
        return rcopy(q_rows(ref, ten), q_rows(ref, ten), 48 + g, y_dev)

    def qg_c(g, ref):
        return rcopy(q_rows(ref, ten), q_rows(ref, ten), 50 + g, c_dev)

    def qg_f(g, ref):
        far = ten + 2 - 4 * y
        return rcopy(q_rows(ref, far), q_rows(ref, far), 52 + g, c_dev)

    def qg_drain(g, ref):
        qg_y(g, ref).wait_send()
        qg_c(g, ref).wait_send()
        qg_f(g, ref).wait_send()

    pump_end(2, 1)

    mid[...] = mid[...] + BRANCH_SCALE * (rs_result(0) + vec[4])
    center = mid[...] - jnp.mean(mid[...], -1, keepdims=True)
    inverse = lax.rsqrt(jnp.mean(center * center, -1, keepdims=True) + EPS)
    scaled = center * inverse
    xhat2[...] = scaled
    inv2[...] = inverse
    hidden[own, :] = (scaled * vec[2] + vec[3]).astype(BF16)
    qg_y(0, hidden).start()
    qg_c(0, hidden).start()

    ag_finish(1)

    bias_up = jnp.concatenate([bias[2 + i] for i in range(4)], 1)

    def forward_units(which):
        rows = rows_at(which * quarter, quarter, quarter)
        hq = hidden[rows, :]
        for t in range(width // 256):
            cols = slice(t * 256, (t + 1) * 256)
            pre = mm(hq, w[1, :, cols]) + bias_up[:, cols]
            square = pre * pre
            tanh = jnp.tanh(GELU_A * (pre + GELU_B * (square * pre)))
            half_up = 0.5 + 0.5 * tanh
            act_s[rows, cols] = (pre * half_up).astype(BF16)
            slope = half_up + 0.5 * pre * (1.0 - tanh * tanh) * (
                GELU_A + (3.0 * GELU_A * GELU_B) * square
            )
            dpre[rows, cols] = slope.astype(BF16)

    units = (
        (0, slice(0, 384)),
        (0, slice(384, 768)),
        (1, slice(0, 768)),
        (2, slice(0, 768)),
    )

    def grad_block(b, left, right, near):
        rows = rows_at((y if near else 1 - y) * 2 * quarter, 2 * quarter, 2 * quarter)

        def tile(t, carry):
            cols = rows_at(t * 256, 256, 256)
            part = mm(left[rows, cols], right[rows, :], TN)
            if not near:
                part = part + gmat[b, cols, :].astype(F32)
            gmat[b, cols, :] = part.astype(BF16)
            return carry

        lax.fori_loop(0, width // 256, tile, 0)

    def g_rows(u, owner):
        b, cols = units[u]
        return gmat.at[b, rows_at(owner * shard, shard, shard), cols]

    def gx(u, zi):
        b, cols = units[u]
        return rcopy(g_rows(u, 2 * zi + 1 - x), xr.at[b, zi, :, cols], 54 + 4 * u + zi, x_dev)

    def gz(u, j):
        b, cols = units[u]
        return rcopy(
            zs.at[b, j - 1, :, cols], zr.at[b, j - 1, :, cols], 70 + 3 * u + j - 1, z_dev(j)
        )

    def g_start(u):
        for j in (3, 2, 1, 0):
            gx(u, z_other(j) if j else z).start()

    def g_pump(u, j):
        b, cols = units[u]
        zo = z_other(j)
        gx(u, zo).wait_recv()
        mine_x = gmat[b, rows_at((2 * zo + x) * shard, shard, shard), cols].astype(F32)
        zs[b, j - 1, :, cols] = (mine_x + xr[b, zo, :, cols].astype(F32)).astype(BF16)
        gz(u, j).start()

    def g_finish(u):
        b, cols = units[u]
        gx(u, z).wait_recv()
        total = gmat[b, mine, cols].astype(F32) + xr[b, z, :, cols].astype(F32)
        for j in (1, 2, 3):
            gz(u, j).wait_recv()
            total = total + zr[b, j - 1, :, cols].astype(F32)
        gsum_o[b, :, cols] = total

    def g_drain(u):
        for zi in range(4):
            gx(u, zi).wait_send()
        for j in (1, 2, 3):
            gz(u, j).wait_send()

    def backward_units(which):
        rows = rows_at(which * quarter, quarter, quarter)
        gq = dmlp[rows, :]
        for t in range(width // 256):
            cols = slice(t * 256, (t + 1) * 256)
            d_act = mm(gq, w[2, :, cols]).astype(BF16).astype(F32)
            d_low = (dpre[rows, cols].astype(F32) * d_act).astype(BF16)
            dpre[rows, cols] = d_low
            sm[6:7, cols] = sm[6:7, cols] + jnp.sum(d_low.astype(F32), 0, keepdims=True)
        return mm(dpre[rows, :], w[1], NT)

    def branch(which):
        rows = rows_at(which * quarter, quarter, quarter)
        return mm(act_s[rows, :], w[2], NT)

    def near_units(s, carry):
        @pl.when(s == 1)
        def _():
            qg_c(0, hidden).wait_recv()

        forward_units(2 * y + lax.rem(s + c, 2))
        return carry

    lax.fori_loop(0, 2, near_units, 0)
    pump_end(2, 2)
    grad_block(2, dmlp, act_s, True)
    for t in range(width // 256):
        cols = slice(t * 256, (t + 1) * 256)
        normed_t[cols, :] = jnp.transpose(normed[:, cols])
    ag_finish(2)
    rs_pair(1, True, backward_units)
    grad_block(1, hidden, dpre, True)
    qg_y(0, hidden).wait_recv()
    qg_f(0, hidden).start()

    def far_units(s, carry):
        @pl.when(s == 1)
        def _():
            qg_f(0, hidden).wait_recv()

        forward_units(2 * (1 - y) + lax.rem(s + c, 2))
        return carry

    def down_gradient():
        grad_block(2, dmlp, act_s, False)
        g_start(3)

    lax.fori_loop(0, 2, far_units, 0)
    rs_pair(1, False, backward_units, filler=down_gradient)
    grad_block(1, hidden, dpre, False)
    g_start(2)
    rs_pair(2, False, branch, start_y=False)
    g_pump(3, 3)
    rs_pair(2, True, branch)
    g_pump(3, 2)
    g_pump(3, 1)

    d_hidden = rs_result(1)
    scaled = xhat2[...]
    sm[2:3, :] = jnp.sum(d_hidden * scaled, 0, keepdims=True)
    sm[3:4, :] = jnp.sum(d_hidden, 0, keepdims=True)
    weighted = d_hidden * vec[2]
    d_mid = cot[own, :] + inv2[...] * (
        weighted
        - jnp.mean(weighted, -1, keepdims=True)
        - scaled * jnp.mean(weighted * scaled, -1, keepdims=True)
    )
    fin[1] = d_mid
    d_attn = (BRANCH_SCALE * d_mid).astype(BF16)
    dattn[own, :] = d_attn
    sm[4:5, :] = jnp.sum(d_attn.astype(F32), 0, keepdims=True)
    qg_y(1, dattn).start()
    qg_c(1, dattn).start()

    dk_s[...] = jnp.zeros_like(dk_s)
    dv_s[...] = jnp.zeros_like(dv_s)

    def attend_back(i, which_heads):
        first, last = i * quarter, (i + 1) * quarter
        rows = slice(first, last)
        for h in which_heads:
            cols = slice((h + 1) * HD, (h + 2) * HD)
            d_out = dmix[rows, cols].astype(F32)
            inverse = linv[h, rows, :]
            d_scaled = d_out * inverse
            inner = jnp.sum(d_scaled * mixed[rows, cols].astype(F32), -1, keepdims=True)
            d_scaled = d_scaled.astype(BF16)
            expo = e_s[h, rows, 0:last]
            d_probs = mm(d_scaled, v_s[h, 0:last, :], NT)
            d_scores = (expo.astype(F32) * (d_probs - inner)).astype(BF16)
            d_q = mm(d_scores, k_s[h, 0:last, :]) * HD**-0.5
            dqkv[rows, 3 * h * HD : (3 * h + 1) * HD] = d_q.astype(BF16)
            dk_s[h, :, 0:last] = dk_s[h, :, 0:last] + mm(q_s[h, rows, :], d_scores, TN)
            dv_s[h, :, 0:last] = dv_s[h, :, 0:last] + mm(d_scaled, expo, TN)

    def back_quarters(near, which_heads, fresh, prepare=None):
        def step(s, carry):
            if prepare is not None:
                prepare(s)
            yq = y if near else 1 - y
            which = 2 * yq + lax.rem(s + c, 2)
            if fresh:
                rows = rows_at(which * quarter, quarter, quarter)
                dmix[rows, :] = mm(dattn[rows, :], w[0, :, 512:768]).astype(BF16)
            for i in range(tokens // quarter):

                @pl.when(which == i)
                def _():
                    attend_back(i, which_heads)

            return carry

        lax.fori_loop(0, 2, step, 0)

    def near_ready(s):
        @pl.when(s == 1)
        def _():
            qg_c(1, dattn).wait_recv()

    def far_ready(s):
        @pl.when(s == 1)
        def _():
            qg_f(1, dattn).wait_recv()

    def keys_values(which_heads):
        for h in which_heads:
            at = 3 * h * HD
            dqkv[:, at + HD : at + 2 * HD] = jnp.transpose(dk_s[h]).astype(BF16)
            dqkv[:, at + 2 * HD : at + 3 * HD] = jnp.transpose(dv_s[h]).astype(BF16)

    def zero_rows(u, zo):
        cols = rows_at(zo * 2 * shard, 2 * shard, 2 * shard)
        left = normed_t[cols, :]
        if u == 0:
            gmat[0, cols, 0:384] = mm(left, dqkv[:, 0:384]).astype(BF16)
        else:
            g_qkv = mm(left, dqkv[:, 384:640])
            g_proj = gproj[cols, :]
            gmat[0, cols, 384:512] = g_qkv[:, 0:128].astype(BF16)
            gmat[0, cols, 512:640] = (g_qkv[:, 128:256] + g_proj[:, 0:128]).astype(BF16)
            gmat[0, cols, 640:768] = g_proj[:, 128:256].astype(BF16)
        gx(u, zo).start()

    def zero_unit(u):
        def step(s, carry):
            odd, half = lax.rem(s, 2), lax.div(s, 2)
            early = (1 - odd) * z_other(3) + odd * z_other(2)
            late = (1 - odd) * z_other(1) + odd * z
            zero_rows(u, (1 - half) * early + half * late)
            return carry

        lax.fori_loop(0, 4, step, 0)

    back_quarters(True, (0, 1, 2), True, near_ready)
    g_pump(2, 3)
    g_pump(2, 2)
    qg_y(1, dattn).wait_recv()
    qg_f(1, dattn).start()
    rs_y(2).start()
    back_quarters(False, (0, 1), True, far_ready)
    keys_values((0, 1))
    zero_unit(0)
    gproj[...] = jnp.transpose(mm(mixed[...], dattn[...], TN))

    g_pump(2, 1)
    back_quarters(False, (2,), False)
    keys_values((2,))
    g_pump(0, 3)

    def first_back(which):
        rows = rows_at(which * quarter, quarter, quarter)
        d_low = dqkv[rows, :]
        part = mm(d_low, w[0, :, 0:640], NT)
        rounded = part.astype(BF16).astype(F32)
        sm[0:1, :] = sm[0:1, :] + jnp.sum(rounded * xhat[rows, :], 0, keepdims=True)
        sm[1:2, :] = sm[1:2, :] + jnp.sum(rounded, 0, keepdims=True)
        sm[7:8, 0:640] = sm[7:8, 0:640] + jnp.sum(d_low.astype(F32), 0, keepdims=True)
        return part

    rs_pair(3, False, first_back)
    rs_pair(3, True, first_back)

    small_x = rcopy(sm, smx, 82, x_dev)
    small_x.start()
    g_pump(0, 2)
    zero_unit(1)
    g_pump(0, 1)
    small_x.wait_recv()
    smz[z] = sm[...] + smx[...]

    def small_z(j):
        return rcopy(smz.at[z], smz.at[z], 83 + j - 1, z_dev(j))

    for j in (3, 2, 1):
        small_z(j).start()
    g_finish(3)
    g_finish(2)
    out_o[...] = mid[...] + BRANCH_SCALE * (rs_result(2) + vec[5])
    g_pump(1, 3)
    g_pump(1, 2)
    d_normed = rs_result(3)
    scaled = xhat[own, :]
    weighted = d_normed * gain_one
    grad_o[...] = fin[1] + inv1[own, :] * (
        weighted
        - jnp.mean(weighted, -1, keepdims=True)
        - scaled * jnp.mean(weighted * scaled, -1, keepdims=True)
    )
    g_pump(1, 1)
    for j in (1, 2, 3):
        rcopy(smz.at[z_other(j)], smz.at[z_other(j)], 83 + j - 1, z_dev(j)).wait_recv()
    smy[0] = (smz[0] + smz[1]) + (smz[2] + smz[3])
    small_y = rcopy(smy.at[0], smy.at[1], 86, y_dev)
    small_y.start()
    g_finish(0)
    small_y.wait_recv()
    smc[0] = smy[0] + smy[1]
    small_c = rcopy(smc.at[0], smc.at[1], 87, c_dev)
    small_c.start()
    g_finish(1)
    small_c.wait_recv()
    small_o[0:6, :] = smc[0, 0:6, :] + smc[1, 0:6, :]
    small_o[6:8, :] = smy[0, 6:8, :]

    for b in range(3):
        ag_drain(b)
    for u in range(4):
        g_drain(u)
    for k in range(4):
        rs_y(k).wait_send()
    for k in (2, 3):
        for half in range(2):
            rs_core(k, half).wait_send()
    qg_drain(0, hidden)
    qg_drain(1, dattn)
    small_x.wait_send()
    for j in (1, 2, 3):
        small_z(j).wait_send()
    small_y.wait_send()
    small_c.wait_send()


def run_block(resid, cotangent, win, wout, bias, vec, rows, n_dp):
    tokens, width = resid.shape
    quarter = tokens // 4
    head_cols = win.shape[2]
    heads = head_cols // HD
    sizes = (tokens, width, quarter, heads, rows)
    vm = pltpu.VMEM
    scratch = [
        vm(win.shape, F32),
        vm(wout.shape, F32),
        vm((tokens, width), F32),
        vm((tokens, width), F32),
        vm((tokens, 1), F32),
        vm((tokens, width), BF16),
        vm((tokens, width), BF16),
        vm((3, width, width), BF16),
        vm((heads, tokens, HD), BF16),
        vm((heads, tokens, HD), BF16),
        vm((heads, tokens, HD), BF16),
        vm((heads, tokens, tokens), BF16),
        vm((heads, tokens, 1), F32),
        vm((tokens, 256), BF16),
        vm((2, 2, quarter, width), BF16),
        vm((4, 2, quarter, width), BF16),
        vm((3, quarter, width), F32),
        vm((4, quarter, width), BF16),
        vm((4, quarter, width), BF16),
        vm((quarter, width), F32),
        vm((quarter, width), F32),
        vm((quarter, 1), F32),
        vm((width, tokens), BF16),
        vm((tokens, width), BF16),
        vm((tokens, width), BF16),
        vm((tokens, width), BF16),
        vm((tokens, width), BF16),
        vm((tokens, 256), BF16),
        vm((heads, HD, tokens), F32),
        vm((heads, HD, tokens), F32),
        vm((tokens, 640), BF16),
        vm((width, 256), F32),
        vm((3, width, width), BF16),
        vm((3, 4, rows, width), BF16),
        vm((3, 3, rows, width), BF16),
        vm((3, 3, rows, width), BF16),
        vm((8, width), F32),
        vm((8, width), F32),
        vm((4, 8, width), F32),
        vm((2, 8, width), F32),
        vm((2, 8, width), F32),
        pltpu.SemaphoreType.DMA((4,)),
        pltpu.SemaphoreType.DMA((90,)),
        pltpu.SemaphoreType.DMA((90,)),
    ]
    whole = pl.BlockSpec(memory_space=pltpu.VMEM)
    return pl.pallas_call(
        functools.partial(block_kernel, sizes),
        out_shape=(
            jax.ShapeDtypeStruct((quarter, width), F32),
            jax.ShapeDtypeStruct((quarter, width), F32),
            jax.ShapeDtypeStruct((3, rows, width), F32),
            jax.ShapeDtypeStruct((8, width), F32),
        ),
        in_specs=[pl.BlockSpec(memory_space=pl.ANY)] * 4 + [whole] * 2,
        out_specs=[whole] * 4,
        scratch_shapes=scratch,
        compiler_params=pltpu.CompilerParams(
            collective_id=1, has_side_effects=True, vmem_limit_bytes=62 << 20
        ),
        name="block",
    )(resid, cotangent, win, wout, bias, vec)


def adam_kernel(hc, out_h, grad_h, gsum_h, small, *refs):
    in_h, out_h_mat = refs[0:3], refs[3:6]
    wb, m1_b, m2_b, wv, m1_v, m2_v = refs[6:12]
    out_o, grad_o = refs[12:14]
    outs = refs[14:26]
    vin, vout, rin, rout = refs[26:29], refs[29:32], refs[32:35], refs[35:38]
    gsum, pass_out, pass_grad, sems = refs[38:42]
    count = [0]

    def copy(src, dst):
        made = pltpu.make_async_copy(src, dst, sems.at[count[0]])
        count[0] += 1
        made.start()
        return made

    loads_g = [copy(gsum_h.at[i], gsum.at[i]) for i in range(3)]
    loads_in = [[copy(a.at[i], v.at[i]) for a, v in zip(in_h, vin)] for i in range(7)]
    loads_out = [[copy(a.at[i], v.at[i]) for a, v in zip(out_h_mat, vout)] for i in range(5)]
    passing = [copy(out_h, pass_out), copy(grad_h, pass_grad)]
    done = []

    for i in range(6):
        new = adam_step(wv[i], m1_v[i], m2_v[i], small[i : i + 1, :], SMALL_RATE, 0.0)
        for ref, value in zip(outs[9:12], new):
            ref[i] = value
        if i < 2:
            heads = [(3 * h + 2 * i) * HD for h in range(hc // HD)]
            part = jnp.concatenate([small[7:8, at : at + HD] for at in heads], 1)
        else:
            part = small[6:7, (i - 2) * hc : (i - 1) * hc]
        new = adam_step(wb[i], m1_b[i], m2_b[i], part, SMALL_RATE, 0.0)
        for ref, value in zip(outs[6:9], new):
            ref[i] = value

    for load in loads_g:
        load.wait()
    for i in range(7):
        for load in loads_in[i]:
            load.wait()
        if i < 3:
            heads = [(3 * h + i) * HD for h in range(hc // HD)]
            part = jnp.concatenate([gsum[0, :, at : at + HD] for at in heads], 1)
        else:
            part = gsum[1, :, (i - 3) * hc : (i - 2) * hc]
        new = adam_step(vin[0][i], vin[1][i], vin[2][i], part, 0.5 * D ** (-0.5), DECAY)
        for v, value, o in zip(rin, new, outs[0:3]):
            v[i] = value
            done.append(copy(v.at[i], o.at[i]))
    for i in range(5):
        for load in loads_out[i]:
            load.wait()
        b, at = (0, 3 * hc) if i < 1 else (2, (i - 1) * hc)
        part = jnp.transpose(gsum[b, :, at : at + hc])
        new = adam_step(vout[0][i], vout[1][i], vout[2][i], part, 2.0 * D ** (-0.5), DECAY)
        for v, value, o in zip(rout, new, outs[3:6]):
            v[i] = value
            done.append(copy(v.at[i], o.at[i]))
    for load in passing:
        load.wait()
    done += [copy(pass_out, out_o), copy(pass_grad, grad_o)]
    for made in done:
        made.wait()


def run_adam(*operands):
    hc = operands[4].shape[2]
    shapes = [operands[0], operands[1], *operands[4:16]]
    hbm = pl.BlockSpec(memory_space=pl.ANY)
    whole = pl.BlockSpec(memory_space=pltpu.VMEM)
    big_in, big_out = operands[4].shape, operands[7].shape
    return pl.pallas_call(
        functools.partial(adam_kernel, hc),
        out_shape=[jax.ShapeDtypeStruct(a.shape, F32) for a in shapes],
        in_specs=[hbm] * 3 + [whole] + [hbm] * 6 + [whole] * 6,
        out_specs=[hbm] * 8 + [whole] * 6,
        scratch_shapes=[pltpu.VMEM(big_in, F32)] * 3
        + [pltpu.VMEM(big_out, F32)] * 3
        + [pltpu.VMEM(big_in, F32)] * 3
        + [pltpu.VMEM(big_out, F32)] * 3
        + [pltpu.VMEM(operands[2].shape, F32)]
        + [pltpu.VMEM(operands[0].shape, F32)] * 2
        + [pltpu.SemaphoreType.DMA((79,))],
        compiler_params=pltpu.CompilerParams(vmem_limit_bytes=62 << 20),
        name="adam",
    )(*operands)


def fused_shards(
    resid,
    cotangent,
    master_in,
    moment1_in,
    moment2_in,
    master_out,
    moment1_out,
    moment2_out,
    master_bias,
    moment1_bias,
    moment2_bias,
    master_vec,
    moment1_vec,
    moment2_vec,
):
    rows = master_in.shape[1]
    hc = master_in.shape[3]
    turned = [jnp.transpose(a[0], (1, 0, 2)) for a in (master_in, moment1_in, moment2_in)]
    plain = [a[0] for a in (master_out, moment1_out, moment2_out)]
    biases = [a.reshape(6, 1, hc) for a in (master_bias, moment1_bias, moment2_bias)]
    vectors = [a.reshape(6, 1, D) for a in (master_vec, moment1_vec, moment2_vec)]
    sums = run_block(
        resid, cotangent, turned[0], plain[0], biases[0], vectors[0], rows, lax.axis_size("dp")
    )
    new = run_adam(*sums, *turned, *plain, *biases, *vectors)
    return (
        new[0],
        new[1],
        *[jnp.transpose(a, (1, 0, 2))[None] for a in new[2:5]],
        *[a[None] for a in new[5:8]],
        *[a.reshape(1, 6, hc) for a in new[8:11]],
        *[a.reshape(1, 6, D) for a in new[11:14]],
    )


def solution(mesh):
    fused = mesh.shape["dp"] == 8 and mesh.shape["tensor"] == 4
    return jax.shard_map(
        fused_shards if fused else shards,
        mesh=mesh,
        in_specs=(
            P("dp", None),
            P("dp", None),
            P(None, "dp", None, "tensor"),
            P(None, "dp", None, "tensor"),
            P(None, "dp", None, "tensor"),
            P(None, None, "tensor", "dp"),
            P(None, None, "tensor", "dp"),
            P(None, None, "tensor", "dp"),
            P(None, None, "tensor"),
            P(None, None, "tensor"),
            P(None, None, "tensor"),
            P(),
            P(),
            P(),
        ),
        out_specs=(
            P(("dp", "tensor"), None),
            P(("dp", "tensor"), None),
            P(None, "dp", None, "tensor"),
            P(None, "dp", None, "tensor"),
            P(None, "dp", None, "tensor"),
            P(None, None, "tensor", "dp"),
            P(None, None, "tensor", "dp"),
            P(None, None, "tensor", "dp"),
            P(None, None, "tensor"),
            P(None, None, "tensor"),
            P(None, None, "tensor"),
            P(),
            P(),
            P(),
        ),
        check_vma=False,
    )
```

```python
import functools

import jax
import jax.numpy as jnp
from jax import lax
from jax.experimental import pallas as pl
from jax.experimental.pallas import tpu as pltpu
from jax.sharding import PartitionSpec as P

D = 768
HD = 64
LEN = 1024
LAYERS = 1
STEP = 10


EPS = 1e-05
BRANCH_SCALE = 48 ** (-0.5)
BETA_ONE = 0.9
BETA_TWO = 0.95
ADAM_EPS = 1e-08
DECAY = 0.1
SMALL_RATE = 0.3
MASKED = -1e30


def norm_rows(stream, gain, shift):
    center = stream - jnp.mean(stream, -1, keepdims=True)
    inverse = lax.rsqrt(jnp.mean(center * center, -1, keepdims=True) + EPS)
    scaled = center * inverse
    return (scaled * gain + shift, scaled, inverse)


def norm_back(grad_out, scaled, inverse, gain):
    weighted = grad_out * gain
    centered = weighted - jnp.mean(weighted, -1, keepdims=True)
    return inverse * (centered - scaled * jnp.mean(weighted * scaled, -1, keepdims=True))


def plain_dot(left, right):
    return jnp.dot(left, right, preferred_element_type=jnp.float32)


def left_dot(left, right):
    return lax.dot_general(
        left, right, (((0,), (0,)), ((), ())), preferred_element_type=jnp.float32
    )


def right_dot(left, right):
    return lax.dot_general(
        left, right, (((1,), (1,)), ((), ())), preferred_element_type=jnp.float32
    )


def smooth_gate(values_in):
    return jax.nn.gelu(values_in, approximate=True)


def tensor_rows(array_in):
    quarter = array_in.shape[0] // lax.axis_size("tensor")
    return lax.dynamic_slice_in_dim(array_in, lax.axis_index("tensor") * quarter, quarter, 0)


def own_rows(array_in):
    return tensor_rows(array_in)


def branch_total(partial_sum):
    return lax.psum(partial_sum.astype(jnp.bfloat16), "tensor").astype(jnp.float32)


def grad_total(partial_sum):
    return lax.psum(partial_sum.astype(jnp.bfloat16), "tensor").astype(jnp.float32)


def causal_scores(queries, key_rows, first, last):
    block_rows = last - first
    scores = jnp.einsum(
        "qhd,khd->hqk", queries[first:last], key_rows[:last], preferred_element_type=jnp.float32
    ) * HD ** (-0.5)
    query_pos = lax.broadcasted_iota(jnp.int32, (block_rows, last), 0) + first
    key_pos = lax.broadcasted_iota(jnp.int32, (block_rows, last), 1)
    return jnp.where(query_pos >= key_pos, scores, MASKED)


def attend_sequence(operands):
    queries, key_rows, value_rows = operands
    block_rows = min(512, LEN)
    outputs = []
    totals = []
    for block_idx in range(LEN // block_rows):
        first = block_idx * block_rows
        last = first + block_rows
        scores = causal_scores(queries, key_rows, first, last)
        highest = jnp.max(scores, -1, keepdims=True)
        expo = jnp.exp(scores - highest)
        summed = jnp.sum(expo, -1, keepdims=True)
        weights = (expo / summed).astype(jnp.bfloat16)
        mixed = jnp.einsum(
            "hqk,khd->qhd", weights, value_rows[:last], preferred_element_type=jnp.float32
        )
        outputs.append(mixed.astype(jnp.bfloat16))
        totals.append((highest + jnp.log(summed))[..., 0])
    return (jnp.concatenate(outputs, 0), jnp.concatenate(totals, 1))


def attend_back(operands):
    queries, key_rows, value_rows, log_total, grad_mixed = operands
    block_rows = min(512, LEN)
    d_keys = jnp.zeros(key_rows.shape, jnp.float32)
    d_values = jnp.zeros(value_rows.shape, jnp.float32)
    d_queries = []
    for block_idx in range(LEN // block_rows):
        first = block_idx * block_rows
        last = first + block_rows
        scores = causal_scores(queries, key_rows, first, last)
        probs = jnp.exp(scores - log_total[:, first:last, None])
        d_probs = jnp.einsum(
            "qhd,khd->hqk",
            grad_mixed[first:last],
            value_rows[:last],
            preferred_element_type=jnp.float32,
        )
        inner = jnp.sum(probs * d_probs, -1, keepdims=True)
        d_scores = (probs * (d_probs - inner)).astype(jnp.bfloat16)
        d_queries.append(
            jnp.einsum(
                "hqk,khd->qhd", d_scores, key_rows[:last], preferred_element_type=jnp.float32
            )
            * HD ** (-0.5)
        )
        key_part = jnp.einsum(
            "hqk,qhd->khd", d_scores, queries[first:last], preferred_element_type=jnp.float32
        ) * HD ** (-0.5)
        value_part = jnp.einsum(
            "hqk,qhd->khd",
            probs.astype(jnp.bfloat16),
            grad_mixed[first:last],
            preferred_element_type=jnp.float32,
        )
        d_keys = d_keys.at[:last].add(key_part)
        d_values = d_values.at[:last].add(value_part)
    return (jnp.concatenate(d_queries, 0), d_keys, d_values)


def layer_forward(stream, w_in, w_out, bias, vector):
    model_width = w_in.shape[0]
    head_cols = w_in.shape[2]
    heads_here = head_cols // HD
    normed, scaled_one, inverse_one = norm_rows(stream, vector[0], vector[1])
    normed_low = normed.astype(jnp.bfloat16)
    seq_count = normed_low.shape[0] // LEN
    shape4 = (seq_count, LEN, heads_here, HD)
    w_qkv = w_in[:, 0:3].reshape(model_width, 3 * head_cols)
    projected = plain_dot(normed_low, w_qkv)
    queries = (projected[:, :head_cols] + bias[0]).astype(jnp.bfloat16).reshape(shape4)
    key_rows = projected[:, head_cols : 2 * head_cols].astype(jnp.bfloat16).reshape(shape4)
    value_rows = (projected[:, 2 * head_cols :] + bias[1]).astype(jnp.bfloat16).reshape(shape4)
    mixed, log_total = lax.map(attend_sequence, (queries, key_rows, value_rows))
    mixed_low = mixed.reshape(-1, head_cols)
    attended = branch_total(plain_dot(mixed_low, w_out[0])) + vector[4]
    middle = stream + BRANCH_SCALE * attended
    hidden, scaled_two, inverse_two = norm_rows(middle, vector[2], vector[3])
    hidden_low = hidden.astype(jnp.bfloat16)
    w_up = w_in[:, 3:].reshape(model_width, 4 * head_cols)
    pre_act = plain_dot(hidden_low, w_up) + bias[2:].reshape(4 * head_cols)
    act_low = smooth_gate(pre_act).astype(jnp.bfloat16)
    w_down = w_out[1:].reshape(4 * head_cols, model_width)
    mlp_out = branch_total(plain_dot(act_low, w_down)) + vector[5]
    result = middle + BRANCH_SCALE * mlp_out
    kept = (
        scaled_one,
        inverse_one,
        normed_low,
        queries,
        key_rows,
        value_rows,
        log_total,
        mixed_low,
        scaled_two,
        inverse_two,
        hidden_low,
        pre_act,
        act_low,
    )
    return (result, kept)


def layer_backward(gradient, w_in, w_out, vector, kept):
    (
        scaled_one,
        inverse_one,
        normed_low,
        queries,
        key_rows,
        value_rows,
        log_total,
        mixed_low,
        scaled_two,
        inverse_two,
        hidden_low,
        pre_act,
        act_low,
    ) = kept
    model_width = w_in.shape[0]
    head_cols = w_in.shape[2]
    w_qkv = w_in[:, 0:3].reshape(model_width, 3 * head_cols)
    w_up = w_in[:, 3:].reshape(model_width, 4 * head_cols)
    w_down = w_out[1:].reshape(4 * head_cols, model_width)
    d_mlp = (BRANCH_SCALE * gradient).astype(jnp.bfloat16)
    g_bdown = jnp.sum(own_rows(d_mlp).astype(jnp.float32), 0)
    g_down = left_dot(act_low, d_mlp).reshape(4, head_cols, model_width)
    d_act = right_dot(d_mlp, w_down).astype(jnp.bfloat16)
    gate_value, gate_pull = jax.vjp(smooth_gate, pre_act)
    d_pre = gate_pull(d_act.astype(jnp.float32))[0].astype(jnp.bfloat16)
    g_bup = jnp.sum(d_pre.astype(jnp.float32), 0)
    g_up = left_dot(hidden_low, d_pre).reshape(model_width, 4, head_cols)
    d_hidden = grad_total(right_dot(d_pre, w_up))
    g_gain_two = jnp.sum(own_rows(d_hidden * scaled_two), 0)
    g_shift_two = jnp.sum(own_rows(d_hidden), 0)
    d_middle = gradient + norm_back(d_hidden, scaled_two, inverse_two, vector[2])
    d_attn = (BRANCH_SCALE * d_middle).astype(jnp.bfloat16)
    g_bproj = jnp.sum(own_rows(d_attn).astype(jnp.float32), 0)
    g_proj = left_dot(mixed_low, d_attn)
    d_mixed = right_dot(d_attn, w_out[0]).astype(jnp.bfloat16)
    d_queries, d_keys, d_values = lax.map(
        attend_back, (queries, key_rows, value_rows, log_total, d_mixed.reshape(queries.shape))
    )
    d_qkv = jnp.concatenate(
        [
            d_queries.reshape(-1, head_cols),
            d_keys.reshape(-1, head_cols),
            d_values.reshape(-1, head_cols),
        ],
        1,
    ).astype(jnp.bfloat16)
    g_qkv = left_dot(normed_low, d_qkv).reshape(model_width, 3, head_cols)
    g_bq = jnp.sum(d_qkv[:, :head_cols].astype(jnp.float32), 0)
    g_bv = jnp.sum(d_qkv[:, 2 * head_cols :].astype(jnp.float32), 0)
    d_normed = grad_total(right_dot(d_qkv, w_qkv))
    g_gain_one = jnp.sum(own_rows(d_normed * scaled_one), 0)
    g_shift_one = jnp.sum(own_rows(d_normed), 0)
    d_stream = d_middle + norm_back(d_normed, scaled_one, inverse_one, vector[0])
    g_in = jnp.concatenate([g_qkv, g_up], 1)
    g_out = jnp.concatenate([g_proj[None], g_down], 0)
    g_bias = jnp.concatenate([g_bq[None], g_bv[None], g_bup.reshape(4, head_cols)], 0)
    g_vector = jnp.stack([g_gain_one, g_shift_one, g_gain_two, g_shift_two, g_bproj, g_bdown])
    return (d_stream, g_in, g_out, g_bias, g_vector)


def adam_step(master, first, second, gradient, rate, decay):
    first_new = BETA_ONE * first + (1 - BETA_ONE) * gradient
    second_new = BETA_TWO * second + (1 - BETA_TWO) * gradient * gradient
    direction = (
        first_new / (1 - BETA_ONE**STEP) / (jnp.sqrt(second_new / (1 - BETA_TWO**STEP)) + ADAM_EPS)
    )
    return (first_new, second_new, master - rate * (direction + decay * master))


def shards(
    resid,
    cotangent,
    master_in,
    moment1_in,
    moment2_in,
    master_out,
    moment1_out,
    moment2_out,
    master_bias,
    moment1_bias,
    moment2_bias,
    master_vec,
    moment1_vec,
    moment2_vec,
):
    weights_in, weights_out = (
        lax.all_gather(master_in.astype(jnp.bfloat16), "dp", axis=1, tiled=True),
        lax.all_gather(master_out.astype(jnp.bfloat16), "dp", axis=3, tiled=True),
    )
    stream = resid
    gradient = cotangent
    layer_idx = 0
    stream, kept = layer_forward(
        stream,
        weights_in[layer_idx],
        weights_out[layer_idx],
        master_bias[layer_idx],
        master_vec[layer_idx],
    )
    kept_list = [kept]
    list_in = [None] * LAYERS
    list_out = [None] * LAYERS
    list_bias = [None] * LAYERS
    list_vector = [None] * LAYERS
    layer_idx = 0
    gradient, g_in, g_out, g_bias, g_vector = layer_backward(
        gradient,
        weights_in[layer_idx],
        weights_out[layer_idx],
        master_vec[layer_idx],
        kept_list[layer_idx],
    )
    list_in[layer_idx] = g_in
    list_out[layer_idx] = g_out
    list_bias[layer_idx] = g_bias
    list_vector[layer_idx] = g_vector
    summed_in = jnp.stack(list_in)
    summed_out = jnp.stack(list_out)
    summed_in, summed_out = (
        lax.psum_scatter(summed_in, "dp", scatter_dimension=1, tiled=True),
        lax.psum_scatter(summed_out, "dp", scatter_dimension=3, tiled=True),
    )
    summed_bias = lax.psum(jnp.stack(list_bias), "dp")
    summed_vector = lax.psum(jnp.stack(list_vector), ("dp", "tensor"))
    first_in, second_in, new_in = adam_step(
        master_in, moment1_in, moment2_in, summed_in, 0.5 * D ** (-0.5), DECAY
    )
    first_out, second_out, new_out = adam_step(
        master_out, moment1_out, moment2_out, summed_out, 2.0 * D ** (-0.5), DECAY
    )
    first_bias, second_bias, new_bias = adam_step(
        master_bias, moment1_bias, moment2_bias, summed_bias, SMALL_RATE, 0.0
    )
    first_vec, second_vec, new_vec = adam_step(
        master_vec, moment1_vec, moment2_vec, summed_vector, SMALL_RATE, 0.0
    )
    return (
        own_rows(stream),
        own_rows(gradient),
        first_in,
        second_in,
        new_in,
        first_out,
        second_out,
        new_out,
        first_bias,
        second_bias,
        new_bias,
        first_vec,
        second_vec,
        new_vec,
    )


MESH_IDS = pl.DeviceIdType.MESH
F32 = jnp.float32
BF16 = jnp.bfloat16
NN = (((1,), (0,)), ((), ()))
NT = (((1,), (1,)), ((), ()))
TN = (((0,), (0,)), ((), ()))
GELU_A = (2.0 / 3.141592653589793) ** 0.5
GELU_B = 0.044715


def mm(left, right, dims=NN):
    return lax.dot_general(left, right, dims, preferred_element_type=F32)


def rows_at(start, size, align):
    return pl.ds(pl.multiple_of(start, align), size)


def block_kernel(
    sizes,
    resid_h,
    cot_h,
    win_h,
    wout_h,
    bias,
    vec,
    out_o,
    grad_o,
    gsum_o,
    small_o,
    win,
    wout,
    resid,
    cot,
    inv1,
    normed,
    dmlp,
    w,
    q_s,
    k_s,
    v_s,
    e_s,
    linv,
    mixed,
    ps,
    crecv,
    fin,
    ysend,
    yrecv,
    mid,
    xhat2,
    inv2,
    normed_t,
    hidden,
    act_s,
    dpre,
    dattn,
    dmix,
    dk_s,
    dv_s,
    dqkv,
    gproj,
    gmat,
    xr,
    zs,
    zr,
    gsum,
    sm,
    smx,
    smz,
    smy,
    smc,
    lsem,
    ssem,
    rsem,
):
    tokens, width, quarter, heads, shard = sizes
    dp = lax.axis_index("dp")
    ten = lax.axis_index("tensor")
    z = lax.div(dp, 2)
    x = lax.rem(dp, 2)
    y = lax.div(ten, 2)
    c = lax.rem(ten, 2)
    x_dev = (dp + 1 - 2 * x, ten)
    c_dev = (dp, ten + 1 - 2 * c)
    y_dev = (dp, ten + 2 - 4 * y)

    def z_other(j):
        if j == 1:
            return z + 1 - 2 * lax.rem(z, 2)
        if j == 2:
            return lax.rem(z + 2, 4)
        return 3 - z

    def z_dev(j):
        return (2 * z_other(j) + x, ten)

    def rcopy(src, dst, send_idx, recv_idx, dev):
        return pltpu.make_async_remote_copy(
            src_ref=src,
            dst_ref=dst,
            send_sem=ssem.at[send_idx],
            recv_sem=rsem.at[recv_idx],
            device_id=dev,
            device_id_type=MESH_IDS,
        )

    barrier = pltpu.get_barrier_semaphore()
    peers = [x_dev, c_dev, y_dev, z_dev(1), z_dev(2), z_dev(3)]
    for dev in peers:
        pl.semaphore_signal(barrier, inc=1, device_id=dev, device_id_type=MESH_IDS)
    load_win = pltpu.make_async_copy(win_h, win, lsem.at[2])
    load_wout = pltpu.make_async_copy(wout_h, wout, lsem.at[3])
    load_win.start()
    load_wout.start()
    load_resid = pltpu.make_async_copy(resid_h, resid, lsem.at[0])
    load_cot = pltpu.make_async_copy(cot_h, cot, lsem.at[1])
    load_resid.start()
    load_cot.start()

    mine = rows_at(dp * shard, shard, shard)
    load_win.wait()
    load_wout.wait()
    out_t = [jnp.transpose(wout[i]) for i in range(5)]
    pairs, last = slice(0, 2 * HD), slice(2 * HD, 3 * HD)
    tiles = [win[0, :, pairs], win[1, :, pairs], win[2, :, pairs], win[0, :, last], win[2, :, last]]
    tiles += [out_t[0][:, pairs], win[1, :, last], out_t[0][:, last]]
    w[0, mine, :] = jnp.concatenate(tiles, 1).astype(BF16)

    w[1, mine, :] = jnp.concatenate([win[3 + i] for i in range(4)], 1).astype(BF16)
    w[2, mine, :] = jnp.concatenate(out_t[1:], 1).astype(BF16)
    pl.semaphore_wait(barrier, len(peers))

    half_cols = width // 2
    units = (
        (0, slice(0, half_cols)),
        (0, slice(half_cols, width)),
        (1, slice(0, width)),
        (2, slice(0, width)),
    )

    is_end = 1 - lax.rem(lax.div(z + 1, 2), 2)
    is_mid = 1 - is_end
    upper = lax.div(z, 2)
    owner_z = (z_other(1), 2 - upper, 3 - 3 * upper)
    pair_dev, mid_dev = (2 * owner_z[0] + x, ten), (2 * owner_z[1] + x, ten)

    def ag_copy(u, zi, send, recv, dev):
        b, cols = units[u]
        src = w.at[b, rows_at((2 * zi + x) * shard, shard, shard), cols]
        return rcopy(src, src, send + u, recv, dev)

    def ag_pair(u):
        return ag_copy(u, z, 4, 3 * u, pair_dev)

    def ag_mid(u):
        return ag_copy(u, z, 4, 3 * u + 1, mid_dev)

    def ag_onward(u, i):
        if i == 0:
            return ag_copy(u, owner_z[0], 4, 3 * u + 2, mid_dev)
        return ag_copy(u, owner_z[i], 4, 3 * u + i, pair_dev)

    def ag_x(u, i):
        return ag_copy(u, z if i == 0 else owner_z[i - 1], 0, 12 + u, x_dev)

    def ag_bytes(u, pieces, send, recv):
        b, cols = units[u]
        ref = w.at[b, 0 : pieces * shard, cols]
        return rcopy(ref, ref, send, recv, x_dev)

    def mid_start(u):
        @pl.when(is_mid == 1)
        def _():
            ag_pair(u).start()
            ag_mid(u).start()

    def ag_arrive(u, i):
        ag_copy(u, owner_z[i], 0, 3 * u + i, x_dev).wait_recv()

    def pump_end(u, i):
        @pl.when(is_end == 1)
        def _():
            ag_arrive(u, i)
            ag_x(u, 1 + i).start()

    def pump_mid(u, i):
        @pl.when(is_mid == 1)
        def _():
            ag_arrive(u, i)
            ag_onward(u, i).start()
            ag_x(u, 1 + i).start()

    def mid_onward(u, i):
        @pl.when(is_mid == 1)
        def _():
            ag_arrive(u, i)
            ag_onward(u, i).start()

    def mid_x(u, i):
        @pl.when(is_mid == 1)
        def _():
            ag_x(u, i).start()

    def ag_finish(u):
        ag_bytes(u, 4, u, 12 + u).wait_recv()

    def ag_drain(u):
        ag_bytes(u, 4, u, 12 + u).wait_send()

        @pl.when(is_end == 1)
        def _():
            ag_bytes(u, 1, 4 + u, 12 + u).wait_send()

        @pl.when(is_mid == 1)
        def _():
            ag_bytes(u, 5, 4 + u, 12 + u).wait_send()

    ag_x(0, 0).start()
    ag_x(1, 0).start()
    mid_start(0)
    mid_start(1)

    @pl.when(is_end == 1)
    def _():
        for u in range(4):
            ag_pair(u).start()

    load_resid.wait()
    load_cot.wait()
    gain_one, shift_one = vec[0], vec[1]

    own = rows_at(ten * quarter, quarter, quarter)
    mid[...] = resid[own, :]
    xhat = resid

    def first_norm(r, carry):
        rows = rows_at(r * 128, 128, 128)
        part = resid[rows, :]
        center = part - jnp.mean(part, -1, keepdims=True)
        inverse = lax.rsqrt(jnp.mean(center * center, -1, keepdims=True) + EPS)
        scaled = center * inverse
        xhat[rows, :] = scaled
        inv1[rows, :] = inverse
        normed[rows, :] = (scaled * gain_one + shift_one).astype(BF16)
        dmlp[rows, :] = (cot[rows, :] * BRANCH_SCALE).astype(BF16)
        return carry

    lax.fori_loop(0, tokens // 128, first_norm, 0)
    for u, i in ((0, 0), (0, 1), (1, 0), (1, 1), (0, 2), (1, 2)):
        pump_mid(u, i)
    for u, i in ((0, 0), (1, 0), (0, 1), (1, 1), (0, 2), (1, 2)):
        pump_end(u, i)
    ag_x(2, 0).start()
    mid_start(2)
    pump_mid(2, 0)
    ag_x(3, 0).start()
    mid_start(3)
    mid_onward(3, 0)

    sm[...] = jnp.zeros_like(sm)
    sm[5:6, :] = jnp.sum(dmlp[own, :].astype(F32), 0, keepdims=True)
    mixed[...] = jnp.zeros_like(mixed)
    dqkv[...] = jnp.zeros_like(dqkv)
    dk_s[...] = jnp.zeros_like(dk_s)
    dv_s[...] = jnp.zeros_like(dv_s)

    hc = heads * HD
    low_half = lax.broadcasted_iota(jnp.int32, (1, 2 * HD), 1) < HD
    bias_v01, bias_q01 = bias[1, :, pairs], bias[0, :, pairs]
    bias_q2v2 = jnp.concatenate([bias[0, :, last], bias[1, :, last]], 1)
    eighth = HD**-0.5

    def project_pair(r):
        rows = slice(r * 256, (r + 1) * 256)
        got = mm(normed[rows, :], w[0, :, 0:384])
        queries = (got[:, 0:128] + bias_q01).astype(BF16).astype(F32) * eighth
        q_s[0, rows, :] = jnp.where(low_half, queries, 0.0).astype(BF16)
        q_s[1, rows, :] = jnp.where(low_half, 0.0, queries).astype(BF16)
        k_s[0, rows, :] = got[:, 128:256].astype(BF16)
        v_s[0, rows, :] = (got[:, 256:384] + bias_v01).astype(BF16)

    def project_last(r):
        rows = slice(r * 256, (r + 1) * 256)
        got = mm(normed[rows, :], w[0, :, 384:768])
        both = (got[:, 0:128] + bias_q2v2).astype(BF16)
        q_s[2, rows, :] = jnp.where(low_half, both.astype(F32) * eighth, 0.0).astype(BF16)
        v_s[1, rows, :] = both
        k_s[1, rows, :] = got[:, 256:384].astype(BF16)

    ag_finish(0)
    for r in range(tokens // 256):
        project_pair(r)
    pump_end(2, 0)
    pump_mid(2, 1)

    def attend(i, which_heads):
        first, last_row = i * quarter, (i + 1) * quarter
        rows = slice(first, last_row)
        causal = lax.broadcasted_iota(jnp.int32, (quarter, quarter), 0) >= lax.broadcasted_iota(
            jnp.int32, (quarter, quarter), 1
        )
        got = {}
        for h in which_heads:
            at = h // 2
            queries = q_s[h, rows, :]
            diag = jnp.where(causal, mm(queries, k_s[at, rows, :], NT), MASKED)
            highest = jnp.max(diag, -1, keepdims=True)
            if i > 0:
                wide = mm(queries, k_s[at, 0:first, :], NT)
                highest = jnp.maximum(highest, jnp.max(wide, -1, keepdims=True))
            e_diag = jnp.exp(diag - highest)
            summed = jnp.sum(e_diag, -1, keepdims=True)
            e_diag = e_diag.astype(BF16)
            e_s[h, rows, first:last_row] = e_diag
            total = mm(e_diag, v_s[at, rows, :])
            if i > 0:
                e_wide = jnp.exp(wide - highest)
                summed = summed + jnp.sum(e_wide, -1, keepdims=True)
                e_wide = e_wide.astype(BF16)
                e_s[h, rows, 0:first] = e_wide
                total = total + mm(e_wide, v_s[at, 0:first, :])
            inverse = 1.0 / summed
            linv[h, rows, :] = inverse
            got[h] = total * inverse
        if 0 in got:
            mixed[rows, 0:128] = jnp.where(low_half, got[0], got[1]).astype(BF16)
        if 2 in got:
            mixed[rows, 128:256] = jnp.where(low_half, 0.0, got[2]).astype(BF16)

    def rs_core(k, half):
        return rcopy(ps.at[k % 2, half], crecv.at[k, half], 16 + 2 * (k % 2) + half, 16 + 2 * k + half, c_dev)

    halves = [slice(0, quarter // 2), slice(quarter // 2, quarter)]

    def rs_y(k, hh):
        src, dst = ysend.at[k, halves[hh], :], yrecv.at[k, halves[hh], :]
        return rcopy(src, dst, 20, 24 + 2 * k + hh, y_dev)

    def rs_y_start(k):
        for hh in range(2):
            rs_y(k, hh).start()

    def rs_pair(k, near, compute, prepare=None, filler=None):
        half = 1 if near else 0
        def step(s, carry):
            yq = y if near else 1 - y
            if prepare is not None:
                prepare(s)
            part = compute(2 * yq + lax.rem(1 - s + c, 2))

            @pl.when(s == 0)
            def _():
                ps[k % 2, half] = part.astype(BF16)
                rs_core(k, half).start()

            @pl.when(s == 1)
            def _():
                if filler is not None:
                    fin[(k + 1) % 3] = part
                    filler()
                    kept = fin[(k + 1) % 3]
                else:
                    kept = part
                rs_core(k, half).wait_recv()
                total = kept + crecv[k, half].astype(F32)
                if near:
                    fin[k % 3] = total
                else:
                    ysend[k] = total.astype(BF16)
                    rs_y_start(k)

            return carry

        lax.fori_loop(0, 2, step, 0)

    def rs_quad(k, compute, held):
        for half in range(2):
            rs_core(k - 2, half).wait_send()

        def step(s, carry):
            half, odd = lax.div(s, 2), lax.rem(s, 2)
            yq = half * y + (1 - half) * (1 - y)
            part = compute(2 * yq + lax.rem(1 - odd + c, 2))

            @pl.when(odd == 0)
            def _():
                ps[k % 2, half] = part.astype(BF16)
                rs_core(k, half).start()

            @pl.when(s == 1)
            def _():
                held[...] = part

            @pl.when(s == 3)
            def _():
                fin[k % 3] = part

            return carry

        lax.fori_loop(0, 4, step, 0)

    def quad_far(k, held):
        rs_core(k, 0).wait_recv()
        ysend[k] = (held[...] + crecv[k, 0].astype(F32)).astype(BF16)

    def quad_near(k):
        rs_core(k, 1).wait_recv()
        fin[k % 3] = fin[k % 3] + crecv[k, 1].astype(F32)

    def rs_result(k, hh):
        rs_y(k, hh).wait_recv()
        return fin[k % 3, halves[hh], :] + yrecv[k, halves[hh], :].astype(F32)

    def attend_quarter(which, which_heads):
        for i in range(tokens // quarter):

            @pl.when(which == i)
            def _():
                attend(i, which_heads)

    def proj(which):
        return mm(mixed[rows_at(which * quarter, quarter, quarter), :], w[0, :, 512:768], NT)

    def far_early(s, carry):
        attend_quarter(2 * (1 - y) + lax.rem(s + c, 2), (0, 1))
        return carry

    def far_proj(which):
        attend_quarter(which, (2,))
        return proj(which)

    def near_proj(which):
        attend_quarter(which, (0, 1, 2))
        return proj(which)

    def near_pumps(s):
        @pl.when(s == 1)
        def _():
            pump_end(2, 2)
            pump_end(3, 0)
            pump_mid(3, 2)

    lax.fori_loop(0, 2, far_early, 0)
    pump_mid(2, 2)
    mid_x(3, 1)
    ag_finish(1)
    for r in range(tokens // 256):
        project_last(r)
    rs_pair(0, False, far_proj)
    pump_end(2, 1)
    pump_mid(3, 1)
    rs_pair(0, True, near_proj, prepare=near_pumps)

    def q_rows(ref, which, hh):
        return ref.at[rows_at(which * quarter + hh * (quarter // 2), quarter // 2, quarter // 2), :]

    def qg_y(g, ref, hh):
        src = q_rows(ref, ten, hh)
        return rcopy(src, src, 21, 32 + 2 * g + hh, y_dev)

    def qg_c(g, ref, hh):
        src = q_rows(ref, ten, hh)
        return rcopy(src, src, 22, 36 + g, c_dev)

    def qg_f(g, ref, hh):
        src = q_rows(ref, ten + 2 - 4 * y, hh)
        return rcopy(src, src, 23, 38 + g, c_dev)

    def qg_start(g, ref, hh):
        qg_y(g, ref, hh).start()
        qg_c(g, ref, hh).start()

    def qg_rows(ref, count, send, recv):
        rows = ref.at[0:count, :]
        return rcopy(rows, rows, send, recv, c_dev)

    def qg_near(g, ref):
        qg_rows(ref, quarter, 22, 36 + g).wait_recv()

    def qg_far(g, ref):
        for hh in range(2):
            qg_y(g, ref, hh).wait_recv()
            qg_f(g, ref, hh).start()

    def qg_last(g, ref):
        qg_rows(ref, quarter, 23, 38 + g).wait_recv()

    pump_end(3, 1)

    for hh in range(2):
        half = halves[hh]
        middle = mid[half, :] + BRANCH_SCALE * (rs_result(0, hh) + vec[4])
        mid[half, :] = middle
        center = middle - jnp.mean(middle, -1, keepdims=True)
        inverse = lax.rsqrt(jnp.mean(center * center, -1, keepdims=True) + EPS)
        scaled = center * inverse
        xhat2[half, :] = scaled
        inv2[half, :] = inverse
        mine_h = rows_at(ten * quarter + hh * (quarter // 2), quarter // 2, quarter // 2)
        hidden[mine_h, :] = (scaled * vec[2] + vec[3]).astype(BF16)
        qg_start(0, hidden, hh)

    pump_end(3, 2)
    ag_finish(2)

    bias_up = jnp.concatenate([bias[2 + i] for i in range(4)], 1)

    def forward_units(which):
        rows = rows_at(which * quarter, quarter, quarter)
        hq = hidden[rows, :]
        for t in range(width // 256):
            cols = slice(t * 256, (t + 1) * 256)
            pre = mm(hq, w[1, :, cols]) + bias_up[:, cols]
            square = pre * pre
            tanh = jnp.tanh(GELU_A * (pre + GELU_B * (square * pre)))
            half_up = 0.5 + 0.5 * tanh
            act_s[rows, cols] = (pre * half_up).astype(BF16)
            slope = half_up + 0.5 * pre * (1.0 - tanh * tanh) * (
                GELU_A + (3.0 * GELU_A * GELU_B) * square
            )
            dpre[rows, cols] = slope.astype(BF16)

    def grad_block(b, left, right, near):
        rows = slice(0, tokens)
        if near is not None:
            rows = rows_at((y if near else 1 - y) * 2 * quarter, 2 * quarter, 2 * quarter)

        def tile(t, carry):
            cols = rows_at(t * 256, 256, 256)
            part = mm(left[rows, cols], right[rows, :], TN)
            if near is False:
                part = part + gmat[b, cols, :].astype(F32)
            gmat[b, cols, :] = part.astype(BF16)
            return carry

        lax.fori_loop(0, width // 256, tile, 0)


    def gx(u, zi):
        b, cols = units[u]
        src = gmat.at[b, rows_at((2 * zi + 1 - x) * shard, shard, shard), cols]
        return rcopy(src, xr.at[b, zi, :, cols], 8 + u, 40 + 4 * u + zi, x_dev)

    def line_to(i):
        if i == 0:
            return pair_dev, 0
        return (2 * (is_end * owner_z[0] + is_mid * owner_z[i]) + x, ten), is_end * i + is_mid * 3

    def gz(u, i):
        b, cols = units[u]
        if u < 2:
            src, dst = zs.at[b, i - 1, :, cols], zr.at[b, i - 1, :, cols]
            return rcopy(src, dst, 12 + u, 56 + u, z_dev(i))
        dev, slot = line_to(i)
        return rcopy(
            zs.at[b, i, :, cols], zr.at[b, slot, :, cols], 12 + u, 58 + 4 * (u - 2) + slot, dev
        )

    def gz_arrive(u, slot):
        b, cols = units[u]
        ref = zr.at[b, slot, :, cols]
        rcopy(ref, ref, 12 + u, 58 + 4 * (u - 2) + slot, x_dev).wait_recv()

    def g_start(u):
        @pl.when(is_end == 1)
        def _():
            for i in (2, 1, 0):
                gx(u, owner_z[i]).start()

        @pl.when(is_mid == 1)
        def _():
            for i in (0, 2, 1):
                gx(u, owner_z[i]).start()

        gx(u, z).start()

    def x_sum(u, zo):
        b, cols = units[u]
        gx(u, zo).wait_recv()
        mine_x = gmat[b, rows_at((2 * zo + x) * shard, shard, shard), cols].astype(F32)
        return mine_x + xr[b, zo, :, cols].astype(F32)

    def g_pump(u, j):
        b, cols = units[u]
        zs[b, j - 1, :, cols] = x_sum(u, z_other(j)).astype(BF16)
        gz(u, j).start()

    def end_pump(u, i):
        b, cols = units[u]

        @pl.when(is_end == 1)
        def _():
            zs[b, i, :, cols] = x_sum(u, owner_z[i]).astype(BF16)
            gz(u, i).start()

    def mid_pump(u, i):
        b, cols = units[u]

        @pl.when(is_mid == 1)
        def _():
            total = x_sum(u, owner_z[i])
            if i > 0:
                gz_arrive(u, i)
                total = total + zr[b, i, :, cols].astype(F32)
            zs[b, i, :, cols] = total.astype(BF16)
            gz(u, i).start()

    def g_finish(u):
        b, cols = units[u]
        total = x_sum(u, z)
        if u < 2:
            three = zr.at[b, 0:3, :, cols]
            rcopy(three, three, 12 + u, 56 + u, x_dev).wait_recv()
            for j in range(3):
                total = total + zr[b, j, :, cols].astype(F32)
        else:
            for slot in (0, 3):
                gz_arrive(u, slot)
                total = total + zr[b, slot, :, cols].astype(F32)
        gsum[b, :, cols] = total
        g_out(u).start()

    def g_out(u):
        b, cols = units[u]
        return pltpu.make_async_copy(gsum.at[b, :, cols], gsum_o.at[b, :, cols], lsem.at[4 + u])

    def g_drain(u):
        b, cols = units[u]
        rcopy(xr.at[b, :, :, cols], xr.at[b, :, :, cols], 8 + u, 56, x_dev).wait_send()
        rcopy(zs.at[b, :, :, cols], zs.at[b, :, :, cols], 12 + u, 56, x_dev).wait_send()
        g_out(u).wait()

    def backward_units(which):
        rows = rows_at(which * quarter, quarter, quarter)
        gq = dmlp[rows, :]
        for t in range(width // 256):
            cols = slice(t * 256, (t + 1) * 256)
            d_act = mm(gq, w[2, :, cols]).astype(BF16).astype(F32)
            d_low = (dpre[rows, cols].astype(F32) * d_act).astype(BF16)
            dpre[rows, cols] = d_low
            sm[6:7, cols] = sm[6:7, cols] + jnp.sum(d_low.astype(F32), 0, keepdims=True)
        return mm(dpre[rows, :], w[1], NT)

    def branch(which):
        rows = rows_at(which * quarter, quarter, quarter)
        return mm(act_s[rows, :], w[2], NT)

    def near_units(s, carry):
        @pl.when(s == 1)
        def _():
            qg_near(0, hidden)

        forward_units(2 * y + lax.rem(s + c, 2))
        return carry

    lax.fori_loop(0, 2, near_units, 0)
    grad_block(2, dmlp, act_s, True)
    for t in range(width // 256):
        cols = slice(t * 256, (t + 1) * 256)
        normed_t[cols, :] = jnp.transpose(normed[:, cols])
    qg_far(0, hidden)

    def far_units(s, carry):
        @pl.when(s == 1)
        def _():
            qg_last(0, hidden)

        forward_units(2 * (1 - y) + lax.rem(s + c, 2))
        return carry

    def down_gradient():
        grad_block(2, dmlp, act_s, False)
        g_start(3)

    lax.fori_loop(0, 2, far_units, 0)
    ag_finish(3)
    rs_pair(1, False, backward_units, filler=down_gradient)
    rs_pair(1, True, backward_units)
    grad_block(1, hidden, dpre, None)
    g_start(2)
    end_pump(3, 2)
    mid_pump(3, 0)
    rs_quad(2, branch, fin.at[0])
    end_pump(3, 1)
    quad_far(2, fin.at[0])
    quad_near(2)

    for hh in range(2):
        half = halves[hh]
        mine_h = rows_at(ten * quarter + hh * (quarter // 2), quarter // 2, quarter // 2)
        d_hidden = rs_result(1, hh)
        scaled = xhat2[half, :]
        sm[2:3, :] = sm[2:3, :] + jnp.sum(d_hidden * scaled, 0, keepdims=True)
        sm[3:4, :] = sm[3:4, :] + jnp.sum(d_hidden, 0, keepdims=True)
        weighted = d_hidden * vec[2]
        d_mid = cot[mine_h, :] + inv2[half, :] * (
            weighted
            - jnp.mean(weighted, -1, keepdims=True)
            - scaled * jnp.mean(weighted * scaled, -1, keepdims=True)
        )
        fin[1, half, :] = d_mid
        d_attn = (BRANCH_SCALE * d_mid).astype(BF16)
        dattn[mine_h, :] = d_attn
        sm[4:5, :] = sm[4:5, :] + jnp.sum(d_attn.astype(F32), 0, keepdims=True)
        qg_start(1, dattn, hh)

    def attend_back(i, which_heads):
        first, last_row = i * quarter, (i + 1) * quarter
        rows = slice(first, last_row)
        got = {}
        for h in which_heads:
            at = h // 2
            tile = slice(at * 128, (at + 1) * 128)
            d_out = dmix[rows, tile].astype(F32) * linv[h, rows, :]
            d_out = jnp.where(low_half, d_out, 0.0) if h == 0 else jnp.where(low_half, 0.0, d_out)
            inner = jnp.sum(d_out * mixed[rows, tile].astype(F32), -1, keepdims=True)
            d_scaled = d_out.astype(BF16)
            expo = e_s[h, rows, 0:last_row]
            d_probs = mm(d_scaled, v_s[at, 0:last_row, :], NT)
            d_scores = (expo.astype(F32) * (d_probs - inner)).astype(BF16)
            got[h] = mm(d_scores, k_s[at, 0:last_row, :]) * eighth
            dk_s[at, :, 0:last_row] = dk_s[at, :, 0:last_row] + mm(q_s[h, rows, :], d_scores, TN)
            dv_s[at, :, 0:last_row] = dv_s[at, :, 0:last_row] + mm(d_scaled, expo, TN)
        if 0 in got:
            dqkv[rows, 0:128] = jnp.where(low_half, got[0], got[1]).astype(BF16)
        if 2 in got:
            dqkv[rows, 384:512] = jnp.where(low_half, got[2], 0.0).astype(BF16)

    def back_quarters(near, which_heads, fresh, prepare=None):
        def step(s, carry):
            if prepare is not None:
                prepare(s)
            yq = y if near else 1 - y
            which = 2 * yq + lax.rem(s + c, 2)
            if fresh:
                rows = rows_at(which * quarter, quarter, quarter)
                dmix[rows, :] = mm(dattn[rows, :], w[0, :, 512:768]).astype(BF16)
            for i in range(tokens // quarter):

                @pl.when(which == i)
                def _():
                    attend_back(i, which_heads)

            return carry

        lax.fori_loop(0, 2, step, 0)

    def near_ready(s):
        @pl.when(s == 1)
        def _():
            qg_near(1, dattn)

    def far_ready(s):
        @pl.when(s == 1)
        def _():
            qg_last(1, dattn)
            end_pump(2, 1)

    def keys_values(at):
        if at == 0:
            dqkv[:, 128:256] = jnp.transpose(dk_s[0]).astype(BF16)
            dqkv[:, 256:384] = jnp.transpose(dv_s[0]).astype(BF16)
        else:
            d_v = jnp.transpose(dv_s[1]).astype(BF16)
            dqkv[:, 384:512] = jnp.where(low_half, dqkv[:, 384:512], d_v)
            dqkv[:, 640:768] = jnp.transpose(dk_s[1]).astype(BF16)

    def zero_rows(u, zo):
        cols = rows_at(zo * 2 * shard, 2 * shard, 2 * shard)
        left = normed_t[cols, :]
        if u == 0:
            gmat[0, cols, 0:384] = mm(left, dqkv[:, 0:384]).astype(BF16)
        else:
            g_qkv = mm(left, dqkv[:, 384:768])
            gmat[0, cols, 384:512] = g_qkv[:, 0:128].astype(BF16)
            gmat[0, cols, 512:768] = (g_qkv[:, 128:384] + gproj[cols, :]).astype(BF16)
        gx(u, zo).start()

    def zero_unit(u):
        def step(s, carry):
            odd, half = lax.rem(s, 2), lax.div(s, 2)
            early = (1 - odd) * z_other(3) + odd * z_other(2)
            late = (1 - odd) * z_other(1) + odd * z
            zero_rows(u, (1 - half) * early + half * late)
            return carry

        lax.fori_loop(0, 4, step, 0)

    end_pump(3, 0)
    mid_pump(3, 2)
    back_quarters(True, (0, 1, 2), True, near_ready)
    mid_pump(3, 1)
    end_pump(2, 2)
    mid_pump(2, 0)
    qg_far(1, dattn)
    rs_y_start(2)
    back_quarters(False, (0, 1), True, far_ready)
    keys_values(0)
    zero_unit(0)
    gproj[...] = jnp.transpose(mm(mixed[...], dattn[...], TN))
    end_pump(2, 0)
    mid_pump(2, 2)
    back_quarters(False, (2,), False)
    keys_values(1)
    mid_pump(2, 1)

    def first_back(which):
        rows = rows_at(which * quarter, quarter, quarter)
        d_low = dqkv[rows, :]
        part = mm(d_low, w[0], NT)
        rounded = part.astype(BF16).astype(F32)
        sm[0:1, :] = sm[0:1, :] + jnp.sum(rounded * xhat[rows, :], 0, keepdims=True)
        sm[1:2, :] = sm[1:2, :] + jnp.sum(rounded, 0, keepdims=True)
        sm[7:8, :] = sm[7:8, :] + jnp.sum(d_low.astype(F32), 0, keepdims=True)
        return part

    rs_quad(3, first_back, xhat2)

    small_x = rcopy(sm, smx, 24, 66, x_dev)
    small_x.start()
    quad_far(3, xhat2)
    rs_y_start(3)
    g_pump(0, 3)
    zero_unit(1)
    quad_near(3)
    g_pump(0, 2)
    small_x.wait_recv()
    smz[z] = sm[...] + smx[...]

    def small_z(j):
        return rcopy(smz.at[z], smz.at[z], 25, 67, z_dev(j))

    for j in (3, 2, 1):
        small_z(j).start()
    g_pump(0, 1)
    g_finish(3)
    g_finish(2)
    for hh in range(2):
        half = halves[hh]
        mid[half, :] = mid[half, :] + BRANCH_SCALE * (rs_result(2, hh) + vec[5])
    put_out = pltpu.make_async_copy(mid, out_o, lsem.at[8])
    put_out.start()
    g_pump(1, 3)
    g_pump(1, 2)

    def first_norm_back(hh):
        half = halves[hh]
        mine_h = rows_at(ten * quarter + hh * (quarter // 2), quarter // 2, quarter // 2)
        d_normed = rs_result(3, hh)
        scaled = xhat[mine_h, :]
        weighted = d_normed * gain_one
        xhat2[half, :] = fin[1, half, :] + inv1[mine_h, :] * (
            weighted
            - jnp.mean(weighted, -1, keepdims=True)
            - scaled * jnp.mean(weighted * scaled, -1, keepdims=True)
        )

    first_norm_back(0)
    g_pump(1, 1)
    first_norm_back(1)
    put_grad = pltpu.make_async_copy(xhat2, grad_o, lsem.at[9])
    put_grad.start()
    three = rcopy(smz.at[0:3], smz.at[0:3], 25, 67, x_dev)
    three.wait_recv()
    smy[0] = (smz[0] + smz[1]) + (smz[2] + smz[3])
    small_y = rcopy(smy.at[0], smy.at[1], 26, 68, y_dev)
    small_y.start()
    g_finish(0)
    small_y.wait_recv()
    smc[0] = smy[0] + smy[1]
    small_c = rcopy(smc.at[0], smc.at[1], 27, 69, c_dev)
    small_c.start()
    g_finish(1)
    small_c.wait_recv()
    small_o[0:6, :] = smc[0, 0:6, :] + smc[1, 0:6, :]
    small_o[6:8, :] = smy[0, 6:8, :]

    for u in range(4):
        ag_drain(u)
        g_drain(u)
    rcopy(ysend, yrecv, 20, 24, y_dev).wait_send()
    for k in (2, 3):
        for half in range(2):
            rs_core(k, half).wait_send()
    for send in (21, 22, 23):
        qg_rows(hidden, 2 * quarter, send, 36).wait_send()
    small_x.wait_send()
    three.wait_send()
    small_y.wait_send()
    small_c.wait_send()
    put_out.wait()
    put_grad.wait()


def run_block(resid, cotangent, win, wout, bias, vec, rows, n_dp):
    tokens, width = resid.shape
    quarter = tokens // 4
    head_cols = win.shape[2]
    heads = head_cols // HD
    sizes = (tokens, width, quarter, heads, rows)
    vm = pltpu.VMEM
    scratch = [
        vm(win.shape, F32),
        vm(wout.shape, F32),
        vm((tokens, width), F32),
        vm((tokens, width), F32),
        vm((tokens, 1), F32),
        vm((tokens, width), BF16),
        vm((tokens, width), BF16),
        vm((3, width, width), BF16),
        vm((heads, tokens, 2 * HD), BF16),
        vm((2, tokens, 2 * HD), BF16),
        vm((2, tokens, 2 * HD), BF16),
        vm((heads, tokens, tokens), BF16),
        vm((heads, tokens, 1), F32),
        vm((tokens, 256), BF16),
        vm((2, 2, quarter, width), BF16),
        vm((4, 2, quarter, width), BF16),
        vm((3, quarter, width), F32),
        vm((4, quarter, width), BF16),
        vm((4, quarter, width), BF16),
        vm((quarter, width), F32),
        vm((quarter, width), F32),
        vm((quarter, 1), F32),
        vm((width, tokens), BF16),
        vm((tokens, width), BF16),
        vm((tokens, width), BF16),
        vm((tokens, width), BF16),
        vm((tokens, width), BF16),
        vm((tokens, 256), BF16),
        vm((2, 2 * HD, tokens), F32),
        vm((2, 2 * HD, tokens), F32),
        vm((tokens, width), BF16),
        vm((width, 256), F32),
        vm((3, width, width), BF16),
        vm((3, 4, rows, width), BF16),
        vm((3, 3, rows, width), BF16),
        vm((3, 4, rows, width), BF16),
        vm((3, rows, width), F32),
        vm((8, width), F32),
        vm((8, width), F32),
        vm((4, 8, width), F32),
        vm((2, 8, width), F32),
        vm((2, 8, width), F32),
        pltpu.SemaphoreType.DMA((10,)),
        pltpu.SemaphoreType.DMA((28,)),
        pltpu.SemaphoreType.DMA((70,)),
    ]
    whole = pl.BlockSpec(memory_space=pltpu.VMEM)
    return pl.pallas_call(
        functools.partial(block_kernel, sizes),
        out_shape=(
            jax.ShapeDtypeStruct((quarter, width), F32),
            jax.ShapeDtypeStruct((quarter, width), F32),
            jax.ShapeDtypeStruct((3, rows, width), F32),
            jax.ShapeDtypeStruct((8, width), F32),
        ),
        in_specs=[pl.BlockSpec(memory_space=pl.ANY)] * 4 + [whole] * 2,
        out_specs=[pl.BlockSpec(memory_space=pl.ANY)] * 3 + [whole],
        scratch_shapes=scratch,
        compiler_params=pltpu.CompilerParams(
            collective_id=1, has_side_effects=True, vmem_limit_bytes=62 << 20
        ),
        name="block",
    )(resid, cotangent, win, wout, bias, vec)


BLOCK_ZERO = (((0, 128), (384, 448)), ((128, 256), (640, 704)), ((256, 384), (448, 512)), ((512, 640), (704, 768)))


def adam_kernel(hc, *refs):
    passed_h, gsum_h, small_h = refs[0:2], refs[2], refs[3]
    in_h, out_h, bias_h, vec_h = refs[4:7], refs[7:10], refs[10:13], refs[13:16]
    passed_o, in_o, out_o, bias_o, vec_o = refs[16:18], refs[18:21], refs[21:24], refs[24:27], refs[27:30]
    vin, vout, vbias, vvec, rin, rout, rbias, rvec, gsum, small, passed, sems = refs[30:42]

    def copy(src, dst, sem):
        pltpu.make_async_copy(src, dst, sems.at[sem]).start()

    def wait(ref, sem):
        pltpu.make_async_copy(ref, ref, sems.at[sem]).wait()

    def columns(ref, rows, kind):
        return jnp.concatenate([ref[rows + (slice(a, b),)] for a, b in BLOCK_ZERO[kind]], 1)

    every = slice(None)
    kinds_in = (3, 4, 5, 6, 0, 1, 2)
    copy(gsum_h.at[1], gsum.at[1], 0)
    for i in kinds_in:
        for a in range(3):
            copy(in_h[a].at[i], vin.at[i, a], 3 + i)
        if i == 6:
            copy(gsum_h.at[0], gsum.at[0], 1)
    copy(small_h, small, 15)
    for a in range(3):
        copy(bias_h[a], vbias.at[a], 16)
        copy(vec_h[a], vvec.at[a], 17)
    copy(gsum_h.at[2], gsum.at[2], 2)
    for i in range(5):
        for a in range(3):
            copy(out_h[a].at[i], vout.at[i, a], 10 + i)
    for a in range(2):
        copy(passed_h[a], passed.at[a], 18)

    wait(gsum.at[1], 0)
    for i in kinds_in:
        wait(vin.at[i], 3 + i)
        if i == 0:
            wait(gsum.at[0], 1)
        part = columns(gsum, (0, every), i) if i < 3 else gsum[1, :, (i - 3) * hc : (i - 2) * hc]
        new = adam_step(vin[i, 0], vin[i, 1], vin[i, 2], part, 0.5 * D ** (-0.5), DECAY)
        for a in range(3):
            rin[i, a] = new[a]
            copy(rin.at[i, a], in_o[a].at[i], 19)
    wait(small, 15)
    wait(vbias, 16)
    wait(vvec, 17)
    for i in range(6):
        new = adam_step(vvec[0, i], vvec[1, i], vvec[2, i], small[i : i + 1, :], SMALL_RATE, 0.0)
        for a in range(3):
            rvec[a, i] = new[a]
        if i < 2:
            part = columns(small, (slice(7, 8),), 2 * i)
        else:
            part = small[6:7, (i - 2) * hc : (i - 1) * hc]
        new = adam_step(vbias[0, i], vbias[1, i], vbias[2, i], part, SMALL_RATE, 0.0)
        for a in range(3):
            rbias[a, i] = new[a]
    for a in range(3):
        copy(rbias.at[a], bias_o[a], 20)
        copy(rvec.at[a], vec_o[a], 21)
    wait(gsum.at[2], 2)
    for i in range(5):
        wait(vout.at[i], 10 + i)
        part = columns(gsum, (0, every), 3) if i == 0 else gsum[2, :, (i - 1) * hc : i * hc]
        part = jnp.transpose(part)
        new = adam_step(vout[i, 0], vout[i, 1], vout[i, 2], part, 2.0 * D ** (-0.5), DECAY)
        for a in range(3):
            rout[i, a] = new[a]
            copy(rout.at[i, a], out_o[a].at[i], 22)
    wait(passed, 18)
    for a in range(2):
        copy(passed.at[a], passed_o[a], 23)
    for ref, sem in ((rin, 19), (rbias, 20), (rvec, 21), (rout, 22), (passed, 23)):
        wait(ref, sem)


def run_adam(*operands):
    hc = operands[4].shape[2]
    out_rows, _, g_sum, small = operands[0:4]
    shapes = [out_rows, out_rows, *operands[4:16]]
    hbm = pl.BlockSpec(memory_space=pl.ANY)
    kinds_in, kinds_out = operands[4].shape, operands[7].shape
    small_bias, small_vec = operands[10].shape, operands[13].shape
    big = [
        pltpu.VMEM((kinds_in[0], 3, *kinds_in[1:]), F32),
        pltpu.VMEM((kinds_out[0], 3, *kinds_out[1:]), F32),
        pltpu.VMEM((3, *small_bias), F32),
        pltpu.VMEM((3, *small_vec), F32),
    ]
    return pl.pallas_call(
        functools.partial(adam_kernel, hc),
        out_shape=[jax.ShapeDtypeStruct(a.shape, F32) for a in shapes],
        in_specs=[hbm] * 16,
        out_specs=[hbm] * 14,
        scratch_shapes=big * 2
        + [pltpu.VMEM(g_sum.shape, F32), pltpu.VMEM(small.shape, F32)]
        + [pltpu.VMEM((2, *out_rows.shape), F32), pltpu.SemaphoreType.DMA((24,))],
        compiler_params=pltpu.CompilerParams(vmem_limit_bytes=62 << 20),
        name="adam",
    )(*operands)


def fused_shards(
    resid,
    cotangent,
    master_in,
    moment1_in,
    moment2_in,
    master_out,
    moment1_out,
    moment2_out,
    master_bias,
    moment1_bias,
    moment2_bias,
    master_vec,
    moment1_vec,
    moment2_vec,
):
    rows = master_in.shape[1]
    hc = master_in.shape[3]
    turned = [jnp.transpose(a[0], (1, 0, 2)) for a in (master_in, moment1_in, moment2_in)]
    plain = [a[0] for a in (master_out, moment1_out, moment2_out)]
    biases = [a.reshape(6, 1, hc) for a in (master_bias, moment1_bias, moment2_bias)]
    vectors = [a.reshape(6, 1, D) for a in (master_vec, moment1_vec, moment2_vec)]
    sums = run_block(
        resid, cotangent, turned[0], plain[0], biases[0], vectors[0], rows, lax.axis_size("dp")
    )
    new = run_adam(*sums, *turned, *plain, *biases, *vectors)
    return (
        new[0],
        new[1],
        *[jnp.transpose(a, (1, 0, 2))[None] for a in new[2:5]],
        *[a[None] for a in new[5:8]],
        *[a.reshape(1, 6, hc) for a in new[8:11]],
        *[a.reshape(1, 6, D) for a in new[11:14]],
    )


def solution(mesh):
    fused = mesh.shape["dp"] == 8 and mesh.shape["tensor"] == 4
    return jax.shard_map(
        fused_shards if fused else shards,
        mesh=mesh,
        in_specs=(
            P("dp", None),
            P("dp", None),
            P(None, "dp", None, "tensor"),
            P(None, "dp", None, "tensor"),
            P(None, "dp", None, "tensor"),
            P(None, None, "tensor", "dp"),
            P(None, None, "tensor", "dp"),
            P(None, None, "tensor", "dp"),
            P(None, None, "tensor"),
            P(None, None, "tensor"),
            P(None, None, "tensor"),
            P(),
            P(),
            P(),
        ),
        out_specs=(
            P(("dp", "tensor"), None),
            P(("dp", "tensor"), None),
            P(None, "dp", None, "tensor"),
            P(None, "dp", None, "tensor"),
            P(None, "dp", None, "tensor"),
            P(None, None, "tensor", "dp"),
            P(None, None, "tensor", "dp"),
            P(None, None, "tensor", "dp"),
            P(None, None, "tensor"),
            P(None, None, "tensor"),
            P(None, None, "tensor"),
            P(),
            P(),
            P(),
        ),
        check_vma=False,
    )
```

```python
import functools

import jax
import jax.numpy as jnp
from jax import lax
from jax.experimental import pallas as pl
from jax.experimental.pallas import tpu as pltpu
from jax.sharding import PartitionSpec as P

D = 768
HD = 64
LEN = 1024
LAYERS = 1
STEP = 10


EPS = 1e-05
BRANCH_SCALE = 48 ** (-0.5)
BETA_ONE = 0.9
BETA_TWO = 0.95
ADAM_EPS = 1e-08
DECAY = 0.1
SMALL_RATE = 0.3
MASKED = -1e30


def norm_rows(stream, gain, shift):
    center = stream - jnp.mean(stream, -1, keepdims=True)
    inverse = lax.rsqrt(jnp.mean(center * center, -1, keepdims=True) + EPS)
    scaled = center * inverse
    return (scaled * gain + shift, scaled, inverse)


def norm_back(grad_out, scaled, inverse, gain):
    weighted = grad_out * gain
    centered = weighted - jnp.mean(weighted, -1, keepdims=True)
    return inverse * (centered - scaled * jnp.mean(weighted * scaled, -1, keepdims=True))


def plain_dot(left, right):
    return jnp.dot(left, right, preferred_element_type=jnp.float32)


def left_dot(left, right):
    return lax.dot_general(
        left, right, (((0,), (0,)), ((), ())), preferred_element_type=jnp.float32
    )


def right_dot(left, right):
    return lax.dot_general(
        left, right, (((1,), (1,)), ((), ())), preferred_element_type=jnp.float32
    )


def smooth_gate(values_in):
    return jax.nn.gelu(values_in, approximate=True)


def tensor_rows(array_in):
    quarter = array_in.shape[0] // lax.axis_size("tensor")
    return lax.dynamic_slice_in_dim(array_in, lax.axis_index("tensor") * quarter, quarter, 0)


def own_rows(array_in):
    return tensor_rows(array_in)


def branch_total(partial_sum):
    return lax.psum(partial_sum.astype(jnp.bfloat16), "tensor").astype(jnp.float32)


def grad_total(partial_sum):
    return lax.psum(partial_sum.astype(jnp.bfloat16), "tensor").astype(jnp.float32)


def causal_scores(queries, key_rows, first, last):
    block_rows = last - first
    scores = jnp.einsum(
        "qhd,khd->hqk", queries[first:last], key_rows[:last], preferred_element_type=jnp.float32
    ) * HD ** (-0.5)
    query_pos = lax.broadcasted_iota(jnp.int32, (block_rows, last), 0) + first
    key_pos = lax.broadcasted_iota(jnp.int32, (block_rows, last), 1)
    return jnp.where(query_pos >= key_pos, scores, MASKED)


def attend_sequence(operands):
    queries, key_rows, value_rows = operands
    block_rows = min(512, LEN)
    outputs = []
    totals = []
    for block_idx in range(LEN // block_rows):
        first = block_idx * block_rows
        last = first + block_rows
        scores = causal_scores(queries, key_rows, first, last)
        highest = jnp.max(scores, -1, keepdims=True)
        expo = jnp.exp(scores - highest)
        summed = jnp.sum(expo, -1, keepdims=True)
        weights = (expo / summed).astype(jnp.bfloat16)
        mixed = jnp.einsum(
            "hqk,khd->qhd", weights, value_rows[:last], preferred_element_type=jnp.float32
        )
        outputs.append(mixed.astype(jnp.bfloat16))
        totals.append((highest + jnp.log(summed))[..., 0])
    return (jnp.concatenate(outputs, 0), jnp.concatenate(totals, 1))


def attend_back(operands):
    queries, key_rows, value_rows, log_total, grad_mixed = operands
    block_rows = min(512, LEN)
    d_keys = jnp.zeros(key_rows.shape, jnp.float32)
    d_values = jnp.zeros(value_rows.shape, jnp.float32)
    d_queries = []
    for block_idx in range(LEN // block_rows):
        first = block_idx * block_rows
        last = first + block_rows
        scores = causal_scores(queries, key_rows, first, last)
        probs = jnp.exp(scores - log_total[:, first:last, None])
        d_probs = jnp.einsum(
            "qhd,khd->hqk",
            grad_mixed[first:last],
            value_rows[:last],
            preferred_element_type=jnp.float32,
        )
        inner = jnp.sum(probs * d_probs, -1, keepdims=True)
        d_scores = (probs * (d_probs - inner)).astype(jnp.bfloat16)
        d_queries.append(
            jnp.einsum(
                "hqk,khd->qhd", d_scores, key_rows[:last], preferred_element_type=jnp.float32
            )
            * HD ** (-0.5)
        )
        key_part = jnp.einsum(
            "hqk,qhd->khd", d_scores, queries[first:last], preferred_element_type=jnp.float32
        ) * HD ** (-0.5)
        value_part = jnp.einsum(
            "hqk,qhd->khd",
            probs.astype(jnp.bfloat16),
            grad_mixed[first:last],
            preferred_element_type=jnp.float32,
        )
        d_keys = d_keys.at[:last].add(key_part)
        d_values = d_values.at[:last].add(value_part)
    return (jnp.concatenate(d_queries, 0), d_keys, d_values)


def layer_forward(stream, w_in, w_out, bias, vector):
    model_width = w_in.shape[0]
    head_cols = w_in.shape[2]
    heads_here = head_cols // HD
    normed, scaled_one, inverse_one = norm_rows(stream, vector[0], vector[1])
    normed_low = normed.astype(jnp.bfloat16)
    seq_count = normed_low.shape[0] // LEN
    shape4 = (seq_count, LEN, heads_here, HD)
    w_qkv = w_in[:, 0:3].reshape(model_width, 3 * head_cols)
    projected = plain_dot(normed_low, w_qkv)
    queries = (projected[:, :head_cols] + bias[0]).astype(jnp.bfloat16).reshape(shape4)
    key_rows = projected[:, head_cols : 2 * head_cols].astype(jnp.bfloat16).reshape(shape4)
    value_rows = (projected[:, 2 * head_cols :] + bias[1]).astype(jnp.bfloat16).reshape(shape4)
    mixed, log_total = lax.map(attend_sequence, (queries, key_rows, value_rows))
    mixed_low = mixed.reshape(-1, head_cols)
    attended = branch_total(plain_dot(mixed_low, w_out[0])) + vector[4]
    middle = stream + BRANCH_SCALE * attended
    hidden, scaled_two, inverse_two = norm_rows(middle, vector[2], vector[3])
    hidden_low = hidden.astype(jnp.bfloat16)
    w_up = w_in[:, 3:].reshape(model_width, 4 * head_cols)
    pre_act = plain_dot(hidden_low, w_up) + bias[2:].reshape(4 * head_cols)
    act_low = smooth_gate(pre_act).astype(jnp.bfloat16)
    w_down = w_out[1:].reshape(4 * head_cols, model_width)
    mlp_out = branch_total(plain_dot(act_low, w_down)) + vector[5]
    result = middle + BRANCH_SCALE * mlp_out
    kept = (
        scaled_one,
        inverse_one,
        normed_low,
        queries,
        key_rows,
        value_rows,
        log_total,
        mixed_low,
        scaled_two,
        inverse_two,
        hidden_low,
        pre_act,
        act_low,
    )
    return (result, kept)


def layer_backward(gradient, w_in, w_out, vector, kept):
    (
        scaled_one,
        inverse_one,
        normed_low,
        queries,
        key_rows,
        value_rows,
        log_total,
        mixed_low,
        scaled_two,
        inverse_two,
        hidden_low,
        pre_act,
        act_low,
    ) = kept
    model_width = w_in.shape[0]
    head_cols = w_in.shape[2]
    w_qkv = w_in[:, 0:3].reshape(model_width, 3 * head_cols)
    w_up = w_in[:, 3:].reshape(model_width, 4 * head_cols)
    w_down = w_out[1:].reshape(4 * head_cols, model_width)
    d_mlp = (BRANCH_SCALE * gradient).astype(jnp.bfloat16)
    g_bdown = jnp.sum(own_rows(d_mlp).astype(jnp.float32), 0)
    g_down = left_dot(act_low, d_mlp).reshape(4, head_cols, model_width)
    d_act = right_dot(d_mlp, w_down).astype(jnp.bfloat16)
    gate_value, gate_pull = jax.vjp(smooth_gate, pre_act)
    d_pre = gate_pull(d_act.astype(jnp.float32))[0].astype(jnp.bfloat16)
    g_bup = jnp.sum(d_pre.astype(jnp.float32), 0)
    g_up = left_dot(hidden_low, d_pre).reshape(model_width, 4, head_cols)
    d_hidden = grad_total(right_dot(d_pre, w_up))
    g_gain_two = jnp.sum(own_rows(d_hidden * scaled_two), 0)
    g_shift_two = jnp.sum(own_rows(d_hidden), 0)
    d_middle = gradient + norm_back(d_hidden, scaled_two, inverse_two, vector[2])
    d_attn = (BRANCH_SCALE * d_middle).astype(jnp.bfloat16)
    g_bproj = jnp.sum(own_rows(d_attn).astype(jnp.float32), 0)
    g_proj = left_dot(mixed_low, d_attn)
    d_mixed = right_dot(d_attn, w_out[0]).astype(jnp.bfloat16)
    d_queries, d_keys, d_values = lax.map(
        attend_back, (queries, key_rows, value_rows, log_total, d_mixed.reshape(queries.shape))
    )
    d_qkv = jnp.concatenate(
        [
            d_queries.reshape(-1, head_cols),
            d_keys.reshape(-1, head_cols),
            d_values.reshape(-1, head_cols),
        ],
        1,
    ).astype(jnp.bfloat16)
    g_qkv = left_dot(normed_low, d_qkv).reshape(model_width, 3, head_cols)
    g_bq = jnp.sum(d_qkv[:, :head_cols].astype(jnp.float32), 0)
    g_bv = jnp.sum(d_qkv[:, 2 * head_cols :].astype(jnp.float32), 0)
    d_normed = grad_total(right_dot(d_qkv, w_qkv))
    g_gain_one = jnp.sum(own_rows(d_normed * scaled_one), 0)
    g_shift_one = jnp.sum(own_rows(d_normed), 0)
    d_stream = d_middle + norm_back(d_normed, scaled_one, inverse_one, vector[0])
    g_in = jnp.concatenate([g_qkv, g_up], 1)
    g_out = jnp.concatenate([g_proj[None], g_down], 0)
    g_bias = jnp.concatenate([g_bq[None], g_bv[None], g_bup.reshape(4, head_cols)], 0)
    g_vector = jnp.stack([g_gain_one, g_shift_one, g_gain_two, g_shift_two, g_bproj, g_bdown])
    return (d_stream, g_in, g_out, g_bias, g_vector)


def adam_step(master, first, second, gradient, rate, decay):
    first_new = BETA_ONE * first + (1 - BETA_ONE) * gradient
    second_new = BETA_TWO * second + (1 - BETA_TWO) * gradient * gradient
    direction = (
        first_new / (1 - BETA_ONE**STEP) / (jnp.sqrt(second_new / (1 - BETA_TWO**STEP)) + ADAM_EPS)
    )
    return (first_new, second_new, master - rate * (direction + decay * master))


def shards(
    resid,
    cotangent,
    master_in,
    moment1_in,
    moment2_in,
    master_out,
    moment1_out,
    moment2_out,
    master_bias,
    moment1_bias,
    moment2_bias,
    master_vec,
    moment1_vec,
    moment2_vec,
):
    weights_in, weights_out = (
        lax.all_gather(master_in.astype(jnp.bfloat16), "dp", axis=1, tiled=True),
        lax.all_gather(master_out.astype(jnp.bfloat16), "dp", axis=3, tiled=True),
    )
    stream = resid
    gradient = cotangent
    layer_idx = 0
    stream, kept = layer_forward(
        stream,
        weights_in[layer_idx],
        weights_out[layer_idx],
        master_bias[layer_idx],
        master_vec[layer_idx],
    )
    kept_list = [kept]
    list_in = [None] * LAYERS
    list_out = [None] * LAYERS
    list_bias = [None] * LAYERS
    list_vector = [None] * LAYERS
    layer_idx = 0
    gradient, g_in, g_out, g_bias, g_vector = layer_backward(
        gradient,
        weights_in[layer_idx],
        weights_out[layer_idx],
        master_vec[layer_idx],
        kept_list[layer_idx],
    )
    list_in[layer_idx] = g_in
    list_out[layer_idx] = g_out
    list_bias[layer_idx] = g_bias
    list_vector[layer_idx] = g_vector
    summed_in = jnp.stack(list_in)
    summed_out = jnp.stack(list_out)
    summed_in, summed_out = (
        lax.psum_scatter(summed_in, "dp", scatter_dimension=1, tiled=True),
        lax.psum_scatter(summed_out, "dp", scatter_dimension=3, tiled=True),
    )
    summed_bias = lax.psum(jnp.stack(list_bias), "dp")
    summed_vector = lax.psum(jnp.stack(list_vector), ("dp", "tensor"))
    first_in, second_in, new_in = adam_step(
        master_in, moment1_in, moment2_in, summed_in, 0.5 * D ** (-0.5), DECAY
    )
    first_out, second_out, new_out = adam_step(
        master_out, moment1_out, moment2_out, summed_out, 2.0 * D ** (-0.5), DECAY
    )
    first_bias, second_bias, new_bias = adam_step(
        master_bias, moment1_bias, moment2_bias, summed_bias, SMALL_RATE, 0.0
    )
    first_vec, second_vec, new_vec = adam_step(
        master_vec, moment1_vec, moment2_vec, summed_vector, SMALL_RATE, 0.0
    )
    return (
        own_rows(stream),
        own_rows(gradient),
        first_in,
        second_in,
        new_in,
        first_out,
        second_out,
        new_out,
        first_bias,
        second_bias,
        new_bias,
        first_vec,
        second_vec,
        new_vec,
    )


MESH_IDS = pl.DeviceIdType.MESH
F32 = jnp.float32
BF16 = jnp.bfloat16
NN = (((1,), (0,)), ((), ()))
NT = (((1,), (1,)), ((), ()))
TN = (((0,), (0,)), ((), ()))
GELU_A = (2.0 / 3.141592653589793) ** 0.5
GELU_B = 0.044715


def mm(left, right, dims=NN):
    return lax.dot_general(left, right, dims, preferred_element_type=F32)


def rows_at(start, size, align):
    return pl.ds(pl.multiple_of(start, align), size)


def block_kernel(
    sizes,
    resid_h,
    cot_h,
    win_h,
    wout_h,
    bias,
    vec,
    out_o,
    grad_o,
    gsum_o,
    small_o,
    win,
    wout,
    resid,
    cot,
    inv1,
    normed,
    dmlp,
    w,
    q_s,
    k_s,
    v_s,
    e_s,
    linv,
    mixed,
    ps,
    crecv,
    fin,
    ysend,
    yrecv,
    mid,
    xhat2,
    inv2,
    normed_t,
    hidden,
    act_s,
    dpre,
    dattn,
    dmix,
    dk_s,
    dv_s,
    dqkv,
    gproj,
    gmat,
    xr,
    zs,
    zr,
    side_r,
    side_s,
    side_xs,
    side_xr,
    gsum,
    sm,
    smp,
    smx,
    smz,
    smy,
    lsem,
    ssem,
    rsem,
):
    tokens, width, quarter, heads, shard = sizes
    dp = lax.axis_index("dp")
    ten = lax.axis_index("tensor")
    z = lax.div(dp, 2)
    x = lax.rem(dp, 2)
    y = lax.div(ten, 2)
    c = lax.rem(ten, 2)
    x_dev = (dp + 1 - 2 * x, ten)
    c_dev = (dp, ten + 1 - 2 * c)
    y_dev = (dp, ten + 2 - 4 * y)

    def z_other(j):
        if j == 1:
            return z + 1 - 2 * lax.rem(z, 2)
        if j == 2:
            return lax.rem(z + 2, 4)
        return 3 - z

    def z_dev(j):
        return (2 * z_other(j) + x, ten)

    def rcopy(src, dst, send_idx, recv_idx, dev):
        return pltpu.make_async_remote_copy(
            src_ref=src,
            dst_ref=dst,
            send_sem=ssem.at[send_idx],
            recv_sem=rsem.at[recv_idx],
            device_id=dev,
            device_id_type=MESH_IDS,
        )

    barrier = pltpu.get_barrier_semaphore()
    cross_dev = (dp + 1 - 2 * x, ten + 1 - 2 * c)
    peers = [x_dev, c_dev, y_dev, cross_dev, z_dev(1), z_dev(2), z_dev(3)]
    for dev in peers:
        pl.semaphore_signal(barrier, inc=1, device_id=dev, device_id_type=MESH_IDS)
    load_win = pltpu.make_async_copy(win_h, win, lsem.at[2])
    load_wout = pltpu.make_async_copy(wout_h, wout, lsem.at[3])
    load_win.start()
    load_wout.start()
    load_resid = pltpu.make_async_copy(resid_h, resid, lsem.at[0])
    load_cot = pltpu.make_async_copy(cot_h, cot, lsem.at[1])
    load_resid.start()
    load_cot.start()

    mine = rows_at(dp * shard, shard, shard)
    load_win.wait()
    load_wout.wait()
    out_t = [jnp.transpose(wout[i]) for i in range(5)]
    pairs, last = slice(0, 2 * HD), slice(2 * HD, 3 * HD)
    tiles = [win[0, :, pairs], win[1, :, pairs], win[2, :, pairs], win[0, :, last], win[2, :, last]]
    tiles += [out_t[0][:, pairs], win[1, :, last], out_t[0][:, last]]
    w[0, mine, :] = jnp.concatenate(tiles, 1).astype(BF16)

    w[1, mine, :] = jnp.concatenate([win[3 + i] for i in range(4)], 1).astype(BF16)
    w[2, mine, :] = jnp.concatenate(out_t[1:], 1).astype(BF16)
    pl.semaphore_wait(barrier, len(peers))

    half_cols = width // 2
    units = (
        (0, slice(0, half_cols)),
        (0, slice(half_cols, width)),
        (1, slice(0, width)),
        (2, slice(0, width)),
    )

    is_end = 1 - lax.rem(lax.div(z + 1, 2), 2)
    is_mid = 1 - is_end
    upper = lax.div(z, 2)
    owner_z = (z_other(1), 2 - upper, 3 - 3 * upper)
    pair_dev, mid_dev = (2 * owner_z[0] + x, ten), (2 * owner_z[1] + x, ten)

    def ag_copy(u, zi, send, recv, dev):
        b, cols = units[u]
        src = w.at[b, rows_at((2 * zi + x) * shard, shard, shard), cols]
        return rcopy(src, src, send + u, recv, dev)

    def ag_pair(u):
        return ag_copy(u, z, 4, 3 * u, pair_dev)

    def ag_mid(u):
        return ag_copy(u, z, 4, 3 * u + 1, mid_dev)

    def ag_end_far(u, i):
        dev = (2 * owner_z[i] + x, ten)
        return ag_copy(u, z, 4, 3 * u + 2, dev)

    def ag_onward(u, i):
        if i == 0:
            return ag_copy(u, owner_z[0], 4, 3 * u + 2, mid_dev)
        return ag_copy(u, owner_z[i], 4, 3 * u + i, pair_dev)

    def ag_x(u, i):
        return ag_copy(u, z if i == 0 else owner_z[i - 1], 0, 12 + u, x_dev)

    def ag_bytes(u, pieces, send, recv):
        b, cols = units[u]
        ref = w.at[b, 0 : pieces * shard, cols]
        return rcopy(ref, ref, send, recv, x_dev)

    def mid_start(u):
        @pl.when(is_mid == 1)
        def _():
            ag_pair(u).start()
            ag_mid(u).start()

    def ag_arrive(u, i):
        ag_copy(u, owner_z[i], 0, 3 * u + i, x_dev).wait_recv()

    def pump_end(u, i):
        @pl.when(is_end == 1)
        def _():
            ag_arrive(u, i)
            ag_x(u, 1 + i).start()

    def pump_mid(u, i):
        @pl.when(is_mid == 1)
        def _():
            ag_arrive(u, i)
            if u > 1 or i == 1:
                ag_onward(u, i).start()
            ag_x(u, 1 + i).start()

    def mid_onward(u, i):
        @pl.when(is_mid == 1)
        def _():
            ag_arrive(u, i)
            ag_onward(u, i).start()

    def mid_x(u, i):
        @pl.when(is_mid == 1)
        def _():
            ag_x(u, i).start()

    def ag_finish(u):
        ag_bytes(u, 4, u, 12 + u).wait_recv()

    def ag_drain(u):
        ag_bytes(u, 4, u, 12 + u).wait_send()

        if u < 2:
            ag_bytes(u, 3, 4 + u, 12 + u).wait_send()
            return

        @pl.when(is_end == 1)
        def _():
            ag_bytes(u, 1, 4 + u, 12 + u).wait_send()

        @pl.when(is_mid == 1)
        def _():
            ag_bytes(u, 5, 4 + u, 12 + u).wait_send()

    ag_x(0, 0).start()
    ag_x(1, 0).start()
    mid_start(0)
    mid_start(1)

    @pl.when(is_end == 1)
    def _():
        for u in range(2):
            ag_pair(u).start()
            ag_end_far(u, 2).start()
            ag_end_far(u, 1).start()

    load_resid.wait()
    load_cot.wait()
    gain_one, shift_one = vec[0], vec[1]

    own = rows_at(ten * quarter, quarter, quarter)
    mid[...] = resid[own, :]
    xhat = resid

    def first_norm(r, carry):
        rows = rows_at(r * 128, 128, 128)
        part = resid[rows, :]
        center = part - jnp.mean(part, -1, keepdims=True)
        inverse = lax.rsqrt(jnp.mean(center * center, -1, keepdims=True) + EPS)
        scaled = center * inverse
        xhat[rows, :] = scaled
        inv1[rows, :] = inverse
        normed[rows, :] = (scaled * gain_one + shift_one).astype(BF16)
        dmlp[rows, :] = (cot[rows, :] * BRANCH_SCALE).astype(BF16)
        return carry

    lax.fori_loop(0, tokens // 128, first_norm, 0)
    for u, i in ((0, 0), (0, 1), (1, 0), (1, 1)):
        pump_mid(u, i)
    mid_start(2)
    pump_mid(0, 2)
    pump_mid(1, 2)
    pump_end(0, 0)
    pump_end(1, 0)

    @pl.when(is_end == 1)
    def _():
        ag_pair(2).start()

    for u, i in ((0, 2), (0, 1), (1, 2), (1, 1)):
        pump_end(u, i)

    @pl.when(is_end == 1)
    def _():
        ag_pair(3).start()

    ag_x(2, 0).start()

    sm[...] = jnp.zeros_like(sm)
    sm[5:6, :] = jnp.sum(dmlp[own, :].astype(F32), 0, keepdims=True)
    mixed[...] = jnp.zeros_like(mixed)
    dqkv[...] = jnp.zeros_like(dqkv)
    dk_s[...] = jnp.zeros_like(dk_s)
    dv_s[...] = jnp.zeros_like(dv_s)

    hc = heads * HD
    low_half = lax.broadcasted_iota(jnp.int32, (1, 2 * HD), 1) < HD
    bias_v01, bias_q01 = bias[1, :, pairs], bias[0, :, pairs]
    bias_q2v2 = jnp.concatenate([bias[0, :, last], bias[1, :, last]], 1)
    eighth = HD**-0.5

    def project_pair(r):
        rows = slice(r * 256, (r + 1) * 256)
        got = mm(normed[rows, :], w[0, :, 0:384])
        queries = (got[:, 0:128] + bias_q01).astype(BF16).astype(F32) * eighth
        q_s[0, rows, :] = jnp.where(low_half, queries, 0.0).astype(BF16)
        q_s[1, rows, :] = jnp.where(low_half, 0.0, queries).astype(BF16)
        k_s[0, rows, :] = got[:, 128:256].astype(BF16)
        v_s[0, rows, :] = (got[:, 256:384] + bias_v01).astype(BF16)

    def project_last(r):
        rows = slice(r * 256, (r + 1) * 256)
        got = mm(normed[rows, :], w[0, :, 384:768])
        both = (got[:, 0:128] + bias_q2v2).astype(BF16)
        q_s[2, rows, :] = jnp.where(low_half, both.astype(F32) * eighth, 0.0).astype(BF16)
        v_s[1, rows, :] = both
        k_s[1, rows, :] = got[:, 256:384].astype(BF16)

    ag_finish(0)
    for r in range(tokens // 256):
        project_pair(r)
    pump_end(2, 0)
    pump_mid(2, 0)
    pump_mid(2, 1)
    ag_x(3, 0).start()
    mid_start(3)

    def attend(i, which_heads):
        first, last_row = i * quarter, (i + 1) * quarter
        rows = slice(first, last_row)
        causal = lax.broadcasted_iota(jnp.int32, (quarter, quarter), 0) >= lax.broadcasted_iota(
            jnp.int32, (quarter, quarter), 1
        )
        got = {}
        for h in which_heads:
            at = h // 2
            queries = q_s[h, rows, :]
            diag = jnp.where(causal, mm(queries, k_s[at, rows, :], NT), MASKED)
            highest = jnp.max(diag, -1, keepdims=True)
            if i > 0:
                wide = mm(queries, k_s[at, 0:first, :], NT)
                highest = jnp.maximum(highest, jnp.max(wide, -1, keepdims=True))
            e_diag = jnp.exp(diag - highest)
            summed = jnp.sum(e_diag, -1, keepdims=True)
            e_diag = e_diag.astype(BF16)
            e_s[h, rows, first:last_row] = e_diag
            total = mm(e_diag, v_s[at, rows, :])
            if i > 0:
                e_wide = jnp.exp(wide - highest)
                summed = summed + jnp.sum(e_wide, -1, keepdims=True)
                e_wide = e_wide.astype(BF16)
                e_s[h, rows, 0:first] = e_wide
                total = total + mm(e_wide, v_s[at, 0:first, :])
            inverse = 1.0 / summed
            linv[h, rows, :] = inverse
            got[h] = total * inverse
        if 0 in got:
            mixed[rows, 0:128] = jnp.where(low_half, got[0], got[1]).astype(BF16)
        if 2 in got:
            mixed[rows, 128:256] = jnp.where(low_half, 0.0, got[2]).astype(BF16)

    def rs_core(k, half):
        return rcopy(ps.at[k % 2, half], crecv.at[k, half], 16 + 2 * (k % 2) + half, 16 + 2 * k + half, c_dev)

    halves = [slice(0, quarter // 2), slice(quarter // 2, quarter)]

    def rs_y(k, hh):
        src, dst = ysend.at[k, halves[hh], :], yrecv.at[k, halves[hh], :]
        return rcopy(src, dst, 20, 24 + 2 * k + hh, y_dev)

    def rs_y_start(k):
        for hh in range(2):
            rs_y(k, hh).start()

    def rs_pair(k, near, compute, prepare=None, filler=None):
        half = 1 if near else 0
        def step(s, carry):
            yq = y if near else 1 - y
            if prepare is not None:
                prepare(s)
            part = compute(2 * yq + lax.rem(1 - s + c, 2))

            @pl.when(s == 0)
            def _():
                ps[k % 2, half] = part.astype(BF16)
                rs_core(k, half).start()

            @pl.when(s == 1)
            def _():
                if filler is not None:
                    fin[(k + 1) % 3] = part
                    filler()
                    kept = fin[(k + 1) % 3]
                else:
                    kept = part
                rs_core(k, half).wait_recv()
                total = kept + crecv[k, half].astype(F32)
                if near:
                    fin[k % 3] = total
                else:
                    ysend[k] = total.astype(BF16)
                    rs_y_start(k)

            return carry

        lax.fori_loop(0, 2, step, 0)

    def rs_quad(k, compute, held, prepare=None):
        for half in range(2):
            rs_core(k - 2, half).wait_send()

        def step(s, carry):
            half, odd = lax.div(s, 2), lax.rem(s, 2)
            yq = half * y + (1 - half) * (1 - y)
            if prepare is not None:

                @pl.when(s == 3)
                def _():
                    prepare()

            part = compute(2 * yq + lax.rem(1 - odd + c, 2))

            @pl.when(odd == 0)
            def _():
                ps[k % 2, half] = part.astype(BF16)
                rs_core(k, half).start()

            @pl.when(s == 1)
            def _():
                held[...] = part

            @pl.when(s == 3)
            def _():
                fin[k % 3] = part

            return carry

        lax.fori_loop(0, 4, step, 0)

    def quad_far(k, held):
        rs_core(k, 0).wait_recv()
        ysend[k] = (held[...] + crecv[k, 0].astype(F32)).astype(BF16)

    def quad_near(k):
        rs_core(k, 1).wait_recv()
        fin[k % 3] = fin[k % 3] + crecv[k, 1].astype(F32)

    def rs_result(k, hh):
        rs_y(k, hh).wait_recv()
        return fin[k % 3, halves[hh], :] + yrecv[k, halves[hh], :].astype(F32)

    def attend_quarter(which, which_heads):
        for i in range(tokens // quarter):

            @pl.when(which == i)
            def _():
                attend(i, which_heads)

    def proj(which):
        return mm(mixed[rows_at(which * quarter, quarter, quarter), :], w[0, :, 512:768], NT)

    def far_early(s, carry):
        attend_quarter(2 * (1 - y) + lax.rem(s + c, 2), (0, 1))
        return carry

    def far_proj(which):
        attend_quarter(which, (2,))
        return proj(which)

    def near_proj(which):
        attend_quarter(which, (0, 1, 2))
        return proj(which)

    lax.fori_loop(0, 2, far_early, 0)
    mid_onward(3, 0)
    ag_finish(1)
    for r in range(tokens // 256):
        project_last(r)
    rs_pair(0, False, far_proj)
    pump_end(2, 1)
    pump_mid(2, 2)
    mid_x(3, 1)
    rs_pair(0, True, near_proj)
    pump_end(2, 2)
    pump_end(3, 0)
    pump_mid(3, 1)

    def q_rows(ref, which, hh):
        return ref.at[rows_at(which * quarter + hh * (quarter // 2), quarter // 2, quarter // 2), :]

    def qg_y(g, ref, hh):
        src = q_rows(ref, ten, hh)
        return rcopy(src, src, 21, 32 + 2 * g + hh, y_dev)

    def qg_c(g, ref, hh):
        src = q_rows(ref, ten, hh)
        return rcopy(src, src, 22, 36 + g, c_dev)

    def qg_f(g, ref, hh):
        src = q_rows(ref, ten + 2 - 4 * y, hh)
        return rcopy(src, src, 23, 38 + 2 * g + hh, c_dev)

    def qg_start(g, ref, hh):
        qg_y(g, ref, hh).start()
        qg_c(g, ref, hh).start()

    def qg_rows(ref, count, send, recv):
        rows = ref.at[0:count, :]
        return rcopy(rows, rows, send, recv, c_dev)

    def qg_near(g, ref):
        qg_rows(ref, quarter, 22, 36 + g).wait_recv()

    def qg_far(g, ref, hh):
        qg_y(g, ref, hh).wait_recv()
        qg_f(g, ref, hh).start()

    def qg_last(g, ref, hh):
        qg_f(g, ref, hh).wait_recv()

    def far_rows(g, ref, compute, between=None):
        def step(hh, carry):
            if between is not None:

                @pl.when(hh == 1)
                def _():
                    between()

            qg_far(g, ref, hh)
            compute(2 * (1 - y) + c, hh)
            qg_last(g, ref, hh)
            compute(2 * (1 - y) + 1 - c, hh)
            return carry

        lax.fori_loop(0, 2, step, 0)

    for hh in range(2):
        if hh == 1:
            pump_end(3, 1)
            pump_mid(3, 2)
        half = halves[hh]
        middle = mid[half, :] + BRANCH_SCALE * (rs_result(0, hh) + vec[4])
        mid[half, :] = middle
        center = middle - jnp.mean(middle, -1, keepdims=True)
        inverse = lax.rsqrt(jnp.mean(center * center, -1, keepdims=True) + EPS)
        scaled = center * inverse
        xhat2[half, :] = scaled
        inv2[half, :] = inverse
        mine_h = rows_at(ten * quarter + hh * (quarter // 2), quarter // 2, quarter // 2)
        hidden[mine_h, :] = (scaled * vec[2] + vec[3]).astype(BF16)
        qg_start(0, hidden, hh)

    pump_end(3, 2)
    ag_finish(2)

    bias_up = jnp.concatenate([bias[2 + i] for i in range(4)], 1)

    def forward_units(which, hh=None):
        rows = rows_at(which * quarter, quarter, quarter)
        if hh is not None:
            rows = rows_at(which * quarter + hh * (quarter // 2), quarter // 2, quarter // 2)
        hq = hidden[rows, :]
        for t in range(width // 256):
            cols = slice(t * 256, (t + 1) * 256)
            pre = mm(hq, w[1, :, cols]) + bias_up[:, cols]
            square = pre * pre
            tanh = jnp.tanh(GELU_A * (pre + GELU_B * (square * pre)))
            half_up = 0.5 + 0.5 * tanh
            act_s[rows, cols] = (pre * half_up).astype(BF16)
            slope = half_up + 0.5 * pre * (1.0 - tanh * tanh) * (
                GELU_A + (3.0 * GELU_A * GELU_B) * square
            )
            dpre[rows, cols] = slope.astype(BF16)

    def grad_block(b, left, right, near):
        rows = slice(0, tokens)
        if near is not None:
            rows = rows_at((y if near else 1 - y) * 2 * quarter, 2 * quarter, 2 * quarter)

        def tile(t, carry):
            cols = rows_at(t * 256, 256, 256)
            part = mm(left[rows, cols], right[rows, :], TN)
            if near is False:
                part = part + gmat[b, cols, :].astype(F32)
            gmat[b, cols, :] = part.astype(BF16)
            return carry

        lax.fori_loop(0, width // 256, tile, 0)

    g_units = (*units[0:3], (2, slice(0, half_cols)))
    right_half = slice(half_cols, width)

    def gx(u, zi):
        b, cols = g_units[u]
        src = gmat.at[b, rows_at((2 * zi + 1 - x) * shard, shard, shard), cols]
        return rcopy(src, xr.at[b, zi, :, cols], 8 + u, 42 + 4 * u + zi, x_dev)

    def line_to(i):
        if i == 0:
            return pair_dev, 0
        return (2 * (is_end * owner_z[0] + is_mid * owner_z[i]) + x, ten), is_end * i + is_mid * 3

    def gz(u, i):
        b, cols = g_units[u]
        dev, slot = line_to(i)
        return rcopy(zs.at[b, i, :, cols], zr.at[b, slot, :, cols], 12 + u, 58 + 4 * u + slot, dev)

    def gz_arrive(u, slot):
        b, cols = g_units[u]
        ref = zr.at[b, slot, :, cols]
        rcopy(ref, ref, 12 + u, 58 + 4 * u + slot, x_dev).wait_recv()

    def g_start(u):
        @pl.when(is_end == 1)
        def _():
            for i in (2, 1, 0):
                gx(u, owner_z[i]).start()

        @pl.when(is_mid == 1)
        def _():
            for i in (0, 2, 1):
                gx(u, owner_z[i]).start()

        gx(u, z).start()

    def x_sum(u, zo):
        b, cols = g_units[u]
        gx(u, zo).wait_recv()
        mine_x = gmat[b, rows_at((2 * zo + x) * shard, shard, shard), cols].astype(F32)
        return mine_x + xr[b, zo, :, cols].astype(F32)

    def end_pump(u, i):
        b, cols = g_units[u]

        @pl.when(is_end == 1)
        def _():
            zs[b, i, :, cols] = x_sum(u, owner_z[i]).astype(BF16)
            gz(u, i).start()

    def mid_pump(u, i):
        b, cols = g_units[u]

        @pl.when(is_mid == 1)
        def _():
            total = x_sum(u, owner_z[i])
            if i > 0:
                gz_arrive(u, i)
                total = total + zr[b, i, :, cols].astype(F32)
            zs[b, i, :, cols] = total.astype(BF16)
            gz(u, i).start()

    def g_finish(u):
        b, cols = g_units[u]
        total = x_sum(u, z)
        for slot in (0, 3):
            gz_arrive(u, slot)
            total = total + zr[b, slot, :, cols].astype(F32)
        gsum[b, :, cols] = total
        if u < 3:
            g_out(u).start()

    def g_out(u):
        b, cols = units[u]
        return pltpu.make_async_copy(gsum.at[b, :, cols], gsum_o.at[b, :, cols], lsem.at[4 + u])

    def g_drain(u):
        b, cols = g_units[u]
        rcopy(xr.at[b, :, :, cols], xr.at[b, :, :, cols], 8 + u, 56, x_dev).wait_send()
        rcopy(zs.at[b, :, :, cols], zs.at[b, :, :, cols], 12 + u, 56, x_dev).wait_send()
        g_out(u).wait()

    def side_rows(zo):
        return gmat.at[2, rows_at(zo * 2 * shard, 2 * shard, 2 * shard), right_half]

    def side_copy(src, i):
        dev, slot = line_to(i)
        return rcopy(src, side_r.at[slot], 28, 78 + slot, dev)

    def side_arrive(slot):
        rcopy(side_r.at[slot], side_r.at[slot], 28, 78 + slot, x_dev).wait_recv()

    def side_start():
        @pl.when(is_end == 1)
        def _():
            for i in (2, 1):
                side_copy(side_rows(owner_z[i]), i).start()

        side_copy(side_rows(owner_z[0]), 0).start()

    def side_middle():
        @pl.when(is_mid == 1)
        def _():
            for i in (2, 1):
                side_arrive(i)
                mine_z = gmat[2, rows_at(owner_z[i] * 2 * shard, 2 * shard, 2 * shard), right_half]
                side_s[i - 1] = (mine_z.astype(F32) + side_r[i].astype(F32)).astype(BF16)
                side_copy(side_s.at[i - 1], i).start()

    def side_x():
        return rcopy(side_xs, side_xr, 29, 82, x_dev)

    def side_cross():
        side_arrive(0)
        side_arrive(3)

        def total(xi):
            at = rows_at(xi * shard, shard, shard)
            got = gmat[2, rows_at((2 * z + xi) * shard, shard, shard), right_half].astype(F32)
            return got + side_r[0, at, :].astype(F32) + side_r[3, at, :].astype(F32)

        side_xs[...] = total(1 - x).astype(BF16)
        side_x().start()
        gsum[2, :, right_half] = total(x)

    def side_finish():
        side_x().wait_recv()
        gsum[2, :, right_half] = gsum[2, :, right_half] + side_xr[...].astype(F32)
        g_out(3).start()

    def backward_units(which):
        rows = rows_at(which * quarter, quarter, quarter)
        gq = dmlp[rows, :]
        for t in range(width // 256):
            cols = slice(t * 256, (t + 1) * 256)
            d_act = mm(gq, w[2, :, cols]).astype(BF16).astype(F32)
            d_low = (dpre[rows, cols].astype(F32) * d_act).astype(BF16)
            dpre[rows, cols] = d_low
            sm[6:7, cols] = sm[6:7, cols] + jnp.sum(d_low.astype(F32), 0, keepdims=True)
        return mm(dpre[rows, :], w[1], NT)

    def branch(which):
        rows = rows_at(which * quarter, quarter, quarter)
        return mm(act_s[rows, :], w[2], NT)

    def near_units(s, carry):
        @pl.when(s == 1)
        def _():
            qg_near(0, hidden)

        forward_units(2 * y + lax.rem(s + c, 2))
        return carry

    lax.fori_loop(0, 2, near_units, 0)
    grad_block(2, dmlp, act_s, True)
    for t in range(width // 256):
        cols = slice(t * 256, (t + 1) * 256)
        normed_t[cols, :] = jnp.transpose(normed[:, cols])
    def down_gradient():
        grad_block(2, dmlp, act_s, False)
        g_start(3)
        side_start()

    far_rows(0, hidden, forward_units)
    ag_finish(3)
    rs_pair(1, False, backward_units, filler=down_gradient)
    rs_pair(1, True, backward_units)
    grad_block(1, hidden, dpre, None)
    g_start(2)
    end_pump(3, 2)
    mid_pump(3, 0)
    def second_norm_back(hh):
        half = halves[hh]
        mine_h = rows_at(ten * quarter + hh * (quarter // 2), quarter // 2, quarter // 2)
        d_hidden = rs_result(1, hh)
        scaled = xhat2[half, :]
        sm[2:3, :] = sm[2:3, :] + jnp.sum(d_hidden * scaled, 0, keepdims=True)
        sm[3:4, :] = sm[3:4, :] + jnp.sum(d_hidden, 0, keepdims=True)
        weighted = d_hidden * vec[2]
        d_mid = cot[mine_h, :] + inv2[half, :] * (
            weighted
            - jnp.mean(weighted, -1, keepdims=True)
            - scaled * jnp.mean(weighted * scaled, -1, keepdims=True)
        )
        fin[1, half, :] = d_mid
        d_attn = (BRANCH_SCALE * d_mid).astype(BF16)
        dattn[mine_h, :] = d_attn
        sm[4:5, :] = sm[4:5, :] + jnp.sum(d_attn.astype(F32), 0, keepdims=True)
        qg_start(1, dattn, hh)

    rs_quad(2, branch, fin.at[0])
    second_norm_back(0)
    end_pump(3, 1)
    quad_far(2, fin.at[0])
    quad_near(2)
    side_middle()
    end_pump(3, 0)
    second_norm_back(1)
    rs_y_start(2)

    def attend_back(i, which_heads, hh=None):
        first, last_row = i * quarter, (i + 1) * quarter
        rows = slice(first, last_row)
        if hh is not None:
            rows = rows_at(first + hh * (quarter // 2), quarter // 2, quarter // 2)
        got, kept = {}, {}
        for h in which_heads:
            at = h // 2
            tile = slice(at * 128, (at + 1) * 128)
            d_out = dmix[rows, tile].astype(F32) * linv[h, rows, :]
            d_out = jnp.where(low_half, d_out, 0.0) if h == 0 else jnp.where(low_half, 0.0, d_out)
            inner = jnp.sum(d_out * mixed[rows, tile].astype(F32), -1, keepdims=True)
            d_scaled = d_out.astype(BF16)
            expo = e_s[h, rows, 0:last_row]
            d_probs = mm(d_scaled, v_s[at, 0:last_row, :], NT)
            d_scores = (expo.astype(F32) * (d_probs - inner)).astype(BF16)
            got[h] = mm(d_scores, k_s[at, 0:last_row, :]) * eighth
            kept[h] = (d_scores, d_scaled, expo)
        for at, group in enumerate(((0, 1), (2,))):
            if group[0] not in got:
                continue
            queries = jnp.concatenate([q_s[h, rows, :] for h in group], 0)
            d_s, d_o, exps = [jnp.concatenate([kept[h][i] for h in group], 0) for i in range(3)]
            dk_s[at, :, 0:last_row] = dk_s[at, :, 0:last_row] + mm(queries, d_s, TN)
            dv_s[at, :, 0:last_row] = dv_s[at, :, 0:last_row] + mm(d_o, exps, TN)
        if 0 in got:
            dqkv[rows, 0:128] = jnp.where(low_half, got[0], got[1]).astype(BF16)
        if 2 in got:
            dqkv[rows, 384:512] = jnp.where(low_half, got[2], 0.0).astype(BF16)

    def back_quarters(near, which_heads, fresh, prepare=None):
        def step(s, carry):
            if prepare is not None:
                prepare(s)
            yq = y if near else 1 - y
            which = 2 * yq + lax.rem(s + c, 2)
            if fresh:
                rows = rows_at(which * quarter, quarter, quarter)
                dmix[rows, :] = mm(dattn[rows, :], w[0, :, 512:768]).astype(BF16)
            for i in range(tokens // quarter):

                @pl.when(which == i)
                def _():
                    attend_back(i, which_heads)

            return carry

        lax.fori_loop(0, 2, step, 0)

    def back_far(which, hh):
        rows = rows_at(which * quarter + hh * (quarter // 2), quarter // 2, quarter // 2)
        dmix[rows, :] = mm(dattn[rows, :], w[0, :, 512:768]).astype(BF16)
        for i in range(tokens // quarter):

            @pl.when(which == i)
            def _():
                attend_back(i, (0, 1), hh)

    def near_ready(s):
        @pl.when(s == 1)
        def _():
            qg_near(1, dattn)

    def keys_values(at):
        if at == 0:
            dqkv[:, 128:256] = jnp.transpose(dk_s[0]).astype(BF16)
            dqkv[:, 256:384] = jnp.transpose(dv_s[0]).astype(BF16)
        else:
            d_v = jnp.transpose(dv_s[1]).astype(BF16)
            dqkv[:, 384:512] = jnp.where(low_half, dqkv[:, 384:512], d_v)
            dqkv[:, 640:768] = jnp.transpose(dk_s[1]).astype(BF16)

    def zero_rows(u, zo):
        cols = rows_at(zo * 2 * shard, 2 * shard, 2 * shard)
        left = normed_t[cols, :]
        if u == 0:
            gmat[0, cols, 0:384] = mm(left, dqkv[:, 0:384]).astype(BF16)
        else:
            g_qkv = mm(left, dqkv[:, 384:768])
            gmat[0, cols, 384:512] = g_qkv[:, 0:128].astype(BF16)
            gmat[0, cols, 512:768] = (g_qkv[:, 128:384] + gproj[cols, :]).astype(BF16)
        gx(u, zo).start()

    def zero_unit(u, steps):
        def step(s, carry):
            odd, half = lax.rem(s, 2), lax.div(s, 2)
            first = is_end * owner_z[2] + is_mid * owner_z[0]
            second = is_end * owner_z[1] + is_mid * owner_z[2]
            third = is_end * owner_z[0] + is_mid * owner_z[1]
            early = (1 - odd) * first + odd * second
            late = (1 - odd) * third + odd * z
            zero_rows(u, (1 - half) * early + half * late)
            return carry

        lax.fori_loop(*steps, step, 0)

    back_quarters(True, (0, 1, 2), True, near_ready)
    mid_pump(3, 2)
    mid_pump(2, 0)
    end_pump(2, 2)
    end_pump(2, 1)
    mid_pump(3, 1)
    far_rows(1, dattn, back_far, side_cross)
    keys_values(0)
    zero_unit(0, (0, 4))
    end_pump(2, 0)
    mid_pump(2, 2)
    gproj[...] = jnp.transpose(mm(mixed[...], dattn[...], TN))
    back_quarters(False, (2,), False)
    keys_values(1)
    mid_pump(2, 1)

    def first_back(which):
        rows = rows_at(which * quarter, quarter, quarter)
        d_low = dqkv[rows, :]
        part = mm(d_low, w[0], NT)
        rounded = part.astype(BF16).astype(F32)
        sm[0:1, :] = sm[0:1, :] + jnp.sum(rounded * xhat[rows, :], 0, keepdims=True)
        sm[1:2, :] = sm[1:2, :] + jnp.sum(rounded, 0, keepdims=True)
        sm[7:8, :] = sm[7:8, :] + jnp.sum(d_low.astype(F32), 0, keepdims=True)
        return part

    end_pump(0, 2)
    mid_pump(0, 0)
    rs_quad(3, first_back, xhat2, lambda: end_pump(0, 1))

    small_c = rcopy(sm, smp, 27, 77, c_dev)
    small_c.start()
    quad_far(3, xhat2)
    rs_y_start(3)
    small_c.wait_recv()
    smx[0, 0:6, :] = sm[0:6, :] + smp[0:6, :]
    smx[0, 6:8, :] = smp[6:8, :]
    small_x = rcopy(smx.at[0], smx.at[1], 24, 74, cross_dev)
    small_x.start()
    end_pump(0, 0)
    zero_unit(1, (0, 4))
    quad_near(3)
    mid_pump(0, 2)
    small_x.wait_recv()
    smz[z, 0:6, :] = smx[0, 0:6, :] + smx[1, 0:6, :]
    smz[z, 6:8, :] = sm[6:8, :] + smx[1, 6:8, :]

    def small_z(j):
        return rcopy(smz.at[z], smz.at[z], 25, 75, z_dev(j))

    for j in (3, 2, 1):
        small_z(j).start()
    mid_pump(0, 1)
    g_finish(3)
    side_finish()
    g_finish(2)
    for hh in range(2):
        half = halves[hh]
        mid[half, :] = mid[half, :] + BRANCH_SCALE * (rs_result(2, hh) + vec[5])
    put_out = pltpu.make_async_copy(mid, out_o, lsem.at[8])
    put_out.start()
    end_pump(1, 2)
    mid_pump(1, 0)
    end_pump(1, 1)

    def first_norm_back(hh):
        half = halves[hh]
        mine_h = rows_at(ten * quarter + hh * (quarter // 2), quarter // 2, quarter // 2)
        d_normed = rs_result(3, hh)
        scaled = xhat[mine_h, :]
        weighted = d_normed * gain_one
        xhat2[half, :] = fin[1, half, :] + inv1[mine_h, :] * (
            weighted
            - jnp.mean(weighted, -1, keepdims=True)
            - scaled * jnp.mean(weighted * scaled, -1, keepdims=True)
        )

    first_norm_back(0)
    end_pump(1, 0)
    three = rcopy(smz.at[0:3], smz.at[0:3], 25, 75, x_dev)
    three.wait_recv()
    smy[0] = (smz[0] + smz[1]) + (smz[2] + smz[3])
    small_y = rcopy(smy.at[0], smy.at[1], 26, 76, y_dev)
    small_y.start()
    mid_pump(1, 2)
    first_norm_back(1)
    put_grad = pltpu.make_async_copy(xhat2, grad_o, lsem.at[9])
    put_grad.start()
    mid_pump(1, 1)
    g_finish(0)
    small_y.wait_recv()
    small_c.wait_send()
    sm[0:6, :] = smy[0, 0:6, :] + smy[1, 0:6, :]
    sm[6:8, :] = smy[0, 6:8, :]
    put_small = pltpu.make_async_copy(sm, small_o, lsem.at[10])
    put_small.start()
    g_finish(1)

    for u in range(4):
        ag_drain(u)
        g_drain(u)
    three_sides = side_r.at[0:3]
    rcopy(three_sides, three_sides, 28, 76, x_dev).wait_send()
    side_x().wait_send()
    rcopy(ysend, yrecv, 20, 24, y_dev).wait_send()
    for k in (2, 3):
        for half in range(2):
            rs_core(k, half).wait_send()
    for send in (21, 22, 23):
        qg_rows(hidden, 2 * quarter, send, 36).wait_send()
    small_x.wait_send()
    three.wait_send()
    small_y.wait_send()
    put_out.wait()
    put_grad.wait()
    put_small.wait()


def run_block(resid, cotangent, win, wout, bias, vec, rows, n_dp):
    tokens, width = resid.shape
    quarter = tokens // 4
    head_cols = win.shape[2]
    heads = head_cols // HD
    sizes = (tokens, width, quarter, heads, rows)
    vm = pltpu.VMEM
    scratch = [
        vm(win.shape, F32),
        vm(wout.shape, F32),
        vm((tokens, width), F32),
        vm((tokens, width), F32),
        vm((tokens, 1), F32),
        vm((tokens, width), BF16),
        vm((tokens, width), BF16),
        vm((3, width, width), BF16),
        vm((heads, tokens, 2 * HD), BF16),
        vm((2, tokens, 2 * HD), BF16),
        vm((2, tokens, 2 * HD), BF16),
        vm((heads, tokens, tokens), BF16),
        vm((heads, tokens, 1), F32),
        vm((tokens, 256), BF16),
        vm((2, 2, quarter, width), BF16),
        vm((4, 2, quarter, width), BF16),
        vm((3, quarter, width), F32),
        vm((4, quarter, width), BF16),
        vm((4, quarter, width), BF16),
        vm((quarter, width), F32),
        vm((quarter, width), F32),
        vm((quarter, 1), F32),
        vm((width, tokens), BF16),
        vm((tokens, width), BF16),
        vm((tokens, width), BF16),
        vm((tokens, width), BF16),
        vm((tokens, width), BF16),
        vm((tokens, 256), BF16),
        vm((2, 2 * HD, tokens), F32),
        vm((2, 2 * HD, tokens), F32),
        vm((tokens, width), BF16),
        vm((width, 256), F32),
        vm((3, width, width), BF16),
        vm((3, 4, rows, width), BF16),
        vm((3, 3, rows, width), BF16),
        vm((3, 4, rows, width), BF16),
        vm((4, 2 * rows, width // 2), BF16),
        vm((2, 2 * rows, width // 2), BF16),
        vm((rows, width // 2), BF16),
        vm((rows, width // 2), BF16),
        vm((3, rows, width), F32),
        vm((8, width), F32),
        vm((8, width), F32),
        vm((2, 8, width), F32),
        vm((4, 8, width), F32),
        vm((2, 8, width), F32),
        pltpu.SemaphoreType.DMA((11,)),
        pltpu.SemaphoreType.DMA((30,)),
        pltpu.SemaphoreType.DMA((83,)),
    ]
    whole = pl.BlockSpec(memory_space=pltpu.VMEM)
    return pl.pallas_call(
        functools.partial(block_kernel, sizes),
        out_shape=(
            jax.ShapeDtypeStruct((quarter, width), F32),
            jax.ShapeDtypeStruct((quarter, width), F32),
            jax.ShapeDtypeStruct((3, rows, width), F32),
            jax.ShapeDtypeStruct((8, width), F32),
        ),
        in_specs=[pl.BlockSpec(memory_space=pl.ANY)] * 4 + [whole] * 2,
        out_specs=[pl.BlockSpec(memory_space=pl.ANY)] * 4,
        scratch_shapes=scratch,
        compiler_params=pltpu.CompilerParams(
            collective_id=1, has_side_effects=True, vmem_limit_bytes=62 << 20
        ),
        name="block",
    )(resid, cotangent, win, wout, bias, vec)


BLOCK_ZERO = (((0, 128), (384, 448)), ((128, 256), (640, 704)), ((256, 384), (448, 512)), ((512, 640), (704, 768)))


def adam_kernel(hc, *refs):
    passed_h, gsum_h, small_h = refs[0:2], refs[2], refs[3]
    in_h, out_h, bias_h, vec_h = refs[4:7], refs[7:10], refs[10:13], refs[13:16]
    passed_o, in_o, out_o, bias_o, vec_o = refs[16:18], refs[18:21], refs[21:24], refs[24:27], refs[27:30]
    vin, vout, vbias, vvec, rin, rout, rbias, rvec, gsum, small, passed, sems = refs[30:42]

    def copy(src, dst, sem):
        pltpu.make_async_copy(src, dst, sems.at[sem]).start()

    def wait(ref, sem):
        pltpu.make_async_copy(ref, ref, sems.at[sem]).wait()

    def columns(ref, rows, kind):
        return jnp.concatenate([ref[rows + (slice(a, b),)] for a, b in BLOCK_ZERO[kind]], 1)

    every = slice(None)
    kinds_in = (3, 4, 5, 6, 0, 1, 2)
    copy(gsum_h.at[1], gsum.at[1], 0)
    for i in kinds_in:
        for a in range(3):
            copy(in_h[a].at[i], vin.at[i, a], 3 + i)
        if i == 6:
            copy(gsum_h.at[0], gsum.at[0], 1)
    copy(small_h, small, 15)
    for a in range(3):
        copy(bias_h[a], vbias.at[a], 16)
        copy(vec_h[a], vvec.at[a], 17)
    copy(gsum_h.at[2], gsum.at[2], 2)
    for i in range(5):
        for a in range(3):
            copy(out_h[a].at[i], vout.at[i, a], 10 + i)
    for a in range(2):
        copy(passed_h[a], passed.at[a], 18)

    wait(gsum.at[1], 0)
    for i in kinds_in:
        wait(vin.at[i], 3 + i)
        if i == 0:
            wait(gsum.at[0], 1)
        part = columns(gsum, (0, every), i) if i < 3 else gsum[1, :, (i - 3) * hc : (i - 2) * hc]
        new = adam_step(vin[i, 0], vin[i, 1], vin[i, 2], part, 0.5 * D ** (-0.5), DECAY)
        for a in range(3):
            rin[i, a] = new[a]
            copy(rin.at[i, a], in_o[a].at[i], 19)
    wait(small, 15)
    wait(vbias, 16)
    wait(vvec, 17)
    for i in range(6):
        new = adam_step(vvec[0, i], vvec[1, i], vvec[2, i], small[i : i + 1, :], SMALL_RATE, 0.0)
        for a in range(3):
            rvec[a, i] = new[a]
        if i < 2:
            part = columns(small, (slice(7, 8),), 2 * i)
        else:
            part = small[6:7, (i - 2) * hc : (i - 1) * hc]
        new = adam_step(vbias[0, i], vbias[1, i], vbias[2, i], part, SMALL_RATE, 0.0)
        for a in range(3):
            rbias[a, i] = new[a]
    for a in range(3):
        copy(rbias.at[a], bias_o[a], 20)
        copy(rvec.at[a], vec_o[a], 21)
    wait(gsum.at[2], 2)
    for i in range(5):
        wait(vout.at[i], 10 + i)
        part = columns(gsum, (0, every), 3) if i == 0 else gsum[2, :, (i - 1) * hc : i * hc]
        part = jnp.transpose(part)
        new = adam_step(vout[i, 0], vout[i, 1], vout[i, 2], part, 2.0 * D ** (-0.5), DECAY)
        for a in range(3):
            rout[i, a] = new[a]
            copy(rout.at[i, a], out_o[a].at[i], 22)
    wait(passed, 18)
    for a in range(2):
        copy(passed.at[a], passed_o[a], 23)
    for ref, sem in ((rin, 19), (rbias, 20), (rvec, 21), (rout, 22), (passed, 23)):
        wait(ref, sem)


def run_adam(*operands):
    hc = operands[4].shape[2]
    out_rows, _, g_sum, small = operands[0:4]
    shapes = [out_rows, out_rows, *operands[4:16]]
    hbm = pl.BlockSpec(memory_space=pl.ANY)
    kinds_in, kinds_out = operands[4].shape, operands[7].shape
    small_bias, small_vec = operands[10].shape, operands[13].shape
    big = [
        pltpu.VMEM((kinds_in[0], 3, *kinds_in[1:]), F32),
        pltpu.VMEM((kinds_out[0], 3, *kinds_out[1:]), F32),
        pltpu.VMEM((3, *small_bias), F32),
        pltpu.VMEM((3, *small_vec), F32),
    ]
    return pl.pallas_call(
        functools.partial(adam_kernel, hc),
        out_shape=[jax.ShapeDtypeStruct(a.shape, F32) for a in shapes],
        in_specs=[hbm] * 16,
        out_specs=[hbm] * 14,
        scratch_shapes=big * 2
        + [pltpu.VMEM(g_sum.shape, F32), pltpu.VMEM(small.shape, F32)]
        + [pltpu.VMEM((2, *out_rows.shape), F32), pltpu.SemaphoreType.DMA((24,))],
        compiler_params=pltpu.CompilerParams(vmem_limit_bytes=62 << 20),
        name="adam",
    )(*operands)


def fused_shards(
    resid,
    cotangent,
    master_in,
    moment1_in,
    moment2_in,
    master_out,
    moment1_out,
    moment2_out,
    master_bias,
    moment1_bias,
    moment2_bias,
    master_vec,
    moment1_vec,
    moment2_vec,
):
    rows = master_in.shape[1]
    hc = master_in.shape[3]
    turned = [jnp.transpose(a[0], (1, 0, 2)) for a in (master_in, moment1_in, moment2_in)]
    plain = [a[0] for a in (master_out, moment1_out, moment2_out)]
    biases = [a.reshape(6, 1, hc) for a in (master_bias, moment1_bias, moment2_bias)]
    vectors = [a.reshape(6, 1, D) for a in (master_vec, moment1_vec, moment2_vec)]
    sums = run_block(
        resid, cotangent, turned[0], plain[0], biases[0], vectors[0], rows, lax.axis_size("dp")
    )
    new = run_adam(*sums, *turned, *plain, *biases, *vectors)
    return (
        new[0],
        new[1],
        *[jnp.transpose(a, (1, 0, 2))[None] for a in new[2:5]],
        *[a[None] for a in new[5:8]],
        *[a.reshape(1, 6, hc) for a in new[8:11]],
        *[a.reshape(1, 6, D) for a in new[11:14]],
    )


def solution(mesh):
    fused = mesh.shape["dp"] == 8 and mesh.shape["tensor"] == 4
    return jax.shard_map(
        fused_shards if fused else shards,
        mesh=mesh,
        in_specs=(
            P("dp", None),
            P("dp", None),
            P(None, "dp", None, "tensor"),
            P(None, "dp", None, "tensor"),
            P(None, "dp", None, "tensor"),
            P(None, None, "tensor", "dp"),
            P(None, None, "tensor", "dp"),
            P(None, None, "tensor", "dp"),
            P(None, None, "tensor"),
            P(None, None, "tensor"),
            P(None, None, "tensor"),
            P(),
            P(),
            P(),
        ),
        out_specs=(
            P(("dp", "tensor"), None),
            P(("dp", "tensor"), None),
            P(None, "dp", None, "tensor"),
            P(None, "dp", None, "tensor"),
            P(None, "dp", None, "tensor"),
            P(None, None, "tensor", "dp"),
            P(None, None, "tensor", "dp"),
            P(None, None, "tensor", "dp"),
            P(None, None, "tensor"),
            P(None, None, "tensor"),
            P(None, None, "tensor"),
            P(),
            P(),
            P(),
        ),
        check_vma=False,
    )
```

```python
import functools

import jax
import jax.numpy as jnp
from jax import lax
from jax.experimental import pallas as pl
from jax.experimental.pallas import tpu as pltpu
from jax.sharding import PartitionSpec as P

D = 768
HD = 64
LEN = 1024
LAYERS = 1
STEP = 10


EPS = 1e-05
BRANCH_SCALE = 48 ** (-0.5)
BETA_ONE = 0.9
BETA_TWO = 0.95
ADAM_EPS = 1e-08
DECAY = 0.1
SMALL_RATE = 0.3
MASKED = -1e30


def norm_rows(stream, gain, shift):
    center = stream - jnp.mean(stream, -1, keepdims=True)
    inverse = lax.rsqrt(jnp.mean(center * center, -1, keepdims=True) + EPS)
    scaled = center * inverse
    return (scaled * gain + shift, scaled, inverse)


def norm_back(grad_out, scaled, inverse, gain):
    weighted = grad_out * gain
    centered = weighted - jnp.mean(weighted, -1, keepdims=True)
    return inverse * (centered - scaled * jnp.mean(weighted * scaled, -1, keepdims=True))


def plain_dot(left, right):
    return jnp.dot(left, right, preferred_element_type=jnp.float32)


def left_dot(left, right):
    return lax.dot_general(
        left, right, (((0,), (0,)), ((), ())), preferred_element_type=jnp.float32
    )


def right_dot(left, right):
    return lax.dot_general(
        left, right, (((1,), (1,)), ((), ())), preferred_element_type=jnp.float32
    )


def smooth_gate(values_in):
    return jax.nn.gelu(values_in, approximate=True)


def tensor_rows(array_in):
    quarter = array_in.shape[0] // lax.axis_size("tensor")
    return lax.dynamic_slice_in_dim(array_in, lax.axis_index("tensor") * quarter, quarter, 0)


def own_rows(array_in):
    return tensor_rows(array_in)


def branch_total(partial_sum):
    return lax.psum(partial_sum.astype(jnp.bfloat16), "tensor").astype(jnp.float32)


def grad_total(partial_sum):
    return lax.psum(partial_sum.astype(jnp.bfloat16), "tensor").astype(jnp.float32)


def causal_scores(queries, key_rows, first, last):
    block_rows = last - first
    scores = jnp.einsum(
        "qhd,khd->hqk", queries[first:last], key_rows[:last], preferred_element_type=jnp.float32
    ) * HD ** (-0.5)
    query_pos = lax.broadcasted_iota(jnp.int32, (block_rows, last), 0) + first
    key_pos = lax.broadcasted_iota(jnp.int32, (block_rows, last), 1)
    return jnp.where(query_pos >= key_pos, scores, MASKED)


def attend_sequence(operands):
    queries, key_rows, value_rows = operands
    block_rows = min(512, LEN)
    outputs = []
    totals = []
    for block_idx in range(LEN // block_rows):
        first = block_idx * block_rows
        last = first + block_rows
        scores = causal_scores(queries, key_rows, first, last)
        highest = jnp.max(scores, -1, keepdims=True)
        expo = jnp.exp(scores - highest)
        summed = jnp.sum(expo, -1, keepdims=True)
        weights = (expo / summed).astype(jnp.bfloat16)
        mixed = jnp.einsum(
            "hqk,khd->qhd", weights, value_rows[:last], preferred_element_type=jnp.float32
        )
        outputs.append(mixed.astype(jnp.bfloat16))
        totals.append((highest + jnp.log(summed))[..., 0])
    return (jnp.concatenate(outputs, 0), jnp.concatenate(totals, 1))


def attend_back(operands):
    queries, key_rows, value_rows, log_total, grad_mixed = operands
    block_rows = min(512, LEN)
    d_keys = jnp.zeros(key_rows.shape, jnp.float32)
    d_values = jnp.zeros(value_rows.shape, jnp.float32)
    d_queries = []
    for block_idx in range(LEN // block_rows):
        first = block_idx * block_rows
        last = first + block_rows
        scores = causal_scores(queries, key_rows, first, last)
        probs = jnp.exp(scores - log_total[:, first:last, None])
        d_probs = jnp.einsum(
            "qhd,khd->hqk",
            grad_mixed[first:last],
            value_rows[:last],
            preferred_element_type=jnp.float32,
        )
        inner = jnp.sum(probs * d_probs, -1, keepdims=True)
        d_scores = (probs * (d_probs - inner)).astype(jnp.bfloat16)
        d_queries.append(
            jnp.einsum(
                "hqk,khd->qhd", d_scores, key_rows[:last], preferred_element_type=jnp.float32
            )
            * HD ** (-0.5)
        )
        key_part = jnp.einsum(
            "hqk,qhd->khd", d_scores, queries[first:last], preferred_element_type=jnp.float32
        ) * HD ** (-0.5)
        value_part = jnp.einsum(
            "hqk,qhd->khd",
            probs.astype(jnp.bfloat16),
            grad_mixed[first:last],
            preferred_element_type=jnp.float32,
        )
        d_keys = d_keys.at[:last].add(key_part)
        d_values = d_values.at[:last].add(value_part)
    return (jnp.concatenate(d_queries, 0), d_keys, d_values)


def layer_forward(stream, w_in, w_out, bias, vector):
    model_width = w_in.shape[0]
    head_cols = w_in.shape[2]
    heads_here = head_cols // HD
    normed, scaled_one, inverse_one = norm_rows(stream, vector[0], vector[1])
    normed_low = normed.astype(jnp.bfloat16)
    seq_count = normed_low.shape[0] // LEN
    shape4 = (seq_count, LEN, heads_here, HD)
    w_qkv = w_in[:, 0:3].reshape(model_width, 3 * head_cols)
    projected = plain_dot(normed_low, w_qkv)
    queries = (projected[:, :head_cols] + bias[0]).astype(jnp.bfloat16).reshape(shape4)
    key_rows = projected[:, head_cols : 2 * head_cols].astype(jnp.bfloat16).reshape(shape4)
    value_rows = (projected[:, 2 * head_cols :] + bias[1]).astype(jnp.bfloat16).reshape(shape4)
    mixed, log_total = lax.map(attend_sequence, (queries, key_rows, value_rows))
    mixed_low = mixed.reshape(-1, head_cols)
    attended = branch_total(plain_dot(mixed_low, w_out[0])) + vector[4]
    middle = stream + BRANCH_SCALE * attended
    hidden, scaled_two, inverse_two = norm_rows(middle, vector[2], vector[3])
    hidden_low = hidden.astype(jnp.bfloat16)
    w_up = w_in[:, 3:].reshape(model_width, 4 * head_cols)
    pre_act = plain_dot(hidden_low, w_up) + bias[2:].reshape(4 * head_cols)
    act_low = smooth_gate(pre_act).astype(jnp.bfloat16)
    w_down = w_out[1:].reshape(4 * head_cols, model_width)
    mlp_out = branch_total(plain_dot(act_low, w_down)) + vector[5]
    result = middle + BRANCH_SCALE * mlp_out
    kept = (
        scaled_one,
        inverse_one,
        normed_low,
        queries,
        key_rows,
        value_rows,
        log_total,
        mixed_low,
        scaled_two,
        inverse_two,
        hidden_low,
        pre_act,
        act_low,
    )
    return (result, kept)


def layer_backward(gradient, w_in, w_out, vector, kept):
    (
        scaled_one,
        inverse_one,
        normed_low,
        queries,
        key_rows,
        value_rows,
        log_total,
        mixed_low,
        scaled_two,
        inverse_two,
        hidden_low,
        pre_act,
        act_low,
    ) = kept
    model_width = w_in.shape[0]
    head_cols = w_in.shape[2]
    w_qkv = w_in[:, 0:3].reshape(model_width, 3 * head_cols)
    w_up = w_in[:, 3:].reshape(model_width, 4 * head_cols)
    w_down = w_out[1:].reshape(4 * head_cols, model_width)
    d_mlp = (BRANCH_SCALE * gradient).astype(jnp.bfloat16)
    g_bdown = jnp.sum(own_rows(d_mlp).astype(jnp.float32), 0)
    g_down = left_dot(act_low, d_mlp).reshape(4, head_cols, model_width)
    d_act = right_dot(d_mlp, w_down).astype(jnp.bfloat16)
    gate_value, gate_pull = jax.vjp(smooth_gate, pre_act)
    d_pre = gate_pull(d_act.astype(jnp.float32))[0].astype(jnp.bfloat16)
    g_bup = jnp.sum(d_pre.astype(jnp.float32), 0)
    g_up = left_dot(hidden_low, d_pre).reshape(model_width, 4, head_cols)
    d_hidden = grad_total(right_dot(d_pre, w_up))
    g_gain_two = jnp.sum(own_rows(d_hidden * scaled_two), 0)
    g_shift_two = jnp.sum(own_rows(d_hidden), 0)
    d_middle = gradient + norm_back(d_hidden, scaled_two, inverse_two, vector[2])
    d_attn = (BRANCH_SCALE * d_middle).astype(jnp.bfloat16)
    g_bproj = jnp.sum(own_rows(d_attn).astype(jnp.float32), 0)
    g_proj = left_dot(mixed_low, d_attn)
    d_mixed = right_dot(d_attn, w_out[0]).astype(jnp.bfloat16)
    d_queries, d_keys, d_values = lax.map(
        attend_back, (queries, key_rows, value_rows, log_total, d_mixed.reshape(queries.shape))
    )
    d_qkv = jnp.concatenate(
        [
            d_queries.reshape(-1, head_cols),
            d_keys.reshape(-1, head_cols),
            d_values.reshape(-1, head_cols),
        ],
        1,
    ).astype(jnp.bfloat16)
    g_qkv = left_dot(normed_low, d_qkv).reshape(model_width, 3, head_cols)
    g_bq = jnp.sum(d_qkv[:, :head_cols].astype(jnp.float32), 0)
    g_bv = jnp.sum(d_qkv[:, 2 * head_cols :].astype(jnp.float32), 0)
    d_normed = grad_total(right_dot(d_qkv, w_qkv))
    g_gain_one = jnp.sum(own_rows(d_normed * scaled_one), 0)
    g_shift_one = jnp.sum(own_rows(d_normed), 0)
    d_stream = d_middle + norm_back(d_normed, scaled_one, inverse_one, vector[0])
    g_in = jnp.concatenate([g_qkv, g_up], 1)
    g_out = jnp.concatenate([g_proj[None], g_down], 0)
    g_bias = jnp.concatenate([g_bq[None], g_bv[None], g_bup.reshape(4, head_cols)], 0)
    g_vector = jnp.stack([g_gain_one, g_shift_one, g_gain_two, g_shift_two, g_bproj, g_bdown])
    return (d_stream, g_in, g_out, g_bias, g_vector)


def adam_step(master, first, second, gradient, rate, decay):
    first_new = BETA_ONE * first + (1 - BETA_ONE) * gradient
    second_new = BETA_TWO * second + (1 - BETA_TWO) * gradient * gradient
    direction = (
        first_new / (1 - BETA_ONE**STEP) / (jnp.sqrt(second_new / (1 - BETA_TWO**STEP)) + ADAM_EPS)
    )
    return (first_new, second_new, master - rate * (direction + decay * master))


def shards(
    resid,
    cotangent,
    master_in,
    moment1_in,
    moment2_in,
    master_out,
    moment1_out,
    moment2_out,
    master_bias,
    moment1_bias,
    moment2_bias,
    master_vec,
    moment1_vec,
    moment2_vec,
):
    weights_in, weights_out = (
        lax.all_gather(master_in.astype(jnp.bfloat16), "dp", axis=1, tiled=True),
        lax.all_gather(master_out.astype(jnp.bfloat16), "dp", axis=3, tiled=True),
    )
    stream = resid
    gradient = cotangent
    layer_idx = 0
    stream, kept = layer_forward(
        stream,
        weights_in[layer_idx],
        weights_out[layer_idx],
        master_bias[layer_idx],
        master_vec[layer_idx],
    )
    kept_list = [kept]
    list_in = [None] * LAYERS
    list_out = [None] * LAYERS
    list_bias = [None] * LAYERS
    list_vector = [None] * LAYERS
    layer_idx = 0
    gradient, g_in, g_out, g_bias, g_vector = layer_backward(
        gradient,
        weights_in[layer_idx],
        weights_out[layer_idx],
        master_vec[layer_idx],
        kept_list[layer_idx],
    )
    list_in[layer_idx] = g_in
    list_out[layer_idx] = g_out
    list_bias[layer_idx] = g_bias
    list_vector[layer_idx] = g_vector
    summed_in = jnp.stack(list_in)
    summed_out = jnp.stack(list_out)
    summed_in, summed_out = (
        lax.psum_scatter(summed_in, "dp", scatter_dimension=1, tiled=True),
        lax.psum_scatter(summed_out, "dp", scatter_dimension=3, tiled=True),
    )
    summed_bias = lax.psum(jnp.stack(list_bias), "dp")
    summed_vector = lax.psum(jnp.stack(list_vector), ("dp", "tensor"))
    first_in, second_in, new_in = adam_step(
        master_in, moment1_in, moment2_in, summed_in, 0.5 * D ** (-0.5), DECAY
    )
    first_out, second_out, new_out = adam_step(
        master_out, moment1_out, moment2_out, summed_out, 2.0 * D ** (-0.5), DECAY
    )
    first_bias, second_bias, new_bias = adam_step(
        master_bias, moment1_bias, moment2_bias, summed_bias, SMALL_RATE, 0.0
    )
    first_vec, second_vec, new_vec = adam_step(
        master_vec, moment1_vec, moment2_vec, summed_vector, SMALL_RATE, 0.0
    )
    return (
        own_rows(stream),
        own_rows(gradient),
        first_in,
        second_in,
        new_in,
        first_out,
        second_out,
        new_out,
        first_bias,
        second_bias,
        new_bias,
        first_vec,
        second_vec,
        new_vec,
    )


MESH_IDS = pl.DeviceIdType.MESH
F32 = jnp.float32
BF16 = jnp.bfloat16
NN = (((1,), (0,)), ((), ()))
NT = (((1,), (1,)), ((), ()))
TN = (((0,), (0,)), ((), ()))
GELU_A = (2.0 / 3.141592653589793) ** 0.5
GELU_B = 0.044715


def mm(left, right, dims=NN):
    return lax.dot_general(left, right, dims, preferred_element_type=F32)


def rows_at(start, size, align):
    return pl.ds(pl.multiple_of(start, align), size)


def block_kernel(
    sizes,
    resid_h,
    cot_h,
    win_h,
    wout_h,
    bias,
    vec,
    out_o,
    grad_o,
    gsum_o,
    small_o,
    win,
    wout,
    resid,
    cot,
    inv1,
    normed,
    dmlp,
    w,
    q_s,
    k_s,
    v_s,
    e_s,
    linv,
    mixed,
    ps,
    crecv,
    fin,
    ysend,
    yrecv,
    mid,
    xhat2,
    inv2,
    normed_t,
    hidden,
    act_s,
    dpre,
    dattn,
    dmix,
    dk_s,
    dv_s,
    dqkv,
    gproj,
    gmat,
    xr,
    zs,
    zr,
    side_r,
    side_s,
    side_xs,
    side_xr,
    gsum,
    sm,
    smp,
    smx,
    smz,
    smy,
    lsem,
    ssem,
    rsem,
):
    tokens, width, quarter, heads, shard = sizes
    dp = lax.axis_index("dp")
    ten = lax.axis_index("tensor")
    z = lax.div(dp, 2)
    x = lax.rem(dp, 2)
    y = lax.div(ten, 2)
    c = lax.rem(ten, 2)
    x_dev = (dp + 1 - 2 * x, ten)
    c_dev = (dp, ten + 1 - 2 * c)
    y_dev = (dp, ten + 2 - 4 * y)

    def z_other(j):
        if j == 1:
            return z + 1 - 2 * lax.rem(z, 2)
        if j == 2:
            return lax.rem(z + 2, 4)
        return 3 - z

    def z_dev(j):
        return (2 * z_other(j) + x, ten)

    def rcopy(src, dst, send_idx, recv_idx, dev):
        return pltpu.make_async_remote_copy(
            src_ref=src,
            dst_ref=dst,
            send_sem=ssem.at[send_idx],
            recv_sem=rsem.at[recv_idx],
            device_id=dev,
            device_id_type=MESH_IDS,
        )

    barrier = pltpu.get_barrier_semaphore()
    cross_dev = (dp + 1 - 2 * x, ten + 1 - 2 * c)
    peers = [x_dev, c_dev, y_dev, cross_dev, z_dev(1), z_dev(2), z_dev(3)]
    for dev in peers:
        pl.semaphore_signal(barrier, inc=1, device_id=dev, device_id_type=MESH_IDS)
    load_win = pltpu.make_async_copy(win_h, win, lsem.at[2])
    load_wout = pltpu.make_async_copy(wout_h, wout, lsem.at[3])
    load_win.start()
    load_wout.start()
    load_resid = pltpu.make_async_copy(resid_h, resid, lsem.at[0])
    load_cot = pltpu.make_async_copy(cot_h, cot, lsem.at[1])
    load_resid.start()
    load_cot.start()

    mine = rows_at(dp * shard, shard, shard)
    load_win.wait()
    load_wout.wait()
    out_t = [jnp.transpose(wout[i]) for i in range(5)]
    pairs, last = slice(0, 2 * HD), slice(2 * HD, 3 * HD)
    tiles = [win[0, :, pairs], win[1, :, pairs], win[2, :, pairs], win[0, :, last], win[2, :, last]]
    tiles += [out_t[0][:, pairs], win[1, :, last], out_t[0][:, last]]
    w[0, mine, :] = jnp.concatenate(tiles, 1).astype(BF16)

    w[1, mine, :] = jnp.concatenate([win[3 + i] for i in range(4)], 1).astype(BF16)
    w[2, mine, :] = jnp.concatenate(out_t[1:], 1).astype(BF16)
    pl.semaphore_wait(barrier, len(peers))

    half_cols = width // 2
    units = (
        (0, slice(0, half_cols)),
        (0, slice(half_cols, width)),
        (1, slice(0, width)),
        (2, slice(0, width)),
    )

    is_end = 1 - lax.rem(lax.div(z + 1, 2), 2)
    is_mid = 1 - is_end
    upper = lax.div(z, 2)
    owner_z = (z_other(1), 2 - upper, 3 - 3 * upper)
    pair_dev, mid_dev = (2 * owner_z[0] + x, ten), (2 * owner_z[1] + x, ten)

    def ag_copy(u, zi, send, recv, dev):
        b, cols = units[u]
        src = w.at[b, rows_at((2 * zi + x) * shard, shard, shard), cols]
        return rcopy(src, src, send + u, recv, dev)

    def ag_pair(u):
        return ag_copy(u, z, 4, 3 * u, pair_dev)

    def ag_mid(u):
        return ag_copy(u, z, 4, 3 * u + 1, mid_dev)

    def ag_end_far(u, i):
        dev = (2 * owner_z[i] + x, ten)
        return ag_copy(u, z, 4, 3 * u + 2, dev)

    def ag_onward(u, i):
        if i == 0:
            return ag_copy(u, owner_z[0], 4, 3 * u + 2, mid_dev)
        return ag_copy(u, owner_z[i], 4, 3 * u + i, pair_dev)

    def ag_x(u, i):
        return ag_copy(u, z if i == 0 else owner_z[i - 1], 0, 12 + u, x_dev)

    def ag_bytes(u, pieces, send, recv):
        b, cols = units[u]
        ref = w.at[b, 0 : pieces * shard, cols]
        return rcopy(ref, ref, send, recv, x_dev)

    def mid_start(u):
        @pl.when(is_mid == 1)
        def _():
            ag_pair(u).start()
            ag_mid(u).start()

    def ag_arrive(u, i):
        ag_copy(u, owner_z[i], 0, 3 * u + i, x_dev).wait_recv()

    def pump_end(u, i):
        @pl.when(is_end == 1)
        def _():
            ag_arrive(u, i)
            ag_x(u, 1 + i).start()

    def pump_mid(u, i):
        @pl.when(is_mid == 1)
        def _():
            ag_arrive(u, i)
            if u > 1 or i == 1:
                ag_onward(u, i).start()
            ag_x(u, 1 + i).start()

    def mid_onward(u, i):
        @pl.when(is_mid == 1)
        def _():
            ag_arrive(u, i)
            ag_onward(u, i).start()

    def mid_x(u, i):
        @pl.when(is_mid == 1)
        def _():
            ag_x(u, i).start()

    def ag_finish(u):
        ag_bytes(u, 4, u, 12 + u).wait_recv()

    def ag_drain(u):
        ag_bytes(u, 4, u, 12 + u).wait_send()

        if u < 2:
            ag_bytes(u, 3, 4 + u, 12 + u).wait_send()
            return

        @pl.when(is_end == 1)
        def _():
            ag_bytes(u, 1, 4 + u, 12 + u).wait_send()

        @pl.when(is_mid == 1)
        def _():
            ag_bytes(u, 5, 4 + u, 12 + u).wait_send()

    ag_x(0, 0).start()
    ag_x(1, 0).start()
    mid_start(0)
    mid_start(1)

    @pl.when(is_end == 1)
    def _():
        for u in range(2):
            ag_pair(u).start()
            ag_end_far(u, 2).start()
            ag_end_far(u, 1).start()

    load_resid.wait()
    load_cot.wait()
    gain_one, shift_one = vec[0], vec[1]

    own = rows_at(ten * quarter, quarter, quarter)
    mid[...] = resid[own, :]
    xhat = resid

    def first_norm(r, carry):
        rows = rows_at(r * 128, 128, 128)
        part = resid[rows, :]
        center = part - jnp.mean(part, -1, keepdims=True)
        inverse = lax.rsqrt(jnp.mean(center * center, -1, keepdims=True) + EPS)
        scaled = center * inverse
        xhat[rows, :] = scaled
        inv1[rows, :] = inverse
        normed[rows, :] = (scaled * gain_one + shift_one).astype(BF16)
        dmlp[rows, :] = (cot[rows, :] * BRANCH_SCALE).astype(BF16)
        return carry

    lax.fori_loop(0, tokens // 128, first_norm, 0)
    for u, i in ((0, 0), (0, 1), (1, 0), (1, 1)):
        pump_mid(u, i)
    mid_start(2)
    pump_mid(0, 2)
    pump_mid(1, 2)
    pump_end(0, 0)
    pump_end(1, 0)

    @pl.when(is_end == 1)
    def _():
        ag_pair(2).start()

    for u, i in ((0, 2), (0, 1), (1, 2), (1, 1)):
        pump_end(u, i)

    @pl.when(is_end == 1)
    def _():
        ag_pair(3).start()

    ag_x(2, 0).start()

    sm[...] = jnp.zeros_like(sm)
    sm[5:6, :] = jnp.sum(dmlp[own, :].astype(F32), 0, keepdims=True)
    mixed[...] = jnp.zeros_like(mixed)
    dqkv[...] = jnp.zeros_like(dqkv)
    dk_s[...] = jnp.zeros_like(dk_s)
    dv_s[...] = jnp.zeros_like(dv_s)

    hc = heads * HD
    low_half = lax.broadcasted_iota(jnp.int32, (1, 2 * HD), 1) < HD
    bias_v01, bias_q01 = bias[1, :, pairs], bias[0, :, pairs]
    bias_q2v2 = jnp.concatenate([bias[0, :, last], bias[1, :, last]], 1)
    eighth = HD**-0.5

    def project_pair(r):
        rows = slice(r * 256, (r + 1) * 256)
        got = mm(normed[rows, :], w[0, :, 0:384])
        queries = (got[:, 0:128] + bias_q01).astype(BF16).astype(F32) * eighth
        q_s[0, rows, :] = jnp.where(low_half, queries, 0.0).astype(BF16)
        q_s[1, rows, :] = jnp.where(low_half, 0.0, queries).astype(BF16)
        k_s[0, rows, :] = got[:, 128:256].astype(BF16)
        v_s[0, rows, :] = (got[:, 256:384] + bias_v01).astype(BF16)

    def project_last(r):
        rows = slice(r * 256, (r + 1) * 256)
        got = mm(normed[rows, :], w[0, :, 384:768])
        both = (got[:, 0:128] + bias_q2v2).astype(BF16)
        q_s[2, rows, :] = jnp.where(low_half, both.astype(F32) * eighth, 0.0).astype(BF16)
        v_s[1, rows, :] = both
        k_s[1, rows, :] = got[:, 256:384].astype(BF16)

    ag_finish(0)
    for r in range(tokens // 256):
        project_pair(r)
    pump_end(2, 0)
    pump_mid(2, 0)
    pump_mid(2, 1)
    ag_x(3, 0).start()
    mid_start(3)

    def attend(i, which_heads):
        first, last_row = i * quarter, (i + 1) * quarter
        rows = slice(first, last_row)
        causal = lax.broadcasted_iota(jnp.int32, (quarter, quarter), 0) >= lax.broadcasted_iota(
            jnp.int32, (quarter, quarter), 1
        )
        got = {}
        for h in which_heads:
            at = h // 2
            queries = q_s[h, rows, :]
            diag = jnp.where(causal, mm(queries, k_s[at, rows, :], NT), MASKED)
            highest = jnp.max(diag, -1, keepdims=True)
            if i > 0:
                wide = mm(queries, k_s[at, 0:first, :], NT)
                highest = jnp.maximum(highest, jnp.max(wide, -1, keepdims=True))
            e_diag = jnp.exp(diag - highest)
            summed = jnp.sum(e_diag, -1, keepdims=True)
            e_diag = e_diag.astype(BF16)
            e_s[h, rows, first:last_row] = e_diag
            total = mm(e_diag, v_s[at, rows, :])
            if i > 0:
                e_wide = jnp.exp(wide - highest)
                summed = summed + jnp.sum(e_wide, -1, keepdims=True)
                e_wide = e_wide.astype(BF16)
                e_s[h, rows, 0:first] = e_wide
                total = total + mm(e_wide, v_s[at, 0:first, :])
            inverse = 1.0 / summed
            linv[h, rows, :] = inverse
            got[h] = total * inverse
        if 0 in got:
            mixed[rows, 0:128] = jnp.where(low_half, got[0], got[1]).astype(BF16)
        if 2 in got:
            mixed[rows, 128:256] = jnp.where(low_half, 0.0, got[2]).astype(BF16)

    def rs_core(k, half):
        return rcopy(ps.at[k % 2, half], crecv.at[k, half], 16 + 2 * (k % 2) + half, 16 + 2 * k + half, c_dev)

    halves = [slice(0, quarter // 2), slice(quarter // 2, quarter)]

    def rs_y(k, hh):
        src, dst = ysend.at[k, halves[hh], :], yrecv.at[k, halves[hh], :]
        return rcopy(src, dst, 20, 24 + 2 * k + hh, y_dev)

    def rs_y_start(k):
        for hh in range(2):
            rs_y(k, hh).start()

    def rs_pair(k, near, compute):
        half = 1 if near else 0
        def step(s, carry):
            yq = y if near else 1 - y
            part = compute(2 * yq + lax.rem(1 - s + c, 2))

            @pl.when(s == 0)
            def _():
                ps[k % 2, half] = part.astype(BF16)
                rs_core(k, half).start()

            @pl.when(s == 1)
            def _():
                rs_core(k, half).wait_recv()
                total = part + crecv[k, half].astype(F32)
                if near:
                    fin[k % 3] = total
                else:
                    ysend[k] = total.astype(BF16)
                    rs_y_start(k)

            return carry

        lax.fori_loop(0, 2, step, 0)

    def rs_quad(k, compute, held):
        for half in range(2):
            rs_core(k - 2, half).wait_send()

        def step(s, carry):
            half, odd = lax.div(s, 2), lax.rem(s, 2)
            yq = half * y + (1 - half) * (1 - y)
            part = compute(2 * yq + lax.rem(1 - odd + c, 2))

            @pl.when(odd == 0)
            def _():
                ps[k % 2, half] = part.astype(BF16)
                rs_core(k, half).start()

            @pl.when(s == 1)
            def _():
                held[...] = part

            @pl.when(s == 3)
            def _():
                fin[k % 3] = part

            return carry

        lax.fori_loop(0, 4, step, 0)

    def quad_far(k, held):
        rs_core(k, 0).wait_recv()
        ysend[k] = (held[...] + crecv[k, 0].astype(F32)).astype(BF16)

    def quad_near(k):
        rs_core(k, 1).wait_recv()
        fin[k % 3] = fin[k % 3] + crecv[k, 1].astype(F32)

    def rs_result(k, hh):
        rs_y(k, hh).wait_recv()
        return fin[k % 3, halves[hh], :] + yrecv[k, halves[hh], :].astype(F32)

    def attend_quarter(which, which_heads):
        for i in range(tokens // quarter):

            @pl.when(which == i)
            def _():
                attend(i, which_heads)

    def proj(which):
        return mm(mixed[rows_at(which * quarter, quarter, quarter), :], w[0, :, 512:768], NT)

    def far_early(s, carry):
        attend_quarter(2 * (1 - y) + lax.rem(s + c, 2), (0, 1))
        return carry

    def far_proj(which):
        attend_quarter(which, (2,))
        return proj(which)

    def near_proj(which):
        attend_quarter(which, (0, 1, 2))
        return proj(which)

    lax.fori_loop(0, 2, far_early, 0)
    mid_onward(3, 0)
    ag_finish(1)
    for r in range(tokens // 256):
        project_last(r)
    rs_pair(0, False, far_proj)
    pump_end(2, 1)
    pump_mid(2, 2)
    mid_x(3, 1)
    rs_pair(0, True, near_proj)
    pump_end(2, 2)
    pump_end(3, 0)
    pump_mid(3, 1)

    def q_rows(ref, which, hh):
        return ref.at[rows_at(which * quarter + hh * (quarter // 2), quarter // 2, quarter // 2), :]

    def qg_y(g, ref, hh):
        src = q_rows(ref, ten, hh)
        return rcopy(src, src, 21, 32 + 2 * g + hh, y_dev)

    def qg_c(g, ref, hh):
        src = q_rows(ref, ten, hh)
        return rcopy(src, src, 22, 36 + g, c_dev)

    def qg_f(g, ref, hh):
        src = q_rows(ref, ten + 2 - 4 * y, hh)
        return rcopy(src, src, 23, 38 + 2 * g + hh, c_dev)

    def qg_start(g, ref, hh):
        qg_y(g, ref, hh).start()
        qg_c(g, ref, hh).start()

    def qg_rows(ref, count, send, recv):
        rows = ref.at[0:count, :]
        return rcopy(rows, rows, send, recv, c_dev)

    def qg_near(g, ref):
        qg_rows(ref, quarter, 22, 36 + g).wait_recv()

    def qg_far(g, ref, hh):
        qg_y(g, ref, hh).wait_recv()
        qg_f(g, ref, hh).start()

    def qg_last(g, ref, hh):
        qg_f(g, ref, hh).wait_recv()

    def far_rows(g, ref, compute, between=None):
        def step(hh, carry):
            if between is not None:

                @pl.when(hh == 1)
                def _():
                    between()

            qg_far(g, ref, hh)
            compute(2 * (1 - y) + c, hh)
            qg_last(g, ref, hh)
            compute(2 * (1 - y) + 1 - c, hh)
            return carry

        lax.fori_loop(0, 2, step, 0)

    for hh in range(2):
        if hh == 1:
            pump_end(3, 1)
            pump_mid(3, 2)
        half = halves[hh]
        middle = mid[half, :] + BRANCH_SCALE * (rs_result(0, hh) + vec[4])
        mid[half, :] = middle
        center = middle - jnp.mean(middle, -1, keepdims=True)
        inverse = lax.rsqrt(jnp.mean(center * center, -1, keepdims=True) + EPS)
        scaled = center * inverse
        xhat2[half, :] = scaled
        inv2[half, :] = inverse
        mine_h = rows_at(ten * quarter + hh * (quarter // 2), quarter // 2, quarter // 2)
        hidden[mine_h, :] = (scaled * vec[2] + vec[3]).astype(BF16)
        qg_start(0, hidden, hh)

    pump_end(3, 2)
    ag_finish(2)

    bias_up = jnp.concatenate([bias[2 + i] for i in range(4)], 1)

    def forward_units(which, hh=None):
        rows = rows_at(which * quarter, quarter, quarter)
        if hh is not None:
            rows = rows_at(which * quarter + hh * (quarter // 2), quarter // 2, quarter // 2)
        hq = hidden[rows, :]
        for t in range(width // 256):
            cols = slice(t * 256, (t + 1) * 256)
            pre = mm(hq, w[1, :, cols]) + bias_up[:, cols]
            square = pre * pre
            tanh = jnp.tanh(GELU_A * (pre + GELU_B * (square * pre)))
            half_up = 0.5 + 0.5 * tanh
            act_s[rows, cols] = (pre * half_up).astype(BF16)
            slope = half_up + 0.5 * pre * (1.0 - tanh * tanh) * (
                GELU_A + (3.0 * GELU_A * GELU_B) * square
            )
            dpre[rows, cols] = slope.astype(BF16)

    def grad_block(b, left, right, near):
        rows = slice(0, tokens)
        if near is not None:
            rows = rows_at((y if near else 1 - y) * 2 * quarter, 2 * quarter, 2 * quarter)

        def tile(t, carry):
            cols = rows_at(t * 256, 256, 256)
            part = mm(left[rows, cols], right[rows, :], TN)
            if near is False:
                part = part + gmat[b, cols, :].astype(F32)
            gmat[b, cols, :] = part.astype(BF16)
            return carry

        lax.fori_loop(0, width // 256, tile, 0)

    g_units = (*units[0:3], (2, slice(0, half_cols)))
    right_half = slice(half_cols, width)

    def gx(u, zi):
        b, cols = g_units[u]
        src = gmat.at[b, rows_at((2 * zi + 1 - x) * shard, shard, shard), cols]
        return rcopy(src, xr.at[b, zi, :, cols], 8 + u, 42 + 4 * u + zi, x_dev)

    def line_to(i):
        if i == 0:
            return pair_dev, 0
        return (2 * (is_end * owner_z[0] + is_mid * owner_z[i]) + x, ten), is_end * i + is_mid * 3

    def gz(u, i):
        b, cols = g_units[u]
        dev, slot = line_to(i)
        return rcopy(zs.at[b, i, :, cols], zr.at[b, slot, :, cols], 12 + u, 58 + 4 * u + slot, dev)

    def gz_arrive(u, slot):
        b, cols = g_units[u]
        ref = zr.at[b, slot, :, cols]
        rcopy(ref, ref, 12 + u, 58 + 4 * u + slot, x_dev).wait_recv()

    def g_start(u):
        @pl.when(is_end == 1)
        def _():
            for i in (2, 1, 0):
                gx(u, owner_z[i]).start()

        @pl.when(is_mid == 1)
        def _():
            for i in (0, 2, 1):
                gx(u, owner_z[i]).start()

        gx(u, z).start()

    def x_sum(u, zo):
        b, cols = g_units[u]
        gx(u, zo).wait_recv()
        mine_x = gmat[b, rows_at((2 * zo + x) * shard, shard, shard), cols].astype(F32)
        return mine_x + xr[b, zo, :, cols].astype(F32)

    def end_pump(u, i):
        b, cols = g_units[u]

        @pl.when(is_end == 1)
        def _():
            zs[b, i, :, cols] = x_sum(u, owner_z[i]).astype(BF16)
            gz(u, i).start()

    def mid_pump(u, i):
        b, cols = g_units[u]

        @pl.when(is_mid == 1)
        def _():
            total = x_sum(u, owner_z[i])
            if i > 0:
                gz_arrive(u, i)
                total = total + zr[b, i, :, cols].astype(F32)
            zs[b, i, :, cols] = total.astype(BF16)
            gz(u, i).start()

    def g_finish(u):
        b, cols = g_units[u]
        total = x_sum(u, z)
        for slot in (0, 3):
            gz_arrive(u, slot)
            total = total + zr[b, slot, :, cols].astype(F32)
        gsum[b, :, cols] = total
        if u < 3:
            g_out(u).start()

    def g_out(u):
        b, cols = units[u]
        return pltpu.make_async_copy(gsum.at[b, :, cols], gsum_o.at[b, :, cols], lsem.at[4 + u])

    def g_drain(u):
        b, cols = g_units[u]
        rcopy(xr.at[b, :, :, cols], xr.at[b, :, :, cols], 8 + u, 56, x_dev).wait_send()
        rcopy(zs.at[b, :, :, cols], zs.at[b, :, :, cols], 12 + u, 56, x_dev).wait_send()
        g_out(u).wait()

    def side_rows(zo):
        return gmat.at[2, rows_at(zo * 2 * shard, 2 * shard, 2 * shard), right_half]

    def side_copy(src, i):
        dev, slot = line_to(i)
        return rcopy(src, side_r.at[slot], 28, 78 + slot, dev)

    def side_arrive(slot):
        rcopy(side_r.at[slot], side_r.at[slot], 28, 78 + slot, x_dev).wait_recv()

    def side_start():
        @pl.when(is_end == 1)
        def _():
            for i in (2, 1):
                side_copy(side_rows(owner_z[i]), i).start()

        side_copy(side_rows(owner_z[0]), 0).start()

    def side_middle():
        @pl.when(is_mid == 1)
        def _():
            for i in (2, 1):
                side_arrive(i)
                mine_z = gmat[2, rows_at(owner_z[i] * 2 * shard, 2 * shard, 2 * shard), right_half]
                side_s[i - 1] = (mine_z.astype(F32) + side_r[i].astype(F32)).astype(BF16)
                side_copy(side_s.at[i - 1], i).start()

    def side_x():
        return rcopy(side_xs, side_xr, 29, 82, x_dev)

    def side_cross():
        side_arrive(0)
        side_arrive(3)

        def total(xi):
            at = rows_at(xi * shard, shard, shard)
            got = gmat[2, rows_at((2 * z + xi) * shard, shard, shard), right_half].astype(F32)
            return got + side_r[0, at, :].astype(F32) + side_r[3, at, :].astype(F32)

        side_xs[...] = total(1 - x).astype(BF16)
        side_x().start()
        gsum[2, :, right_half] = total(x)

    def side_finish():
        side_x().wait_recv()
        gsum[2, :, right_half] = gsum[2, :, right_half] + side_xr[...].astype(F32)
        g_out(3).start()

    def backward_units(which):
        rows = rows_at(which * quarter, quarter, quarter)
        gq = dmlp[rows, :]
        for t in range(width // 256):
            cols = slice(t * 256, (t + 1) * 256)
            d_act = mm(gq, w[2, :, cols]).astype(BF16).astype(F32)
            d_low = (dpre[rows, cols].astype(F32) * d_act).astype(BF16)
            dpre[rows, cols] = d_low
            sm[6:7, cols] = sm[6:7, cols] + jnp.sum(d_low.astype(F32), 0, keepdims=True)
        return mm(dpre[rows, :], w[1], NT)

    def branch(which):
        rows = rows_at(which * quarter, quarter, quarter)
        return mm(act_s[rows, :], w[2], NT)

    def near_units(s, carry):
        @pl.when(s == 1)
        def _():
            qg_near(0, hidden)

        forward_units(2 * y + lax.rem(s + c, 2))
        return carry

    lax.fori_loop(0, 2, near_units, 0)
    grad_block(2, dmlp, act_s, True)
    for t in range(width // 256):
        cols = slice(t * 256, (t + 1) * 256)
        normed_t[cols, :] = jnp.transpose(normed[:, cols])
    far_rows(0, hidden, forward_units)
    ag_finish(3)
    rs_pair(1, False, backward_units)
    grad_block(2, dmlp, act_s, False)
    g_start(3)
    side_start()
    rs_pair(1, True, backward_units)
    grad_block(1, hidden, dpre, None)
    g_start(2)
    end_pump(3, 2)
    mid_pump(3, 0)
    def second_norm_back(hh):
        half = halves[hh]
        mine_h = rows_at(ten * quarter + hh * (quarter // 2), quarter // 2, quarter // 2)
        d_hidden = rs_result(1, hh)
        scaled = xhat2[half, :]
        sm[2:3, :] = sm[2:3, :] + jnp.sum(d_hidden * scaled, 0, keepdims=True)
        sm[3:4, :] = sm[3:4, :] + jnp.sum(d_hidden, 0, keepdims=True)
        weighted = d_hidden * vec[2]
        d_mid = cot[mine_h, :] + inv2[half, :] * (
            weighted
            - jnp.mean(weighted, -1, keepdims=True)
            - scaled * jnp.mean(weighted * scaled, -1, keepdims=True)
        )
        fin[1, half, :] = d_mid
        d_attn = (BRANCH_SCALE * d_mid).astype(BF16)
        dattn[mine_h, :] = d_attn
        sm[4:5, :] = sm[4:5, :] + jnp.sum(d_attn.astype(F32), 0, keepdims=True)
        qg_start(1, dattn, hh)

    rs_quad(2, branch, fin.at[0])
    second_norm_back(0)
    end_pump(3, 1)
    quad_far(2, fin.at[0])
    quad_near(2)
    side_middle()
    end_pump(3, 0)
    second_norm_back(1)
    rs_y_start(2)

    def attend_back(i, which_heads, hh=None):
        first, last_row = i * quarter, (i + 1) * quarter
        rows = slice(first, last_row)
        if hh is not None:
            rows = rows_at(first + hh * (quarter // 2), quarter // 2, quarter // 2)
        got, kept = {}, {}
        for h in which_heads:
            at = h // 2
            tile = slice(at * 128, (at + 1) * 128)
            d_out = dmix[rows, tile].astype(F32) * linv[h, rows, :]
            d_out = jnp.where(low_half, d_out, 0.0) if h == 0 else jnp.where(low_half, 0.0, d_out)
            inner = jnp.sum(d_out * mixed[rows, tile].astype(F32), -1, keepdims=True)
            d_scaled = d_out.astype(BF16)
            expo = e_s[h, rows, 0:last_row]
            d_probs = mm(d_scaled, v_s[at, 0:last_row, :], NT)
            d_scores = (expo.astype(F32) * (d_probs - inner)).astype(BF16)
            got[h] = mm(d_scores, k_s[at, 0:last_row, :]) * eighth
            kept[h] = (d_scores, d_scaled, expo)
        for at, group in enumerate(((0, 1), (2,))):
            if group[0] not in got:
                continue
            queries = jnp.concatenate([q_s[h, rows, :] for h in group], 0)
            d_s, d_o, exps = [jnp.concatenate([kept[h][i] for h in group], 0) for i in range(3)]
            dk_s[at, :, 0:last_row] = dk_s[at, :, 0:last_row] + mm(queries, d_s, TN)
            dv_s[at, :, 0:last_row] = dv_s[at, :, 0:last_row] + mm(d_o, exps, TN)
        if 0 in got:
            dqkv[rows, 0:128] = jnp.where(low_half, got[0], got[1]).astype(BF16)
        if 2 in got:
            dqkv[rows, 384:512] = jnp.where(low_half, got[2], 0.0).astype(BF16)

    def back_quarters(near, which_heads, fresh, prepare=None):
        def step(s, carry):
            if prepare is not None:
                prepare(s)
            yq = y if near else 1 - y
            which = 2 * yq + lax.rem(s + c, 2)
            if fresh:
                rows = rows_at(which * quarter, quarter, quarter)
                dmix[rows, :] = mm(dattn[rows, :], w[0, :, 512:768]).astype(BF16)
            for i in range(tokens // quarter):

                @pl.when(which == i)
                def _():
                    attend_back(i, which_heads)

            return carry

        lax.fori_loop(0, 2, step, 0)

    def back_far(which, hh):
        rows = rows_at(which * quarter + hh * (quarter // 2), quarter // 2, quarter // 2)
        dmix[rows, :] = mm(dattn[rows, :], w[0, :, 512:768]).astype(BF16)
        for i in range(tokens // quarter):

            @pl.when(which == i)
            def _():
                attend_back(i, (0, 1), hh)

    def near_ready(s):
        @pl.when(s == 1)
        def _():
            qg_near(1, dattn)

    def keys_values(at):
        if at == 0:
            dqkv[:, 128:256] = jnp.transpose(dk_s[0]).astype(BF16)
            dqkv[:, 256:384] = jnp.transpose(dv_s[0]).astype(BF16)
        else:
            d_v = jnp.transpose(dv_s[1]).astype(BF16)
            dqkv[:, 384:512] = jnp.where(low_half, dqkv[:, 384:512], d_v)
            dqkv[:, 640:768] = jnp.transpose(dk_s[1]).astype(BF16)

    def zero_rows(u, zo):
        cols = rows_at(zo * 2 * shard, 2 * shard, 2 * shard)
        left = normed_t[cols, :]
        if u == 0:
            gmat[0, cols, 0:384] = mm(left, dqkv[:, 0:384]).astype(BF16)
        else:
            g_qkv = mm(left, dqkv[:, 384:768])
            gmat[0, cols, 384:512] = g_qkv[:, 0:128].astype(BF16)
            gmat[0, cols, 512:768] = (g_qkv[:, 128:384] + gproj[cols, :]).astype(BF16)
        gx(u, zo).start()

    def zero_unit(u, steps):
        def step(s, carry):
            odd, half = lax.rem(s, 2), lax.div(s, 2)
            first = is_end * owner_z[2] + is_mid * owner_z[0]
            second = is_end * owner_z[1] + is_mid * owner_z[2]
            third = is_end * owner_z[0] + is_mid * owner_z[1]
            early = (1 - odd) * first + odd * second
            late = (1 - odd) * third + odd * z
            zero_rows(u, (1 - half) * early + half * late)
            return carry

        lax.fori_loop(*steps, step, 0)

    back_quarters(True, (0, 1, 2), True, near_ready)
    mid_pump(3, 2)
    mid_pump(2, 0)
    end_pump(2, 2)
    end_pump(2, 1)
    mid_pump(3, 1)
    far_rows(1, dattn, back_far, side_cross)
    keys_values(0)
    zero_unit(0, (0, 4))
    end_pump(2, 0)
    mid_pump(2, 2)
    gproj[...] = jnp.transpose(mm(mixed[...], dattn[...], TN))
    back_quarters(False, (2,), False)
    keys_values(1)
    mid_pump(2, 1)

    def first_back(which):
        rows = rows_at(which * quarter, quarter, quarter)
        d_low = dqkv[rows, :]
        part = mm(d_low, w[0], NT)
        rounded = part.astype(BF16).astype(F32)
        sm[0:1, :] = sm[0:1, :] + jnp.sum(rounded * xhat[rows, :], 0, keepdims=True)
        sm[1:2, :] = sm[1:2, :] + jnp.sum(rounded, 0, keepdims=True)
        sm[7:8, :] = sm[7:8, :] + jnp.sum(d_low.astype(F32), 0, keepdims=True)
        return part

    end_pump(0, 2)
    mid_pump(0, 0)
    rs_quad(3, first_back, xhat2)
    end_pump(0, 1)

    small_c = rcopy(sm, smp, 27, 77, c_dev)
    small_c.start()
    quad_far(3, xhat2)
    rs_y_start(3)
    small_c.wait_recv()
    smx[0, 0:6, :] = sm[0:6, :] + smp[0:6, :]
    smx[0, 6:8, :] = smp[6:8, :]
    small_x = rcopy(smx.at[0], smx.at[1], 24, 74, cross_dev)
    small_x.start()
    end_pump(0, 0)
    zero_unit(1, (0, 4))
    quad_near(3)
    mid_pump(0, 2)
    small_x.wait_recv()
    smz[z, 0:6, :] = smx[0, 0:6, :] + smx[1, 0:6, :]
    smz[z, 6:8, :] = sm[6:8, :] + smx[1, 6:8, :]

    def small_z(j):
        return rcopy(smz.at[z], smz.at[z], 25, 75, z_dev(j))

    for j in (3, 2, 1):
        small_z(j).start()
    mid_pump(0, 1)
    g_finish(3)
    side_finish()
    g_finish(2)
    for hh in range(2):
        half = halves[hh]
        mid[half, :] = mid[half, :] + BRANCH_SCALE * (rs_result(2, hh) + vec[5])
    put_out = pltpu.make_async_copy(mid, out_o, lsem.at[8])
    put_out.start()
    end_pump(1, 2)
    mid_pump(1, 0)
    end_pump(1, 1)

    def first_norm_back(hh):
        half = halves[hh]
        mine_h = rows_at(ten * quarter + hh * (quarter // 2), quarter // 2, quarter // 2)
        d_normed = rs_result(3, hh)
        scaled = xhat[mine_h, :]
        weighted = d_normed * gain_one
        xhat2[half, :] = fin[1, half, :] + inv1[mine_h, :] * (
            weighted
            - jnp.mean(weighted, -1, keepdims=True)
            - scaled * jnp.mean(weighted * scaled, -1, keepdims=True)
        )

    first_norm_back(0)
    end_pump(1, 0)
    three = rcopy(smz.at[0:3], smz.at[0:3], 25, 75, x_dev)
    three.wait_recv()
    smy[0] = (smz[0] + smz[1]) + (smz[2] + smz[3])
    small_y = rcopy(smy.at[0], smy.at[1], 26, 76, y_dev)
    small_y.start()
    mid_pump(1, 2)
    first_norm_back(1)
    put_grad = pltpu.make_async_copy(xhat2, grad_o, lsem.at[9])
    put_grad.start()
    mid_pump(1, 1)
    for u in range(4):
        ag_drain(u)
    three_sides = side_r.at[0:3]
    rcopy(three_sides, three_sides, 28, 78, x_dev).wait_send()
    side_x().wait_send()
    rcopy(ysend, yrecv, 20, 24, y_dev).wait_send()
    for k in (2, 3):
        for half in range(2):
            rs_core(k, half).wait_send()
    for send in (21, 22, 23):
        qg_rows(hidden, 2 * quarter, send, 36).wait_send()
    small_x.wait_send()
    three.wait_send()
    g_finish(0)
    for u in (3, 2, 0):
        g_drain(u)
    small_y.wait_recv()
    small_c.wait_send()
    sm[0:6, :] = smy[0, 0:6, :] + smy[1, 0:6, :]
    sm[6:8, :] = smy[0, 6:8, :]
    put_small = pltpu.make_async_copy(sm, small_o, lsem.at[10])
    put_small.start()
    g_finish(1)

    g_drain(1)
    small_y.wait_send()
    for made in (put_out, put_grad, put_small):
        made.wait()


def run_block(resid, cotangent, win, wout, bias, vec, rows, n_dp):
    tokens, width = resid.shape
    quarter = tokens // 4
    head_cols = win.shape[2]
    heads = head_cols // HD
    sizes = (tokens, width, quarter, heads, rows)
    vm = pltpu.VMEM
    scratch = [
        vm(win.shape, F32),
        vm(wout.shape, F32),
        vm((tokens, width), F32),
        vm((tokens, width), F32),
        vm((tokens, 1), F32),
        vm((tokens, width), BF16),
        vm((tokens, width), BF16),
        vm((3, width, width), BF16),
        vm((heads, tokens, 2 * HD), BF16),
        vm((2, tokens, 2 * HD), BF16),
        vm((2, tokens, 2 * HD), BF16),
        vm((heads, tokens, tokens), BF16),
        vm((heads, tokens, 1), F32),
        vm((tokens, 256), BF16),
        vm((2, 2, quarter, width), BF16),
        vm((4, 2, quarter, width), BF16),
        vm((3, quarter, width), F32),
        vm((4, quarter, width), BF16),
        vm((4, quarter, width), BF16),
        vm((quarter, width), F32),
        vm((quarter, width), F32),
        vm((quarter, 1), F32),
        vm((width, tokens), BF16),
        vm((tokens, width), BF16),
        vm((tokens, width), BF16),
        vm((tokens, width), BF16),
        vm((tokens, width), BF16),
        vm((tokens, 256), BF16),
        vm((2, 2 * HD, tokens), F32),
        vm((2, 2 * HD, tokens), F32),
        vm((tokens, width), BF16),
        vm((width, 256), F32),
        vm((3, width, width), BF16),
        vm((3, 4, rows, width), BF16),
        vm((3, 3, rows, width), BF16),
        vm((3, 4, rows, width), BF16),
        vm((4, 2 * rows, width // 2), BF16),
        vm((2, 2 * rows, width // 2), BF16),
        vm((rows, width // 2), BF16),
        vm((rows, width // 2), BF16),
        vm((3, rows, width), F32),
        vm((8, width), F32),
        vm((8, width), F32),
        vm((2, 8, width), F32),
        vm((4, 8, width), F32),
        vm((2, 8, width), F32),
        pltpu.SemaphoreType.DMA((11,)),
        pltpu.SemaphoreType.DMA((30,)),
        pltpu.SemaphoreType.DMA((83,)),
    ]
    whole = pl.BlockSpec(memory_space=pltpu.VMEM)
    return pl.pallas_call(
        functools.partial(block_kernel, sizes),
        out_shape=(
            jax.ShapeDtypeStruct((quarter, width), F32),
            jax.ShapeDtypeStruct((quarter, width), F32),
            jax.ShapeDtypeStruct((3, rows, width), F32),
            jax.ShapeDtypeStruct((8, width), F32),
        ),
        in_specs=[pl.BlockSpec(memory_space=pl.ANY)] * 4 + [whole] * 2,
        out_specs=[pl.BlockSpec(memory_space=pl.ANY)] * 4,
        scratch_shapes=scratch,
        compiler_params=pltpu.CompilerParams(
            collective_id=1, has_side_effects=True, vmem_limit_bytes=62 << 20
        ),
        name="block",
    )(resid, cotangent, win, wout, bias, vec)


BLOCK_ZERO = (((0, 128), (384, 448)), ((128, 256), (640, 704)), ((256, 384), (448, 512)), ((512, 640), (704, 768)))


def adam_kernel(hc, *refs):
    passed_h, gsum_h, small_h = refs[0:2], refs[2], refs[3]
    in_h, out_h, bias_h, vec_h = refs[4:7], refs[7:10], refs[10:13], refs[13:16]
    passed_o, in_o, out_o, bias_o, vec_o = refs[16:18], refs[18:21], refs[21:24], refs[24:27], refs[27:30]
    vin, vout, vbias, vvec, rin, rout, rbias, rvec, gsum, small, passed, sems = refs[30:42]

    def copy(src, dst, sem):
        pltpu.make_async_copy(src, dst, sems.at[sem]).start()

    def wait(ref, sem):
        pltpu.make_async_copy(ref, ref, sems.at[sem]).wait()

    def columns(ref, rows, kind):
        return jnp.concatenate([ref[rows + (slice(a, b),)] for a, b in BLOCK_ZERO[kind]], 1)

    every = slice(None)
    kinds_in = (3, 4, 5, 6, 0, 1, 2)
    copy(gsum_h.at[1], gsum.at[1], 0)
    for i in kinds_in:
        if i == 5:
            for a in range(2):
                copy(passed_h[a], passed.at[a], 18)
        for a in range(3):
            copy(in_h[a].at[i], vin.at[i, a], 3 + i)
        if i == 6:
            copy(gsum_h.at[0], gsum.at[0], 1)
    copy(small_h, small, 15)
    for a in range(3):
        copy(bias_h[a], vbias.at[a], 16)
        copy(vec_h[a], vvec.at[a], 17)
    copy(gsum_h.at[2], gsum.at[2], 2)
    for i in range(5):
        for a in range(3):
            copy(out_h[a].at[i], vout.at[i, a], 10 + i)

    wait(gsum.at[1], 0)
    for i in kinds_in:
        wait(vin.at[i], 3 + i)
        if i == 0:
            wait(gsum.at[0], 1)
        part = columns(gsum, (0, every), i) if i < 3 else gsum[1, :, (i - 3) * hc : (i - 2) * hc]
        new = adam_step(vin[i, 0], vin[i, 1], vin[i, 2], part, 0.5 * D ** (-0.5), DECAY)
        for a in range(3):
            rin[i, a] = new[a]
            copy(rin.at[i, a], in_o[a].at[i], 19)
    wait(passed, 18)
    for a in range(2):
        copy(passed.at[a], passed_o[a], 23)
    wait(small, 15)
    wait(vbias, 16)
    wait(vvec, 17)
    for i in range(6):
        new = adam_step(vvec[0, i], vvec[1, i], vvec[2, i], small[i : i + 1, :], SMALL_RATE, 0.0)
        for a in range(3):
            rvec[a, i] = new[a]
        if i < 2:
            part = columns(small, (slice(7, 8),), 2 * i)
        else:
            part = small[6:7, (i - 2) * hc : (i - 1) * hc]
        new = adam_step(vbias[0, i], vbias[1, i], vbias[2, i], part, SMALL_RATE, 0.0)
        for a in range(3):
            rbias[a, i] = new[a]
    for a in range(3):
        copy(rbias.at[a], bias_o[a], 20)
        copy(rvec.at[a], vec_o[a], 21)
    wait(gsum.at[2], 2)
    for i in range(5):
        wait(vout.at[i], 10 + i)
        part = columns(gsum, (0, every), 3) if i == 0 else gsum[2, :, (i - 1) * hc : i * hc]
        part = jnp.transpose(part)
        new = adam_step(vout[i, 0], vout[i, 1], vout[i, 2], part, 2.0 * D ** (-0.5), DECAY)
        for a in range(3):
            rout[i, a] = new[a]
            copy(rout.at[i, a], out_o[a].at[i], 22)
    for ref, sem in ((rin, 19), (rbias, 20), (rvec, 21), (rout, 22), (passed, 23)):
        wait(ref, sem)


def run_adam(*operands):
    hc = operands[4].shape[2]
    out_rows, _, g_sum, small = operands[0:4]
    shapes = [out_rows, out_rows, *operands[4:16]]
    hbm = pl.BlockSpec(memory_space=pl.ANY)
    kinds_in, kinds_out = operands[4].shape, operands[7].shape
    small_bias, small_vec = operands[10].shape, operands[13].shape
    big = [
        pltpu.VMEM((kinds_in[0], 3, *kinds_in[1:]), F32),
        pltpu.VMEM((kinds_out[0], 3, *kinds_out[1:]), F32),
        pltpu.VMEM((3, *small_bias), F32),
        pltpu.VMEM((3, *small_vec), F32),
    ]
    return pl.pallas_call(
        functools.partial(adam_kernel, hc),
        out_shape=[jax.ShapeDtypeStruct(a.shape, F32) for a in shapes],
        in_specs=[hbm] * 16,
        out_specs=[hbm] * 14,
        scratch_shapes=big * 2
        + [pltpu.VMEM(g_sum.shape, F32), pltpu.VMEM(small.shape, F32)]
        + [pltpu.VMEM((2, *out_rows.shape), F32), pltpu.SemaphoreType.DMA((24,))],
        compiler_params=pltpu.CompilerParams(vmem_limit_bytes=62 << 20),
        name="adam",
    )(*operands)


def fused_shards(
    resid,
    cotangent,
    master_in,
    moment1_in,
    moment2_in,
    master_out,
    moment1_out,
    moment2_out,
    master_bias,
    moment1_bias,
    moment2_bias,
    master_vec,
    moment1_vec,
    moment2_vec,
):
    rows = master_in.shape[1]
    hc = master_in.shape[3]
    turned = [jnp.transpose(a[0], (1, 0, 2)) for a in (master_in, moment1_in, moment2_in)]
    plain = [a[0] for a in (master_out, moment1_out, moment2_out)]
    biases = [a.reshape(6, 1, hc) for a in (master_bias, moment1_bias, moment2_bias)]
    vectors = [a.reshape(6, 1, D) for a in (master_vec, moment1_vec, moment2_vec)]
    sums = run_block(
        resid, cotangent, turned[0], plain[0], biases[0], vectors[0], rows, lax.axis_size("dp")
    )
    new = run_adam(*sums, *turned, *plain, *biases, *vectors)
    return (
        new[0],
        new[1],
        *[jnp.transpose(a, (1, 0, 2))[None] for a in new[2:5]],
        *[a[None] for a in new[5:8]],
        *[a.reshape(1, 6, hc) for a in new[8:11]],
        *[a.reshape(1, 6, D) for a in new[11:14]],
    )


def solution(mesh):
    fused = mesh.shape["dp"] == 8 and mesh.shape["tensor"] == 4
    return jax.shard_map(
        fused_shards if fused else shards,
        mesh=mesh,
        in_specs=(
            P("dp", None),
            P("dp", None),
            P(None, "dp", None, "tensor"),
            P(None, "dp", None, "tensor"),
            P(None, "dp", None, "tensor"),
            P(None, None, "tensor", "dp"),
            P(None, None, "tensor", "dp"),
            P(None, None, "tensor", "dp"),
            P(None, None, "tensor"),
            P(None, None, "tensor"),
            P(None, None, "tensor"),
            P(),
            P(),
            P(),
        ),
        out_specs=(
            P(("dp", "tensor"), None),
            P(("dp", "tensor"), None),
            P(None, "dp", None, "tensor"),
            P(None, "dp", None, "tensor"),
            P(None, "dp", None, "tensor"),
            P(None, None, "tensor", "dp"),
            P(None, None, "tensor", "dp"),
            P(None, None, "tensor", "dp"),
            P(None, None, "tensor"),
            P(None, None, "tensor"),
            P(None, None, "tensor"),
            P(),
            P(),
            P(),
        ),
        check_vma=False,
    )
```

```python
import functools

import jax
import jax.numpy as jnp
from jax import lax
from jax.experimental import pallas as pl
from jax.experimental.pallas import tpu as pltpu
from jax.sharding import PartitionSpec as P

D = 768
HD = 64
LEN = 1024
LAYERS = 1
STEP = 10


EPS = 1e-05
BRANCH_SCALE = 48 ** (-0.5)
BETA_ONE = 0.9
BETA_TWO = 0.95
ADAM_EPS = 1e-08
DECAY = 0.1
SMALL_RATE = 0.3
MASKED = -1e30


def norm_rows(stream, gain, shift):
    center = stream - jnp.mean(stream, -1, keepdims=True)
    inverse = lax.rsqrt(jnp.mean(center * center, -1, keepdims=True) + EPS)
    scaled = center * inverse
    return (scaled * gain + shift, scaled, inverse)


def norm_back(grad_out, scaled, inverse, gain):
    weighted = grad_out * gain
    centered = weighted - jnp.mean(weighted, -1, keepdims=True)
    return inverse * (centered - scaled * jnp.mean(weighted * scaled, -1, keepdims=True))


def plain_dot(left, right):
    return jnp.dot(left, right, preferred_element_type=jnp.float32)


def left_dot(left, right):
    return lax.dot_general(
        left, right, (((0,), (0,)), ((), ())), preferred_element_type=jnp.float32
    )


def right_dot(left, right):
    return lax.dot_general(
        left, right, (((1,), (1,)), ((), ())), preferred_element_type=jnp.float32
    )


def smooth_gate(values_in):
    return jax.nn.gelu(values_in, approximate=True)


def tensor_rows(array_in):
    quarter = array_in.shape[0] // lax.axis_size("tensor")
    return lax.dynamic_slice_in_dim(array_in, lax.axis_index("tensor") * quarter, quarter, 0)


def own_rows(array_in):
    return tensor_rows(array_in)


def branch_total(partial_sum):
    return lax.psum(partial_sum.astype(jnp.bfloat16), "tensor").astype(jnp.float32)


def grad_total(partial_sum):
    return lax.psum(partial_sum.astype(jnp.bfloat16), "tensor").astype(jnp.float32)


def causal_scores(queries, key_rows, first, last):
    block_rows = last - first
    scores = jnp.einsum(
        "qhd,khd->hqk", queries[first:last], key_rows[:last], preferred_element_type=jnp.float32
    ) * HD ** (-0.5)
    query_pos = lax.broadcasted_iota(jnp.int32, (block_rows, last), 0) + first
    key_pos = lax.broadcasted_iota(jnp.int32, (block_rows, last), 1)
    return jnp.where(query_pos >= key_pos, scores, MASKED)


def attend_sequence(operands):
    queries, key_rows, value_rows = operands
    block_rows = min(512, LEN)
    outputs = []
    totals = []
    for block_idx in range(LEN // block_rows):
        first = block_idx * block_rows
        last = first + block_rows
        scores = causal_scores(queries, key_rows, first, last)
        highest = jnp.max(scores, -1, keepdims=True)
        expo = jnp.exp(scores - highest)
        summed = jnp.sum(expo, -1, keepdims=True)
        weights = (expo / summed).astype(jnp.bfloat16)
        mixed = jnp.einsum(
            "hqk,khd->qhd", weights, value_rows[:last], preferred_element_type=jnp.float32
        )
        outputs.append(mixed.astype(jnp.bfloat16))
        totals.append((highest + jnp.log(summed))[..., 0])
    return (jnp.concatenate(outputs, 0), jnp.concatenate(totals, 1))


def attend_back(operands):
    queries, key_rows, value_rows, log_total, grad_mixed = operands
    block_rows = min(512, LEN)
    d_keys = jnp.zeros(key_rows.shape, jnp.float32)
    d_values = jnp.zeros(value_rows.shape, jnp.float32)
    d_queries = []
    for block_idx in range(LEN // block_rows):
        first = block_idx * block_rows
        last = first + block_rows
        scores = causal_scores(queries, key_rows, first, last)
        probs = jnp.exp(scores - log_total[:, first:last, None])
        d_probs = jnp.einsum(
            "qhd,khd->hqk",
            grad_mixed[first:last],
            value_rows[:last],
            preferred_element_type=jnp.float32,
        )
        inner = jnp.sum(probs * d_probs, -1, keepdims=True)
        d_scores = (probs * (d_probs - inner)).astype(jnp.bfloat16)
        d_queries.append(
            jnp.einsum(
                "hqk,khd->qhd", d_scores, key_rows[:last], preferred_element_type=jnp.float32
            )
            * HD ** (-0.5)
        )
        key_part = jnp.einsum(
            "hqk,qhd->khd", d_scores, queries[first:last], preferred_element_type=jnp.float32
        ) * HD ** (-0.5)
        value_part = jnp.einsum(
            "hqk,qhd->khd",
            probs.astype(jnp.bfloat16),
            grad_mixed[first:last],
            preferred_element_type=jnp.float32,
        )
        d_keys = d_keys.at[:last].add(key_part)
        d_values = d_values.at[:last].add(value_part)
    return (jnp.concatenate(d_queries, 0), d_keys, d_values)


def layer_forward(stream, w_in, w_out, bias, vector):
    model_width = w_in.shape[0]
    head_cols = w_in.shape[2]
    heads_here = head_cols // HD
    normed, scaled_one, inverse_one = norm_rows(stream, vector[0], vector[1])
    normed_low = normed.astype(jnp.bfloat16)
    seq_count = normed_low.shape[0] // LEN
    shape4 = (seq_count, LEN, heads_here, HD)
    w_qkv = w_in[:, 0:3].reshape(model_width, 3 * head_cols)
    projected = plain_dot(normed_low, w_qkv)
    queries = (projected[:, :head_cols] + bias[0]).astype(jnp.bfloat16).reshape(shape4)
    key_rows = projected[:, head_cols : 2 * head_cols].astype(jnp.bfloat16).reshape(shape4)
    value_rows = (projected[:, 2 * head_cols :] + bias[1]).astype(jnp.bfloat16).reshape(shape4)
    mixed, log_total = lax.map(attend_sequence, (queries, key_rows, value_rows))
    mixed_low = mixed.reshape(-1, head_cols)
    attended = branch_total(plain_dot(mixed_low, w_out[0])) + vector[4]
    middle = stream + BRANCH_SCALE * attended
    hidden, scaled_two, inverse_two = norm_rows(middle, vector[2], vector[3])
    hidden_low = hidden.astype(jnp.bfloat16)
    w_up = w_in[:, 3:].reshape(model_width, 4 * head_cols)
    pre_act = plain_dot(hidden_low, w_up) + bias[2:].reshape(4 * head_cols)
    act_low = smooth_gate(pre_act).astype(jnp.bfloat16)
    w_down = w_out[1:].reshape(4 * head_cols, model_width)
    mlp_out = branch_total(plain_dot(act_low, w_down)) + vector[5]
    result = middle + BRANCH_SCALE * mlp_out
    kept = (
        scaled_one,
        inverse_one,
        normed_low,
        queries,
        key_rows,
        value_rows,
        log_total,
        mixed_low,
        scaled_two,
        inverse_two,
        hidden_low,
        pre_act,
        act_low,
    )
    return (result, kept)


def layer_backward(gradient, w_in, w_out, vector, kept):
    (
        scaled_one,
        inverse_one,
        normed_low,
        queries,
        key_rows,
        value_rows,
        log_total,
        mixed_low,
        scaled_two,
        inverse_two,
        hidden_low,
        pre_act,
        act_low,
    ) = kept
    model_width = w_in.shape[0]
    head_cols = w_in.shape[2]
    w_qkv = w_in[:, 0:3].reshape(model_width, 3 * head_cols)
    w_up = w_in[:, 3:].reshape(model_width, 4 * head_cols)
    w_down = w_out[1:].reshape(4 * head_cols, model_width)
    d_mlp = (BRANCH_SCALE * gradient).astype(jnp.bfloat16)
    g_bdown = jnp.sum(own_rows(d_mlp).astype(jnp.float32), 0)
    g_down = left_dot(act_low, d_mlp).reshape(4, head_cols, model_width)
    d_act = right_dot(d_mlp, w_down).astype(jnp.bfloat16)
    gate_value, gate_pull = jax.vjp(smooth_gate, pre_act)
    d_pre = gate_pull(d_act.astype(jnp.float32))[0].astype(jnp.bfloat16)
    g_bup = jnp.sum(d_pre.astype(jnp.float32), 0)
    g_up = left_dot(hidden_low, d_pre).reshape(model_width, 4, head_cols)
    d_hidden = grad_total(right_dot(d_pre, w_up))
    g_gain_two = jnp.sum(own_rows(d_hidden * scaled_two), 0)
    g_shift_two = jnp.sum(own_rows(d_hidden), 0)
    d_middle = gradient + norm_back(d_hidden, scaled_two, inverse_two, vector[2])
    d_attn = (BRANCH_SCALE * d_middle).astype(jnp.bfloat16)
    g_bproj = jnp.sum(own_rows(d_attn).astype(jnp.float32), 0)
    g_proj = left_dot(mixed_low, d_attn)
    d_mixed = right_dot(d_attn, w_out[0]).astype(jnp.bfloat16)
    d_queries, d_keys, d_values = lax.map(
        attend_back, (queries, key_rows, value_rows, log_total, d_mixed.reshape(queries.shape))
    )
    d_qkv = jnp.concatenate(
        [
            d_queries.reshape(-1, head_cols),
            d_keys.reshape(-1, head_cols),
            d_values.reshape(-1, head_cols),
        ],
        1,
    ).astype(jnp.bfloat16)
    g_qkv = left_dot(normed_low, d_qkv).reshape(model_width, 3, head_cols)
    g_bq = jnp.sum(d_qkv[:, :head_cols].astype(jnp.float32), 0)
    g_bv = jnp.sum(d_qkv[:, 2 * head_cols :].astype(jnp.float32), 0)
    d_normed = grad_total(right_dot(d_qkv, w_qkv))
    g_gain_one = jnp.sum(own_rows(d_normed * scaled_one), 0)
    g_shift_one = jnp.sum(own_rows(d_normed), 0)
    d_stream = d_middle + norm_back(d_normed, scaled_one, inverse_one, vector[0])
    g_in = jnp.concatenate([g_qkv, g_up], 1)
    g_out = jnp.concatenate([g_proj[None], g_down], 0)
    g_bias = jnp.concatenate([g_bq[None], g_bv[None], g_bup.reshape(4, head_cols)], 0)
    g_vector = jnp.stack([g_gain_one, g_shift_one, g_gain_two, g_shift_two, g_bproj, g_bdown])
    return (d_stream, g_in, g_out, g_bias, g_vector)


def adam_step(master, first, second, gradient, rate, decay):
    first_new = BETA_ONE * first + (1 - BETA_ONE) * gradient
    second_new = BETA_TWO * second + (1 - BETA_TWO) * gradient * gradient
    direction = (
        first_new / (1 - BETA_ONE**STEP) / (jnp.sqrt(second_new / (1 - BETA_TWO**STEP)) + ADAM_EPS)
    )
    return (first_new, second_new, master - rate * (direction + decay * master))


def shards(
    resid,
    cotangent,
    master_in,
    moment1_in,
    moment2_in,
    master_out,
    moment1_out,
    moment2_out,
    master_bias,
    moment1_bias,
    moment2_bias,
    master_vec,
    moment1_vec,
    moment2_vec,
):
    weights_in, weights_out = (
        lax.all_gather(master_in.astype(jnp.bfloat16), "dp", axis=1, tiled=True),
        lax.all_gather(master_out.astype(jnp.bfloat16), "dp", axis=3, tiled=True),
    )
    stream = resid
    gradient = cotangent
    layer_idx = 0
    stream, kept = layer_forward(
        stream,
        weights_in[layer_idx],
        weights_out[layer_idx],
        master_bias[layer_idx],
        master_vec[layer_idx],
    )
    kept_list = [kept]
    list_in = [None] * LAYERS
    list_out = [None] * LAYERS
    list_bias = [None] * LAYERS
    list_vector = [None] * LAYERS
    layer_idx = 0
    gradient, g_in, g_out, g_bias, g_vector = layer_backward(
        gradient,
        weights_in[layer_idx],
        weights_out[layer_idx],
        master_vec[layer_idx],
        kept_list[layer_idx],
    )
    list_in[layer_idx] = g_in
    list_out[layer_idx] = g_out
    list_bias[layer_idx] = g_bias
    list_vector[layer_idx] = g_vector
    summed_in = jnp.stack(list_in)
    summed_out = jnp.stack(list_out)
    summed_in, summed_out = (
        lax.psum_scatter(summed_in, "dp", scatter_dimension=1, tiled=True),
        lax.psum_scatter(summed_out, "dp", scatter_dimension=3, tiled=True),
    )
    summed_bias = lax.psum(jnp.stack(list_bias), "dp")
    summed_vector = lax.psum(jnp.stack(list_vector), ("dp", "tensor"))
    first_in, second_in, new_in = adam_step(
        master_in, moment1_in, moment2_in, summed_in, 0.5 * D ** (-0.5), DECAY
    )
    first_out, second_out, new_out = adam_step(
        master_out, moment1_out, moment2_out, summed_out, 2.0 * D ** (-0.5), DECAY
    )
    first_bias, second_bias, new_bias = adam_step(
        master_bias, moment1_bias, moment2_bias, summed_bias, SMALL_RATE, 0.0
    )
    first_vec, second_vec, new_vec = adam_step(
        master_vec, moment1_vec, moment2_vec, summed_vector, SMALL_RATE, 0.0
    )
    return (
        own_rows(stream),
        own_rows(gradient),
        first_in,
        second_in,
        new_in,
        first_out,
        second_out,
        new_out,
        first_bias,
        second_bias,
        new_bias,
        first_vec,
        second_vec,
        new_vec,
    )


MESH_IDS = pl.DeviceIdType.MESH
F32 = jnp.float32
BF16 = jnp.bfloat16
NN = (((1,), (0,)), ((), ()))
NT = (((1,), (1,)), ((), ()))
TN = (((0,), (0,)), ((), ()))
GELU_A = (2.0 / 3.141592653589793) ** 0.5
GELU_B = 0.044715


def mm(left, right, dims=NN):
    return lax.dot_general(left, right, dims, preferred_element_type=F32)


def rows_at(start, size, align):
    return pl.ds(pl.multiple_of(start, align), size)


def block_kernel(
    sizes,
    resid_h,
    cot_h,
    win_h,
    wout_h,
    bias_h,
    vec_h,
    out_o,
    grad_o,
    gsum_o,
    small_o,
    win,
    wout,
    bias,
    vec,
    resid,
    cot,
    inv1,
    normed,
    dmlp,
    w,
    q_s,
    k_s,
    v_s,
    e_s,
    linv,
    mixed,
    ps,
    crecv,
    fin,
    ysend,
    yrecv,
    mid,
    xhat2,
    inv2,
    normed_t,
    hidden,
    act_s,
    dpre,
    dattn,
    dmix,
    dk_s,
    dv_s,
    dqkv,
    gproj,
    gmat,
    xr,
    zs,
    zr,
    side_r,
    side_s,
    side_xs,
    side_xr,
    gsum,
    sm,
    smp,
    smx,
    smz,
    smy,
    lsem,
    ssem,
    rsem,
):
    tokens, width, quarter, heads, shard = sizes
    dp = lax.axis_index("dp")
    ten = lax.axis_index("tensor")
    z = lax.div(dp, 2)
    x = lax.rem(dp, 2)
    y = lax.div(ten, 2)
    c = lax.rem(ten, 2)
    x_dev = (dp + 1 - 2 * x, ten)
    c_dev = (dp, ten + 1 - 2 * c)
    y_dev = (dp, ten + 2 - 4 * y)

    def z_other(j):
        if j == 1:
            return z + 1 - 2 * lax.rem(z, 2)
        if j == 2:
            return lax.rem(z + 2, 4)
        return 3 - z

    def z_dev(j):
        return (2 * z_other(j) + x, ten)

    def rcopy(src, dst, send_idx, recv_idx, dev):
        return pltpu.make_async_remote_copy(
            src_ref=src,
            dst_ref=dst,
            send_sem=ssem.at[send_idx],
            recv_sem=rsem.at[recv_idx],
            device_id=dev,
            device_id_type=MESH_IDS,
        )

    barrier = pltpu.get_barrier_semaphore()
    cross_dev = (dp + 1 - 2 * x, ten + 1 - 2 * c)
    peers = [x_dev, c_dev, y_dev, cross_dev, z_dev(1), z_dev(2), z_dev(3)]
    for dev in peers:
        pl.semaphore_signal(barrier, inc=1, device_id=dev, device_id_type=MESH_IDS)
    load_win = pltpu.make_async_copy(win_h, win, lsem.at[2])
    load_wout = pltpu.make_async_copy(wout_h, wout, lsem.at[3])
    load_win.start()
    load_wout.start()
    load_resid = pltpu.make_async_copy(resid_h, resid, lsem.at[0])
    load_cot = pltpu.make_async_copy(cot_h, cot, lsem.at[1])
    load_vec = pltpu.make_async_copy(vec_h, vec, lsem.at[11])
    load_bias = pltpu.make_async_copy(bias_h, bias, lsem.at[12])
    load_vec.start()
    load_resid.start()
    load_cot.start()
    load_bias.start()

    mine = rows_at(dp * shard, shard, shard)
    load_win.wait()
    load_wout.wait()
    out_t = [jnp.transpose(wout[i]) for i in range(5)]
    pairs, last = slice(0, 2 * HD), slice(2 * HD, 3 * HD)
    tiles = [win[0, :, pairs], win[1, :, pairs], win[2, :, pairs], win[0, :, last], win[2, :, last]]
    tiles += [out_t[0][:, pairs], win[1, :, last], out_t[0][:, last]]
    w[0, mine, :] = jnp.concatenate(tiles, 1).astype(BF16)

    pl.semaphore_wait(barrier, len(peers))

    half_cols = width // 2
    units = (
        (0, slice(0, half_cols)),
        (0, slice(half_cols, width)),
        (1, slice(0, width)),
        (2, slice(0, width)),
    )

    is_end = 1 - lax.rem(lax.div(z + 1, 2), 2)
    is_mid = 1 - is_end
    upper = lax.div(z, 2)
    owner_z = (z_other(1), 2 - upper, 3 - 3 * upper)
    pair_dev, mid_dev = (2 * owner_z[0] + x, ten), (2 * owner_z[1] + x, ten)

    def ag_copy(u, zi, send, recv, dev):
        b, cols = units[u]
        src = w.at[b, rows_at((2 * zi + x) * shard, shard, shard), cols]
        return rcopy(src, src, send + u, recv, dev)

    def ag_pair(u):
        return ag_copy(u, z, 4, 3 * u, pair_dev)

    def ag_mid(u):
        return ag_copy(u, z, 4, 3 * u + 1, mid_dev)

    def ag_end_far(u, i):
        dev = (2 * owner_z[i] + x, ten)
        return ag_copy(u, z, 4, 3 * u + 2, dev)

    def ag_onward(u, i):
        if i == 0:
            return ag_copy(u, owner_z[0], 4, 3 * u + 2, mid_dev)
        return ag_copy(u, owner_z[i], 4, 3 * u + i, pair_dev)

    def ag_x(u, i):
        return ag_copy(u, z if i == 0 else owner_z[i - 1], 0, 12 + u, x_dev)

    def ag_bytes(u, pieces, send, recv):
        b, cols = units[u]
        ref = w.at[b, 0 : pieces * shard, cols]
        return rcopy(ref, ref, send, recv, x_dev)

    def mid_start(u):
        @pl.when(is_mid == 1)
        def _():
            ag_pair(u).start()
            ag_mid(u).start()

    def ag_arrive(u, i):
        ag_copy(u, owner_z[i], 0, 3 * u + i, x_dev).wait_recv()

    def pump_end(u, i):
        @pl.when(is_end == 1)
        def _():
            ag_arrive(u, i)
            ag_x(u, 1 + i).start()

    def pump_mid(u, i):
        @pl.when(is_mid == 1)
        def _():
            ag_arrive(u, i)
            if u > 1 or i == 1:
                ag_onward(u, i).start()
            ag_x(u, 1 + i).start()

    def mid_onward(u, i):
        @pl.when(is_mid == 1)
        def _():
            ag_arrive(u, i)
            ag_onward(u, i).start()

    def mid_x(u, i):
        @pl.when(is_mid == 1)
        def _():
            ag_x(u, i).start()

    def ag_finish(u):
        ag_bytes(u, 4, u, 12 + u).wait_recv()

    def ag_drain(u):
        ag_bytes(u, 4, u, 12 + u).wait_send()

        if u < 2:
            ag_bytes(u, 3, 4 + u, 12 + u).wait_send()
            return

        @pl.when(is_end == 1)
        def _():
            ag_bytes(u, 1, 4 + u, 12 + u).wait_send()

        @pl.when(is_mid == 1)
        def _():
            ag_bytes(u, 5, 4 + u, 12 + u).wait_send()

    ag_x(0, 0).start()
    ag_x(1, 0).start()
    mid_start(0)
    mid_start(1)

    @pl.when(is_end == 1)
    def _():
        for u in range(2):
            ag_pair(u).start()
            ag_end_far(u, 2).start()
            ag_end_far(u, 1).start()

    w[1, mine, :] = jnp.concatenate([win[3 + i] for i in range(4)], 1).astype(BF16)
    w[2, mine, :] = jnp.concatenate(out_t[1:], 1).astype(BF16)

    load_vec.wait()
    load_bias.wait()
    load_resid.wait()
    load_cot.wait()
    gain_one, shift_one = vec[0], vec[1]

    own = rows_at(ten * quarter, quarter, quarter)
    mid[...] = resid[own, :]
    xhat = resid

    def first_norm(r, carry):
        rows = rows_at(r * 128, 128, 128)
        part = resid[rows, :]
        center = part - jnp.mean(part, -1, keepdims=True)
        inverse = lax.rsqrt(jnp.mean(center * center, -1, keepdims=True) + EPS)
        scaled = center * inverse
        xhat[rows, :] = scaled
        inv1[rows, :] = inverse
        normed[rows, :] = (scaled * gain_one + shift_one).astype(BF16)
        dmlp[rows, :] = (cot[rows, :] * BRANCH_SCALE).astype(BF16)
        return carry

    lax.fori_loop(0, tokens // 128, first_norm, 0)
    for u, i in ((0, 0), (0, 1), (1, 0), (1, 1)):
        pump_mid(u, i)
    mid_start(2)
    pump_mid(0, 2)
    pump_mid(1, 2)
    pump_end(0, 0)
    pump_end(1, 0)

    @pl.when(is_end == 1)
    def _():
        ag_pair(2).start()

    for u, i in ((0, 2), (0, 1), (1, 2), (1, 1)):
        pump_end(u, i)

    @pl.when(is_end == 1)
    def _():
        ag_pair(3).start()

    ag_x(2, 0).start()

    sm[...] = jnp.zeros_like(sm)
    sm[5:6, :] = jnp.sum(dmlp[own, :].astype(F32), 0, keepdims=True)
    mixed[...] = jnp.zeros_like(mixed)
    dqkv[...] = jnp.zeros_like(dqkv)
    dk_s[...] = jnp.zeros_like(dk_s)
    dv_s[...] = jnp.zeros_like(dv_s)

    hc = heads * HD
    low_half = lax.broadcasted_iota(jnp.int32, (1, 2 * HD), 1) < HD
    bias_v01, bias_q01 = bias[1, :, pairs], bias[0, :, pairs]
    bias_q2v2 = jnp.concatenate([bias[0, :, last], bias[1, :, last]], 1)
    eighth = HD**-0.5

    def project_pair(r):
        rows = slice(r * 256, (r + 1) * 256)
        got = mm(normed[rows, :], w[0, :, 0:384])
        queries = (got[:, 0:128] + bias_q01).astype(BF16).astype(F32) * eighth
        q_s[0, rows, :] = jnp.where(low_half, queries, 0.0).astype(BF16)
        q_s[1, rows, :] = jnp.where(low_half, 0.0, queries).astype(BF16)
        k_s[0, rows, :] = got[:, 128:256].astype(BF16)
        v_s[0, rows, :] = (got[:, 256:384] + bias_v01).astype(BF16)

    def project_last(r):
        rows = slice(r * 256, (r + 1) * 256)
        got = mm(normed[rows, :], w[0, :, 384:768])
        both = (got[:, 0:128] + bias_q2v2).astype(BF16)
        q_s[2, rows, :] = jnp.where(low_half, both.astype(F32) * eighth, 0.0).astype(BF16)
        v_s[1, rows, :] = both
        k_s[1, rows, :] = got[:, 256:384].astype(BF16)

    ag_finish(0)
    for r in range(tokens // 256):
        project_pair(r)
    pump_end(2, 0)
    pump_mid(2, 0)
    pump_mid(2, 1)
    ag_x(3, 0).start()
    mid_start(3)

    def attend(i, which_heads):
        first, last_row = i * quarter, (i + 1) * quarter
        rows = slice(first, last_row)
        causal = lax.broadcasted_iota(jnp.int32, (quarter, quarter), 0) >= lax.broadcasted_iota(
            jnp.int32, (quarter, quarter), 1
        )
        got = {}
        for h in which_heads:
            at = h // 2
            queries = q_s[h, rows, :]
            diag = jnp.where(causal, mm(queries, k_s[at, rows, :], NT), MASKED)
            highest = jnp.max(diag, -1, keepdims=True)
            if i > 0:
                wide = mm(queries, k_s[at, 0:first, :], NT)
                highest = jnp.maximum(highest, jnp.max(wide, -1, keepdims=True))
            e_diag = jnp.exp(diag - highest)
            summed = jnp.sum(e_diag, -1, keepdims=True)
            e_diag = e_diag.astype(BF16)
            e_s[h, rows, first:last_row] = e_diag
            total = mm(e_diag, v_s[at, rows, :])
            if i > 0:
                e_wide = jnp.exp(wide - highest)
                summed = summed + jnp.sum(e_wide, -1, keepdims=True)
                e_wide = e_wide.astype(BF16)
                e_s[h, rows, 0:first] = e_wide
                total = total + mm(e_wide, v_s[at, 0:first, :])
            inverse = 1.0 / summed
            linv[h, rows, :] = inverse
            got[h] = total * inverse
        if 0 in got:
            mixed[rows, 0:128] = jnp.where(low_half, got[0], got[1]).astype(BF16)
        if 2 in got:
            mixed[rows, 128:256] = jnp.where(low_half, 0.0, got[2]).astype(BF16)

    def rs_core(k, half):
        return rcopy(ps.at[k % 2, half], crecv.at[k, half], 16 + 2 * (k % 2) + half, 16 + 2 * k + half, c_dev)

    halves = [slice(0, quarter // 2), slice(quarter // 2, quarter)]

    def rs_y(k, hh):
        src, dst = ysend.at[k, halves[hh], :], yrecv.at[k, halves[hh], :]
        return rcopy(src, dst, 20, 24 + 2 * k + hh, y_dev)

    def rs_y_start(k):
        for hh in range(2):
            rs_y(k, hh).start()

    def rs_pair(k, near, compute):
        half = 1 if near else 0
        def step(s, carry):
            yq = y if near else 1 - y
            part = compute(2 * yq + lax.rem(1 - s + c, 2))

            @pl.when(s == 0)
            def _():
                ps[k % 2, half] = part.astype(BF16)
                rs_core(k, half).start()

            @pl.when(s == 1)
            def _():
                rs_core(k, half).wait_recv()
                total = part + crecv[k, half].astype(F32)
                if near:
                    fin[k % 3] = total
                else:
                    ysend[k] = total.astype(BF16)
                    rs_y_start(k)

            return carry

        lax.fori_loop(0, 2, step, 0)

    def rs_quad(k, compute, held, between=None):
        for half in range(2):
            rs_core(k - 2, half).wait_send()

        def step(s, carry):
            half, odd = lax.div(s, 2), lax.rem(s, 2)
            yq = half * y + (1 - half) * (1 - y)
            if between is not None:

                @pl.when(s == 2)
                def _():
                    between()

            part = compute(2 * yq + lax.rem(1 - odd + c, 2))

            @pl.when(odd == 0)
            def _():
                ps[k % 2, half] = part.astype(BF16)
                rs_core(k, half).start()

            @pl.when(s == 1)
            def _():
                held[...] = part

            @pl.when(s == 3)
            def _():
                fin[k % 3] = part

            return carry

        lax.fori_loop(0, 4, step, 0)

    def quad_far(k, held):
        rs_core(k, 0).wait_recv()
        ysend[k] = (held[...] + crecv[k, 0].astype(F32)).astype(BF16)

    def quad_near(k):
        rs_core(k, 1).wait_recv()
        fin[k % 3] = fin[k % 3] + crecv[k, 1].astype(F32)

    def rs_result(k, hh):
        rs_y(k, hh).wait_recv()
        return fin[k % 3, halves[hh], :] + yrecv[k, halves[hh], :].astype(F32)

    def attend_quarter(which, which_heads):
        for i in range(tokens // quarter):

            @pl.when(which == i)
            def _():
                attend(i, which_heads)

    def proj(which):
        return mm(mixed[rows_at(which * quarter, quarter, quarter), :], w[0, :, 512:768], NT)

    def far_early(s, carry):
        attend_quarter(2 * (1 - y) + lax.rem(s + c, 2), (0, 1))
        return carry

    def far_proj(which):
        attend_quarter(which, (2,))
        return proj(which)

    def near_proj(which):
        attend_quarter(which, (0, 1, 2))
        return proj(which)

    lax.fori_loop(0, 2, far_early, 0)
    mid_onward(3, 0)
    ag_finish(1)
    for r in range(tokens // 256):
        project_last(r)
    rs_pair(0, False, far_proj)
    pump_end(2, 1)
    pump_mid(2, 2)
    mid_x(3, 1)
    rs_pair(0, True, near_proj)
    pump_end(2, 2)
    pump_end(3, 0)
    pump_mid(3, 1)

    def q_rows(ref, which, hh):
        return ref.at[rows_at(which * quarter + hh * (quarter // 2), quarter // 2, quarter // 2), :]

    def qg_y(g, ref, hh):
        src = q_rows(ref, ten, hh)
        return rcopy(src, src, 21, 32 + 2 * g + hh, y_dev)

    def qg_c(g, ref, hh):
        src = q_rows(ref, ten, hh)
        return rcopy(src, src, 22, 36 + g, c_dev)

    def qg_f(g, ref, hh):
        src = q_rows(ref, ten + 2 - 4 * y, hh)
        return rcopy(src, src, 23, 38 + 2 * g + hh, c_dev)

    def qg_start(g, ref, hh):
        qg_y(g, ref, hh).start()
        qg_c(g, ref, hh).start()

    def qg_rows(ref, count, send, recv):
        rows = ref.at[0:count, :]
        return rcopy(rows, rows, send, recv, c_dev)

    def qg_near(g, ref):
        qg_rows(ref, quarter, 22, 36 + g).wait_recv()

    def qg_far(g, ref, hh):
        qg_y(g, ref, hh).wait_recv()
        qg_f(g, ref, hh).start()

    def qg_last(g, ref, hh):
        qg_f(g, ref, hh).wait_recv()

    def far_rows(g, ref, compute, between=None):
        def step(hh, carry):
            if between is not None:

                @pl.when(hh == 1)
                def _():
                    between()

            qg_far(g, ref, hh)
            compute(2 * (1 - y) + c, hh)
            qg_last(g, ref, hh)
            compute(2 * (1 - y) + 1 - c, hh)
            return carry

        lax.fori_loop(0, 2, step, 0)

    for hh in range(2):
        if hh == 1:
            pump_end(3, 1)
            pump_mid(3, 2)
        half = halves[hh]
        middle = mid[half, :] + BRANCH_SCALE * (rs_result(0, hh) + vec[4])
        mid[half, :] = middle
        center = middle - jnp.mean(middle, -1, keepdims=True)
        inverse = lax.rsqrt(jnp.mean(center * center, -1, keepdims=True) + EPS)
        scaled = center * inverse
        xhat2[half, :] = scaled
        inv2[half, :] = inverse
        mine_h = rows_at(ten * quarter + hh * (quarter // 2), quarter // 2, quarter // 2)
        hidden[mine_h, :] = (scaled * vec[2] + vec[3]).astype(BF16)
        qg_start(0, hidden, hh)

    pump_end(3, 2)
    ag_finish(2)

    bias_up = jnp.concatenate([bias[2 + i] for i in range(4)], 1)

    def forward_units(which, hh=None):
        rows = rows_at(which * quarter, quarter, quarter)
        if hh is not None:
            rows = rows_at(which * quarter + hh * (quarter // 2), quarter // 2, quarter // 2)
        hq = hidden[rows, :]
        for t in range(width // 256):
            cols = slice(t * 256, (t + 1) * 256)
            pre = mm(hq, w[1, :, cols]) + bias_up[:, cols]
            square = pre * pre
            tanh = jnp.tanh(GELU_A * (pre + GELU_B * (square * pre)))
            half_up = 0.5 + 0.5 * tanh
            act_s[rows, cols] = (pre * half_up).astype(BF16)
            slope = half_up + 0.5 * pre * (1.0 - tanh * tanh) * (
                GELU_A + (3.0 * GELU_A * GELU_B) * square
            )
            dpre[rows, cols] = slope.astype(BF16)

    def grad_block(b, left, right, near):
        rows = slice(0, tokens)
        if near is not None:
            rows = rows_at((y if near else 1 - y) * 2 * quarter, 2 * quarter, 2 * quarter)

        def tile(t, carry):
            cols = rows_at(t * 256, 256, 256)
            part = mm(left[rows, cols], right[rows, :], TN)
            if near is False:
                part = part + gmat[b, cols, :].astype(F32)
            gmat[b, cols, :] = part.astype(BF16)
            return carry

        lax.fori_loop(0, width // 256, tile, 0)

    g_units = (*units[0:3], (2, slice(0, half_cols)))
    right_half = slice(half_cols, width)

    def gx(u, zi):
        b, cols = g_units[u]
        src = gmat.at[b, rows_at((2 * zi + 1 - x) * shard, shard, shard), cols]
        return rcopy(src, xr.at[b, zi, :, cols], 8 + u, 42 + 4 * u + zi, x_dev)

    def line_to(i):
        if i == 0:
            return pair_dev, 0
        return (2 * (is_end * owner_z[0] + is_mid * owner_z[i]) + x, ten), is_end * i + is_mid * 3

    def gz(u, i):
        b, cols = g_units[u]
        dev, slot = line_to(i)
        return rcopy(zs.at[b, i, :, cols], zr.at[b, slot, :, cols], 12 + u, 58 + 4 * u + slot, dev)

    def gz_arrive(u, slot):
        b, cols = g_units[u]
        ref = zr.at[b, slot, :, cols]
        rcopy(ref, ref, 12 + u, 58 + 4 * u + slot, x_dev).wait_recv()

    def g_start(u):
        @pl.when(is_end == 1)
        def _():
            for i in (2, 1, 0):
                gx(u, owner_z[i]).start()

        @pl.when(is_mid == 1)
        def _():
            for i in (0, 2, 1):
                gx(u, owner_z[i]).start()

        gx(u, z).start()

    def x_sum(u, zo):
        b, cols = g_units[u]
        gx(u, zo).wait_recv()
        mine_x = gmat[b, rows_at((2 * zo + x) * shard, shard, shard), cols].astype(F32)
        return mine_x + xr[b, zo, :, cols].astype(F32)

    def end_pump(u, i):
        b, cols = g_units[u]

        @pl.when(is_end == 1)
        def _():
            zs[b, i, :, cols] = x_sum(u, owner_z[i]).astype(BF16)
            gz(u, i).start()

    def mid_pump(u, i):
        b, cols = g_units[u]

        @pl.when(is_mid == 1)
        def _():
            total = x_sum(u, owner_z[i])
            if i > 0:
                gz_arrive(u, i)
                total = total + zr[b, i, :, cols].astype(F32)
            zs[b, i, :, cols] = total.astype(BF16)
            gz(u, i).start()

    def g_finish(u):
        b, cols = g_units[u]
        total = x_sum(u, z)
        for slot in (0, 3):
            gz_arrive(u, slot)
            total = total + zr[b, slot, :, cols].astype(F32)
        gsum[b, :, cols] = total
        if u < 3:
            g_out(u).start()

    def g_out(u):
        b, cols = units[u]
        return pltpu.make_async_copy(gsum.at[b, :, cols], gsum_o.at[b, :, cols], lsem.at[4 + u])

    def g_drain(u):
        b, cols = g_units[u]
        rcopy(xr.at[b, :, :, cols], xr.at[b, :, :, cols], 8 + u, 56, x_dev).wait_send()
        rcopy(zs.at[b, :, :, cols], zs.at[b, :, :, cols], 12 + u, 56, x_dev).wait_send()
        g_out(u).wait()

    def side_rows(zo):
        return gmat.at[2, rows_at(zo * 2 * shard, 2 * shard, 2 * shard), right_half]

    def side_copy(src, i):
        dev, slot = line_to(i)
        return rcopy(src, side_r.at[slot], 28, 78 + slot, dev)

    def side_arrive(slot):
        rcopy(side_r.at[slot], side_r.at[slot], 28, 78 + slot, x_dev).wait_recv()

    def side_start():
        @pl.when(is_end == 1)
        def _():
            for i in (2, 1):
                side_copy(side_rows(owner_z[i]), i).start()

        side_copy(side_rows(owner_z[0]), 0).start()

    def side_middle():
        @pl.when(is_mid == 1)
        def _():
            for i in (2, 1):
                side_arrive(i)
                mine_z = gmat[2, rows_at(owner_z[i] * 2 * shard, 2 * shard, 2 * shard), right_half]
                side_s[i - 1] = (mine_z.astype(F32) + side_r[i].astype(F32)).astype(BF16)
                side_copy(side_s.at[i - 1], i).start()

    def side_x():
        return rcopy(side_xs, side_xr, 29, 82, x_dev)

    def side_cross():
        side_arrive(0)
        side_arrive(3)

        def total(xi):
            at = rows_at(xi * shard, shard, shard)
            got = gmat[2, rows_at((2 * z + xi) * shard, shard, shard), right_half].astype(F32)
            return got + side_r[0, at, :].astype(F32) + side_r[3, at, :].astype(F32)

        side_xs[...] = total(1 - x).astype(BF16)
        side_x().start()
        gsum[2, :, right_half] = total(x)

    def side_finish():
        side_x().wait_recv()
        gsum[2, :, right_half] = gsum[2, :, right_half] + side_xr[...].astype(F32)
        g_out(3).start()

    def backward_units(which):
        rows = rows_at(which * quarter, quarter, quarter)
        gq = dmlp[rows, :]
        for t in range(width // 256):
            cols = slice(t * 256, (t + 1) * 256)
            d_act = mm(gq, w[2, :, cols]).astype(BF16).astype(F32)
            d_low = (dpre[rows, cols].astype(F32) * d_act).astype(BF16)
            dpre[rows, cols] = d_low
            sm[6:7, cols] = sm[6:7, cols] + jnp.sum(d_low.astype(F32), 0, keepdims=True)
        return mm(dpre[rows, :], w[1], NT)

    def branch(which):
        rows = rows_at(which * quarter, quarter, quarter)
        return mm(act_s[rows, :], w[2], NT)

    def near_units(s, carry):
        @pl.when(s == 1)
        def _():
            qg_near(0, hidden)

        forward_units(2 * y + lax.rem(s + c, 2))
        return carry

    lax.fori_loop(0, 2, near_units, 0)
    grad_block(2, dmlp, act_s, True)
    for t in range(width // 256):
        cols = slice(t * 256, (t + 1) * 256)
        normed_t[cols, :] = jnp.transpose(normed[:, cols])
    far_rows(0, hidden, forward_units)
    ag_finish(3)
    rs_pair(1, False, backward_units)
    grad_block(2, dmlp, act_s, False)
    g_start(3)
    side_start()
    rs_pair(1, True, backward_units)
    grad_block(1, hidden, dpre, None)
    g_start(2)
    end_pump(3, 2)
    mid_pump(3, 0)
    def second_norm_back(hh):
        half = halves[hh]
        mine_h = rows_at(ten * quarter + hh * (quarter // 2), quarter // 2, quarter // 2)
        d_hidden = rs_result(1, hh)
        scaled = xhat2[half, :]
        sm[2:3, :] = sm[2:3, :] + jnp.sum(d_hidden * scaled, 0, keepdims=True)
        sm[3:4, :] = sm[3:4, :] + jnp.sum(d_hidden, 0, keepdims=True)
        weighted = d_hidden * vec[2]
        d_mid = cot[mine_h, :] + inv2[half, :] * (
            weighted
            - jnp.mean(weighted, -1, keepdims=True)
            - scaled * jnp.mean(weighted * scaled, -1, keepdims=True)
        )
        fin[1, half, :] = d_mid
        d_attn = (BRANCH_SCALE * d_mid).astype(BF16)
        dattn[mine_h, :] = d_attn
        sm[4:5, :] = sm[4:5, :] + jnp.sum(d_attn.astype(F32), 0, keepdims=True)
        qg_start(1, dattn, hh)

    rs_quad(2, branch, fin.at[0])
    second_norm_back(0)
    end_pump(3, 1)
    quad_far(2, fin.at[0])
    quad_near(2)
    side_middle()
    end_pump(3, 0)
    second_norm_back(1)
    rs_y_start(2)

    def attend_back(i, which_heads, hh=None):
        first, last_row = i * quarter, (i + 1) * quarter
        size = quarter
        rows = slice(first, last_row)
        if hh is not None:
            size = quarter // 2
            rows = rows_at(first + hh * size, size, size)
        for at, group in enumerate(((0, 1), (2,))):
            if group[0] not in which_heads:
                continue
            count = len(group)
            tile = slice(at * 128, (at + 1) * 128)
            d_tile, out_tile = dmix[rows, tile].astype(F32), mixed[rows, tile].astype(F32)
            d_out = []
            for h in group:
                scaled = d_tile * linv[h, rows, :]
                d_out += [jnp.where(low_half, scaled, 0.0) if h == 0 else jnp.where(low_half, 0.0, scaled)]
            d_out = jnp.concatenate(d_out, 0)
            inner = jnp.sum(d_out * jnp.concatenate([out_tile] * count, 0), -1, keepdims=True)
            d_scaled = d_out.astype(BF16)
            heads_here = slice(group[0], group[-1] + 1)
            expo = e_s[heads_here, rows, 0:last_row].reshape(count * size, last_row)
            queries = q_s[heads_here, rows, :].reshape(count * size, 2 * HD)
            d_probs = mm(d_scaled, v_s[at, 0:last_row, :], NT)
            d_scores = (expo.astype(F32) * (d_probs - inner)).astype(BF16)
            d_q = mm(d_scores, k_s[at, 0:last_row, :]) * eighth
            dk_s[at, :, 0:last_row] = dk_s[at, :, 0:last_row] + mm(queries, d_scores, TN)
            dv_s[at, :, 0:last_row] = dv_s[at, :, 0:last_row] + mm(d_scaled, expo, TN)
            if at == 0:
                dqkv[rows, 0:128] = jnp.where(low_half, d_q[0:size], d_q[size:]).astype(BF16)
            else:
                dqkv[rows, 384:512] = jnp.where(low_half, d_q, 0.0).astype(BF16)

    def back_quarters(near, which_heads, fresh, prepare=None):
        def step(s, carry):
            if prepare is not None:
                prepare(s)
            yq = y if near else 1 - y
            which = 2 * yq + lax.rem(s + c, 2)
            if fresh:
                rows = rows_at(which * quarter, quarter, quarter)
                dmix[rows, :] = mm(dattn[rows, :], w[0, :, 512:768]).astype(BF16)
            for i in range(tokens // quarter):

                @pl.when(which == i)
                def _():
                    attend_back(i, which_heads)

            return carry

        lax.fori_loop(0, 2, step, 0)

    def back_far(which, hh):
        rows = rows_at(which * quarter + hh * (quarter // 2), quarter // 2, quarter // 2)
        dmix[rows, :] = mm(dattn[rows, :], w[0, :, 512:768]).astype(BF16)
        for i in range(tokens // quarter):

            @pl.when(which == i)
            def _():
                attend_back(i, (0, 1), hh)

    def near_ready(s):
        @pl.when(s == 1)
        def _():
            qg_near(1, dattn)

    def keys_values(at):
        if at == 0:
            dqkv[:, 128:256] = jnp.transpose(dk_s[0]).astype(BF16)
            dqkv[:, 256:384] = jnp.transpose(dv_s[0]).astype(BF16)
        else:
            d_v = jnp.transpose(dv_s[1]).astype(BF16)
            dqkv[:, 384:512] = jnp.where(low_half, dqkv[:, 384:512], d_v)
            dqkv[:, 640:768] = jnp.transpose(dk_s[1]).astype(BF16)

    def zero_rows(u, zo):
        cols = rows_at(zo * 2 * shard, 2 * shard, 2 * shard)
        left = normed_t[cols, :]
        if u == 0:
            gmat[0, cols, 0:384] = mm(left, dqkv[:, 0:384]).astype(BF16)
        else:
            g_qkv = mm(left, dqkv[:, 384:768])
            gmat[0, cols, 384:512] = g_qkv[:, 0:128].astype(BF16)
            gmat[0, cols, 512:768] = (g_qkv[:, 128:384] + gproj[cols, :]).astype(BF16)
        gx(u, zo).start()

    def zero_unit(u, steps):
        def step(s, carry):
            odd, half = lax.rem(s, 2), lax.div(s, 2)
            first = is_end * owner_z[2] + is_mid * owner_z[0]
            second = is_end * owner_z[1] + is_mid * owner_z[2]
            third = is_end * owner_z[0] + is_mid * owner_z[1]
            early = (1 - odd) * first + odd * second
            late = (1 - odd) * third + odd * z
            zero_rows(u, (1 - half) * early + half * late)
            return carry

        lax.fori_loop(*steps, step, 0)

    back_quarters(True, (0, 1, 2), True, near_ready)
    mid_pump(3, 2)
    mid_pump(2, 0)
    end_pump(2, 2)
    end_pump(2, 1)
    mid_pump(3, 1)
    far_rows(1, dattn, back_far, side_cross)
    keys_values(0)
    zero_unit(0, (0, 4))
    end_pump(2, 0)
    mid_pump(2, 2)
    gproj[...] = jnp.transpose(mm(mixed[...], dattn[...], TN))
    back_quarters(False, (2,), False)
    keys_values(1)
    mid_pump(2, 1)

    def first_back(which):
        rows = rows_at(which * quarter, quarter, quarter)
        d_low = dqkv[rows, :]
        part = mm(d_low, w[0], NT)
        rounded = part.astype(BF16).astype(F32)
        sm[0:1, :] = sm[0:1, :] + jnp.sum(rounded * xhat[rows, :], 0, keepdims=True)
        sm[1:2, :] = sm[1:2, :] + jnp.sum(rounded, 0, keepdims=True)
        sm[7:8, :] = sm[7:8, :] + jnp.sum(d_low.astype(F32), 0, keepdims=True)
        return part


    def first_pumps():
        end_pump(0, 2)
        mid_pump(0, 0)

    rs_quad(3, first_back, xhat2, first_pumps)
    end_pump(0, 1)

    small_c = rcopy(sm, smp, 27, 77, c_dev)
    small_c.start()
    quad_far(3, xhat2)
    rs_y_start(3)
    small_c.wait_recv()
    smx[0, 0:6, :] = sm[0:6, :] + smp[0:6, :]
    smx[0, 6:8, :] = smp[6:8, :]
    small_x = rcopy(smx.at[0], smx.at[1], 24, 74, cross_dev)
    small_x.start()
    end_pump(0, 0)
    zero_unit(1, (0, 4))
    quad_near(3)
    mid_pump(0, 2)
    small_x.wait_recv()
    smz[z, 0:6, :] = smx[0, 0:6, :] + smx[1, 0:6, :]
    smz[z, 6:8, :] = sm[6:8, :] + smx[1, 6:8, :]

    def small_z(j):
        return rcopy(smz.at[z], smz.at[z], 25, 75, z_dev(j))

    for j in (3, 2, 1):
        small_z(j).start()
    mid_pump(0, 1)
    g_finish(3)
    side_finish()
    g_finish(2)
    for hh in range(2):
        half = halves[hh]
        mid[half, :] = mid[half, :] + BRANCH_SCALE * (rs_result(2, hh) + vec[5])
    put_out = pltpu.make_async_copy(mid, out_o, lsem.at[8])
    put_out.start()
    end_pump(1, 2)
    mid_pump(1, 0)
    end_pump(1, 1)

    def first_norm_back(hh):
        half = halves[hh]
        mine_h = rows_at(ten * quarter + hh * (quarter // 2), quarter // 2, quarter // 2)
        d_normed = rs_result(3, hh)
        scaled = xhat[mine_h, :]
        weighted = d_normed * gain_one
        xhat2[half, :] = fin[1, half, :] + inv1[mine_h, :] * (
            weighted
            - jnp.mean(weighted, -1, keepdims=True)
            - scaled * jnp.mean(weighted * scaled, -1, keepdims=True)
        )

    first_norm_back(0)
    end_pump(1, 0)
    three = rcopy(smz.at[0:3], smz.at[0:3], 25, 75, x_dev)
    three.wait_recv()
    smy[0] = (smz[0] + smz[1]) + (smz[2] + smz[3])
    small_y = rcopy(smy.at[0], smy.at[1], 26, 76, y_dev)
    small_y.start()
    mid_pump(1, 2)
    first_norm_back(1)
    put_grad = pltpu.make_async_copy(xhat2, grad_o, lsem.at[9])
    put_grad.start()
    mid_pump(1, 1)
    for u in range(4):
        ag_drain(u)
    three_sides = side_r.at[0:3]
    rcopy(three_sides, three_sides, 28, 78, x_dev).wait_send()
    side_x().wait_send()
    rcopy(ysend, yrecv, 20, 24, y_dev).wait_send()
    for k in (2, 3):
        for half in range(2):
            rs_core(k, half).wait_send()
    for send in (21, 22, 23):
        qg_rows(hidden, 2 * quarter, send, 36).wait_send()
    small_x.wait_send()
    three.wait_send()
    g_finish(0)
    for u in (3, 2, 0):
        g_drain(u)
    small_y.wait_recv()
    small_c.wait_send()
    sm[0:6, :] = smy[0, 0:6, :] + smy[1, 0:6, :]
    sm[6:8, :] = smy[0, 6:8, :]
    put_small = pltpu.make_async_copy(sm, small_o, lsem.at[10])
    put_small.start()
    g_finish(1)

    g_drain(1)
    small_y.wait_send()
    for made in (put_out, put_grad, put_small):
        made.wait()


def run_block(resid, cotangent, win, wout, bias, vec, rows, n_dp):
    tokens, width = resid.shape
    quarter = tokens // 4
    head_cols = win.shape[2]
    heads = head_cols // HD
    sizes = (tokens, width, quarter, heads, rows)
    vm = pltpu.VMEM
    scratch = [
        vm(win.shape, F32),
        vm(wout.shape, F32),
        vm(bias.shape, F32),
        vm(vec.shape, F32),
        vm((tokens, width), F32),
        vm((tokens, width), F32),
        vm((tokens, 1), F32),
        vm((tokens, width), BF16),
        vm((tokens, width), BF16),
        vm((3, width, width), BF16),
        vm((heads, tokens, 2 * HD), BF16),
        vm((2, tokens, 2 * HD), BF16),
        vm((2, tokens, 2 * HD), BF16),
        vm((heads, tokens, tokens), BF16),
        vm((heads, tokens, 1), F32),
        vm((tokens, 256), BF16),
        vm((2, 2, quarter, width), BF16),
        vm((4, 2, quarter, width), BF16),
        vm((3, quarter, width), F32),
        vm((4, quarter, width), BF16),
        vm((4, quarter, width), BF16),
        vm((quarter, width), F32),
        vm((quarter, width), F32),
        vm((quarter, 1), F32),
        vm((width, tokens), BF16),
        vm((tokens, width), BF16),
        vm((tokens, width), BF16),
        vm((tokens, width), BF16),
        vm((tokens, width), BF16),
        vm((tokens, 256), BF16),
        vm((2, 2 * HD, tokens), F32),
        vm((2, 2 * HD, tokens), F32),
        vm((tokens, width), BF16),
        vm((width, 256), F32),
        vm((3, width, width), BF16),
        vm((3, 4, rows, width), BF16),
        vm((3, 3, rows, width), BF16),
        vm((3, 4, rows, width), BF16),
        vm((4, 2 * rows, width // 2), BF16),
        vm((2, 2 * rows, width // 2), BF16),
        vm((rows, width // 2), BF16),
        vm((rows, width // 2), BF16),
        vm((3, rows, width), F32),
        vm((8, width), F32),
        vm((8, width), F32),
        vm((2, 8, width), F32),
        vm((4, 8, width), F32),
        vm((2, 8, width), F32),
        pltpu.SemaphoreType.DMA((13,)),
        pltpu.SemaphoreType.DMA((30,)),
        pltpu.SemaphoreType.DMA((83,)),
    ]
    return pl.pallas_call(
        functools.partial(block_kernel, sizes),
        out_shape=(
            jax.ShapeDtypeStruct((quarter, width), F32),
            jax.ShapeDtypeStruct((quarter, width), F32),
            jax.ShapeDtypeStruct((3, rows, width), F32),
            jax.ShapeDtypeStruct((8, width), F32),
        ),
        in_specs=[pl.BlockSpec(memory_space=pl.ANY)] * 6,
        out_specs=[pl.BlockSpec(memory_space=pl.ANY)] * 4,
        scratch_shapes=scratch,
        compiler_params=pltpu.CompilerParams(
            collective_id=1, has_side_effects=True, vmem_limit_bytes=62 << 20
        ),
        name="block",
    )(resid, cotangent, win, wout, bias, vec)


BLOCK_ZERO = (((0, 128), (384, 448)), ((128, 256), (640, 704)), ((256, 384), (448, 512)), ((512, 640), (704, 768)))


def adam_kernel(hc, *refs):
    passed_h, gsum_h, small_h = refs[0:2], refs[2], refs[3]
    in_h, out_h, bias_h, vec_h = refs[4:7], refs[7:10], refs[10:13], refs[13:16]
    passed_o, in_o, out_o, bias_o, vec_o = refs[16:18], refs[18:21], refs[21:24], refs[24:27], refs[27:30]
    vin, vout, vbias, vvec, rin, rout, rbias, rvec, gsum, small, passed, sems = refs[30:42]

    def copy(src, dst, sem):
        pltpu.make_async_copy(src, dst, sems.at[sem]).start()

    def wait(ref, sem):
        pltpu.make_async_copy(ref, ref, sems.at[sem]).wait()

    def columns(ref, rows, kind):
        return jnp.concatenate([ref[rows + (slice(a, b),)] for a, b in BLOCK_ZERO[kind]], 1)

    every = slice(None)
    kinds_in = (3, 4, 5, 6, 0, 1, 2)
    copy(gsum_h.at[1], gsum.at[1], 0)
    for i in kinds_in:
        if i == 5:
            for a in range(2):
                copy(passed_h[a], passed.at[a], 18)
        for a in range(3):
            copy(in_h[a].at[i], vin.at[i, a], 3 + i)
        if i == 6:
            copy(gsum_h.at[0], gsum.at[0], 1)
    copy(small_h, small, 15)
    for a in range(3):
        copy(bias_h[a], vbias.at[a], 16)
        copy(vec_h[a], vvec.at[a], 17)
    copy(gsum_h.at[2], gsum.at[2], 2)
    for i in range(5):
        for a in range(3):
            copy(out_h[a].at[i], vout.at[i, a], 10 + i)

    wait(gsum.at[1], 0)
    for i in kinds_in:
        wait(vin.at[i], 3 + i)
        if i == 0:
            wait(gsum.at[0], 1)
        part = columns(gsum, (0, every), i) if i < 3 else gsum[1, :, (i - 3) * hc : (i - 2) * hc]
        new = adam_step(vin[i, 0], vin[i, 1], vin[i, 2], part, 0.5 * D ** (-0.5), DECAY)
        for a in range(3):
            rin[i, a] = new[a]
            copy(rin.at[i, a], in_o[a].at[i], 19)
    wait(passed, 18)
    for a in range(2):
        copy(passed.at[a], passed_o[a], 23)
    wait(small, 15)
    wait(vbias, 16)
    wait(vvec, 17)
    for i in range(6):
        new = adam_step(vvec[0, i], vvec[1, i], vvec[2, i], small[i : i + 1, :], SMALL_RATE, 0.0)
        for a in range(3):
            rvec[a, i] = new[a]
        if i < 2:
            part = columns(small, (slice(7, 8),), 2 * i)
        else:
            part = small[6:7, (i - 2) * hc : (i - 1) * hc]
        new = adam_step(vbias[0, i], vbias[1, i], vbias[2, i], part, SMALL_RATE, 0.0)
        for a in range(3):
            rbias[a, i] = new[a]
    for a in range(3):
        copy(rbias.at[a], bias_o[a], 20)
        copy(rvec.at[a], vec_o[a], 21)
    wait(gsum.at[2], 2)
    for i in range(5):
        wait(vout.at[i], 10 + i)
        part = columns(gsum, (0, every), 3) if i == 0 else gsum[2, :, (i - 1) * hc : i * hc]
        part = jnp.transpose(part)
        new = adam_step(vout[i, 0], vout[i, 1], vout[i, 2], part, 2.0 * D ** (-0.5), DECAY)
        for a in range(3):
            rout[i, a] = new[a]
            copy(rout.at[i, a], out_o[a].at[i], 22)
    for ref, sem in ((rin, 19), (rbias, 20), (rvec, 21), (rout, 22), (passed, 23)):
        wait(ref, sem)


def run_adam(*operands):
    hc = operands[4].shape[2]
    out_rows, _, g_sum, small = operands[0:4]
    shapes = [out_rows, out_rows, *operands[4:16]]
    hbm = pl.BlockSpec(memory_space=pl.ANY)
    kinds_in, kinds_out = operands[4].shape, operands[7].shape
    small_bias, small_vec = operands[10].shape, operands[13].shape
    big = [
        pltpu.VMEM((kinds_in[0], 3, *kinds_in[1:]), F32),
        pltpu.VMEM((kinds_out[0], 3, *kinds_out[1:]), F32),
        pltpu.VMEM((3, *small_bias), F32),
        pltpu.VMEM((3, *small_vec), F32),
    ]
    return pl.pallas_call(
        functools.partial(adam_kernel, hc),
        out_shape=[jax.ShapeDtypeStruct(a.shape, F32) for a in shapes],
        in_specs=[hbm] * 16,
        out_specs=[hbm] * 14,
        scratch_shapes=big * 2
        + [pltpu.VMEM(g_sum.shape, F32), pltpu.VMEM(small.shape, F32)]
        + [pltpu.VMEM((2, *out_rows.shape), F32), pltpu.SemaphoreType.DMA((24,))],
        compiler_params=pltpu.CompilerParams(vmem_limit_bytes=62 << 20),
        name="adam",
    )(*operands)


def fused_shards(
    resid,
    cotangent,
    master_in,
    moment1_in,
    moment2_in,
    master_out,
    moment1_out,
    moment2_out,
    master_bias,
    moment1_bias,
    moment2_bias,
    master_vec,
    moment1_vec,
    moment2_vec,
):
    rows = master_in.shape[1]
    hc = master_in.shape[3]
    turned = [jnp.transpose(a[0], (1, 0, 2)) for a in (master_in, moment1_in, moment2_in)]
    plain = [a[0] for a in (master_out, moment1_out, moment2_out)]
    biases = [a.reshape(6, 1, hc) for a in (master_bias, moment1_bias, moment2_bias)]
    vectors = [a.reshape(6, 1, D) for a in (master_vec, moment1_vec, moment2_vec)]
    sums = run_block(
        resid, cotangent, turned[0], plain[0], biases[0], vectors[0], rows, lax.axis_size("dp")
    )
    new = run_adam(*sums, *turned, *plain, *biases, *vectors)
    return (
        new[0],
        new[1],
        *[jnp.transpose(a, (1, 0, 2))[None] for a in new[2:5]],
        *[a[None] for a in new[5:8]],
        *[a.reshape(1, 6, hc) for a in new[8:11]],
        *[a.reshape(1, 6, D) for a in new[11:14]],
    )


def solution(mesh):
    fused = mesh.shape["dp"] == 8 and mesh.shape["tensor"] == 4
    return jax.shard_map(
        fused_shards if fused else shards,
        mesh=mesh,
        in_specs=(
            P("dp", None),
            P("dp", None),
            P(None, "dp", None, "tensor"),
            P(None, "dp", None, "tensor"),
            P(None, "dp", None, "tensor"),
            P(None, None, "tensor", "dp"),
            P(None, None, "tensor", "dp"),
            P(None, None, "tensor", "dp"),
            P(None, None, "tensor"),
            P(None, None, "tensor"),
            P(None, None, "tensor"),
            P(),
            P(),
            P(),
        ),
        out_specs=(
            P(("dp", "tensor"), None),
            P(("dp", "tensor"), None),
            P(None, "dp", None, "tensor"),
            P(None, "dp", None, "tensor"),
            P(None, "dp", None, "tensor"),
            P(None, None, "tensor", "dp"),
            P(None, None, "tensor", "dp"),
            P(None, None, "tensor", "dp"),
            P(None, None, "tensor"),
            P(None, None, "tensor"),
            P(None, None, "tensor"),
            P(),
            P(),
            P(),
        ),
        check_vma=False,
    )
```

```python
import functools

import jax
import jax.numpy as jnp
from jax import lax
from jax.experimental import pallas as pl
from jax.experimental.pallas import tpu as pltpu
from jax.sharding import PartitionSpec as P

D = 768
HD = 64
LEN = 1024
LAYERS = 1
STEP = 10


EPS = 1e-05
BRANCH_SCALE = 48 ** (-0.5)
BETA_ONE = 0.9
BETA_TWO = 0.95
ADAM_EPS = 1e-08
DECAY = 0.1
SMALL_RATE = 0.3
MASKED = -1e30


def norm_rows(stream, gain, shift):
    center = stream - jnp.mean(stream, -1, keepdims=True)
    inverse = lax.rsqrt(jnp.mean(center * center, -1, keepdims=True) + EPS)
    scaled = center * inverse
    return (scaled * gain + shift, scaled, inverse)


def norm_back(grad_out, scaled, inverse, gain):
    weighted = grad_out * gain
    centered = weighted - jnp.mean(weighted, -1, keepdims=True)
    return inverse * (centered - scaled * jnp.mean(weighted * scaled, -1, keepdims=True))


def plain_dot(left, right):
    return jnp.dot(left, right, preferred_element_type=jnp.float32)


def left_dot(left, right):
    return lax.dot_general(
        left, right, (((0,), (0,)), ((), ())), preferred_element_type=jnp.float32
    )


def right_dot(left, right):
    return lax.dot_general(
        left, right, (((1,), (1,)), ((), ())), preferred_element_type=jnp.float32
    )


def smooth_gate(values_in):
    return jax.nn.gelu(values_in, approximate=True)


def tensor_rows(array_in):
    quarter = array_in.shape[0] // lax.axis_size("tensor")
    return lax.dynamic_slice_in_dim(array_in, lax.axis_index("tensor") * quarter, quarter, 0)


def own_rows(array_in):
    return tensor_rows(array_in)


def branch_total(partial_sum):
    return lax.psum(partial_sum.astype(jnp.bfloat16), "tensor").astype(jnp.float32)


def grad_total(partial_sum):
    return lax.psum(partial_sum.astype(jnp.bfloat16), "tensor").astype(jnp.float32)


def causal_scores(queries, key_rows, first, last):
    block_rows = last - first
    scores = jnp.einsum(
        "qhd,khd->hqk", queries[first:last], key_rows[:last], preferred_element_type=jnp.float32
    ) * HD ** (-0.5)
    query_pos = lax.broadcasted_iota(jnp.int32, (block_rows, last), 0) + first
    key_pos = lax.broadcasted_iota(jnp.int32, (block_rows, last), 1)
    return jnp.where(query_pos >= key_pos, scores, MASKED)


def attend_sequence(operands):
    queries, key_rows, value_rows = operands
    block_rows = min(512, LEN)
    outputs = []
    totals = []
    for block_idx in range(LEN // block_rows):
        first = block_idx * block_rows
        last = first + block_rows
        scores = causal_scores(queries, key_rows, first, last)
        highest = jnp.max(scores, -1, keepdims=True)
        expo = jnp.exp(scores - highest)
        summed = jnp.sum(expo, -1, keepdims=True)
        weights = (expo / summed).astype(jnp.bfloat16)
        mixed = jnp.einsum(
            "hqk,khd->qhd", weights, value_rows[:last], preferred_element_type=jnp.float32
        )
        outputs.append(mixed.astype(jnp.bfloat16))
        totals.append((highest + jnp.log(summed))[..., 0])
    return (jnp.concatenate(outputs, 0), jnp.concatenate(totals, 1))


def attend_back(operands):
    queries, key_rows, value_rows, log_total, grad_mixed = operands
    block_rows = min(512, LEN)
    d_keys = jnp.zeros(key_rows.shape, jnp.float32)
    d_values = jnp.zeros(value_rows.shape, jnp.float32)
    d_queries = []
    for block_idx in range(LEN // block_rows):
        first = block_idx * block_rows
        last = first + block_rows
        scores = causal_scores(queries, key_rows, first, last)
        probs = jnp.exp(scores - log_total[:, first:last, None])
        d_probs = jnp.einsum(
            "qhd,khd->hqk",
            grad_mixed[first:last],
            value_rows[:last],
            preferred_element_type=jnp.float32,
        )
        inner = jnp.sum(probs * d_probs, -1, keepdims=True)
        d_scores = (probs * (d_probs - inner)).astype(jnp.bfloat16)
        d_queries.append(
            jnp.einsum(
                "hqk,khd->qhd", d_scores, key_rows[:last], preferred_element_type=jnp.float32
            )
            * HD ** (-0.5)
        )
        key_part = jnp.einsum(
            "hqk,qhd->khd", d_scores, queries[first:last], preferred_element_type=jnp.float32
        ) * HD ** (-0.5)
        value_part = jnp.einsum(
            "hqk,qhd->khd",
            probs.astype(jnp.bfloat16),
            grad_mixed[first:last],
            preferred_element_type=jnp.float32,
        )
        d_keys = d_keys.at[:last].add(key_part)
        d_values = d_values.at[:last].add(value_part)
    return (jnp.concatenate(d_queries, 0), d_keys, d_values)


def layer_forward(stream, w_in, w_out, bias, vector):
    model_width = w_in.shape[0]
    head_cols = w_in.shape[2]
    heads_here = head_cols // HD
    normed, scaled_one, inverse_one = norm_rows(stream, vector[0], vector[1])
    normed_low = normed.astype(jnp.bfloat16)
    seq_count = normed_low.shape[0] // LEN
    shape4 = (seq_count, LEN, heads_here, HD)
    w_qkv = w_in[:, 0:3].reshape(model_width, 3 * head_cols)
    projected = plain_dot(normed_low, w_qkv)
    queries = (projected[:, :head_cols] + bias[0]).astype(jnp.bfloat16).reshape(shape4)
    key_rows = projected[:, head_cols : 2 * head_cols].astype(jnp.bfloat16).reshape(shape4)
    value_rows = (projected[:, 2 * head_cols :] + bias[1]).astype(jnp.bfloat16).reshape(shape4)
    mixed, log_total = lax.map(attend_sequence, (queries, key_rows, value_rows))
    mixed_low = mixed.reshape(-1, head_cols)
    attended = branch_total(plain_dot(mixed_low, w_out[0])) + vector[4]
    middle = stream + BRANCH_SCALE * attended
    hidden, scaled_two, inverse_two = norm_rows(middle, vector[2], vector[3])
    hidden_low = hidden.astype(jnp.bfloat16)
    w_up = w_in[:, 3:].reshape(model_width, 4 * head_cols)
    pre_act = plain_dot(hidden_low, w_up) + bias[2:].reshape(4 * head_cols)
    act_low = smooth_gate(pre_act).astype(jnp.bfloat16)
    w_down = w_out[1:].reshape(4 * head_cols, model_width)
    mlp_out = branch_total(plain_dot(act_low, w_down)) + vector[5]
    result = middle + BRANCH_SCALE * mlp_out
    kept = (
        scaled_one,
        inverse_one,
        normed_low,
        queries,
        key_rows,
        value_rows,
        log_total,
        mixed_low,
        scaled_two,
        inverse_two,
        hidden_low,
        pre_act,
        act_low,
    )
    return (result, kept)


def layer_backward(gradient, w_in, w_out, vector, kept):
    (
        scaled_one,
        inverse_one,
        normed_low,
        queries,
        key_rows,
        value_rows,
        log_total,
        mixed_low,
        scaled_two,
        inverse_two,
        hidden_low,
        pre_act,
        act_low,
    ) = kept
    model_width = w_in.shape[0]
    head_cols = w_in.shape[2]
    w_qkv = w_in[:, 0:3].reshape(model_width, 3 * head_cols)
    w_up = w_in[:, 3:].reshape(model_width, 4 * head_cols)
    w_down = w_out[1:].reshape(4 * head_cols, model_width)
    d_mlp = (BRANCH_SCALE * gradient).astype(jnp.bfloat16)
    g_bdown = jnp.sum(own_rows(d_mlp).astype(jnp.float32), 0)
    g_down = left_dot(act_low, d_mlp).reshape(4, head_cols, model_width)
    d_act = right_dot(d_mlp, w_down).astype(jnp.bfloat16)
    gate_value, gate_pull = jax.vjp(smooth_gate, pre_act)
    d_pre = gate_pull(d_act.astype(jnp.float32))[0].astype(jnp.bfloat16)
    g_bup = jnp.sum(d_pre.astype(jnp.float32), 0)
    g_up = left_dot(hidden_low, d_pre).reshape(model_width, 4, head_cols)
    d_hidden = grad_total(right_dot(d_pre, w_up))
    g_gain_two = jnp.sum(own_rows(d_hidden * scaled_two), 0)
    g_shift_two = jnp.sum(own_rows(d_hidden), 0)
    d_middle = gradient + norm_back(d_hidden, scaled_two, inverse_two, vector[2])
    d_attn = (BRANCH_SCALE * d_middle).astype(jnp.bfloat16)
    g_bproj = jnp.sum(own_rows(d_attn).astype(jnp.float32), 0)
    g_proj = left_dot(mixed_low, d_attn)
    d_mixed = right_dot(d_attn, w_out[0]).astype(jnp.bfloat16)
    d_queries, d_keys, d_values = lax.map(
        attend_back, (queries, key_rows, value_rows, log_total, d_mixed.reshape(queries.shape))
    )
    d_qkv = jnp.concatenate(
        [
            d_queries.reshape(-1, head_cols),
            d_keys.reshape(-1, head_cols),
            d_values.reshape(-1, head_cols),
        ],
        1,
    ).astype(jnp.bfloat16)
    g_qkv = left_dot(normed_low, d_qkv).reshape(model_width, 3, head_cols)
    g_bq = jnp.sum(d_qkv[:, :head_cols].astype(jnp.float32), 0)
    g_bv = jnp.sum(d_qkv[:, 2 * head_cols :].astype(jnp.float32), 0)
    d_normed = grad_total(right_dot(d_qkv, w_qkv))
    g_gain_one = jnp.sum(own_rows(d_normed * scaled_one), 0)
    g_shift_one = jnp.sum(own_rows(d_normed), 0)
    d_stream = d_middle + norm_back(d_normed, scaled_one, inverse_one, vector[0])
    g_in = jnp.concatenate([g_qkv, g_up], 1)
    g_out = jnp.concatenate([g_proj[None], g_down], 0)
    g_bias = jnp.concatenate([g_bq[None], g_bv[None], g_bup.reshape(4, head_cols)], 0)
    g_vector = jnp.stack([g_gain_one, g_shift_one, g_gain_two, g_shift_two, g_bproj, g_bdown])
    return (d_stream, g_in, g_out, g_bias, g_vector)


def adam_step(master, first, second, gradient, rate, decay):
    first_new = BETA_ONE * first + (1 - BETA_ONE) * gradient
    second_new = BETA_TWO * second + (1 - BETA_TWO) * gradient * gradient
    direction = (
        first_new / (1 - BETA_ONE**STEP) / (jnp.sqrt(second_new / (1 - BETA_TWO**STEP)) + ADAM_EPS)
    )
    return (first_new, second_new, master - rate * (direction + decay * master))


def shards(
    resid,
    cotangent,
    master_in,
    moment1_in,
    moment2_in,
    master_out,
    moment1_out,
    moment2_out,
    master_bias,
    moment1_bias,
    moment2_bias,
    master_vec,
    moment1_vec,
    moment2_vec,
):
    weights_in, weights_out = (
        lax.all_gather(master_in.astype(jnp.bfloat16), "dp", axis=1, tiled=True),
        lax.all_gather(master_out.astype(jnp.bfloat16), "dp", axis=3, tiled=True),
    )
    stream = resid
    gradient = cotangent
    layer_idx = 0
    stream, kept = layer_forward(
        stream,
        weights_in[layer_idx],
        weights_out[layer_idx],
        master_bias[layer_idx],
        master_vec[layer_idx],
    )
    kept_list = [kept]
    list_in = [None] * LAYERS
    list_out = [None] * LAYERS
    list_bias = [None] * LAYERS
    list_vector = [None] * LAYERS
    layer_idx = 0
    gradient, g_in, g_out, g_bias, g_vector = layer_backward(
        gradient,
        weights_in[layer_idx],
        weights_out[layer_idx],
        master_vec[layer_idx],
        kept_list[layer_idx],
    )
    list_in[layer_idx] = g_in
    list_out[layer_idx] = g_out
    list_bias[layer_idx] = g_bias
    list_vector[layer_idx] = g_vector
    summed_in = jnp.stack(list_in)
    summed_out = jnp.stack(list_out)
    summed_in, summed_out = (
        lax.psum_scatter(summed_in, "dp", scatter_dimension=1, tiled=True),
        lax.psum_scatter(summed_out, "dp", scatter_dimension=3, tiled=True),
    )
    summed_bias = lax.psum(jnp.stack(list_bias), "dp")
    summed_vector = lax.psum(jnp.stack(list_vector), ("dp", "tensor"))
    first_in, second_in, new_in = adam_step(
        master_in, moment1_in, moment2_in, summed_in, 0.5 * D ** (-0.5), DECAY
    )
    first_out, second_out, new_out = adam_step(
        master_out, moment1_out, moment2_out, summed_out, 2.0 * D ** (-0.5), DECAY
    )
    first_bias, second_bias, new_bias = adam_step(
        master_bias, moment1_bias, moment2_bias, summed_bias, SMALL_RATE, 0.0
    )
    first_vec, second_vec, new_vec = adam_step(
        master_vec, moment1_vec, moment2_vec, summed_vector, SMALL_RATE, 0.0
    )
    return (
        own_rows(stream),
        own_rows(gradient),
        first_in,
        second_in,
        new_in,
        first_out,
        second_out,
        new_out,
        first_bias,
        second_bias,
        new_bias,
        first_vec,
        second_vec,
        new_vec,
    )


MESH_IDS = pl.DeviceIdType.MESH
F32 = jnp.float32
BF16 = jnp.bfloat16
NN = (((1,), (0,)), ((), ()))
NT = (((1,), (1,)), ((), ()))
TN = (((0,), (0,)), ((), ()))
GELU_A = (2.0 / 3.141592653589793) ** 0.5
GELU_B = 0.044715


def mm(left, right, dims=NN):
    return lax.dot_general(left, right, dims, preferred_element_type=F32)


def rows_at(start, size, align):
    return pl.ds(pl.multiple_of(start, align), size)


def block_kernel(
    sizes,
    resid_h,
    cot_h,
    win_h,
    wout_h,
    bias_h,
    vec_h,
    out_o,
    grad_o,
    gsum_o,
    small_o,
    win,
    wout,
    bias,
    vec,
    resid,
    cot,
    inv1,
    normed,
    dmlp,
    w,
    q_s,
    k_s,
    v_s,
    e_s,
    linv,
    mixed,
    ps,
    crecv,
    fin,
    ysend,
    yrecv,
    mid,
    xhat2,
    inv2,
    normed_t,
    hidden,
    act_s,
    dpre,
    dattn,
    dmix,
    dk_s,
    dv_s,
    dqkv,
    gproj,
    gmat,
    xr,
    zs,
    zr,
    side_r,
    side_s,
    side_xs,
    side_xr,
    gsum,
    sm,
    smp,
    smx,
    smz,
    smy,
    lsem,
    ssem,
    rsem,
):
    tokens, width, quarter, heads, shard = sizes
    dp = lax.axis_index("dp")
    ten = lax.axis_index("tensor")
    z = lax.div(dp, 2)
    x = lax.rem(dp, 2)
    y = lax.div(ten, 2)
    c = lax.rem(ten, 2)
    x_dev = (dp + 1 - 2 * x, ten)
    c_dev = (dp, ten + 1 - 2 * c)
    y_dev = (dp, ten + 2 - 4 * y)

    def z_other(j):
        if j == 1:
            return z + 1 - 2 * lax.rem(z, 2)
        if j == 2:
            return lax.rem(z + 2, 4)
        return 3 - z

    def z_dev(j):
        return (2 * z_other(j) + x, ten)

    def rcopy(src, dst, send_idx, recv_idx, dev):
        return pltpu.make_async_remote_copy(
            src_ref=src,
            dst_ref=dst,
            send_sem=ssem.at[send_idx],
            recv_sem=rsem.at[recv_idx],
            device_id=dev,
            device_id_type=MESH_IDS,
        )

    barrier = pltpu.get_barrier_semaphore()
    cross_dev = (dp + 1 - 2 * x, ten + 1 - 2 * c)
    peers = [x_dev, c_dev, y_dev, cross_dev, z_dev(1), z_dev(2), z_dev(3)]
    for dev in peers:
        pl.semaphore_signal(barrier, inc=1, device_id=dev, device_id_type=MESH_IDS)
    load_win = pltpu.make_async_copy(win_h, win, lsem.at[2])
    load_wout = pltpu.make_async_copy(wout_h, wout, lsem.at[3])
    load_win.start()
    load_wout.start()
    load_resid = pltpu.make_async_copy(resid_h, resid, lsem.at[0])
    load_cot = pltpu.make_async_copy(cot_h, cot, lsem.at[1])
    load_vec = pltpu.make_async_copy(vec_h, vec, lsem.at[11])
    load_bias = pltpu.make_async_copy(bias_h, bias, lsem.at[12])
    load_vec.start()
    load_resid.start()
    load_cot.start()
    load_bias.start()

    mine = rows_at(dp * shard, shard, shard)
    load_win.wait()
    load_wout.wait()
    out_t = [jnp.transpose(wout[i]) for i in range(5)]
    pairs, last = slice(0, 2 * HD), slice(2 * HD, 3 * HD)
    tiles = [win[0, :, pairs], win[1, :, pairs], win[2, :, pairs], win[0, :, last], win[2, :, last]]
    tiles += [out_t[0][:, pairs], win[1, :, last], out_t[0][:, last]]
    w[0, mine, :] = jnp.concatenate(tiles, 1).astype(BF16)

    pl.semaphore_wait(barrier, len(peers))

    half_cols = width // 2
    units = (
        (0, slice(0, half_cols)),
        (0, slice(half_cols, width)),
        (1, slice(0, width)),
        (2, slice(0, width)),
    )

    is_end = 1 - lax.rem(lax.div(z + 1, 2), 2)
    is_mid = 1 - is_end
    upper = lax.div(z, 2)
    owner_z = (z_other(1), 2 - upper, 3 - 3 * upper)
    pair_dev, mid_dev = (2 * owner_z[0] + x, ten), (2 * owner_z[1] + x, ten)

    def ag_copy(u, zi, send, recv, dev):
        b, cols = units[u]
        src = w.at[b, rows_at((2 * zi + x) * shard, shard, shard), cols]
        return rcopy(src, src, send + u, recv, dev)

    def ag_pair(u):
        return ag_copy(u, z, 4, 3 * u, pair_dev)

    def ag_mid(u):
        return ag_copy(u, z, 4, 3 * u + 1, mid_dev)

    def ag_end_far(u, i):
        dev = (2 * owner_z[i] + x, ten)
        return ag_copy(u, z, 4, 3 * u + 2, dev)

    def ag_onward(u, i):
        if i == 0:
            return ag_copy(u, owner_z[0], 4, 3 * u + 2, mid_dev)
        return ag_copy(u, owner_z[i], 4, 3 * u + i, pair_dev)

    def ag_x(u, i):
        return ag_copy(u, z if i == 0 else owner_z[i - 1], 0, 12 + u, x_dev)

    def ag_bytes(u, pieces, send, recv):
        b, cols = units[u]
        ref = w.at[b, 0 : pieces * shard, cols]
        return rcopy(ref, ref, send, recv, x_dev)

    def mid_start(u):
        @pl.when(is_mid == 1)
        def _():
            ag_pair(u).start()
            ag_mid(u).start()

    def ag_arrive(u, i):
        ag_copy(u, owner_z[i], 0, 3 * u + i, x_dev).wait_recv()

    def pump_end(u, i):
        @pl.when(is_end == 1)
        def _():
            ag_arrive(u, i)
            ag_x(u, 1 + i).start()

    def pump_mid(u, i):
        @pl.when(is_mid == 1)
        def _():
            ag_arrive(u, i)
            if u > 1 or i == 1:
                ag_onward(u, i).start()
            ag_x(u, 1 + i).start()

    def mid_onward(u, i):
        @pl.when(is_mid == 1)
        def _():
            ag_arrive(u, i)
            ag_onward(u, i).start()

    def mid_x(u, i):
        @pl.when(is_mid == 1)
        def _():
            ag_x(u, i).start()

    def ag_finish(u):
        ag_bytes(u, 4, u, 12 + u).wait_recv()

    def ag_drain(u):
        ag_bytes(u, 4, u, 12 + u).wait_send()

        if u < 2:
            ag_bytes(u, 3, 4 + u, 12 + u).wait_send()
            return

        @pl.when(is_end == 1)
        def _():
            ag_bytes(u, 1, 4 + u, 12 + u).wait_send()

        @pl.when(is_mid == 1)
        def _():
            ag_bytes(u, 5, 4 + u, 12 + u).wait_send()

    ag_x(0, 0).start()
    ag_x(1, 0).start()
    mid_start(0)
    mid_start(1)

    @pl.when(is_end == 1)
    def _():
        for u in range(2):
            ag_pair(u).start()
            ag_end_far(u, 2).start()
            ag_end_far(u, 1).start()

    w[1, mine, :] = jnp.concatenate([win[3 + i] for i in range(4)], 1).astype(BF16)
    w[2, mine, :] = jnp.concatenate(out_t[1:], 1).astype(BF16)

    load_vec.wait()
    load_bias.wait()
    load_resid.wait()
    load_cot.wait()
    gain_one, shift_one = vec[0], vec[1]

    own = rows_at(ten * quarter, quarter, quarter)
    mid[...] = resid[own, :]
    xhat = resid

    def first_norm(r, carry):
        rows = rows_at(r * 128, 128, 128)
        part = resid[rows, :]
        center = part - jnp.mean(part, -1, keepdims=True)
        inverse = lax.rsqrt(jnp.mean(center * center, -1, keepdims=True) + EPS)
        scaled = center * inverse
        xhat[rows, :] = scaled
        inv1[rows, :] = inverse
        normed[rows, :] = (scaled * gain_one + shift_one).astype(BF16)
        dmlp[rows, :] = (cot[rows, :] * BRANCH_SCALE).astype(BF16)
        return carry

    lax.fori_loop(0, tokens // 128, first_norm, 0)
    for u, i in ((0, 0), (0, 1), (1, 1), (0, 2), (1, 0)):
        pump_mid(u, i)
    mid_start(2)
    pump_mid(1, 2)
    pump_end(0, 0)
    pump_end(1, 0)

    @pl.when(is_end == 1)
    def _():
        ag_pair(2).start()

    for u, i in ((0, 2), (0, 1), (1, 1), (1, 2)):
        pump_end(u, i)

    @pl.when(is_end == 1)
    def _():
        ag_pair(3).start()

    ag_x(2, 0).start()

    sm[...] = jnp.zeros_like(sm)
    sm[5:6, :] = jnp.sum(dmlp[own, :].astype(F32), 0, keepdims=True)
    mixed[...] = jnp.zeros_like(mixed)
    dqkv[...] = jnp.zeros_like(dqkv)
    dk_s[...] = jnp.zeros_like(dk_s)
    dv_s[...] = jnp.zeros_like(dv_s)

    hc = heads * HD
    low_half = lax.broadcasted_iota(jnp.int32, (1, 2 * HD), 1) < HD
    bias_v01, bias_q01 = bias[1, :, pairs], bias[0, :, pairs]
    bias_q2v2 = jnp.concatenate([bias[0, :, last], bias[1, :, last]], 1)
    eighth = HD**-0.5

    def project_pair(r):
        rows = slice(r * 256, (r + 1) * 256)
        got = mm(normed[rows, :], w[0, :, 0:384])
        queries = (got[:, 0:128] + bias_q01).astype(BF16).astype(F32) * eighth
        q_s[0, rows, :] = jnp.where(low_half, queries, 0.0).astype(BF16)
        q_s[1, rows, :] = jnp.where(low_half, 0.0, queries).astype(BF16)
        k_s[0, rows, :] = got[:, 128:256].astype(BF16)
        v_s[0, rows, :] = (got[:, 256:384] + bias_v01).astype(BF16)

    def project_last(r):
        rows = slice(r * 256, (r + 1) * 256)
        got = mm(normed[rows, :], w[0, :, 384:768])
        both = (got[:, 0:128] + bias_q2v2).astype(BF16)
        q_s[2, rows, :] = jnp.where(low_half, both.astype(F32) * eighth, 0.0).astype(BF16)
        v_s[1, rows, :] = both
        k_s[1, rows, :] = got[:, 256:384].astype(BF16)

    ag_finish(0)
    for r in range(tokens // 256):
        project_pair(r)
    pump_end(2, 0)
    pump_mid(2, 0)
    pump_mid(2, 1)
    ag_x(3, 0).start()
    mid_start(3)

    def attend(i, which_heads):
        first, last_row = i * quarter, (i + 1) * quarter
        rows = slice(first, last_row)
        causal = lax.broadcasted_iota(jnp.int32, (quarter, quarter), 0) >= lax.broadcasted_iota(
            jnp.int32, (quarter, quarter), 1
        )
        got = {}
        for h in which_heads:
            at = h // 2
            queries = q_s[h, rows, :]
            diag = jnp.where(causal, mm(queries, k_s[at, rows, :], NT), MASKED)
            highest = jnp.max(diag, -1, keepdims=True)
            if i > 0:
                wide = mm(queries, k_s[at, 0:first, :], NT)
                highest = jnp.maximum(highest, jnp.max(wide, -1, keepdims=True))
            e_diag = jnp.exp(diag - highest)
            summed = jnp.sum(e_diag, -1, keepdims=True)
            e_diag = e_diag.astype(BF16)
            e_s[h, rows, first:last_row] = e_diag
            total = mm(e_diag, v_s[at, rows, :])
            if i > 0:
                e_wide = jnp.exp(wide - highest)
                summed = summed + jnp.sum(e_wide, -1, keepdims=True)
                e_wide = e_wide.astype(BF16)
                e_s[h, rows, 0:first] = e_wide
                total = total + mm(e_wide, v_s[at, 0:first, :])
            inverse = 1.0 / summed
            linv[h, rows, :] = inverse
            got[h] = total * inverse
        if 0 in got:
            mixed[rows, 0:128] = jnp.where(low_half, got[0], got[1]).astype(BF16)
        if 2 in got:
            mixed[rows, 128:256] = jnp.where(low_half, 0.0, got[2]).astype(BF16)

    def rs_core(k, half):
        return rcopy(ps.at[k % 2, half], crecv.at[k, half], 16 + 2 * (k % 2) + half, 16 + 2 * (k % 2) + half, c_dev)

    halves = [slice(0, quarter // 2), slice(quarter // 2, quarter)]

    def rs_y(k, hh):
        src, dst = ysend.at[k, halves[hh], :], yrecv.at[k, halves[hh], :]
        return rcopy(src, dst, 20, 20 + 2 * (k % 2) + hh, y_dev)

    def rs_y_start(k):
        for hh in range(2):
            rs_y(k, hh).start()

    def rs_pair(k, near, compute):
        half = 1 if near else 0
        def step(s, carry):
            yq = y if near else 1 - y
            part = compute(2 * yq + lax.rem(1 - s + c, 2))

            @pl.when(s == 0)
            def _():
                ps[k % 2, half] = part.astype(BF16)
                rs_core(k, half).start()

            @pl.when(s == 1)
            def _():
                rs_core(k, half).wait_recv()
                total = part + crecv[k, half].astype(F32)
                if near:
                    fin[k % 3] = total
                else:
                    ysend[k] = total.astype(BF16)
                    rs_y_start(k)

            return carry

        lax.fori_loop(0, 2, step, 0)

    def rs_quad(k, compute, held, between=None):
        for half in range(2):
            rs_core(k - 2, half).wait_send()

        def step(s, carry):
            half, odd = lax.div(s, 2), lax.rem(s, 2)
            yq = half * y + (1 - half) * (1 - y)
            if between is not None:

                @pl.when(s == 2)
                def _():
                    between()

            part = compute(2 * yq + lax.rem(1 - odd + c, 2))

            @pl.when(odd == 0)
            def _():
                ps[k % 2, half] = part.astype(BF16)
                rs_core(k, half).start()

            @pl.when(s == 1)
            def _():
                held[...] = part

            @pl.when(s == 3)
            def _():
                fin[k % 3] = part

            return carry

        lax.fori_loop(0, 4, step, 0)

    def quad_far(k, held):
        rs_core(k, 0).wait_recv()
        ysend[k] = (held[...] + crecv[k, 0].astype(F32)).astype(BF16)

    def quad_near(k):
        rs_core(k, 1).wait_recv()
        fin[k % 3] = fin[k % 3] + crecv[k, 1].astype(F32)

    def rs_result(k, hh):
        rs_y(k, hh).wait_recv()
        return fin[k % 3, halves[hh], :] + yrecv[k, halves[hh], :].astype(F32)

    def attend_quarter(which, which_heads):
        for i in range(tokens // quarter):

            @pl.when(which == i)
            def _():
                attend(i, which_heads)

    def proj(which):
        return mm(mixed[rows_at(which * quarter, quarter, quarter), :], w[0, :, 512:768], NT)

    def far_early(s, carry):
        attend_quarter(2 * (1 - y) + lax.rem(s + c, 2), (0, 1))
        return carry

    def far_proj(which):
        attend_quarter(which, (2,))
        return proj(which)

    def near_proj(which):
        attend_quarter(which, (0, 1, 2))
        return proj(which)

    lax.fori_loop(0, 2, far_early, 0)
    mid_onward(3, 0)
    ag_finish(1)
    for r in range(tokens // 256):
        project_last(r)
    rs_pair(0, False, far_proj)
    pump_end(2, 1)
    pump_mid(2, 2)
    mid_x(3, 1)
    rs_pair(0, True, near_proj)
    pump_end(2, 2)
    pump_end(3, 0)
    pump_mid(3, 1)

    def q_rows(ref, which, hh):
        return ref.at[rows_at(which * quarter + hh * (quarter // 2), quarter // 2, quarter // 2), :]

    def qg_y(g, ref, hh):
        src = q_rows(ref, ten, hh)
        return rcopy(src, src, 21, 24 + hh, y_dev)

    def qg_c(g, ref, hh):
        src = q_rows(ref, ten, hh)
        return rcopy(src, src, 22, 26, c_dev)

    def qg_f(g, ref, hh):
        src = q_rows(ref, ten + 2 - 4 * y, hh)
        return rcopy(src, src, 23, 27 + hh, c_dev)

    def qg_start(g, ref, hh):
        qg_y(g, ref, hh).start()
        qg_c(g, ref, hh).start()

    def qg_rows(ref, count, send, recv):
        rows = ref.at[0:count, :]
        return rcopy(rows, rows, send, recv, c_dev)

    def qg_near(g, ref):
        qg_rows(ref, quarter, 22, 26).wait_recv()

    def qg_far(g, ref, hh):
        qg_y(g, ref, hh).wait_recv()
        qg_f(g, ref, hh).start()

    def qg_last(g, ref, hh):
        qg_f(g, ref, hh).wait_recv()

    def far_rows(g, ref, compute, between=None):
        def step(hh, carry):
            if between is not None:

                @pl.when(hh == 1)
                def _():
                    between()

            qg_far(g, ref, hh)
            compute(2 * (1 - y) + c, hh)
            qg_last(g, ref, hh)
            compute(2 * (1 - y) + 1 - c, hh)
            return carry

        lax.fori_loop(0, 2, step, 0)

    for hh in range(2):
        if hh == 1:
            pump_end(3, 1)
            pump_mid(3, 2)
        half = halves[hh]
        middle = mid[half, :] + BRANCH_SCALE * (rs_result(0, hh) + vec[4])
        mid[half, :] = middle
        center = middle - jnp.mean(middle, -1, keepdims=True)
        inverse = lax.rsqrt(jnp.mean(center * center, -1, keepdims=True) + EPS)
        scaled = center * inverse
        xhat2[half, :] = scaled
        inv2[half, :] = inverse
        mine_h = rows_at(ten * quarter + hh * (quarter // 2), quarter // 2, quarter // 2)
        hidden[mine_h, :] = (scaled * vec[2] + vec[3]).astype(BF16)
        qg_start(0, hidden, hh)

    pump_end(3, 2)
    ag_finish(2)

    bias_up = jnp.concatenate([bias[2 + i] for i in range(4)], 1)

    def forward_units(which, hh=None):
        rows = rows_at(which * quarter, quarter, quarter)
        if hh is not None:
            rows = rows_at(which * quarter + hh * (quarter // 2), quarter // 2, quarter // 2)
        hq = hidden[rows, :]
        for t in range(width // 256):
            cols = slice(t * 256, (t + 1) * 256)
            pre = mm(hq, w[1, :, cols]) + bias_up[:, cols]
            square = pre * pre
            tanh = jnp.tanh(GELU_A * (pre + GELU_B * (square * pre)))
            half_up = 0.5 + 0.5 * tanh
            act_s[rows, cols] = (pre * half_up).astype(BF16)
            slope = half_up + 0.5 * pre * (1.0 - tanh * tanh) * (
                GELU_A + (3.0 * GELU_A * GELU_B) * square
            )
            dpre[rows, cols] = slope.astype(BF16)

    def grad_block(b, left, right, near):
        rows = slice(0, tokens)
        if near is not None:
            rows = rows_at((y if near else 1 - y) * 2 * quarter, 2 * quarter, 2 * quarter)

        def tile(t, carry):
            cols = rows_at(t * 256, 256, 256)
            part = mm(left[rows, cols], right[rows, :], TN)
            if near is False:
                part = part + gmat[b, cols, :].astype(F32)
            gmat[b, cols, :] = part.astype(BF16)
            return carry

        lax.fori_loop(0, width // 256, tile, 0)

    g_units = (*units[0:3], (2, slice(0, half_cols)))
    right_half = slice(half_cols, width)

    def gx(u, zi):
        b, cols = g_units[u]
        src = gmat.at[b, rows_at((2 * zi + 1 - x) * shard, shard, shard), cols]
        return rcopy(src, xr.at[b, zi, :, cols], 8 + u, 29 + 4 * u + zi, x_dev)

    def line_to(i):
        if i == 0:
            return pair_dev, 0
        return (2 * (is_end * owner_z[0] + is_mid * owner_z[i]) + x, ten), is_end * i + is_mid * 3

    def gz(u, i):
        b, cols = g_units[u]
        dev, slot = line_to(i)
        return rcopy(zs.at[b, i, :, cols], zr.at[b, slot, :, cols], 12 + u, 45 + 4 * u + slot, dev)

    def gz_arrive(u, slot):
        b, cols = g_units[u]
        ref = zr.at[b, slot, :, cols]
        rcopy(ref, ref, 12 + u, 45 + 4 * u + slot, x_dev).wait_recv()

    def g_start(u):
        @pl.when(is_end == 1)
        def _():
            for i in (2, 1, 0):
                gx(u, owner_z[i]).start()

        @pl.when(is_mid == 1)
        def _():
            for i in (0, 2, 1):
                gx(u, owner_z[i]).start()

        gx(u, z).start()

    def x_sum(u, zo):
        b, cols = g_units[u]
        gx(u, zo).wait_recv()
        mine_x = gmat[b, rows_at((2 * zo + x) * shard, shard, shard), cols].astype(F32)
        return mine_x + xr[b, zo, :, cols].astype(F32)

    def end_pump(u, i):
        b, cols = g_units[u]

        @pl.when(is_end == 1)
        def _():
            zs[b, i, :, cols] = x_sum(u, owner_z[i]).astype(BF16)
            gz(u, i).start()

    def mid_pump(u, i):
        b, cols = g_units[u]

        @pl.when(is_mid == 1)
        def _():
            total = x_sum(u, owner_z[i])
            if i > 0:
                gz_arrive(u, i)
                total = total + zr[b, i, :, cols].astype(F32)
            zs[b, i, :, cols] = total.astype(BF16)
            gz(u, i).start()

    def g_finish(u):
        b, cols = g_units[u]
        total = x_sum(u, z)
        for slot in (0, 3):
            gz_arrive(u, slot)
            total = total + zr[b, slot, :, cols].astype(F32)
        gsum[b, :, cols] = total
        if u < 3:
            g_out(u).start()

    def g_out(u):
        b, cols = units[u]
        return pltpu.make_async_copy(gsum.at[b, :, cols], gsum_o.at[b, :, cols], lsem.at[4 + u])

    def g_drain(u):
        b, cols = g_units[u]
        rcopy(xr.at[b, :, :, cols], xr.at[b, :, :, cols], 8 + u, 56, x_dev).wait_send()
        rcopy(zs.at[b, :, :, cols], zs.at[b, :, :, cols], 12 + u, 56, x_dev).wait_send()
        g_out(u).wait()

    def side_rows(zo):
        return gmat.at[2, rows_at(zo * 2 * shard, 2 * shard, 2 * shard), right_half]

    def side_copy(src, i):
        dev, slot = line_to(i)
        return rcopy(src, side_r.at[slot], 28, 65 + slot, dev)

    def side_arrive(slot):
        rcopy(side_r.at[slot], side_r.at[slot], 28, 65 + slot, x_dev).wait_recv()

    def side_start():
        @pl.when(is_end == 1)
        def _():
            for i in (2, 1):
                side_copy(side_rows(owner_z[i]), i).start()

        side_copy(side_rows(owner_z[0]), 0).start()

    def side_middle():
        @pl.when(is_mid == 1)
        def _():
            for i in (2, 1):
                side_arrive(i)
                mine_z = gmat[2, rows_at(owner_z[i] * 2 * shard, 2 * shard, 2 * shard), right_half]
                side_s[i - 1] = (mine_z.astype(F32) + side_r[i].astype(F32)).astype(BF16)
                side_copy(side_s.at[i - 1], i).start()

    def side_x():
        return rcopy(side_xs, side_xr, 29, 69, x_dev)

    def side_cross():
        side_arrive(0)
        side_arrive(3)

        def total(xi):
            at = rows_at(xi * shard, shard, shard)
            got = gmat[2, rows_at((2 * z + xi) * shard, shard, shard), right_half].astype(F32)
            return got + side_r[0, at, :].astype(F32) + side_r[3, at, :].astype(F32)

        side_xs[...] = total(1 - x).astype(BF16)
        side_x().start()
        gsum[2, :, right_half] = total(x)

    def side_finish():
        side_x().wait_recv()
        gsum[2, :, right_half] = gsum[2, :, right_half] + side_xr[...].astype(F32)
        g_out(3).start()

    def backward_units(which):
        rows = rows_at(which * quarter, quarter, quarter)
        gq = dmlp[rows, :]
        for t in range(width // 256):
            cols = slice(t * 256, (t + 1) * 256)
            d_act = mm(gq, w[2, :, cols]).astype(BF16).astype(F32)
            d_low = (dpre[rows, cols].astype(F32) * d_act).astype(BF16)
            dpre[rows, cols] = d_low
            sm[6:7, cols] = sm[6:7, cols] + jnp.sum(d_low.astype(F32), 0, keepdims=True)
        return mm(dpre[rows, :], w[1], NT)

    def branch(which):
        rows = rows_at(which * quarter, quarter, quarter)
        return mm(act_s[rows, :], w[2], NT)

    def near_units(s, carry):
        @pl.when(s == 1)
        def _():
            qg_near(0, hidden)

        forward_units(2 * y + lax.rem(s + c, 2))
        return carry

    lax.fori_loop(0, 2, near_units, 0)
    grad_block(2, dmlp, act_s, True)
    for t in range(width // 256):
        cols = slice(t * 256, (t + 1) * 256)
        normed_t[cols, :] = jnp.transpose(normed[:, cols])
    far_rows(0, hidden, forward_units)
    ag_finish(3)
    rs_pair(1, False, backward_units)
    grad_block(2, dmlp, act_s, False)
    g_start(3)
    side_start()
    rs_pair(1, True, backward_units)
    grad_block(1, hidden, dpre, None)
    g_start(2)
    end_pump(3, 2)
    mid_pump(3, 0)
    def second_norm_back(hh):
        half = halves[hh]
        mine_h = rows_at(ten * quarter + hh * (quarter // 2), quarter // 2, quarter // 2)
        d_hidden = rs_result(1, hh)
        scaled = xhat2[half, :]
        sm[2:3, :] = sm[2:3, :] + jnp.sum(d_hidden * scaled, 0, keepdims=True)
        sm[3:4, :] = sm[3:4, :] + jnp.sum(d_hidden, 0, keepdims=True)
        weighted = d_hidden * vec[2]
        d_mid = cot[mine_h, :] + inv2[half, :] * (
            weighted
            - jnp.mean(weighted, -1, keepdims=True)
            - scaled * jnp.mean(weighted * scaled, -1, keepdims=True)
        )
        fin[1, half, :] = d_mid
        d_attn = (BRANCH_SCALE * d_mid).astype(BF16)
        dattn[mine_h, :] = d_attn
        sm[4:5, :] = sm[4:5, :] + jnp.sum(d_attn.astype(F32), 0, keepdims=True)
        qg_start(1, dattn, hh)

    rs_quad(2, branch, fin.at[0])
    second_norm_back(0)
    end_pump(3, 1)
    quad_far(2, fin.at[0])
    quad_near(2)
    side_middle()
    end_pump(3, 0)
    second_norm_back(1)
    rs_y_start(2)

    def attend_back(i, which_heads, hh=None):
        first, last_row = i * quarter, (i + 1) * quarter
        size = quarter
        rows = slice(first, last_row)
        if hh is not None:
            size = quarter // 2
            rows = rows_at(first + hh * size, size, size)
        for at, group in enumerate(((0, 1), (2,))):
            if group[0] not in which_heads:
                continue
            count = len(group)
            tile = slice(at * 128, (at + 1) * 128)
            d_tile, out_tile = dmix[rows, tile].astype(F32), mixed[rows, tile].astype(F32)
            d_out = []
            for h in group:
                scaled = d_tile * linv[h, rows, :]
                d_out += [jnp.where(low_half, scaled, 0.0) if h == 0 else jnp.where(low_half, 0.0, scaled)]
            d_out = jnp.concatenate(d_out, 0)
            inner = jnp.sum(d_out * jnp.concatenate([out_tile] * count, 0), -1, keepdims=True)
            d_scaled = d_out.astype(BF16)
            heads_here = slice(group[0], group[-1] + 1)
            expo = e_s[heads_here, rows, 0:last_row].reshape(count * size, last_row)
            queries = q_s[heads_here, rows, :].reshape(count * size, 2 * HD)
            d_probs = mm(d_scaled, v_s[at, 0:last_row, :], NT)
            d_scores = (expo.astype(F32) * (d_probs - inner)).astype(BF16)
            d_q = mm(d_scores, k_s[at, 0:last_row, :]) * eighth
            dk_s[at, :, 0:last_row] = dk_s[at, :, 0:last_row] + mm(queries, d_scores, TN)
            dv_s[at, :, 0:last_row] = dv_s[at, :, 0:last_row] + mm(d_scaled, expo, TN)
            if at == 0:
                dqkv[rows, 0:128] = jnp.where(low_half, d_q[0:size], d_q[size:]).astype(BF16)
            else:
                dqkv[rows, 384:512] = jnp.where(low_half, d_q, 0.0).astype(BF16)

    def back_quarters(near, which_heads, fresh, prepare=None):
        def step(s, carry):
            if prepare is not None:
                prepare(s)
            yq = y if near else 1 - y
            which = 2 * yq + lax.rem(s + c, 2)
            if fresh:
                rows = rows_at(which * quarter, quarter, quarter)
                dmix[rows, :] = mm(dattn[rows, :], w[0, :, 512:768]).astype(BF16)
            for i in range(tokens // quarter):

                @pl.when(which == i)
                def _():
                    attend_back(i, which_heads)

            return carry

        lax.fori_loop(0, 2, step, 0)

    def back_far(which, hh):
        rows = rows_at(which * quarter + hh * (quarter // 2), quarter // 2, quarter // 2)
        dmix[rows, :] = mm(dattn[rows, :], w[0, :, 512:768]).astype(BF16)
        for i in range(tokens // quarter):

            @pl.when(which == i)
            def _():
                attend_back(i, (0, 1), hh)

    def near_ready(s):
        @pl.when(s == 1)
        def _():
            qg_near(1, dattn)

    def keys_values(at):
        if at == 0:
            dqkv[:, 128:256] = jnp.transpose(dk_s[0]).astype(BF16)
            dqkv[:, 256:384] = jnp.transpose(dv_s[0]).astype(BF16)
        else:
            d_v = jnp.transpose(dv_s[1]).astype(BF16)
            dqkv[:, 384:512] = jnp.where(low_half, dqkv[:, 384:512], d_v)
            dqkv[:, 640:768] = jnp.transpose(dk_s[1]).astype(BF16)

    def zero_rows(u, zo, send=True):
        cols = rows_at(zo * 2 * shard, 2 * shard, 2 * shard)
        left = normed_t[cols, :]
        if u == 0:
            gmat[0, cols, 0:384] = mm(left, dqkv[:, 0:384]).astype(BF16)
        else:
            g_qkv = mm(left, dqkv[:, 384:768])
            gmat[0, cols, 384:512] = g_qkv[:, 0:128].astype(BF16)
            gmat[0, cols, 512:768] = (g_qkv[:, 128:384] + gproj[cols, :]).astype(BF16)
        if send:
            gx(u, zo).start()

    def zero_unit(u, steps, send=True):
        def step(s, carry):
            odd, half = lax.rem(s, 2), lax.div(s, 2)
            first = is_end * owner_z[2] + is_mid * owner_z[0]
            second = is_end * owner_z[1] + is_mid * owner_z[2]
            third = is_end * owner_z[0] + is_mid * owner_z[1]
            early = (1 - odd) * first + odd * second
            late = (1 - odd) * third + odd * z
            zero_rows(u, (1 - half) * early + half * late, send)
            return carry

        lax.fori_loop(*steps, step, 0)

    back_quarters(True, (0, 1, 2), True, near_ready)
    mid_pump(3, 2)
    mid_pump(2, 0)
    end_pump(2, 2)
    end_pump(2, 1)
    mid_pump(3, 1)
    far_rows(1, dattn, back_far, side_cross)
    keys_values(0)
    zero_unit(0, (0, 4))
    end_pump(2, 0)
    mid_pump(2, 2)
    gproj[...] = jnp.transpose(mm(mixed[...], dattn[...], TN))
    back_quarters(False, (2,), False)
    keys_values(1)
    mid_pump(2, 1)

    def first_back(which):
        rows = rows_at(which * quarter, quarter, quarter)
        d_low = dqkv[rows, :]
        part = mm(d_low, w[0], NT)
        rounded = part.astype(BF16).astype(F32)
        sm[0:1, :] = sm[0:1, :] + jnp.sum(rounded * xhat[rows, :], 0, keepdims=True)
        sm[1:2, :] = sm[1:2, :] + jnp.sum(rounded, 0, keepdims=True)
        sm[7:8, :] = sm[7:8, :] + jnp.sum(d_low.astype(F32), 0, keepdims=True)
        return part


    def first_pumps():
        end_pump(0, 2)
        mid_pump(0, 0)

    rs_quad(3, first_back, xhat2, first_pumps)
    end_pump(0, 1)

    small_c = rcopy(sm, smp, 27, 64, c_dev)
    small_c.start()
    quad_far(3, xhat2)
    rs_y_start(3)
    zero_unit(1, (0, 2), False)
    small_c.wait_recv()
    smx[0, 0:6, :] = sm[0:6, :] + smp[0:6, :]
    smx[0, 6:8, :] = smp[6:8, :]
    small_x = rcopy(smx.at[0], smx.at[1], 24, 61, cross_dev)
    small_x.start()

    @pl.when(is_end == 1)
    def _():
        for i in (2, 1):
            gx(1, owner_z[i]).start()

    @pl.when(is_mid == 1)
    def _():
        for i in (0, 2):
            gx(1, owner_z[i]).start()

    zero_unit(1, (2, 4))
    end_pump(0, 0)
    quad_near(3)
    mid_pump(0, 2)
    small_x.wait_recv()
    smz[z, 0:6, :] = smx[0, 0:6, :] + smx[1, 0:6, :]
    smz[z, 6:8, :] = sm[6:8, :] + smx[1, 6:8, :]

    def small_z(j):
        return rcopy(smz.at[z], smz.at[z], 25, 62, z_dev(j))

    for j in (3, 2, 1):
        small_z(j).start()
    mid_pump(0, 1)
    g_finish(3)
    side_finish()
    g_finish(2)
    for hh in range(2):
        half = halves[hh]
        mid[half, :] = mid[half, :] + BRANCH_SCALE * (rs_result(2, hh) + vec[5])
    put_out = pltpu.make_async_copy(mid, out_o, lsem.at[8])
    put_out.start()
    end_pump(1, 2)
    mid_pump(1, 0)
    end_pump(1, 1)

    def first_norm_back(hh):
        half = halves[hh]
        mine_h = rows_at(ten * quarter + hh * (quarter // 2), quarter // 2, quarter // 2)
        d_normed = rs_result(3, hh)
        scaled = xhat[mine_h, :]
        weighted = d_normed * gain_one
        xhat2[half, :] = fin[1, half, :] + inv1[mine_h, :] * (
            weighted
            - jnp.mean(weighted, -1, keepdims=True)
            - scaled * jnp.mean(weighted * scaled, -1, keepdims=True)
        )

    first_norm_back(0)
    end_pump(1, 0)
    three = rcopy(smz.at[0:3], smz.at[0:3], 25, 62, x_dev)
    three.wait_recv()
    smy[0] = (smz[0] + smz[1]) + (smz[2] + smz[3])
    small_y = rcopy(smy.at[0], smy.at[1], 26, 63, y_dev)
    small_y.start()
    mid_pump(1, 2)
    first_norm_back(1)
    put_grad = pltpu.make_async_copy(xhat2, grad_o, lsem.at[9])
    put_grad.start()
    mid_pump(1, 1)
    for u in range(4):
        ag_drain(u)
    three_sides = side_r.at[0:3]
    rcopy(three_sides, three_sides, 28, 65, x_dev).wait_send()
    side_x().wait_send()
    rcopy(ysend, yrecv, 20, 24, y_dev).wait_send()
    for k in (2, 3):
        for half in range(2):
            rs_core(k, half).wait_send()
    for send in (21, 22, 23):
        qg_rows(hidden, 2 * quarter, send, 26).wait_send()
    small_x.wait_send()
    three.wait_send()
    g_finish(0)
    for u in (3, 2, 0):
        g_drain(u)
    small_y.wait_recv()
    small_c.wait_send()
    sm[0:6, :] = smy[0, 0:6, :] + smy[1, 0:6, :]
    sm[6:8, :] = smy[0, 6:8, :]
    put_small = pltpu.make_async_copy(sm, small_o, lsem.at[10])
    put_small.start()
    g_finish(1)

    g_drain(1)
    small_y.wait_send()
    for made in (put_out, put_grad, put_small):
        made.wait()


def run_block(resid, cotangent, win, wout, bias, vec, rows, n_dp):
    tokens, width = resid.shape
    quarter = tokens // 4
    head_cols = win.shape[2]
    heads = head_cols // HD
    sizes = (tokens, width, quarter, heads, rows)
    vm = pltpu.VMEM
    scratch = [
        vm(win.shape, F32),
        vm(wout.shape, F32),
        vm(bias.shape, F32),
        vm(vec.shape, F32),
        vm((tokens, width), F32),
        vm((tokens, width), F32),
        vm((tokens, 1), F32),
        vm((tokens, width), BF16),
        vm((tokens, width), BF16),
        vm((3, width, width), BF16),
        vm((heads, tokens, 2 * HD), BF16),
        vm((2, tokens, 2 * HD), BF16),
        vm((2, tokens, 2 * HD), BF16),
        vm((heads, tokens, tokens), BF16),
        vm((heads, tokens, 1), F32),
        vm((tokens, 256), BF16),
        vm((2, 2, quarter, width), BF16),
        vm((4, 2, quarter, width), BF16),
        vm((3, quarter, width), F32),
        vm((4, quarter, width), BF16),
        vm((4, quarter, width), BF16),
        vm((quarter, width), F32),
        vm((quarter, width), F32),
        vm((quarter, 1), F32),
        vm((width, tokens), BF16),
        vm((tokens, width), BF16),
        vm((tokens, width), BF16),
        vm((tokens, width), BF16),
        vm((tokens, width), BF16),
        vm((tokens, 256), BF16),
        vm((2, 2 * HD, tokens), F32),
        vm((2, 2 * HD, tokens), F32),
        vm((tokens, width), BF16),
        vm((width, 256), F32),
        vm((3, width, width), BF16),
        vm((3, 4, rows, width), BF16),
        vm((3, 3, rows, width), BF16),
        vm((3, 4, rows, width), BF16),
        vm((4, 2 * rows, width // 2), BF16),
        vm((2, 2 * rows, width // 2), BF16),
        vm((rows, width // 2), BF16),
        vm((rows, width // 2), BF16),
        vm((3, rows, width), F32),
        vm((8, width), F32),
        vm((8, width), F32),
        vm((2, 8, width), F32),
        vm((4, 8, width), F32),
        vm((2, 8, width), F32),
        pltpu.SemaphoreType.DMA((13,)),
        pltpu.SemaphoreType.DMA((30,)),
        pltpu.SemaphoreType.DMA((70,)),
    ]
    return pl.pallas_call(
        functools.partial(block_kernel, sizes),
        out_shape=(
            jax.ShapeDtypeStruct((quarter, width), F32),
            jax.ShapeDtypeStruct((quarter, width), F32),
            jax.ShapeDtypeStruct((3, rows, width), F32),
            jax.ShapeDtypeStruct((8, width), F32),
        ),
        in_specs=[pl.BlockSpec(memory_space=pl.ANY)] * 6,
        out_specs=[pl.BlockSpec(memory_space=pl.ANY)] * 4,
        scratch_shapes=scratch,
        compiler_params=pltpu.CompilerParams(
            collective_id=1, has_side_effects=True, vmem_limit_bytes=62 << 20
        ),
        name="block",
    )(resid, cotangent, win, wout, bias, vec)


BLOCK_ZERO = (((0, 128), (384, 448)), ((128, 256), (640, 704)), ((256, 384), (448, 512)), ((512, 640), (704, 768)))


def adam_kernel(hc, *refs):
    passed_h, gsum_h, small_h = refs[0:2], refs[2], refs[3]
    in_h, out_h, bias_h, vec_h = refs[4:7], refs[7:10], refs[10:13], refs[13:16]
    passed_o, in_o, out_o, bias_o, vec_o = refs[16:18], refs[18:21], refs[21:24], refs[24:27], refs[27:30]
    vin, vout, vbias, vvec, rin, rout, rbias, rvec, gsum, small, passed, sems = refs[30:42]

    def copy(src, dst, sem):
        pltpu.make_async_copy(src, dst, sems.at[sem]).start()

    def wait(ref, sem):
        pltpu.make_async_copy(ref, ref, sems.at[sem]).wait()

    def columns(ref, rows, kind):
        return jnp.concatenate([ref[rows + (slice(a, b),)] for a, b in BLOCK_ZERO[kind]], 1)

    every = slice(None)
    kinds_in = (3, 4, 5, 6, 0, 1, 2)
    copy(gsum_h.at[1], gsum.at[1], 0)
    for i in kinds_in:
        if i == 5:
            for a in range(2):
                copy(passed_h[a], passed.at[a], 18)
        for a in range(3):
            copy(in_h[a].at[i], vin.at[i, a], 3 + i)
        if i == 6:
            copy(gsum_h.at[0], gsum.at[0], 1)
    copy(small_h, small, 15)
    for a in range(3):
        copy(bias_h[a], vbias.at[a], 16)
        copy(vec_h[a], vvec.at[a], 17)
    copy(gsum_h.at[2], gsum.at[2], 2)
    for i in range(5):
        for a in range(3):
            copy(out_h[a].at[i], vout.at[i, a], 10 + i)

    wait(gsum.at[1], 0)
    for i in kinds_in:
        wait(vin.at[i], 3 + i)
        if i == 0:
            wait(gsum.at[0], 1)
        part = columns(gsum, (0, every), i) if i < 3 else gsum[1, :, (i - 3) * hc : (i - 2) * hc]
        new = adam_step(vin[i, 0], vin[i, 1], vin[i, 2], part, 0.5 * D ** (-0.5), DECAY)
        for a in range(3):
            rin[i, a] = new[a]
            copy(rin.at[i, a], in_o[a].at[i], 19)
    wait(passed, 18)
    for a in range(2):
        copy(passed.at[a], passed_o[a], 23)
    wait(small, 15)
    wait(vbias, 16)
    wait(vvec, 17)
    for i in range(6):
        new = adam_step(vvec[0, i], vvec[1, i], vvec[2, i], small[i : i + 1, :], SMALL_RATE, 0.0)
        for a in range(3):
            rvec[a, i] = new[a]
        if i < 2:
            part = columns(small, (slice(7, 8),), 2 * i)
        else:
            part = small[6:7, (i - 2) * hc : (i - 1) * hc]
        new = adam_step(vbias[0, i], vbias[1, i], vbias[2, i], part, SMALL_RATE, 0.0)
        for a in range(3):
            rbias[a, i] = new[a]
    for a in range(3):
        copy(rbias.at[a], bias_o[a], 20)
        copy(rvec.at[a], vec_o[a], 21)
    wait(gsum.at[2], 2)
    for i in range(5):
        wait(vout.at[i], 10 + i)
        part = columns(gsum, (0, every), 3) if i == 0 else gsum[2, :, (i - 1) * hc : i * hc]
        part = jnp.transpose(part)
        new = adam_step(vout[i, 0], vout[i, 1], vout[i, 2], part, 2.0 * D ** (-0.5), DECAY)
        for a in range(3):
            rout[i, a] = new[a]
            copy(rout.at[i, a], out_o[a].at[i], 22)
    for ref, sem in ((rin, 19), (rbias, 20), (rvec, 21), (rout, 22), (passed, 23)):
        wait(ref, sem)


def run_adam(*operands):
    hc = operands[4].shape[2]
    out_rows, _, g_sum, small = operands[0:4]
    shapes = [out_rows, out_rows, *operands[4:16]]
    hbm = pl.BlockSpec(memory_space=pl.ANY)
    kinds_in, kinds_out = operands[4].shape, operands[7].shape
    small_bias, small_vec = operands[10].shape, operands[13].shape
    big = [
        pltpu.VMEM((kinds_in[0], 3, *kinds_in[1:]), F32),
        pltpu.VMEM((kinds_out[0], 3, *kinds_out[1:]), F32),
        pltpu.VMEM((3, *small_bias), F32),
        pltpu.VMEM((3, *small_vec), F32),
    ]
    return pl.pallas_call(
        functools.partial(adam_kernel, hc),
        out_shape=[jax.ShapeDtypeStruct(a.shape, F32) for a in shapes],
        in_specs=[hbm] * 16,
        out_specs=[hbm] * 14,
        scratch_shapes=big * 2
        + [pltpu.VMEM(g_sum.shape, F32), pltpu.VMEM(small.shape, F32)]
        + [pltpu.VMEM((2, *out_rows.shape), F32), pltpu.SemaphoreType.DMA((24,))],
        compiler_params=pltpu.CompilerParams(vmem_limit_bytes=62 << 20),
        name="adam",
    )(*operands)


def fused_shards(
    resid,
    cotangent,
    master_in,
    moment1_in,
    moment2_in,
    master_out,
    moment1_out,
    moment2_out,
    master_bias,
    moment1_bias,
    moment2_bias,
    master_vec,
    moment1_vec,
    moment2_vec,
):
    rows = master_in.shape[1]
    hc = master_in.shape[3]
    turned = [jnp.transpose(a[0], (1, 0, 2)) for a in (master_in, moment1_in, moment2_in)]
    plain = [a[0] for a in (master_out, moment1_out, moment2_out)]
    biases = [a.reshape(6, 1, hc) for a in (master_bias, moment1_bias, moment2_bias)]
    vectors = [a.reshape(6, 1, D) for a in (master_vec, moment1_vec, moment2_vec)]
    sums = run_block(
        resid, cotangent, turned[0], plain[0], biases[0], vectors[0], rows, lax.axis_size("dp")
    )
    new = run_adam(*sums, *turned, *plain, *biases, *vectors)
    return (
        new[0],
        new[1],
        *[jnp.transpose(a, (1, 0, 2))[None] for a in new[2:5]],
        *[a[None] for a in new[5:8]],
        *[a.reshape(1, 6, hc) for a in new[8:11]],
        *[a.reshape(1, 6, D) for a in new[11:14]],
    )


def solution(mesh):
    fused = mesh.shape["dp"] == 8 and mesh.shape["tensor"] == 4
    return jax.shard_map(
        fused_shards if fused else shards,
        mesh=mesh,
        in_specs=(
            P("dp", None),
            P("dp", None),
            P(None, "dp", None, "tensor"),
            P(None, "dp", None, "tensor"),
            P(None, "dp", None, "tensor"),
            P(None, None, "tensor", "dp"),
            P(None, None, "tensor", "dp"),
            P(None, None, "tensor", "dp"),
            P(None, None, "tensor"),
            P(None, None, "tensor"),
            P(None, None, "tensor"),
            P(),
            P(),
            P(),
        ),
        out_specs=(
            P(("dp", "tensor"), None),
            P(("dp", "tensor"), None),
            P(None, "dp", None, "tensor"),
            P(None, "dp", None, "tensor"),
            P(None, "dp", None, "tensor"),
            P(None, None, "tensor", "dp"),
            P(None, None, "tensor", "dp"),
            P(None, None, "tensor", "dp"),
            P(None, None, "tensor"),
            P(None, None, "tensor"),
            P(None, None, "tensor"),
            P(),
            P(),
            P(),
        ),
        check_vma=False,
    )
```
